32 devices in a mesh: outer: 8 (over z, x), inner: 4 (over y, core).
Axes of the slice: x: 2, y: 2, z: 4, core: 2. Of those that a mesh axis runs over, the one named last changes fastest.
Arguments:
- tokens: bfloat16 [4096, 1024], P(('outer', 'inner')), may hold values from -6 to 6
- router_weight: bfloat16 [1024, 32], replicated, may hold values from -0.1875 to 0.1875
- in_weight: bfloat16 [32, 1024, 4096], P(('outer', 'inner')), may hold values from -0.1875 to 0.1875
- out_weight: bfloat16 [32, 4096, 1024], P(('outer', 'inner')), may hold values from -0.09375 to 0.09375
- expert_ids: int32 [4096, 2], P(('outer', 'inner')), may hold values from 0 to 31, as said below
- slot_ids: int32 [4096, 2], P(('outer', 'inner')), may hold values from 0 to 12, as said below
- cotangent: bfloat16 [4096, 1024], P(('outer', 'inner')), may hold values from -6 to 6
Outputs:
- mixed: bfloat16 [4096, 1024], P(('outer', 'inner'))
- grad_tokens: bfloat16 [4096, 1024], P(('outer', 'inner'))
- grad_router: float32 [1024, 32], replicated
The draws below stay inside these ranges and needn't reach their ends.
Inputs may be any that keep to these rules, and one draw needn't show every extreme that they name: `expert_ids`: the two ids of a token differ. slot_ids[t, k] is the number of earlier choices naming the same expert among the rows of the same device, all first choices in token order counted before all second choices, capped at 12; the value 12 marks a dropped choice.
All inputs are finite; a program needn't handle non-finite values.
Results may differ from the reference program's by a relative error of at most 0.017.
Values may be sent and summed in bfloat16 or wider, within the bound.
No kernel may reach another device: no remote copies, remote signals or barrier semaphores. Data moves between devices by JAX's collectives and lax.ppermute only.
A program may use at most 64 MiB of HBM per device.

```python
import jax
import jax.numpy as jnp
from jax import lax

D = 1024
FF = 4096
TOK_DEV = 128
EXPERTS = 32
TOKENS = 4096
CAP = 12


def routing(key):
    blocks = TOKENS // TOK_DEV
    expert_order = jax.random.permutation(jax.random.fold_in(key, 101), EXPERTS)
    first_pick = jax.random.randint(jax.random.fold_in(key, 102), (blocks, TOK_DEV), 0, EXPERTS)
    other_pick = jax.random.randint(jax.random.fold_in(key, 103), (blocks, TOK_DEV), 0, EXPERTS)
    primary = expert_order[jnp.minimum(first_pick, other_pick)]
    crowded = jax.random.randint(jax.random.fold_in(key, 104), (), 0, EXPERTS)
    leading = jnp.arange(TOK_DEV) <= CAP
    primary = jnp.where(leading[None, :], crowded, primary)
    offsets = jax.random.randint(jax.random.fold_in(key, 105), (blocks, TOK_DEV), 1, EXPERTS)
    secondary = (primary + offsets) % EXPERTS
    sequence = jnp.concatenate([primary, secondary], axis=1)
    member = (sequence[:, :, None] == jnp.arange(EXPERTS)).astype(jnp.int32)
    position = jnp.sum((jnp.cumsum(member, axis=1) - member) * member, axis=2)
    position = jnp.minimum(position, CAP)
    chosen = jnp.stack([primary, secondary], axis=2).reshape(TOKENS, 2)
    slot_table = jnp.stack([position[:, :TOK_DEV], position[:, TOK_DEV:]], axis=2).reshape(TOKENS, 2)
    return (chosen.astype(jnp.int32), slot_table.astype(jnp.int32))


def draw_expert_ids(key, part):
    return routing(key)[0]


def draw_slot_ids(key, part):
    return routing(key)[1]


def block_levels(stream_key, shape, split, low, largest):
    loudness = 1.0
    for axis_at, shards_of in split:
        steps = jax.random.uniform(jax.random.fold_in(jax.random.fold_in(stream_key, 6), axis_at), (shards_of,), jnp.float32, low / len(split), largest / len(split))
        loudness = loudness * jnp.repeat(jnp.exp(steps), shape[axis_at] // shards_of).reshape((-1,) + (1,) * (len(shape) - 1 - axis_at))
    return loudness


def normal_values(rng, dims, scale, reach, split=(), kind=jnp.bfloat16):
    factor_of = block_levels(rng, dims, split, -0.22, 0.18) if split else 1.0
    drawn = jax.random.normal(rng, dims, jnp.float32) * scale * factor_of
    return jnp.minimum(jnp.maximum(drawn, -reach), reach).astype(kind)


def setup_inputs(seed: int = 0) -> dict:
    splits = jax.random.split(jax.random.key(seed), 8)
    return {
        "tokens": normal_values(splits[0], (TOKENS, D), 1.0, 6.0, ((0, 32),)),
        "router_weight": normal_values(splits[1], (D, EXPERTS), D ** -0.5, 0.1875),
        "in_weight": normal_values(splits[2], (EXPERTS, D, FF), D ** -0.5, 0.1875, ((0, 32),)),
        "out_weight": normal_values(splits[3], (EXPERTS, FF, D), FF ** -0.5, 0.09375, ((0, 32),)),
        "expert_ids": draw_expert_ids(jax.random.fold_in(splits[7], 71), 0),
        "slot_ids": draw_slot_ids(jax.random.fold_in(splits[7], 71), 0),
        "cotangent": normal_values(splits[6], (TOKENS, D), 1.0, 6.0, ((0, 32),)),
    }


def reference(tokens, router_weight, in_weight, out_weight, expert_ids, slot_ids, cotangent):
    sources = TOKENS // TOK_DEV
    kept_mask = slot_ids < CAP
    logits = jnp.dot(tokens, router_weight, preferred_element_type=jnp.float32)
    picked = jnp.take_along_axis(logits, expert_ids, axis=1)
    gate_pair = jnp.stack([jax.nn.sigmoid(picked[:, 0] - picked[:, 1]), jax.nn.sigmoid(picked[:, 1] - picked[:, 0])], axis=1)
    scaled = (gate_pair[:, :, None] * cotangent.astype(jnp.float32)[:, None, :]).astype(jnp.bfloat16)
    anchor = (jnp.arange(TOKENS, dtype=jnp.int32) // TOK_DEV)[:, None]
    slot_total = EXPERTS * sources * CAP
    target = jnp.where(kept_mask, (expert_ids * sources + anchor) * CAP + slot_ids, slot_total).astype(jnp.int32)
    choice_index = jnp.arange(2 * TOKENS, dtype=jnp.int32)
    slot_table = jnp.full((slot_total + 1,), 2 * TOKENS, jnp.int32).at[target.reshape(-1)].set(choice_index)
    slot_table = slot_table[:slot_total].reshape(EXPERTS, sources * CAP)
    zero_row = jnp.zeros((1, D), jnp.bfloat16)
    doubled = jnp.concatenate([jnp.repeat(tokens, 2, axis=0), zero_row], axis=0)
    grad_flat = jnp.concatenate([scaled.reshape(2 * TOKENS, D), zero_row], axis=0)

    def expert(operands):
        slot_index, weight_in, weight_out = operands
        arrived = doubled[slot_index]
        grad_rows = grad_flat[slot_index]
        pre_act = jnp.dot(arrived, weight_in, preferred_element_type=jnp.float32)
        hidden = jnp.maximum(pre_act, 0.0).astype(jnp.bfloat16)
        produced = jnp.dot(hidden, weight_out, preferred_element_type=jnp.float32).astype(jnp.bfloat16)
        back_grad = jnp.dot(grad_rows, weight_out.T, preferred_element_type=jnp.float32)
        back_grad = jnp.where(pre_act > 0, back_grad, 0.0).astype(jnp.bfloat16)
        returned = jnp.dot(back_grad, weight_in.T, preferred_element_type=jnp.float32).astype(jnp.bfloat16)
        return produced, returned

    produced, returned = lax.map(expert, (slot_table, in_weight, out_weight))
    produced_flat = jnp.concatenate([produced.reshape(slot_total, D), zero_row], axis=0)
    returned_flat = jnp.concatenate([returned.reshape(slot_total, D), zero_row], axis=0)
    y_choice = produced_flat[target].astype(jnp.float32)
    dx_choice = returned_flat[target].astype(jnp.float32)
    mixed = jnp.sum(gate_pair[:, :, None] * y_choice, axis=1).astype(jnp.bfloat16)
    actions = jnp.sum(y_choice * cotangent.astype(jnp.float32)[:, None, :], axis=2)
    logit_slope = gate_pair[:, 0] * gate_pair[:, 1] * (actions[:, 0] - actions[:, 1])
    onehot = (expert_ids[:, :, None] == jnp.arange(EXPERTS, dtype=jnp.int32)).astype(jnp.float32)
    logit_grads = (onehot[:, 0] - onehot[:, 1]) * logit_slope[:, None]
    router_back = jnp.dot(logit_grads, router_weight.astype(jnp.float32).T, precision=lax.Precision.HIGHEST)
    grad_tokens = (dx_choice[:, 0] + dx_choice[:, 1] + router_back).astype(jnp.bfloat16)
    grad_router = jnp.dot(tokens.astype(jnp.float32).T, logit_grads, precision=lax.Precision.HIGHEST) / TOK_DEV
    return mixed, grad_tokens, grad_router
```

```python
import jax
import jax.numpy as jnp
from jax import lax
from jax.sharding import PartitionSpec as P


def expert_block(arrived, grad_rows, in_weight, out_weight):
    pre_act = jnp.einsum("slcd,ldf->slcf", arrived, in_weight, preferred_element_type=jnp.float32)
    hidden = jnp.maximum(pre_act, 0.0).astype(jnp.bfloat16)
    produced = jnp.einsum(
        "slcf,lfd->slcd", hidden, out_weight, preferred_element_type=jnp.float32
    ).astype(jnp.bfloat16)
    back_grad = jnp.einsum(
        "slcd,lfd->slcf", grad_rows, out_weight, preferred_element_type=jnp.float32
    )
    back_grad = jnp.where(pre_act > 0, back_grad, 0.0).astype(jnp.bfloat16)
    returned = jnp.einsum(
        "slcf,ldf->slcd", back_grad, in_weight, preferred_element_type=jnp.float32
    ).astype(jnp.bfloat16)
    return (produced, returned)


def on_device(tokens, router_weight, in_weight, out_weight, expert_ids, slot_ids, cotangent):
    tok_rows, model_width = tokens.shape
    experts = router_weight.shape[1]
    local_count = in_weight.shape[0]
    capacity = 3 * tok_rows // experts
    outer_count = lax.axis_size("outer")
    inner_count = lax.axis_size("inner")
    source_count = outer_count * inner_count
    slot_total = experts * capacity
    kept_mask = slot_ids < capacity
    logits = jnp.dot(tokens, router_weight, preferred_element_type=jnp.float32)
    onehot = (expert_ids[:, :, None] == jnp.arange(experts, dtype=jnp.int32)).astype(jnp.float32)
    picked = jnp.einsum("tke,te->tk", onehot, logits, precision=lax.Precision.HIGHEST)
    gate_pair = jnp.stack(
        [jax.nn.sigmoid(picked[:, 0] - picked[:, 1]), jax.nn.sigmoid(picked[:, 1] - picked[:, 0])],
        axis=1,
    )
    scaled = (gate_pair[:, :, None] * cotangent[:, None, :].astype(jnp.float32)).astype(
        jnp.bfloat16
    )
    target = jnp.where(kept_mask, expert_ids * capacity + slot_ids, slot_total)
    placement = (target[:, :, None] == jnp.arange(slot_total, dtype=jnp.int32)).astype(jnp.bfloat16)
    sent_tokens = jnp.einsum(
        "tkf,td->fd", placement, tokens, preferred_element_type=jnp.float32
    ).astype(jnp.bfloat16)
    sent_grads = jnp.einsum(
        "tkf,tkd->fd", placement, scaled, preferred_element_type=jnp.float32
    ).astype(jnp.bfloat16)
    outbound = (
        sent_tokens.reshape(experts, capacity, model_width),
        sent_grads.reshape(experts, capacity, model_width),
    )
    arrived = lax.all_to_all(
        outbound[0], ("outer", "inner"), split_axis=0, concat_axis=0, tiled=True
    )
    grad_rows = lax.all_to_all(
        outbound[1], ("outer", "inner"), split_axis=0, concat_axis=0, tiled=True
    )
    pieces = arrived.shape[1]
    shaped = (source_count, local_count, pieces, model_width)
    produced, returned = expert_block(
        arrived.reshape(shaped), grad_rows.reshape(shaped), in_weight, out_weight
    )
    back_shape = (source_count * local_count, pieces, model_width)
    produced_back = lax.all_to_all(
        produced.reshape(back_shape), ("outer", "inner"), split_axis=0, concat_axis=0, tiled=True
    ).reshape(slot_total, model_width)
    returned_back = lax.all_to_all(
        returned.reshape(back_shape), ("outer", "inner"), split_axis=0, concat_axis=0, tiled=True
    ).reshape(slot_total, model_width)
    y_choice = jnp.einsum(
        "tkf,fd->tkd", placement, produced_back, preferred_element_type=jnp.float32
    )
    dx_choice = jnp.einsum(
        "tkf,fd->tkd", placement, returned_back, preferred_element_type=jnp.float32
    )
    mixed = jnp.sum(gate_pair[:, :, None] * y_choice, axis=1).astype(jnp.bfloat16)
    actions = jnp.sum(y_choice * cotangent[:, None, :].astype(jnp.float32), axis=2)
    logit_slope = gate_pair[:, 0] * gate_pair[:, 1] * (actions[:, 0] - actions[:, 1])
    logit_grads = (onehot[:, 0] - onehot[:, 1]) * logit_slope[:, None]
    router_back = jnp.dot(
        logit_grads, router_weight.astype(jnp.float32).T, precision=lax.Precision.HIGHEST
    )
    grad_tokens = (dx_choice[:, 0] + dx_choice[:, 1] + router_back).astype(jnp.bfloat16)
    partial_grad = lax.dot_general(
        logit_grads,
        tokens.astype(jnp.float32),
        (((0,), (0,)), ((), ())),
        precision=lax.Precision.HIGHEST,
    ).reshape(source_count, 8, experts * model_width // (8 * source_count))
    terms = lax.all_to_all(
        partial_grad, ("outer", "inner"), split_axis=0, concat_axis=0, tiled=True
    )
    own_rows = jnp.sum(terms, axis=0) * (1.0 / tok_rows)
    all_rows = lax.all_to_all(
        jnp.broadcast_to(own_rows[None], terms.shape),
        ("outer", "inner"),
        split_axis=0,
        concat_axis=0,
        tiled=True,
    )
    grad_router = all_rows.reshape(experts, model_width).T
    return (mixed, grad_tokens, grad_router)


def solution(mesh):
    placed = (
        P(("outer", "inner"), None),
        P(),
        P(("outer", "inner"), None, None),
        P(("outer", "inner"), None, None),
        P(("outer", "inner"), None),
        P(("outer", "inner"), None),
        P(("outer", "inner"), None),
    )
    return jax.shard_map(
        on_device,
        mesh=mesh,
        in_specs=placed,
        out_specs=(P(("outer", "inner"), None), P(("outer", "inner"), None), P()),
        check_vma=False,
    )
```

```python
import functools

import jax
import jax.numpy as jnp
from jax import lax
from jax.experimental import pallas as pl
from jax.experimental.pallas import tpu as pltpu
from jax.sharding import PartitionSpec as P

AXES = ("outer", "inner")
F32 = jnp.float32
BF16 = jnp.bfloat16
GROUP = 8
VMEM_BYTES = 40 * 1024 * 1024


class Layout:
    def __init__(self, capacity, model_width):
        self.full, left = divmod(capacity, GROUP)
        self.rest = 0
        if left:
            self.rest = 1
            while self.rest < left:
                self.rest *= 2
        if self.rest == GROUP:
            self.full, self.rest = self.full + 1, 0
        self.capacity = capacity
        self.width = model_width
        self.cuts = GROUP // self.rest if self.rest else 1
        self.piece = model_width // self.cuts
        self.base = self.full * model_width
        self.columns = self.base + (self.piece if self.rest else 0)
        self.rows = self.full * GROUP + self.rest


def dot(a, b):
    return jnp.dot(a, b, preferred_element_type=F32)


def dot_nt(a, b):
    return lax.dot_general(a, b, (((1,), (1,)), ((), ())), preferred_element_type=F32)


def iota(shape, dim):
    return lax.broadcasted_iota(jnp.int32, shape, dim)


def as_column(row):
    count = row.shape[1]
    eye = iota((count, count), 0) == iota((count, count), 1)
    return jnp.sum(jnp.where(eye, row, 0.0), axis=1, keepdims=True)


def as_row(column):
    count = column.shape[0]
    eye = iota((count, count), 0) == iota((count, count), 1)
    return jnp.sum(jnp.where(eye, column, 0.0), axis=0, keepdims=True)


def targets(lay, ids, slots):
    found = []
    kept = slots < lay.capacity
    for group in range(lay.full):
        inside = kept & (slots >= group * GROUP) & (slots < (group + 1) * GROUP)
        found.append(jnp.where(inside, ids * GROUP + slots - group * GROUP, -1))
    if lay.rest:
        inside = kept & (slots >= lay.full * GROUP)
        found.append(jnp.where(inside, ids * GROUP + slots - lay.full * GROUP, -1))
    return found


def shifted(row, by):
    return jnp.where(row >= 0, row + by, -1)


def place(lay, row_targets, values, out_ref):
    count = out_ref.shape[0]
    toks = values[0].shape[0]
    row_at = iota((count, toks), 0)
    stacked = jnp.concatenate(values, axis=0) if len(values) > 1 else values[0]

    def onehot(rows):
        hit = functools.reduce(jnp.logical_or, [row_at == row for row in rows])
        return jnp.where(hit, 1.0, 0.0).astype(BF16)

    for group in range(lay.full):
        hot = [onehot([t[group] for t in ranks]) for ranks in row_targets]
        hot = jnp.concatenate(hot, axis=1) if len(hot) > 1 else hot[0]
        out_ref[:, group * lay.width : (group + 1) * lay.width] = dot(hot, stacked).astype(BF16)
    if lay.rest:
        hot, pieces = [], []
        for cut in range(lay.cuts):
            for ranks in row_targets:
                hot.append(onehot([shifted(t[lay.full], cut * lay.rest) for t in ranks]))
            pieces.append(stacked[:, cut * lay.piece : (cut + 1) * lay.piece])
        out_ref[:, lay.base :] = dot(
            jnp.concatenate(hot, axis=1), jnp.concatenate(pieces, axis=0)
        ).astype(BF16)


def pick(lay, ranks, message_ref):
    count = message_ref.shape[0]
    toks = ranks[0][0].shape[0]
    row_at = iota((toks, count), 1)

    def onehot(rows):
        hit = functools.reduce(jnp.logical_or, [row_at == row for row in rows])
        return jnp.where(hit, 1.0, 0.0).astype(BF16)

    whole = [onehot([t[group] for t in ranks]) for group in range(lay.full)]
    pieces = []
    for cut in range(lay.cuts):
        left = cut * lay.piece
        total = None
        for group in range(lay.full):
            start = group * lay.width + left
            term = dot(whole[group], message_ref[:, start : start + lay.piece])
            total = term if total is None else total + term
        if lay.rest:
            hot = onehot([shifted(t[lay.full], cut * lay.rest) for t in ranks])
            term = dot(hot, message_ref[:, lay.base : lay.base + lay.piece])
            total = term if total is None else total + term
        pieces.append(total)
    return jnp.concatenate(pieces, axis=1) if len(pieces) > 1 else pieces[0]


def rest_selection(lay, count):
    small = count // GROUP * lay.rest
    row = iota((small, count), 0)
    col = iota((small, count), 1)
    shift = lay.rest.bit_length() - 1
    home = lax.shift_right_logical(row, shift) * GROUP + (row & (lay.rest - 1))
    return [jnp.where(col == home + cut * lay.rest, 1.0, 0.0).astype(BF16) for cut in range(lay.cuts)]


def unpack(lay, message_ref, out_ref):
    count = message_ref.shape[0]
    for group in range(lay.full):
        out_ref[group * count : (group + 1) * count, :] = message_ref[
            :, group * lay.width : (group + 1) * lay.width
        ]
    if lay.rest:
        tail = message_ref[:, lay.base :]
        for cut, chosen in enumerate(rest_selection(lay, count)):
            out_ref[lay.full * count :, cut * lay.piece : (cut + 1) * lay.piece] = dot(
                chosen, tail
            ).astype(BF16)


def pack(lay, rows_ref, message_ref):
    count = message_ref.shape[0]
    for group in range(lay.full):
        message_ref[:, group * lay.width : (group + 1) * lay.width] = rows_ref[
            group * count : (group + 1) * count, :
        ].astype(BF16)
    if lay.rest:
        total = None
        for cut, chosen in enumerate(rest_selection(lay, count)):
            part = rows_ref[
                lay.full * count :, cut * lay.piece : (cut + 1) * lay.piece
            ].astype(BF16)
            term = lax.dot_general(
                chosen, part, (((0,), (0,)), ((), ())), preferred_element_type=F32
            )
            total = term if total is None else total + term
        message_ref[:, lay.base :] = total.astype(BF16)


def send_tokens_kernel(lay, ids_ref, slots_ref, tokens_ref, out_ref):
    first = targets(lay, ids_ref[0:1, :], slots_ref[0:1, :])
    second = targets(lay, ids_ref[1:2, :], slots_ref[1:2, :])
    place(lay, [[first, second]], [tokens_ref[...]], out_ref)


def send_grads_kernel(
    lay, ids_ref, slots_ref, tokens_ref, router_ref, cot_ref, out_ref, gates_ref
):
    logits = dot_nt(router_ref[...], tokens_ref[...])
    expert_at = iota(logits.shape, 0)
    picked = [
        jnp.sum(jnp.where(expert_at == ids_ref[k : k + 1, :], logits, 0.0), axis=0, keepdims=True)
        for k in range(2)
    ]
    gates = [jax.nn.sigmoid(picked[0] - picked[1]), jax.nn.sigmoid(picked[1] - picked[0])]
    gates_ref[0:1, :] = gates[0]
    gates_ref[1:2, :] = gates[1]
    cot = cot_ref[...].astype(F32)
    scaled = [(as_column(gate) * cot).astype(BF16) for gate in gates]
    ranks = [[targets(lay, ids_ref[k : k + 1, :], slots_ref[k : k + 1, :])] for k in range(2)]
    place(lay, ranks, scaled, out_ref)


def forward_kernel(lay, message_ref, win_ref, wout_ref, out_ref, hidden_ref, rows_ref, total_ref):
    step = pl.program_id(0)

    @pl.when(step == 0)
    def _():
        unpack(lay, message_ref, rows_ref)

    hidden = jnp.maximum(dot(rows_ref[...], win_ref[0]), 0.0).astype(BF16)
    hidden_ref[...] = hidden
    term = dot(hidden, wout_ref[0])

    @pl.when(step == 0)
    def _():
        total_ref[...] = term

    @pl.when(step > 0)
    def _():
        total_ref[...] += term

    @pl.when(step == pl.num_programs(0) - 1)
    def _():
        pack(lay, total_ref, out_ref)


def backward_kernel(lay, message_ref, hidden_ref, win_ref, wout_ref, out_ref, rows_ref, total_ref):
    step = pl.program_id(0)

    @pl.when(step == 0)
    def _():
        unpack(lay, message_ref, rows_ref)

    back = dot_nt(rows_ref[...], wout_ref[0])
    back = jnp.where(hidden_ref[...].astype(F32) > 0.0, back, 0.0).astype(BF16)
    term = dot_nt(back, win_ref[0])

    @pl.when(step == 0)
    def _():
        total_ref[...] = term

    @pl.when(step > 0)
    def _():
        total_ref[...] += term

    @pl.when(step == pl.num_programs(0) - 1)
    def _():
        pack(lay, total_ref, out_ref)


def column_targets(lay, ids_ref, slots_ref):
    ids = [as_column(ids_ref[k : k + 1, :].astype(F32)).astype(jnp.int32) for k in range(2)]
    slots = [as_column(slots_ref[k : k + 1, :].astype(F32)).astype(jnp.int32) for k in range(2)]
    return ids, [targets(lay, ids[k], slots[k]) for k in range(2)]


def split_in_two(x):
    high = x.astype(BF16)
    return high, (x - high.astype(F32)).astype(BF16)


def mix_kernel(
    lay,
    ids_ref,
    slots_ref,
    gates_ref,
    message_ref,
    cot_ref,
    tokens_ref,
    router_ref,
    mixed_ref,
    back_ref,
    partial_ref,
):
    experts = router_ref.shape[0]
    toks = tokens_ref.shape[0]
    ids, ranks = column_targets(lay, ids_ref, slots_ref)
    gates = [as_column(gates_ref[k : k + 1, :]) for k in range(2)]
    cot = cot_ref[...].astype(F32)
    choice = [pick(lay, [ranks[k]], message_ref) for k in range(2)]
    mixed_ref[...] = (gates[0] * choice[0] + gates[1] * choice[1]).astype(BF16)
    actions = [jnp.sum(choice[k] * cot, axis=1, keepdims=True) for k in range(2)]
    slope = gates[0] * gates[1] * (actions[0] - actions[1])

    expert_at = iota((toks, experts), 1)
    signs = jnp.where(expert_at == ids[0], 1.0, 0.0) - jnp.where(expert_at == ids[1], 1.0, 0.0)
    high, low = split_in_two(signs * slope)
    router = router_ref[...]
    back_ref[...] = dot(high, router) + dot(low, router)

    expert_at = iota((experts, toks), 0)
    signs = jnp.where(expert_at == ids_ref[0:1, :], 1.0, 0.0) - jnp.where(
        expert_at == ids_ref[1:2, :], 1.0, 0.0
    )
    high, low = split_in_two(signs * as_row(slope))
    tokens = tokens_ref[...]
    partial_ref[...] = dot(high, tokens) + dot(low, tokens)


def grad_kernel(lay, ids_ref, slots_ref, message_ref, back_ref, out_ref):
    _, ranks = column_targets(lay, ids_ref, slots_ref)
    out_ref[...] = (pick(lay, ranks, message_ref) + back_ref[...]).astype(BF16)


def call(kernel, out_shape, flops, args):
    moved = sum(a.size * a.dtype.itemsize for a in args)
    moved += sum(o.size * o.dtype.itemsize for o in jax.tree.leaves(out_shape))
    return pl.pallas_call(
        kernel,
        out_shape=out_shape,
        compiler_params=pltpu.CompilerParams(vmem_limit_bytes=VMEM_BYTES),
        cost_estimate=pl.CostEstimate(flops=flops, bytes_accessed=moved, transcendentals=0),
    )(*args)


def expert_call(kernel, lay, message, hidden, in_weight, out_weight):
    count = message.shape[0]
    ff = in_weight.shape[2]
    tile = min(512, ff)
    rows = count // GROUP * lay.rows
    whole = pl.BlockSpec(message.shape, lambda j: (0, 0))
    win = pl.BlockSpec((1, lay.width, tile), lambda j: (0, 0, j))
    wout = pl.BlockSpec((1, tile, lay.width), lambda j: (0, j, 0))
    hid = pl.BlockSpec((rows, tile), lambda j: (0, j))
    forward = hidden is None
    operands = (message, in_weight, out_weight) if forward else (message, hidden, in_weight, out_weight)
    message_out = jax.ShapeDtypeStruct(message.shape, BF16)
    return pl.pallas_call(
        functools.partial(kernel, lay),
        grid=(ff // tile,),
        in_specs=[whole, win, wout] if forward else [whole, hid, win, wout],
        out_specs=[whole, hid] if forward else whole,
        out_shape=[message_out, jax.ShapeDtypeStruct((rows, ff), BF16)] if forward else message_out,
        scratch_shapes=[pltpu.VMEM((rows, lay.width), BF16), pltpu.VMEM((rows, lay.width), F32)],
        compiler_params=pltpu.CompilerParams(vmem_limit_bytes=VMEM_BYTES),
        cost_estimate=pl.CostEstimate(
            flops=4 * rows * lay.width * ff,
            bytes_accessed=4 * lay.width * ff + 2 * rows * ff + 4 * message.size,
            transcendentals=0,
        ),
    )(*operands)


def exchange(x):
    return lax.all_to_all(x, AXES, split_axis=0, concat_axis=0, tiled=True)


def on_device(tokens, router_weight, in_weight, out_weight, expert_ids, slot_ids, cotangent):
    tok_rows, model_width = tokens.shape
    experts = router_weight.shape[1]
    devices = lax.axis_size("outer") * lax.axis_size("inner")
    lay = Layout(3 * tok_rows // experts, model_width)
    message = jax.ShapeDtypeStruct((experts * GROUP, lay.columns), BF16)
    ids, slots, router = expert_ids.T, slot_ids.T, router_weight.T
    place_flops = 4 * experts * GROUP * tok_rows * model_width

    sent_tokens = call(
        functools.partial(send_tokens_kernel, lay), message, place_flops, (ids, slots, tokens)
    )
    sent_grads, gates = call(
        functools.partial(send_grads_kernel, lay),
        [message, jax.ShapeDtypeStruct((2, tok_rows), F32)],
        2 * place_flops,
        (ids, slots, tokens, router, cotangent),
    )
    arrived = exchange(sent_tokens)
    grad_rows = exchange(sent_grads)
    produced, hidden = expert_call(forward_kernel, lay, arrived, None, in_weight, out_weight)
    produced_back = exchange(produced)
    returned = expert_call(backward_kernel, lay, grad_rows, hidden, in_weight, out_weight)
    returned_back = exchange(returned)

    mixed, router_back, partial_grad = call(
        functools.partial(mix_kernel, lay),
        [
            jax.ShapeDtypeStruct((tok_rows, model_width), BF16),
            jax.ShapeDtypeStruct((tok_rows, model_width), F32),
            jax.ShapeDtypeStruct((experts, model_width), F32),
        ],
        2 * place_flops,
        (ids, slots, gates, produced_back, cotangent, tokens, router),
    )
    grad_tokens = call(
        functools.partial(grad_kernel, lay),
        jax.ShapeDtypeStruct((tok_rows, model_width), BF16),
        place_flops,
        (ids, slots, returned_back, router_back),
    )

    share = (devices, 8, experts * model_width // (8 * devices))
    terms = exchange(partial_grad.reshape(share))
    own_rows = jnp.sum(terms, axis=0) * (1.0 / tok_rows)
    all_rows = exchange(jnp.broadcast_to(own_rows[None], share))
    grad_router = all_rows.reshape(experts, model_width).T
    return (mixed, grad_tokens, grad_router)


def solution(mesh):
    placed = (
        P(AXES, None),
        P(),
        P(AXES, None, None),
        P(AXES, None, None),
        P(AXES, None),
        P(AXES, None),
        P(AXES, None),
    )
    return jax.shard_map(
        on_device,
        mesh=mesh,
        in_specs=placed,
        out_specs=(P(AXES, None), P(AXES, None), P()),
        check_vma=False,
    )
```

```python
import functools

import jax
import jax.numpy as jnp
from jax import lax
from jax.experimental import pallas as pl
from jax.experimental.pallas import tpu as pltpu
from jax.sharding import PartitionSpec as P

AXES = ("outer", "inner")
F32 = jnp.float32
BF16 = jnp.bfloat16
GROUP = 8
VMEM_BYTES = 60 * 1024 * 1024


class Layout:
    def __init__(self, capacity, model_width):
        self.full, left = divmod(capacity, GROUP)
        self.rest = 0
        if left:
            self.rest = 1
            while self.rest < left:
                self.rest *= 2
        if self.rest == GROUP:
            self.full, self.rest = self.full + 1, 0
        self.capacity = capacity
        self.width = model_width
        self.cuts = GROUP // self.rest if self.rest else 1
        self.piece = model_width // self.cuts
        self.base = self.full * model_width
        self.columns = self.base + (self.piece if self.rest else 0)
        self.rows = self.full * GROUP + self.rest


def dot(a, b):
    return jnp.dot(a, b, preferred_element_type=F32)


def dot_nt(a, b):
    return lax.dot_general(a, b, (((1,), (1,)), ((), ())), preferred_element_type=F32)


def iota(shape, dim):
    return lax.broadcasted_iota(jnp.int32, shape, dim)


def as_column(row):
    count = row.shape[1]
    eye = iota((count, count), 0) == iota((count, count), 1)
    return jnp.sum(jnp.where(eye, row, 0.0), axis=1, keepdims=True)


def as_row(column):
    count = column.shape[0]
    eye = iota((count, count), 0) == iota((count, count), 1)
    return jnp.sum(jnp.where(eye, column, 0.0), axis=0, keepdims=True)


def targets(lay, ids, slots):
    found = []
    kept = slots < lay.capacity
    for group in range(lay.full):
        inside = kept & (slots >= group * GROUP) & (slots < (group + 1) * GROUP)
        found.append(jnp.where(inside, ids * GROUP + slots - group * GROUP, -1))
    if lay.rest:
        inside = kept & (slots >= lay.full * GROUP)
        found.append(jnp.where(inside, ids * GROUP + slots - lay.full * GROUP, -1))
    return found


def shifted(row, by):
    return jnp.where(row >= 0, row + by, -1)


def place(lay, row_targets, values, out_ref):
    count = out_ref.shape[0]
    toks = values[0].shape[0]
    row_at = iota((count, toks), 0)
    stacked = jnp.concatenate(values, axis=0) if len(values) > 1 else values[0]

    def onehot(rows):
        hit = functools.reduce(jnp.logical_or, [row_at == row for row in rows])
        return jnp.where(hit, 1.0, 0.0).astype(BF16)

    for group in range(lay.full):
        hot = [onehot([t[group] for t in ranks]) for ranks in row_targets]
        hot = jnp.concatenate(hot, axis=1) if len(hot) > 1 else hot[0]
        out_ref[:, group * lay.width : (group + 1) * lay.width] = dot(hot, stacked).astype(BF16)
    if lay.rest:
        hot, pieces = [], []
        for cut in range(lay.cuts):
            for ranks in row_targets:
                hot.append(onehot([shifted(t[lay.full], cut * lay.rest) for t in ranks]))
            pieces.append(stacked[:, cut * lay.piece : (cut + 1) * lay.piece])
        out_ref[:, lay.base :] = dot(
            jnp.concatenate(hot, axis=1), jnp.concatenate(pieces, axis=0)
        ).astype(BF16)


def pick(lay, ranks, message_ref):
    count = message_ref.shape[0]
    toks = ranks[0][0].shape[0]
    row_at = iota((toks, count), 1)

    def onehot(rows):
        hit = functools.reduce(jnp.logical_or, [row_at == row for row in rows])
        return jnp.where(hit, 1.0, 0.0).astype(BF16)

    whole = [onehot([t[group] for t in ranks]) for group in range(lay.full)]
    pieces = []
    for cut in range(lay.cuts):
        left = cut * lay.piece
        total = None
        for group in range(lay.full):
            start = group * lay.width + left
            term = dot(whole[group], message_ref[:, start : start + lay.piece])
            total = term if total is None else total + term
        if lay.rest:
            hot = onehot([shifted(t[lay.full], cut * lay.rest) for t in ranks])
            term = dot(hot, message_ref[:, lay.base : lay.base + lay.piece])
            total = term if total is None else total + term
        pieces.append(total)
    return jnp.concatenate(pieces, axis=1) if len(pieces) > 1 else pieces[0]


def rest_selection(lay, count):
    small = count // GROUP * lay.rest
    row = iota((small, count), 0)
    col = iota((small, count), 1)
    shift = lay.rest.bit_length() - 1
    home = lax.shift_right_logical(row, shift) * GROUP + (row & (lay.rest - 1))
    return [jnp.where(col == home + cut * lay.rest, 1.0, 0.0).astype(BF16) for cut in range(lay.cuts)]


def unpack(lay, message_ref, out_ref):
    count = message_ref.shape[0]
    for group in range(lay.full):
        out_ref[group * count : (group + 1) * count, :] = message_ref[
            :, group * lay.width : (group + 1) * lay.width
        ]
    if lay.rest:
        tail = message_ref[:, lay.base :]
        for cut, chosen in enumerate(rest_selection(lay, count)):
            out_ref[lay.full * count :, cut * lay.piece : (cut + 1) * lay.piece] = dot(
                chosen, tail
            ).astype(BF16)


def pack(lay, rows_ref, message_ref):
    count = message_ref.shape[0]
    for group in range(lay.full):
        message_ref[:, group * lay.width : (group + 1) * lay.width] = rows_ref[
            group * count : (group + 1) * count, :
        ].astype(BF16)
    if lay.rest:
        total = None
        for cut, chosen in enumerate(rest_selection(lay, count)):
            part = rows_ref[
                lay.full * count :, cut * lay.piece : (cut + 1) * lay.piece
            ].astype(BF16)
            term = lax.dot_general(
                chosen, part, (((0,), (0,)), ((), ())), preferred_element_type=F32
            )
            total = term if total is None else total + term
        message_ref[:, lay.base :] = total.astype(BF16)


def send_tokens_kernel(lay, ids_ref, slots_ref, tokens_ref, out_ref):
    first = targets(lay, ids_ref[0:1, :], slots_ref[0:1, :])
    second = targets(lay, ids_ref[1:2, :], slots_ref[1:2, :])
    place(lay, [[first, second]], [tokens_ref[...]], out_ref)


def send_grads_kernel(
    lay, ids_ref, slots_ref, tokens_ref, router_ref, cot_ref, out_ref, gates_ref
):
    logits = dot_nt(router_ref[...], tokens_ref[...])
    expert_at = iota(logits.shape, 0)
    picked = [
        jnp.sum(jnp.where(expert_at == ids_ref[k : k + 1, :], logits, 0.0), axis=0, keepdims=True)
        for k in range(2)
    ]
    gates = [jax.nn.sigmoid(picked[0] - picked[1]), jax.nn.sigmoid(picked[1] - picked[0])]
    gates_ref[0:1, :] = gates[0]
    gates_ref[1:2, :] = gates[1]
    cot = cot_ref[...].astype(F32)
    scaled = [(as_column(gate) * cot).astype(BF16) for gate in gates]
    ranks = [[targets(lay, ids_ref[k : k + 1, :], slots_ref[k : k + 1, :])] for k in range(2)]
    place(lay, ranks, scaled, out_ref)


def forward_kernel(lay, message_ref, win_ref, wout_ref, out_ref, hidden_ref, rows_ref, total_ref):
    step = pl.program_id(0)

    @pl.when(step == 0)
    def _():
        unpack(lay, message_ref, rows_ref)

    hidden = jnp.maximum(dot(rows_ref[...], win_ref[0]), 0.0).astype(BF16)
    hidden_ref[...] = hidden
    term = dot(hidden, wout_ref[0])

    @pl.when(step == 0)
    def _():
        total_ref[...] = term

    @pl.when(step > 0)
    def _():
        total_ref[...] += term

    @pl.when(step == pl.num_programs(0) - 1)
    def _():
        pack(lay, total_ref, out_ref)


def backward_kernel(lay, message_ref, hidden_ref, win_ref, wout_ref, out_ref, rows_ref, total_ref):
    step = pl.program_id(0)

    @pl.when(step == 0)
    def _():
        unpack(lay, message_ref, rows_ref)

    back = dot_nt(rows_ref[...], wout_ref[0])
    back = jnp.where(hidden_ref[...].astype(F32) > 0.0, back, 0.0).astype(BF16)
    term = dot_nt(back, win_ref[0])

    @pl.when(step == 0)
    def _():
        total_ref[...] = term

    @pl.when(step > 0)
    def _():
        total_ref[...] += term

    @pl.when(step == pl.num_programs(0) - 1)
    def _():
        pack(lay, total_ref, out_ref)


def column_targets(lay, ids_ref, slots_ref):
    ids = [as_column(ids_ref[k : k + 1, :].astype(F32)).astype(jnp.int32) for k in range(2)]
    slots = [as_column(slots_ref[k : k + 1, :].astype(F32)).astype(jnp.int32) for k in range(2)]
    return ids, [targets(lay, ids[k], slots[k]) for k in range(2)]


def split_in_two(x):
    high = x.astype(BF16)
    return high, (x - high.astype(F32)).astype(BF16)


def mix_kernel(
    lay,
    ids_ref,
    slots_ref,
    gates_ref,
    message_ref,
    cot_ref,
    tokens_ref,
    router_ref,
    mixed_ref,
    back_ref,
    partial_ref,
):
    experts = router_ref.shape[0]
    toks = tokens_ref.shape[0]
    ids, ranks = column_targets(lay, ids_ref, slots_ref)
    gates = [as_column(gates_ref[k : k + 1, :]) for k in range(2)]
    cot = cot_ref[...].astype(F32)
    choice = [pick(lay, [ranks[k]], message_ref) for k in range(2)]
    mixed_ref[...] = (gates[0] * choice[0] + gates[1] * choice[1]).astype(BF16)
    actions = [jnp.sum(choice[k] * cot, axis=1, keepdims=True) for k in range(2)]
    slope = gates[0] * gates[1] * (actions[0] - actions[1])

    expert_at = iota((toks, experts), 1)
    signs = jnp.where(expert_at == ids[0], 1.0, 0.0) - jnp.where(expert_at == ids[1], 1.0, 0.0)
    high, low = split_in_two(signs * slope)
    router = router_ref[...]
    back_ref[...] = dot(high, router) + dot(low, router)

    expert_at = iota((experts, toks), 0)
    signs = jnp.where(expert_at == ids_ref[0:1, :], 1.0, 0.0) - jnp.where(
        expert_at == ids_ref[1:2, :], 1.0, 0.0
    )
    high, low = split_in_two(signs * as_row(slope))
    tokens = tokens_ref[...]
    partial_ref[...] = (dot(high, tokens) + dot(low, tokens)) * (1.0 / toks)


def grad_kernel(lay, ids_ref, slots_ref, message_ref, back_ref, out_ref):
    _, ranks = column_targets(lay, ids_ref, slots_ref)
    out_ref[...] = (pick(lay, ranks, message_ref) + back_ref[...]).astype(BF16)


def call(kernel, out_shape, flops, args):
    moved = sum(a.size * a.dtype.itemsize for a in args)
    moved += sum(o.size * o.dtype.itemsize for o in jax.tree.leaves(out_shape))
    return pl.pallas_call(
        kernel,
        out_shape=out_shape,
        compiler_params=pltpu.CompilerParams(vmem_limit_bytes=VMEM_BYTES),
        cost_estimate=pl.CostEstimate(flops=flops, bytes_accessed=moved, transcendentals=0),
    )(*args)


def expert_call(kernel, lay, message, hidden, in_weight, out_weight):
    count = message.shape[0]
    ff = in_weight.shape[2]
    tile = min(512, ff)
    rows = count // GROUP * lay.rows
    whole = pl.BlockSpec(message.shape, lambda j: (0, 0))
    win = pl.BlockSpec((1, lay.width, tile), lambda j: (0, 0, j))
    wout = pl.BlockSpec((1, tile, lay.width), lambda j: (0, j, 0))
    hid = pl.BlockSpec((rows, tile), lambda j: (0, j))
    forward = hidden is None
    operands = (message, in_weight, out_weight) if forward else (message, hidden, in_weight, out_weight)
    message_out = jax.ShapeDtypeStruct(message.shape, BF16)
    return pl.pallas_call(
        functools.partial(kernel, lay),
        grid=(ff // tile,),
        in_specs=[whole, win, wout] if forward else [whole, hid, win, wout],
        out_specs=[whole, hid] if forward else whole,
        out_shape=[message_out, jax.ShapeDtypeStruct((rows, ff), BF16)] if forward else message_out,
        scratch_shapes=[pltpu.VMEM((rows, lay.width), BF16), pltpu.VMEM((rows, lay.width), F32)],
        compiler_params=pltpu.CompilerParams(vmem_limit_bytes=VMEM_BYTES),
        cost_estimate=pl.CostEstimate(
            flops=4 * rows * lay.width * ff,
            bytes_accessed=4 * lay.width * ff + 2 * rows * ff + 4 * message.size,
            transcendentals=0,
        ),
    )(*operands)


def exchange(x):
    return lax.all_to_all(x, AXES, split_axis=0, concat_axis=0, tiled=True)


def from_device(x, bits, devices):
    return lax.ppermute(x, AXES, [(d, d ^ bits) for d in range(devices)])


def sum_over_devices(x, devices):
    half = x.shape[0] // 2
    core = lax.axis_index("inner") % 2
    own = lax.dynamic_slice_in_dim(x, core * half, half, 0)
    other = lax.dynamic_slice_in_dim(x, (1 - core) * half, half, 0)
    own = own + from_device(other, 1, devices)
    bit = 2
    while bit < devices:
        if 2 * bit < devices:
            near = own + from_device(own, bit, devices)
            far = from_device(own, 2 * bit, devices) + from_device(own, 3 * bit, devices)
            own = near + far
        else:
            own = own + from_device(own, bit, devices)
        bit *= 4
    other = from_device(own, 1, devices)
    first = core == 0
    return jnp.concatenate([jnp.where(first, own, other), jnp.where(first, other, own)], axis=0)


def on_device(tokens, router_weight, in_weight, out_weight, expert_ids, slot_ids, cotangent):
    tok_rows, model_width = tokens.shape
    experts = router_weight.shape[1]
    devices = lax.axis_size("outer") * lax.axis_size("inner")
    lay = Layout(3 * tok_rows // experts, model_width)
    message = jax.ShapeDtypeStruct((experts * GROUP, lay.columns), BF16)
    ids, slots, router = expert_ids.T, slot_ids.T, router_weight.T
    place_flops = 4 * experts * GROUP * tok_rows * model_width

    sent_tokens = call(
        functools.partial(send_tokens_kernel, lay), message, place_flops, (ids, slots, tokens)
    )
    sent_grads, gates = call(
        functools.partial(send_grads_kernel, lay),
        [message, jax.ShapeDtypeStruct((2, tok_rows), F32)],
        2 * place_flops,
        (ids, slots, tokens, router, cotangent),
    )
    arrived = exchange(sent_tokens)
    arrived, sent_grads = lax.optimization_barrier((arrived, sent_grads))
    grad_rows = exchange(sent_grads)
    produced, hidden = expert_call(forward_kernel, lay, arrived, None, in_weight, out_weight)
    produced, grad_rows = lax.optimization_barrier((produced, grad_rows))
    produced_back = exchange(produced)
    returned = expert_call(backward_kernel, lay, grad_rows, hidden, in_weight, out_weight)
    returned, produced_back = lax.optimization_barrier((returned, produced_back))
    returned_back = exchange(returned)

    mixed, router_back, partial_grad = call(
        functools.partial(mix_kernel, lay),
        [
            jax.ShapeDtypeStruct((tok_rows, model_width), BF16),
            jax.ShapeDtypeStruct((tok_rows, model_width), F32),
            jax.ShapeDtypeStruct((experts, model_width), F32),
        ],
        2 * place_flops,
        (ids, slots, gates, produced_back, cotangent, tokens, router),
    )
    grad_router = sum_over_devices(partial_grad, devices).T
    grad_tokens = call(
        functools.partial(grad_kernel, lay),
        jax.ShapeDtypeStruct((tok_rows, model_width), BF16),
        place_flops,
        (ids, slots, returned_back, router_back),
    )
    return (mixed, grad_tokens, grad_router)


def solution(mesh):
    placed = (
        P(AXES, None),
        P(),
        P(AXES, None, None),
        P(AXES, None, None),
        P(AXES, None),
        P(AXES, None),
        P(AXES, None),
    )
    return jax.shard_map(
        on_device,
        mesh=mesh,
        in_specs=placed,
        out_specs=(P(AXES, None), P(AXES, None), P()),
        check_vma=False,
    )
```

```python
import functools

import jax
import jax.numpy as jnp
from jax import lax
from jax.experimental import pallas as pl
from jax.experimental.pallas import tpu as pltpu
from jax.sharding import PartitionSpec as P

AXES = ("outer", "inner")
F32 = jnp.float32
BF16 = jnp.bfloat16
GROUP = 8
VMEM_BYTES = 60 * 1024 * 1024


class Layout:
    def __init__(self, capacity, model_width):
        self.full, left = divmod(capacity, GROUP)
        self.rest = 0
        if left:
            self.rest = 1
            while self.rest < left:
                self.rest *= 2
        if self.rest == GROUP:
            self.full, self.rest = self.full + 1, 0
        self.capacity = capacity
        self.width = model_width
        self.cuts = GROUP // self.rest if self.rest else 1
        self.piece = model_width // self.cuts
        self.base = self.full * model_width
        self.columns = self.base + (self.piece if self.rest else 0)
        self.rows = self.full * GROUP + self.rest


def dot(a, b):
    return jnp.dot(a, b, preferred_element_type=F32)


def dot_nt(a, b):
    return lax.dot_general(a, b, (((1,), (1,)), ((), ())), preferred_element_type=F32)


def iota(shape, dim):
    return lax.broadcasted_iota(jnp.int32, shape, dim)


def as_column(row):
    count = row.shape[1]
    eye = iota((count, count), 0) == iota((count, count), 1)
    return jnp.sum(jnp.where(eye, row, 0.0), axis=1, keepdims=True)


def as_row(column):
    count = column.shape[0]
    eye = iota((count, count), 0) == iota((count, count), 1)
    return jnp.sum(jnp.where(eye, column, 0.0), axis=0, keepdims=True)


def targets(lay, ids, slots):
    found = []
    kept = slots < lay.capacity
    for group in range(lay.full):
        inside = kept & (slots >= group * GROUP) & (slots < (group + 1) * GROUP)
        found.append(jnp.where(inside, ids * GROUP + slots - group * GROUP, -1))
    if lay.rest:
        inside = kept & (slots >= lay.full * GROUP)
        found.append(jnp.where(inside, ids * GROUP + slots - lay.full * GROUP, -1))
    return found


def shifted(row, by):
    return jnp.where(row >= 0, row + by, -1)


class Order:
    def __init__(self, high, low, by_high):
        self.high, self.low, self.by_high = high, low, by_high
        self.arrays = high if by_high else low
        self.inside = low if by_high else high
        self.rows = self.inside * GROUP

    def position(self, block):
        if self.by_high:
            return block
        shift = self.low.bit_length() - 1
        return (block & (self.low - 1)) * self.high + lax.shift_right_logical(block, shift)

    def block(self, position):
        if self.by_high:
            return position
        part, high = divmod(position, self.high)
        return high * self.low + part


def this_device():
    return lax.axis_index("outer") * lax.axis_size("inner") + lax.axis_index("inner")


def read_all(refs):
    return jnp.concatenate([ref[...] for ref in refs], axis=0)


def write_all(order, refs, start, values):
    for at, ref in enumerate(refs):
        ref[:, start : start + values.shape[1]] = values[at * order.rows : (at + 1) * order.rows, :]


def place(lay, order, row_targets, values, out_refs):
    count = order.arrays * order.rows
    toks = values[0].shape[0]
    row_at = iota((count, toks), 0)
    stacked = jnp.concatenate(values, axis=0) if len(values) > 1 else values[0]

    def onehot(rows):
        hit = functools.reduce(jnp.logical_or, [row_at == row for row in rows])
        return jnp.where(hit, 1.0, 0.0).astype(BF16)

    for group in range(lay.full):
        hot = [onehot([t[group] for t in ranks]) for ranks in row_targets]
        hot = jnp.concatenate(hot, axis=1) if len(hot) > 1 else hot[0]
        write_all(order, out_refs, group * lay.width, dot(hot, stacked).astype(BF16))
    if lay.rest:
        hot, pieces = [], []
        for cut in range(lay.cuts):
            for ranks in row_targets:
                hot.append(onehot([shifted(t[lay.full], cut * lay.rest) for t in ranks]))
            pieces.append(stacked[:, cut * lay.piece : (cut + 1) * lay.piece])
        placed = dot(jnp.concatenate(hot, axis=1), jnp.concatenate(pieces, axis=0))
        write_all(order, out_refs, lay.base, placed.astype(BF16))


def pick(lay, ranks, message):
    count = message.shape[0]
    toks = ranks[0][0].shape[0]
    row_at = iota((toks, count), 1)

    def onehot(rows):
        hit = functools.reduce(jnp.logical_or, [row_at == row for row in rows])
        return jnp.where(hit, 1.0, 0.0).astype(BF16)

    whole = [onehot([t[group] for t in ranks]) for group in range(lay.full)]
    pieces = []
    for cut in range(lay.cuts):
        left = cut * lay.piece
        total = None
        for group in range(lay.full):
            start = group * lay.width + left
            term = dot(whole[group], message[:, start : start + lay.piece])
            total = term if total is None else total + term
        if lay.rest:
            hot = onehot([shifted(t[lay.full], cut * lay.rest) for t in ranks])
            term = dot(hot, message[:, lay.base : lay.base + lay.piece])
            total = term if total is None else total + term
        pieces.append(total)
    return jnp.concatenate(pieces, axis=1) if len(pieces) > 1 else pieces[0]


def rest_selection(lay, order):
    count = order.arrays * order.rows
    small = count // GROUP * lay.rest
    row = iota((small, count), 0)
    col = iota((small, count), 1)
    shift = lay.rest.bit_length() - 1
    home = order.position(lax.shift_right_logical(row, shift)) * GROUP + (row & (lay.rest - 1))
    return [jnp.where(col == home + cut * lay.rest, 1.0, 0.0).astype(BF16) for cut in range(lay.cuts)]


def unpack(lay, order, message_refs, out_ref):
    count = order.arrays * order.rows
    message = read_all(message_refs)
    for group in range(lay.full):
        part = message[:, group * lay.width : (group + 1) * lay.width]
        if not order.by_high:
            part = part.astype(F32)
            blocks = [
                part[at * GROUP : (at + 1) * GROUP, :]
                for at in sorted(range(count // GROUP), key=order.block)
            ]
            part = jnp.concatenate(blocks, axis=0).astype(BF16)
        out_ref[group * count : (group + 1) * count, :] = part
    if lay.rest:
        tail = message[:, lay.base :]
        for cut, chosen in enumerate(rest_selection(lay, order)):
            out_ref[lay.full * count :, cut * lay.piece : (cut + 1) * lay.piece] = dot(
                chosen, tail
            ).astype(BF16)


def pack(lay, order, rows_ref, message_refs):
    count = order.arrays * order.rows
    for group in range(lay.full):
        part = rows_ref[group * count : (group + 1) * count, :]
        if not order.by_high:
            blocks = [order.block(at) * GROUP for at in range(count // GROUP)]
            part = jnp.concatenate([part[at : at + GROUP, :] for at in blocks], axis=0)
        write_all(order, message_refs, group * lay.width, part.astype(BF16))
    if lay.rest:
        total = None
        for cut, chosen in enumerate(rest_selection(lay, order)):
            part = rows_ref[
                lay.full * count :, cut * lay.piece : (cut + 1) * lay.piece
            ].astype(BF16)
            term = lax.dot_general(
                chosen, part, (((0,), (0,)), ((), ())), preferred_element_type=F32
            )
            total = term if total is None else total + term
        write_all(order, message_refs, lay.base, total.astype(BF16))


def repack_kernel(order, *refs):
    sources, outs = refs[: order.arrays], refs[order.arrays :]
    for part, out_ref in enumerate(outs):
        blocks = [ref[part * GROUP : (part + 1) * GROUP, :] for ref in sources]
        out_ref[...] = jnp.concatenate(blocks, axis=0)


def blocks_of(order, ids):
    return order.position(ids ^ this_device())


def send_tokens_kernel(lay, order, ids_ref, slots_ref, tokens_ref, *out_refs):
    blocks = blocks_of(order, ids_ref[...])
    ranks = [targets(lay, blocks[k : k + 1, :], slots_ref[k : k + 1, :]) for k in range(2)]
    place(lay, order, [ranks], [tokens_ref[...]], out_refs)


def send_grads_kernel(
    lay, order, ids_ref, slots_ref, tokens_ref, router_ref, cot_ref, gates_ref, *out_refs
):
    logits = dot_nt(router_ref[...], tokens_ref[...])
    expert_at = iota(logits.shape, 0)
    picked = [
        jnp.sum(jnp.where(expert_at == ids_ref[k : k + 1, :], logits, 0.0), axis=0, keepdims=True)
        for k in range(2)
    ]
    gates = [jax.nn.sigmoid(picked[0] - picked[1]), jax.nn.sigmoid(picked[1] - picked[0])]
    gates_ref[0:1, :] = gates[0]
    gates_ref[1:2, :] = gates[1]
    cot = cot_ref[...].astype(F32)
    scaled = [(as_column(gate) * cot).astype(BF16) for gate in gates]
    blocks = blocks_of(order, ids_ref[...])
    ranks = [[targets(lay, blocks[k : k + 1, :], slots_ref[k : k + 1, :])] for k in range(2)]
    place(lay, order, ranks, scaled, out_refs)


def forward_kernel(lay, order, out_order, *refs):
    message_refs = refs[: order.arrays]
    win_ref, wout_ref, hidden_ref = refs[order.arrays : order.arrays + 3]
    out_refs, (rows_ref, total_ref) = refs[order.arrays + 3 : -2], refs[-2:]
    step = pl.program_id(0)

    @pl.when(step == 0)
    def _():
        unpack(lay, order, message_refs, rows_ref)

    hidden = jnp.maximum(dot(rows_ref[...], win_ref[0]), 0.0).astype(BF16)
    hidden_ref[...] = hidden
    term = dot(hidden, wout_ref[0])

    @pl.when(step == 0)
    def _():
        total_ref[...] = term

    @pl.when(step > 0)
    def _():
        total_ref[...] += term

    @pl.when(step == pl.num_programs(0) - 1)
    def _():
        pack(lay, out_order, total_ref, out_refs)


def backward_kernel(lay, order, out_order, *refs):
    message_refs = refs[: order.arrays]
    win_ref, wout_ref, hidden_ref = refs[order.arrays : order.arrays + 3]
    out_refs, (rows_ref, total_ref) = refs[order.arrays + 3 : -2], refs[-2:]
    step = pl.program_id(0)

    @pl.when(step == 0)
    def _():
        unpack(lay, order, message_refs, rows_ref)

    back = dot_nt(rows_ref[...], wout_ref[0])
    back = jnp.where(hidden_ref[...].astype(F32) > 0.0, back, 0.0).astype(BF16)
    term = dot_nt(back, win_ref[0])

    @pl.when(step == 0)
    def _():
        total_ref[...] = term

    @pl.when(step > 0)
    def _():
        total_ref[...] += term

    @pl.when(step == pl.num_programs(0) - 1)
    def _():
        pack(lay, out_order, total_ref, out_refs)


def column_targets(lay, order, ids_ref, slots_ref):
    ids = [as_column(ids_ref[k : k + 1, :].astype(F32)).astype(jnp.int32) for k in range(2)]
    slots = [as_column(slots_ref[k : k + 1, :].astype(F32)).astype(jnp.int32) for k in range(2)]
    return ids, [targets(lay, blocks_of(order, ids[k]), slots[k]) for k in range(2)]


def split_in_two(x):
    high = x.astype(BF16)
    return high, (x - high.astype(F32)).astype(BF16)


def mix_kernel(lay, order, ids_ref, slots_ref, gates_ref, cot_ref, tokens_ref, router_ref, *refs):
    message_refs, (mixed_ref, back_ref, partial_ref) = refs[: order.arrays], refs[order.arrays :]
    experts = router_ref.shape[0]
    toks = tokens_ref.shape[0]
    ids, ranks = column_targets(lay, order, ids_ref, slots_ref)
    gates = [as_column(gates_ref[k : k + 1, :]) for k in range(2)]
    cot = cot_ref[...].astype(F32)
    message = read_all(message_refs)
    choice = [pick(lay, [ranks[k]], message) for k in range(2)]
    mixed_ref[...] = (gates[0] * choice[0] + gates[1] * choice[1]).astype(BF16)
    actions = [jnp.sum(choice[k] * cot, axis=1, keepdims=True) for k in range(2)]
    slope = gates[0] * gates[1] * (actions[0] - actions[1])

    expert_at = iota((toks, experts), 1)
    signs = jnp.where(expert_at == ids[0], 1.0, 0.0) - jnp.where(expert_at == ids[1], 1.0, 0.0)
    high, low = split_in_two(signs * slope)
    router = router_ref[...]
    back_ref[...] = dot(high, router) + dot(low, router)

    expert_at = iota((experts, toks), 0)
    signs = jnp.where(expert_at == ids_ref[0:1, :], 1.0, 0.0) - jnp.where(
        expert_at == ids_ref[1:2, :], 1.0, 0.0
    )
    high, low = split_in_two(signs * as_row(slope))
    tokens = tokens_ref[...]
    partial_ref[...] = (dot(high, tokens) + dot(low, tokens)) * (1.0 / toks)


def grad_kernel(lay, order, ids_ref, slots_ref, back_ref, *refs):
    message_refs, out_ref = refs[: order.arrays], refs[order.arrays]
    _, ranks = column_targets(lay, order, ids_ref, slots_ref)
    message = read_all(message_refs)
    out_ref[...] = (pick(lay, ranks, message) + back_ref[...]).astype(BF16)


def call(kernel, out_shape, flops, args):
    moved = sum(a.size * a.dtype.itemsize for a in args)
    moved += sum(o.size * o.dtype.itemsize for o in jax.tree.leaves(out_shape))
    return pl.pallas_call(
        kernel,
        out_shape=out_shape,
        compiler_params=pltpu.CompilerParams(vmem_limit_bytes=VMEM_BYTES),
        cost_estimate=pl.CostEstimate(flops=flops, bytes_accessed=moved, transcendentals=0),
    )(*args)


def messages_of(lay, order):
    return [jax.ShapeDtypeStruct((order.rows, lay.columns), BF16)] * order.arrays


def expert_call(kernel, lay, order, out_order, message, hidden, in_weight, out_weight):
    ff = in_weight.shape[2]
    tile = min(512, ff)
    rows = order.arrays * order.inside * lay.rows
    win = pl.BlockSpec((1, lay.width, tile), lambda j: (0, 0, j))
    wout = pl.BlockSpec((1, tile, lay.width), lambda j: (0, j, 0))
    hid = pl.BlockSpec((rows, tile), lambda j: (0, j))

    def whole(of):
        return [pl.BlockSpec((of.rows, lay.columns), lambda j: (0, 0))] * of.arrays

    forward = hidden is None
    hidden_shape = [jax.ShapeDtypeStruct((rows, ff), BF16)]
    return pl.pallas_call(
        functools.partial(kernel, lay, order, out_order),
        grid=(ff // tile,),
        in_specs=whole(order) + [win, wout] + ([] if forward else [hid]),
        out_specs=([hid] if forward else []) + whole(out_order),
        out_shape=(hidden_shape if forward else []) + messages_of(lay, out_order),
        scratch_shapes=[pltpu.VMEM((rows, lay.width), BF16), pltpu.VMEM((rows, lay.width), F32)],
        compiler_params=pltpu.CompilerParams(vmem_limit_bytes=VMEM_BYTES),
        cost_estimate=pl.CostEstimate(
            flops=4 * rows * lay.width * ff,
            bytes_accessed=4 * lay.width * ff + 2 * rows * ff + 4 * rows * lay.width,
            transcendentals=0,
        ),
    )(*message, in_weight, out_weight, *([] if forward else [hidden]))


def repack(lay, order, message):
    other = Order(order.high, order.low, not order.by_high)
    return call(
        functools.partial(repack_kernel, order), messages_of(lay, other), 0, tuple(message)
    )


def step_of(order, message):
    devices = order.high * order.low
    unit = order.low if order.by_high else 1
    return [message[0]] + [
        from_device(message[part], part * unit, devices) for part in range(1, order.arrays)
    ]


def tied(first, second):
    out = lax.optimization_barrier(tuple(first) + tuple(second))
    return list(out[: len(first)]), list(out[len(first) :])


def from_device(x, bits, devices):
    return lax.ppermute(x, AXES, [(d, d ^ bits) for d in range(devices)])


def sum_over_devices(x, devices):
    half = x.shape[0] // 2
    core = lax.axis_index("inner") % 2
    own = lax.dynamic_slice_in_dim(x, core * half, half, 0)
    other = lax.dynamic_slice_in_dim(x, (1 - core) * half, half, 0)
    own = own + from_device(other, 1, devices)
    bit = 2
    while bit < devices:
        if 2 * bit < devices:
            near = own + from_device(own, bit, devices)
            far = from_device(own, 2 * bit, devices) + from_device(own, 3 * bit, devices)
            own = near + far
        else:
            own = own + from_device(own, bit, devices)
        bit *= 4
    other = from_device(own, 1, devices)
    first = core == 0
    return jnp.concatenate([jnp.where(first, own, other), jnp.where(first, other, own)], axis=0)


def on_device(tokens, router_weight, in_weight, out_weight, expert_ids, slot_ids, cotangent):
    tok_rows, model_width = tokens.shape
    experts = router_weight.shape[1]
    devices = lax.axis_size("outer") * lax.axis_size("inner")
    lay = Layout(3 * tok_rows // experts, model_width)
    high = 4 if devices >= 16 else 1
    by_high, by_low = (Order(high, devices // high, flag) for flag in (True, False))
    ids, slots, router = expert_ids.T, slot_ids.T, router_weight.T
    place_flops = 4 * experts * GROUP * tok_rows * model_width

    sent_tokens = call(
        functools.partial(send_tokens_kernel, lay, by_high),
        messages_of(lay, by_high),
        place_flops,
        (ids, slots, tokens),
    )
    token_half = step_of(by_high, sent_tokens)

    gates, *sent_grads = call(
        functools.partial(send_grads_kernel, lay, by_low),
        [jax.ShapeDtypeStruct((2, tok_rows), F32)] + messages_of(lay, by_low),
        2 * place_flops,
        (ids, slots, tokens, router, cotangent),
    )
    grad_half = repack(lay, by_low, step_of(by_low, sent_grads))
    token_half, grad_half = tied(token_half, grad_half)
    grad_rows = step_of(by_high, grad_half)
    arrived = step_of(by_low, repack(lay, by_high, token_half))

    hidden, *produced = expert_call(
        forward_kernel, lay, by_low, by_high, arrived, None, in_weight, out_weight
    )
    produced, grad_rows = tied(produced, grad_rows)
    produced_half = step_of(by_high, produced)
    returned = expert_call(
        backward_kernel, lay, by_high, by_low, grad_rows, hidden, in_weight, out_weight
    )
    returned_half = repack(lay, by_low, step_of(by_low, returned))
    produced_half, returned_half = tied(produced_half, returned_half)
    returned_back = step_of(by_high, returned_half)
    produced_back = step_of(by_low, repack(lay, by_high, produced_half))

    mixed, router_back, partial_grad = call(
        functools.partial(mix_kernel, lay, by_low),
        [
            jax.ShapeDtypeStruct((tok_rows, model_width), BF16),
            jax.ShapeDtypeStruct((tok_rows, model_width), F32),
            jax.ShapeDtypeStruct((experts, model_width), F32),
        ],
        2 * place_flops,
        (ids, slots, gates, cotangent, tokens, router, *produced_back),
    )
    grad_router = sum_over_devices(partial_grad, devices).T
    grad_tokens = call(
        functools.partial(grad_kernel, lay, by_high),
        jax.ShapeDtypeStruct((tok_rows, model_width), BF16),
        place_flops,
        (ids, slots, router_back, *returned_back),
    )
    return (mixed, grad_tokens, grad_router)


def solution(mesh):
    placed = (
        P(AXES, None),
        P(),
        P(AXES, None, None),
        P(AXES, None, None),
        P(AXES, None),
        P(AXES, None),
        P(AXES, None),
    )
    return jax.shard_map(
        on_device,
        mesh=mesh,
        in_specs=placed,
        out_specs=(P(AXES, None), P(AXES, None), P()),
        check_vma=False,
    )
```

```python
import functools

import jax
import jax.numpy as jnp
from jax import lax
from jax.experimental import pallas as pl
from jax.experimental.pallas import tpu as pltpu
from jax.sharding import PartitionSpec as P

AXES = ("outer", "inner")
F32 = jnp.float32
BF16 = jnp.bfloat16
GROUP = 8
VMEM_BYTES = 60 * 1024 * 1024


class Layout:
    def __init__(self, capacity, model_width):
        self.full, left = divmod(capacity, GROUP)
        self.rest = 0
        if left:
            self.rest = 1
            while self.rest < left:
                self.rest *= 2
        if self.rest == GROUP:
            self.full, self.rest = self.full + 1, 0
        self.capacity = capacity
        self.width = model_width
        self.cuts = GROUP // self.rest if self.rest else 1
        self.piece = model_width // self.cuts
        self.base = self.full * model_width
        self.columns = self.base + (self.piece if self.rest else 0)
        self.rows = self.full * GROUP + self.rest


def dot(a, b):
    return jnp.dot(a, b, preferred_element_type=F32)


def dot_nt(a, b):
    return lax.dot_general(a, b, (((1,), (1,)), ((), ())), preferred_element_type=F32)


def iota(shape, dim):
    return lax.broadcasted_iota(jnp.int32, shape, dim)


def as_column(row):
    count = row.shape[1]
    eye = iota((count, count), 0) == iota((count, count), 1)
    return jnp.sum(jnp.where(eye, row, 0.0), axis=1, keepdims=True)


def as_row(column):
    count = column.shape[0]
    eye = iota((count, count), 0) == iota((count, count), 1)
    return jnp.sum(jnp.where(eye, column, 0.0), axis=0, keepdims=True)


def targets(lay, ids, slots):
    found = []
    kept = slots < lay.capacity
    for group in range(lay.full):
        inside = kept & (slots >= group * GROUP) & (slots < (group + 1) * GROUP)
        found.append(jnp.where(inside, ids * GROUP + slots - group * GROUP, -1))
    if lay.rest:
        inside = kept & (slots >= lay.full * GROUP)
        found.append(jnp.where(inside, ids * GROUP + slots - lay.full * GROUP, -1))
    return found


def shifted(row, by):
    return jnp.where(row >= 0, row + by, -1)


class Order:
    def __init__(self, half, apart):
        self.half, self.apart = half, apart
        self.arrays = 2 if apart else 1
        self.rows = 2 * half * GROUP // self.arrays
        self.blocks = 2 * half

    def position(self, block):
        if self.apart:
            return block
        shift = self.half.bit_length() - 1
        return (block & (self.half - 1)) * 2 + lax.shift_right_logical(block, shift)

    def block(self, position):
        if self.apart:
            return position
        return (position % 2) * self.half + position // 2


def this_device():
    return lax.axis_index("outer") * lax.axis_size("inner") + lax.axis_index("inner")


def read_all(refs):
    return jnp.concatenate([ref[...] for ref in refs], axis=0)


def write_all(order, refs, start, values):
    for at, ref in enumerate(refs):
        ref[:, start : start + values.shape[1]] = values[at * order.rows : (at + 1) * order.rows, :]


def place(lay, order, row_targets, values, out_refs):
    count = len(out_refs) * order.rows
    toks = values[0].shape[0]
    row_at = iota((count, toks), 0)
    stacked = jnp.concatenate(values, axis=0) if len(values) > 1 else values[0]

    def onehot(rows):
        hit = functools.reduce(jnp.logical_or, [row_at == row for row in rows])
        return jnp.where(hit, 1.0, 0.0).astype(BF16)

    for group in range(lay.full):
        hot = [onehot([t[group] for t in ranks]) for ranks in row_targets]
        hot = jnp.concatenate(hot, axis=1) if len(hot) > 1 else hot[0]
        write_all(order, out_refs, group * lay.width, dot(hot, stacked).astype(BF16))
    if lay.rest:
        hot, pieces = [], []
        for cut in range(lay.cuts):
            for ranks in row_targets:
                hot.append(onehot([shifted(t[lay.full], cut * lay.rest) for t in ranks]))
            pieces.append(stacked[:, cut * lay.piece : (cut + 1) * lay.piece])
        placed = dot(jnp.concatenate(hot, axis=1), jnp.concatenate(pieces, axis=0))
        write_all(order, out_refs, lay.base, placed.astype(BF16))


def pick(lay, ranks, message):
    count = message.shape[0]
    toks = ranks[0][0].shape[0]
    row_at = iota((toks, count), 1)

    def onehot(rows):
        hit = functools.reduce(jnp.logical_or, [row_at == row for row in rows])
        return jnp.where(hit, 1.0, 0.0).astype(BF16)

    whole = [onehot([t[group] for t in ranks]) for group in range(lay.full)]
    pieces = []
    for cut in range(lay.cuts):
        left = cut * lay.piece
        total = None
        for group in range(lay.full):
            start = group * lay.width + left
            term = dot(whole[group], message[:, start : start + lay.piece])
            total = term if total is None else total + term
        if lay.rest:
            hot = onehot([shifted(t[lay.full], cut * lay.rest) for t in ranks])
            term = dot(hot, message[:, lay.base : lay.base + lay.piece])
            total = term if total is None else total + term
        pieces.append(total)
    return jnp.concatenate(pieces, axis=1) if len(pieces) > 1 else pieces[0]


def rest_selection(lay, order):
    count = order.arrays * order.rows
    small = count // GROUP * lay.rest
    row = iota((small, count), 0)
    col = iota((small, count), 1)
    shift = lay.rest.bit_length() - 1
    home = order.position(lax.shift_right_logical(row, shift)) * GROUP + (row & (lay.rest - 1))
    return [jnp.where(col == home + cut * lay.rest, 1.0, 0.0).astype(BF16) for cut in range(lay.cuts)]


def unpack(lay, order, message_refs, out_ref):
    count = order.arrays * order.rows
    message = read_all(message_refs)
    for group in range(lay.full):
        part = message[:, group * lay.width : (group + 1) * lay.width]
        if not order.apart:
            part = part.astype(F32)
            blocks = [
                part[at * GROUP : (at + 1) * GROUP, :]
                for at in sorted(range(count // GROUP), key=order.block)
            ]
            part = jnp.concatenate(blocks, axis=0).astype(BF16)
        out_ref[group * count : (group + 1) * count, :] = part
    if lay.rest:
        tail = message[:, lay.base :]
        for cut, chosen in enumerate(rest_selection(lay, order)):
            out_ref[lay.full * count :, cut * lay.piece : (cut + 1) * lay.piece] = dot(
                chosen, tail
            ).astype(BF16)


def pack(lay, order, rows_ref, message_refs):
    count = order.arrays * order.rows
    for group in range(lay.full):
        part = rows_ref[group * count : (group + 1) * count, :]
        if not order.apart:
            blocks = [order.block(at) * GROUP for at in range(count // GROUP)]
            part = jnp.concatenate([part[at : at + GROUP, :] for at in blocks], axis=0)
        write_all(order, message_refs, group * lay.width, part.astype(BF16))
    if lay.rest:
        total = None
        for cut, chosen in enumerate(rest_selection(lay, order)):
            part = rows_ref[
                lay.full * count :, cut * lay.piece : (cut + 1) * lay.piece
            ].astype(BF16)
            term = lax.dot_general(
                chosen, part, (((0,), (0,)), ((), ())), preferred_element_type=F32
            )
            total = term if total is None else total + term
        write_all(order, message_refs, lay.base, total.astype(BF16))


def blocks_of(order, ids, mirrored):
    device = lax.axis_index("outer") * lax.axis_size("inner") + lax.axis_index("inner")
    inside = ids - (device & -order.half)
    inside = jnp.where((inside >= 0) & (inside < order.half), inside, -1)
    return jnp.where(inside >= 0, order.position(inside + mirrored * order.half), -1)


def row_targets(lay, order, routes_ref, mirrored, k):
    blocks = blocks_of(order, routes_ref[k : k + 1, :], mirrored)
    slots = jnp.where(blocks >= 0, routes_ref[2 + k : 3 + k, :], lay.capacity)
    return targets(lay, blocks, slots)


def column_targets(lay, order, routes_ref, mirrored, k):
    ids = as_column(routes_ref[k : k + 1, :].astype(F32)).astype(jnp.int32)
    slots = as_column(routes_ref[2 + k : 3 + k, :].astype(F32)).astype(jnp.int32)
    blocks = blocks_of(order, ids, mirrored)
    return targets(lay, blocks, jnp.where(blocks >= 0, slots, lay.capacity))


def send_tokens_kernel(lay, order, routes_ref, tokens_ref, out_ref):
    ranks = [row_targets(lay, order, routes_ref, 0, k) for k in range(2)]
    place(lay, order, [ranks], [tokens_ref[...]], [out_ref])


def send_grads_kernel(
    lay,
    order,
    routes_ref,
    tokens_ref,
    cot_ref,
    mirror_routes_ref,
    mirror_tokens_ref,
    mirror_cot_ref,
    router_ref,
    gates_ref,
    out_ref,
):
    router = router_ref[...]
    ranks, scaled = [], []
    parts = ((routes_ref, tokens_ref, cot_ref), (mirror_routes_ref, mirror_tokens_ref, mirror_cot_ref))
    for mirrored, (routes, tokens, cotangent) in enumerate(parts):
        logits = dot_nt(router, tokens[...])
        expert_at = iota(logits.shape, 0)
        picked = [
            jnp.sum(jnp.where(expert_at == routes[k : k + 1, :], logits, 0.0), axis=0, keepdims=True)
            for k in range(2)
        ]
        gates = [jax.nn.sigmoid(picked[0] - picked[1]), jax.nn.sigmoid(picked[1] - picked[0])]
        cot = cotangent[...].astype(F32)
        for k in range(2):
            gates_ref[2 * mirrored + k : 2 * mirrored + k + 1, :] = gates[k]
            scaled.append((as_column(gates[k]) * cot).astype(BF16))
            ranks.append([row_targets(lay, order, routes, mirrored, k)])
    place(lay, order, ranks, scaled, [out_ref])


def forward_kernel(lay, order, out_order, *refs):
    message_refs = refs[: order.arrays]
    win_ref, wout_ref, hidden_ref = refs[order.arrays : order.arrays + 3]
    out_refs, (rows_ref, total_ref) = refs[order.arrays + 3 : -2], refs[-2:]
    step = pl.program_id(0)

    @pl.when(step == 0)
    def _():
        unpack(lay, order, message_refs, rows_ref)

    hidden = jnp.maximum(dot(rows_ref[...], win_ref[0]), 0.0).astype(BF16)
    hidden_ref[...] = hidden
    term = dot(hidden, wout_ref[0])

    @pl.when(step == 0)
    def _():
        total_ref[...] = term

    @pl.when(step > 0)
    def _():
        total_ref[...] += term

    @pl.when(step == pl.num_programs(0) - 1)
    def _():
        pack(lay, out_order, total_ref, out_refs)


def backward_kernel(lay, order, out_order, *refs):
    message_refs = refs[: order.arrays]
    win_ref, wout_ref, hidden_ref = refs[order.arrays : order.arrays + 3]
    out_refs, (rows_ref, total_ref) = refs[order.arrays + 3 : -2], refs[-2:]
    step = pl.program_id(0)

    @pl.when(step == 0)
    def _():
        unpack(lay, order, message_refs, rows_ref)

    back = dot_nt(rows_ref[...], wout_ref[0])
    back = jnp.where(hidden_ref[...].astype(F32) > 0.0, back, 0.0).astype(BF16)
    term = dot_nt(back, win_ref[0])

    @pl.when(step == 0)
    def _():
        total_ref[...] = term

    @pl.when(step > 0)
    def _():
        total_ref[...] += term

    @pl.when(step == pl.num_programs(0) - 1)
    def _():
        pack(lay, out_order, total_ref, out_refs)


def split_in_two(x):
    high = x.astype(BF16)
    return high, (x - high.astype(F32)).astype(BF16)


def mix_kernel(lay, order, mirrored, routes_ref, gates_ref, cot_ref, message_ref, mixed_ref, actions_ref):
    cot = cot_ref[...].astype(F32)
    message = message_ref[...]
    mixed = None
    for k in range(2):
        choice = pick(lay, [column_targets(lay, order, routes_ref, mirrored, k)], message)
        gate = as_column(gates_ref[2 * mirrored + k : 2 * mirrored + k + 1, :])
        mixed = gate * choice if mixed is None else mixed + gate * choice
        action = jnp.sum(choice * cot, axis=1, keepdims=True)
        actions_ref[k : k + 1, :] = as_row(action)
    mixed_ref[...] = mixed.astype(mixed_ref.dtype)


def slope_kernel(
    routes_ref, gates_ref, actions_ref, mirror_actions_ref, tokens_ref, router_ref, back_ref, partial_ref
):
    experts = router_ref.shape[0]
    toks = tokens_ref.shape[0]
    actions = actions_ref[...] + mirror_actions_ref[...]
    slope = gates_ref[0:1, :] * gates_ref[1:2, :] * (actions[0:1, :] - actions[1:2, :])
    expert_at = iota((experts, toks), 0)
    signs = jnp.where(expert_at == routes_ref[0:1, :], 1.0, 0.0) - jnp.where(
        expert_at == routes_ref[1:2, :], 1.0, 0.0
    )
    parts = split_in_two(signs * slope)
    tokens, router = tokens_ref[...], router_ref[...]
    partial_ref[...] = (dot(parts[0], tokens) + dot(parts[1], tokens)) * (1.0 / toks)
    back = [
        lax.dot_general(part, router, (((0,), (0,)), ((), ())), preferred_element_type=F32)
        for part in parts
    ]
    back_ref[...] = back[0] + back[1]


def grad_kernel(lay, order, mirrored, routes_ref, message_ref, *refs):
    ranks = [column_targets(lay, order, routes_ref, mirrored, k) for k in range(2)]
    total = pick(lay, ranks, message_ref[...])
    if len(refs) > 1:
        total = total + refs[0][...]
    refs[-1][...] = total.astype(refs[-1].dtype)


def call(kernel, out_shape, flops, args):
    moved = sum(a.size * a.dtype.itemsize for a in args)
    moved += sum(o.size * o.dtype.itemsize for o in jax.tree.leaves(out_shape))
    return pl.pallas_call(
        kernel,
        out_shape=out_shape,
        compiler_params=pltpu.CompilerParams(vmem_limit_bytes=VMEM_BYTES),
        cost_estimate=pl.CostEstimate(flops=flops, bytes_accessed=moved, transcendentals=0),
    )(*args)


def messages_of(lay, order):
    return [jax.ShapeDtypeStruct((order.rows, lay.columns), BF16)] * order.arrays


def expert_call(kernel, lay, order, out_order, message, hidden, in_weight, out_weight):
    ff = in_weight.shape[2]
    tile = min(512, ff)
    rows = order.blocks * lay.rows
    win = pl.BlockSpec((1, lay.width, tile), lambda j: (0, 0, j))
    wout = pl.BlockSpec((1, tile, lay.width), lambda j: (0, j, 0))
    hid = pl.BlockSpec((rows, tile), lambda j: (0, j))

    def whole(of):
        return [pl.BlockSpec((of.rows, lay.columns), lambda j: (0, 0))] * of.arrays

    forward = hidden is None
    hidden_shape = [jax.ShapeDtypeStruct((rows, ff), BF16)]
    return pl.pallas_call(
        functools.partial(kernel, lay, order, out_order),
        grid=(ff // tile,),
        in_specs=whole(order) + [win, wout] + ([] if forward else [hid]),
        out_specs=([hid] if forward else []) + whole(out_order),
        out_shape=(hidden_shape if forward else []) + messages_of(lay, out_order),
        scratch_shapes=[pltpu.VMEM((rows, lay.width), BF16), pltpu.VMEM((rows, lay.width), F32)],
        compiler_params=pltpu.CompilerParams(vmem_limit_bytes=VMEM_BYTES),
        cost_estimate=pl.CostEstimate(
            flops=4 * rows * lay.width * ff,
            bytes_accessed=4 * lay.width * ff + 2 * rows * ff + 4 * rows * lay.width,
            transcendentals=0,
        ),
    )(*message, in_weight, out_weight, *([] if forward else [hidden]))


def tied(first, second):
    return lax.optimization_barrier((first, second))


def exchange(x, devices):
    half = devices // 2
    groups = [list(range(half)), list(range(half, devices))]
    return lax.all_to_all(x, AXES, split_axis=0, concat_axis=0, tiled=True, axis_index_groups=groups)


def from_device(x, bits, devices):
    return lax.ppermute(x, AXES, [(d, d ^ bits) for d in range(devices)])


def sum_over_devices(x, devices):
    half = x.shape[0] // 2
    core = lax.axis_index("inner") % 2
    own = lax.dynamic_slice_in_dim(x, core * half, half, 0)
    other = lax.dynamic_slice_in_dim(x, (1 - core) * half, half, 0)
    own = own + from_device(other, 1, devices)
    bit = 2
    while bit < devices:
        if 2 * bit < devices:
            near = own + from_device(own, bit, devices)
            far = from_device(own, 2 * bit, devices) + from_device(own, 3 * bit, devices)
            own = near + far
        else:
            own = own + from_device(own, bit, devices)
        bit *= 4
    other = from_device(own, 1, devices)
    first = core == 0
    return jnp.concatenate([jnp.where(first, own, other), jnp.where(first, other, own)], axis=0)


def on_device(tokens, router_weight, in_weight, out_weight, expert_ids, slot_ids, cotangent):
    tok_rows, model_width = tokens.shape
    experts = router_weight.shape[1]
    devices = lax.axis_size("outer") * lax.axis_size("inner")
    lay = Layout(3 * tok_rows // experts, model_width)
    half = devices // 2
    apart, joined = Order(half, True), Order(half, False)
    router = router_weight.T
    place_flops = 4 * experts * GROUP * tok_rows * model_width
    wide = jax.ShapeDtypeStruct((tok_rows, model_width), F32)
    narrow = jax.ShapeDtypeStruct((tok_rows, model_width), BF16)
    pair = jax.ShapeDtypeStruct((2, tok_rows), F32)

    routes = jnp.concatenate([expert_ids.T, slot_ids.T], axis=0)
    mirror_tokens = from_device(tokens, half, devices)
    mirror_routes = from_device(routes, half, devices)
    mirror_tokens, late_cotangent = tied(mirror_tokens, cotangent)
    mirror_cot = from_device(late_cotangent, half, devices)

    def send_tokens(where, rows):
        message = messages_of(lay, apart)[0]
        return call(
            functools.partial(send_tokens_kernel, lay, apart), message, place_flops, (where, rows)
        )

    arrived = exchange(send_tokens(routes, tokens), devices)
    sent_mirror = send_tokens(mirror_routes, mirror_tokens)
    arrived, sent_mirror = tied(arrived, sent_mirror)
    arrived_mirror = exchange(sent_mirror, devices)
    gates, sent_grads = call(
        functools.partial(send_grads_kernel, lay, joined),
        [jax.ShapeDtypeStruct((4, tok_rows), F32)] + messages_of(lay, joined),
        4 * place_flops,
        (routes, tokens, cotangent, mirror_routes, mirror_tokens, mirror_cot, router),
    )
    arrived_mirror, sent_grads = tied(arrived_mirror, sent_grads)
    grad_rows = exchange(sent_grads, devices)

    hidden, produced = expert_call(
        forward_kernel, lay, apart, joined, [arrived, arrived_mirror], None, in_weight, out_weight
    )
    produced, grad_rows = tied(produced, grad_rows)
    produced_back = exchange(produced, devices)
    (returned,) = expert_call(
        backward_kernel, lay, joined, joined, [grad_rows], hidden, in_weight, out_weight
    )
    returned, produced_back = tied(returned, produced_back)
    returned_back = exchange(returned, devices)

    def mix(mirrored, where, cot, out):
        return call(
            functools.partial(mix_kernel, lay, joined, mirrored),
            [out, pair],
            2 * place_flops,
            (where, gates, cot, produced_back),
        )

    their_mixed, their_actions = mix(1, mirror_routes, mirror_cot, narrow)
    mirror_actions = from_device(their_actions, half, devices)
    mirror_mixed = from_device(their_mixed, half, devices)
    own_mixed, actions = mix(0, routes, cotangent, wide)
    router_back, partial_grad = call(
        slope_kernel,
        [wide, jax.ShapeDtypeStruct((experts, model_width), F32)],
        place_flops // 4,
        (routes, gates, actions, mirror_actions, tokens, router),
    )
    grad_router = sum_over_devices(partial_grad, devices).T
    mixed = (own_mixed + mirror_mixed.astype(F32)).astype(BF16)

    their_grad = call(
        functools.partial(grad_kernel, lay, joined, 1),
        narrow,
        place_flops,
        (mirror_routes, returned_back),
    )
    mirror_grad = from_device(their_grad, half, devices)
    own_grad = call(
        functools.partial(grad_kernel, lay, joined, 0),
        wide,
        place_flops,
        (routes, returned_back, router_back),
    )
    grad_tokens = (own_grad + mirror_grad.astype(F32)).astype(BF16)
    return (mixed, grad_tokens, grad_router)


def solution(mesh):
    placed = (
        P(AXES, None),
        P(),
        P(AXES, None, None),
        P(AXES, None, None),
        P(AXES, None),
        P(AXES, None),
        P(AXES, None),
    )
    return jax.shard_map(
        on_device,
        mesh=mesh,
        in_specs=placed,
        out_specs=(P(AXES, None), P(AXES, None), P()),
        check_vma=False,
    )
```

```python
import functools

import jax
import jax.numpy as jnp
from jax import lax
from jax.experimental import pallas as pl
from jax.experimental.pallas import tpu as pltpu
from jax.sharding import PartitionSpec as P

AXES = ("outer", "inner")
F32 = jnp.float32
BF16 = jnp.bfloat16
GROUP = 8
PLANE = 8
VMEM_BYTES = 60 * 1024 * 1024


class Layout:
    def __init__(self, capacity, model_width):
        self.full, left = divmod(capacity, GROUP)
        self.rest = 0
        if left:
            self.rest = 1
            while self.rest < left:
                self.rest *= 2
        if self.rest == GROUP:
            self.full, self.rest = self.full + 1, 0
        self.capacity = capacity
        self.width = model_width
        self.cuts = GROUP // self.rest if self.rest else 1
        self.piece = model_width // self.cuts
        self.base = self.full * model_width
        self.columns = self.base + (self.piece if self.rest else 0)
        self.rows = self.full * GROUP + self.rest


def dot(a, b):
    return jnp.dot(a, b, preferred_element_type=F32)


def dot_nt(a, b):
    return lax.dot_general(a, b, (((1,), (1,)), ((), ())), preferred_element_type=F32)


def iota(shape, dim):
    return lax.broadcasted_iota(jnp.int32, shape, dim)


def number():
    return lax.axis_index("outer") * lax.axis_size("inner") + lax.axis_index("inner")


def as_column(row):
    count = row.shape[1]
    eye = iota((count, count), 0) == iota((count, count), 1)
    return jnp.sum(jnp.where(eye, row, 0.0), axis=1, keepdims=True)


def as_row(column):
    count = column.shape[0]
    eye = iota((count, count), 0) == iota((count, count), 1)
    return jnp.sum(jnp.where(eye, column, 0.0), axis=0, keepdims=True)


def targets(lay, ids, slots):
    found = []
    kept = slots < lay.capacity
    for group in range(lay.full):
        inside = kept & (slots >= group * GROUP) & (slots < (group + 1) * GROUP)
        found.append(jnp.where(inside, ids * GROUP + slots - group * GROUP, -1))
    if lay.rest:
        inside = kept & (slots >= lay.full * GROUP)
        found.append(jnp.where(inside, ids * GROUP + slots - lay.full * GROUP, -1))
    return found


def shifted(row, by):
    return jnp.where(row >= 0, row + by, -1)


def place(lay, row_targets, values, out_ref):
    count = out_ref.shape[0]
    toks = values[0].shape[0]
    row_at = iota((count, toks), 0)
    stacked = jnp.concatenate(values, axis=0) if len(values) > 1 else values[0]

    def onehot(rows):
        hit = functools.reduce(jnp.logical_or, [row_at == row for row in rows])
        return jnp.where(hit, 1.0, 0.0).astype(BF16)

    for group in range(lay.full):
        hot = [onehot([t[group] for t in ranks]) for ranks in row_targets]
        hot = jnp.concatenate(hot, axis=1) if len(hot) > 1 else hot[0]
        out_ref[:, group * lay.width : (group + 1) * lay.width] = dot(hot, stacked).astype(BF16)
    if lay.rest:
        hot, pieces = [], []
        for cut in range(lay.cuts):
            for ranks in row_targets:
                hot.append(onehot([shifted(t[lay.full], cut * lay.rest) for t in ranks]))
            pieces.append(stacked[:, cut * lay.piece : (cut + 1) * lay.piece])
        out_ref[:, lay.base :] = dot(
            jnp.concatenate(hot, axis=1), jnp.concatenate(pieces, axis=0)
        ).astype(BF16)


def pick(lay, ranks, message_ref):
    count = message_ref.shape[0]
    toks = ranks[0][0].shape[0]
    row_at = iota((toks, count), 1)

    def onehot(rows):
        hit = functools.reduce(jnp.logical_or, [row_at == row for row in rows])
        return jnp.where(hit, 1.0, 0.0).astype(BF16)

    whole = [onehot([t[group] for t in ranks]) for group in range(lay.full)]
    pieces = []
    for cut in range(lay.cuts):
        left = cut * lay.piece
        total = None
        for group in range(lay.full):
            start = group * lay.width + left
            term = dot(whole[group], message_ref[:, start : start + lay.piece])
            total = term if total is None else total + term
        if lay.rest:
            hot = onehot([shifted(t[lay.full], cut * lay.rest) for t in ranks])
            term = dot(hot, message_ref[:, lay.base : lay.base + lay.piece])
            total = term if total is None else total + term
        pieces.append(total)
    return jnp.concatenate(pieces, axis=1) if len(pieces) > 1 else pieces[0]


def rest_selection(lay, count):
    small = count // GROUP * lay.rest
    row = iota((small, count), 0)
    col = iota((small, count), 1)
    shift = lay.rest.bit_length() - 1
    home = lax.shift_right_logical(row, shift) * GROUP + (row & (lay.rest - 1))
    return [jnp.where(col == home + cut * lay.rest, 1.0, 0.0).astype(BF16) for cut in range(lay.cuts)]


def unpack(lay, message_ref, out_ref):
    count = message_ref.shape[0]
    for group in range(lay.full):
        out_ref[group * count : (group + 1) * count, :] = message_ref[
            :, group * lay.width : (group + 1) * lay.width
        ]
    if lay.rest:
        tail = message_ref[:, lay.base :]
        for cut, chosen in enumerate(rest_selection(lay, count)):
            out_ref[lay.full * count :, cut * lay.piece : (cut + 1) * lay.piece] = dot(
                chosen, tail
            ).astype(BF16)


def pack(lay, rows_ref, message_ref):
    count = message_ref.shape[0]
    for group in range(lay.full):
        message_ref[:, group * lay.width : (group + 1) * lay.width] = rows_ref[
            group * count : (group + 1) * count, :
        ].astype(BF16)
    if lay.rest:
        total = None
        for cut, chosen in enumerate(rest_selection(lay, count)):
            part = rows_ref[
                lay.full * count :, cut * lay.piece : (cut + 1) * lay.piece
            ].astype(BF16)
            term = lax.dot_general(
                chosen, part, (((0,), (0,)), ((), ())), preferred_element_type=F32
            )
            total = term if total is None else total + term
        message_ref[:, lay.base :] = total.astype(BF16)


def send_tokens_kernel(lay, ids_ref, slots_ref, tokens_ref, out_ref):
    first = targets(lay, ids_ref[0:1, :], slots_ref[0:1, :])
    second = targets(lay, ids_ref[1:2, :], slots_ref[1:2, :])
    place(lay, [[first, second]], [tokens_ref[...]], out_ref)


def send_grads_kernel(
    lay, ids_ref, slots_ref, tokens_ref, router_ref, cot_ref, out_ref, gates_ref
):
    logits = dot_nt(router_ref[...], tokens_ref[...])
    expert_at = iota(logits.shape, 0)
    picked = [
        jnp.sum(jnp.where(expert_at == ids_ref[k : k + 1, :], logits, 0.0), axis=0, keepdims=True)
        for k in range(2)
    ]
    gates = [jax.nn.sigmoid(picked[0] - picked[1]), jax.nn.sigmoid(picked[1] - picked[0])]
    gates_ref[0:1, :] = gates[0]
    gates_ref[1:2, :] = gates[1]
    cot = cot_ref[...].astype(F32)
    scaled = [(as_column(gate) * cot).astype(BF16) for gate in gates]
    ranks = [[targets(lay, ids_ref[k : k + 1, :], slots_ref[k : k + 1, :])] for k in range(2)]
    place(lay, ranks, scaled, out_ref)


def forward_kernel(lay, message_ref, win_ref, wout_ref, out_ref, hidden_ref, rows_ref, total_ref):
    step = pl.program_id(0)

    @pl.when(step == 0)
    def _():
        unpack(lay, message_ref, rows_ref)

    hidden = jnp.maximum(dot(rows_ref[...], win_ref[0]), 0.0).astype(BF16)
    hidden_ref[...] = hidden
    term = dot(hidden, wout_ref[0])

    @pl.when(step == 0)
    def _():
        total_ref[...] = term

    @pl.when(step > 0)
    def _():
        total_ref[...] += term

    @pl.when(step == pl.num_programs(0) - 1)
    def _():
        pack(lay, total_ref, out_ref)


def backward_kernel(lay, message_ref, hidden_ref, win_ref, wout_ref, out_ref, rows_ref, total_ref):
    step = pl.program_id(0)

    @pl.when(step == 0)
    def _():
        unpack(lay, message_ref, rows_ref)

    back = dot_nt(rows_ref[...], wout_ref[0])
    back = jnp.where(hidden_ref[...].astype(F32) > 0.0, back, 0.0).astype(BF16)
    term = dot_nt(back, win_ref[0])

    @pl.when(step == 0)
    def _():
        total_ref[...] = term

    @pl.when(step > 0)
    def _():
        total_ref[...] += term

    @pl.when(step == pl.num_programs(0) - 1)
    def _():
        pack(lay, total_ref, out_ref)


def column_targets(lay, ids_ref, slots_ref):
    ids = [as_column(ids_ref[k : k + 1, :].astype(F32)).astype(jnp.int32) for k in range(2)]
    slots = [as_column(slots_ref[k : k + 1, :].astype(F32)).astype(jnp.int32) for k in range(2)]
    return ids, [targets(lay, ids[k], slots[k]) for k in range(2)]


def split_in_two(x):
    high = x.astype(BF16)
    return high, (x - high.astype(F32)).astype(BF16)


def mix_kernel(
    lay,
    ids_ref,
    slots_ref,
    gates_ref,
    message_ref,
    cot_ref,
    tokens_ref,
    router_ref,
    mixed_ref,
    back_ref,
    partial_ref,
):
    experts = router_ref.shape[0]
    toks = tokens_ref.shape[0]
    ids, ranks = column_targets(lay, ids_ref, slots_ref)
    gates = [as_column(gates_ref[k : k + 1, :]) for k in range(2)]
    cot = cot_ref[...].astype(F32)
    choice = [pick(lay, [ranks[k]], message_ref) for k in range(2)]
    mixed_ref[...] = (gates[0] * choice[0] + gates[1] * choice[1]).astype(BF16)
    actions = [jnp.sum(choice[k] * cot, axis=1, keepdims=True) for k in range(2)]
    slope = gates[0] * gates[1] * (actions[0] - actions[1])

    expert_at = iota((toks, experts), 1)
    signs = jnp.where(expert_at == ids[0], 1.0, 0.0) - jnp.where(expert_at == ids[1], 1.0, 0.0)
    high, low = split_in_two(signs * slope)
    router = router_ref[...]
    back_ref[...] = dot(high, router) + dot(low, router)

    expert_at = expert_of(iota((experts, toks), 0), experts // PLANE)
    signs = jnp.where(expert_at == ids_ref[0:1, :], 1.0, 0.0) - jnp.where(
        expert_at == ids_ref[1:2, :], 1.0, 0.0
    )
    high, low = split_in_two(signs * as_row(slope))
    tokens = tokens_ref[...]
    partial_ref[...] = (dot(high, tokens) + dot(low, tokens)) * (1.0 / toks)


def grad_kernel(
    lay, ids_ref, slots_ref, message_ref, back_ref, own_ref, other_ref, out_ref, router_ref
):
    _, ranks = column_targets(lay, ids_ref, slots_ref)
    out_ref[...] = (pick(lay, ranks, message_ref) + back_ref[...]).astype(BF16)

    group = own_ref.shape[0] // 4
    device = number()
    swapped = (device & 1) == 1
    own, other = own_ref[...], other_ref[...]
    cores = (jnp.where(swapped, other, own), jnp.where(swapped, own, other))
    for core, rows in enumerate(cores):
        parts = [rows[part * group : (part + 1) * group] for part in range(4)]
        for bit in range(2):
            swapped = (lax.shift_right_logical(device, bit + 1) & 1) == 1
            parts = [jnp.where(swapped, parts[at ^ (1 << bit)], parts[at]) for at in range(4)]
        for chip in range(4):
            for row in range(group):
                at = row * PLANE + chip * 2 + core
                router_ref[at : at + 1, :] = parts[chip][row : row + 1]


def call(kernel, out_shape, flops, args):
    moved = sum(a.size * a.dtype.itemsize for a in args)
    moved += sum(o.size * o.dtype.itemsize for o in jax.tree.leaves(out_shape))
    return pl.pallas_call(
        kernel,
        out_shape=out_shape,
        compiler_params=pltpu.CompilerParams(vmem_limit_bytes=VMEM_BYTES),
        cost_estimate=pl.CostEstimate(flops=flops, bytes_accessed=moved, transcendentals=0),
    )(*args)


def expert_call(kernel, lay, message, hidden, in_weight, out_weight):
    count = message.shape[0]
    ff = in_weight.shape[2]
    tile = min(512, ff)
    rows = count // GROUP * lay.rows
    whole = pl.BlockSpec(message.shape, lambda j: (0, 0))
    win = pl.BlockSpec((1, lay.width, tile), lambda j: (0, 0, j))
    wout = pl.BlockSpec((1, tile, lay.width), lambda j: (0, j, 0))
    hid = pl.BlockSpec((rows, tile), lambda j: (0, j))
    forward = hidden is None
    operands = (message, in_weight, out_weight) if forward else (message, hidden, in_weight, out_weight)
    message_out = jax.ShapeDtypeStruct(message.shape, BF16)
    return pl.pallas_call(
        functools.partial(kernel, lay),
        grid=(ff // tile,),
        in_specs=[whole, win, wout] if forward else [whole, hid, win, wout],
        out_specs=[whole, hid] if forward else whole,
        out_shape=[message_out, jax.ShapeDtypeStruct((rows, ff), BF16)] if forward else message_out,
        scratch_shapes=[pltpu.VMEM((rows, lay.width), BF16), pltpu.VMEM((rows, lay.width), F32)],
        compiler_params=pltpu.CompilerParams(vmem_limit_bytes=VMEM_BYTES),
        cost_estimate=pl.CostEstimate(
            flops=4 * rows * lay.width * ff,
            bytes_accessed=4 * lay.width * ff + 2 * rows * ff + 4 * message.size,
            transcendentals=0,
        ),
    )(*operands)


def exchange(x):
    return lax.all_to_all(x, AXES, split_axis=0, concat_axis=0, tiled=True)


def from_device(x, bits, devices):
    return lax.ppermute(x, AXES, [(d, d ^ bits) for d in range(devices)])


def expert_of(row, group):
    shift = group.bit_length() - 1
    part = lax.shift_right_logical(row, shift)
    low = ((part & 3) << 1) | lax.shift_right_logical(part, 2)
    return ((row & (group - 1)) * PLANE) | (low ^ (number() & (PLANE - 1)))


def sum_over_devices(x, devices):
    half, group = x.shape[0] // 2, x.shape[0] // PLANE
    own = x[:half] + from_device(x[half:], 1, devices)
    parts = [own[part * group : (part + 1) * group] for part in range(4)]
    parts[1:] = [from_device(parts[part], part * 2, devices) for part in range(1, 4)]
    mine = (parts[0] + parts[1]) + (parts[2] + parts[3])
    bit = PLANE
    while bit < devices:
        if 2 * bit < devices:
            near = mine + from_device(mine, bit, devices)
            far = from_device(mine, 2 * bit, devices) + from_device(mine, 3 * bit, devices)
            mine = near + far
        else:
            mine = mine + from_device(mine, bit, devices)
        bit *= 4
    own = jnp.concatenate([mine] + [from_device(mine, part * 2, devices) for part in range(1, 4)], axis=0)
    return own, from_device(own, 1, devices)


def on_device(tokens, router_weight, in_weight, out_weight, expert_ids, slot_ids, cotangent):
    tok_rows, model_width = tokens.shape
    experts = router_weight.shape[1]
    devices = lax.axis_size("outer") * lax.axis_size("inner")
    lay = Layout(3 * tok_rows // experts, model_width)
    message = jax.ShapeDtypeStruct((experts * GROUP, lay.columns), BF16)
    ids, slots, router = expert_ids.T, slot_ids.T, router_weight.T
    place_flops = 4 * experts * GROUP * tok_rows * model_width

    sent_tokens = call(
        functools.partial(send_tokens_kernel, lay), message, place_flops, (ids, slots, tokens)
    )
    sent_grads, gates = call(
        functools.partial(send_grads_kernel, lay),
        [message, jax.ShapeDtypeStruct((2, tok_rows), F32)],
        2 * place_flops,
        (ids, slots, tokens, router, cotangent),
    )
    arrived = exchange(sent_tokens)
    arrived, sent_grads = lax.optimization_barrier((arrived, sent_grads))
    grad_rows = exchange(sent_grads)
    produced, hidden = expert_call(forward_kernel, lay, arrived, None, in_weight, out_weight)
    produced, grad_rows = lax.optimization_barrier((produced, grad_rows))
    produced_back = exchange(produced)
    returned = expert_call(backward_kernel, lay, grad_rows, hidden, in_weight, out_weight)
    returned, produced_back = lax.optimization_barrier((returned, produced_back))
    returned_back = exchange(returned)

    mixed, router_back, partial_grad = call(
        functools.partial(mix_kernel, lay),
        [
            jax.ShapeDtypeStruct((tok_rows, model_width), BF16),
            jax.ShapeDtypeStruct((tok_rows, model_width), F32),
            jax.ShapeDtypeStruct((experts, model_width), F32),
        ],
        2 * place_flops,
        (ids, slots, gates, produced_back, cotangent, tokens, router),
    )
    own_rows, other_rows = sum_over_devices(partial_grad, devices)
    grad_tokens, grad_router = call(
        functools.partial(grad_kernel, lay),
        [
            jax.ShapeDtypeStruct((tok_rows, model_width), BF16),
            jax.ShapeDtypeStruct((experts, model_width), F32),
        ],
        place_flops,
        (ids, slots, returned_back, router_back, own_rows, other_rows),
    )
    return (mixed, grad_tokens, grad_router.T)


def solution(mesh):
    placed = (
        P(AXES, None),
        P(),
        P(AXES, None, None),
        P(AXES, None, None),
        P(AXES, None),
        P(AXES, None),
        P(AXES, None),
    )
    return jax.shard_map(
        on_device,
        mesh=mesh,
        in_specs=placed,
        out_specs=(P(AXES, None), P(AXES, None), P()),
        check_vma=False,
    )
```

```python
import functools

import jax
import jax.numpy as jnp
from jax import lax
from jax.experimental import pallas as pl
from jax.experimental.pallas import tpu as pltpu
from jax.sharding import PartitionSpec as P

AXES = ("outer", "inner")
F32 = jnp.float32
BF16 = jnp.bfloat16
GROUP = 8
PLANE = 8
LANES = 128
VMEM_BYTES = 60 * 1024 * 1024


class Layout:
    def __init__(self, capacity, model_width):
        self.full, left = divmod(capacity, GROUP)
        self.rest = 0
        if left:
            self.rest = 1
            while self.rest < left:
                self.rest *= 2
        if self.rest == GROUP:
            self.full, self.rest = self.full + 1, 0
        self.capacity = capacity
        self.width = model_width
        self.cuts = GROUP // self.rest if self.rest else 1
        self.piece = model_width // self.cuts
        self.base = self.full * model_width
        self.columns = self.base + (self.piece if self.rest else 0)
        self.rows = self.full * GROUP + self.rest


def dot(a, b):
    return jnp.dot(a, b, preferred_element_type=F32)


def dot_nt(a, b):
    return lax.dot_general(a, b, (((1,), (1,)), ((), ())), preferred_element_type=F32)


def iota(shape, dim):
    return lax.broadcasted_iota(jnp.int32, shape, dim)


def number():
    return lax.axis_index("outer") * lax.axis_size("inner") + lax.axis_index("inner")


def as_column(row):
    count = row.shape[1]
    eye = iota((count, count), 0) == iota((count, count), 1)
    return jnp.sum(jnp.where(eye, row, 0.0), axis=1, keepdims=True)


def as_row(column):
    count = column.shape[0]
    eye = iota((count, count), 0) == iota((count, count), 1)
    return jnp.sum(jnp.where(eye, column, 0.0), axis=0, keepdims=True)


def targets(lay, ids, slots):
    found = []
    kept = slots < lay.capacity
    for group in range(lay.full):
        inside = kept & (slots >= group * GROUP) & (slots < (group + 1) * GROUP)
        found.append(jnp.where(inside, ids * GROUP + slots - group * GROUP, -1))
    if lay.rest:
        inside = kept & (slots >= lay.full * GROUP)
        found.append(jnp.where(inside, ids * GROUP + slots - lay.full * GROUP, -1))
    return found


def shifted(row, by):
    return jnp.where(row >= 0, row + by, -1)


def place(lay, row_targets, values, out_ref):
    count = out_ref.shape[0]
    toks = values[0].shape[0]
    row_at = iota((count, toks), 0)
    stacked = jnp.concatenate(values, axis=0) if len(values) > 1 else values[0]

    def onehot(rows):
        hit = functools.reduce(jnp.logical_or, [row_at == row for row in rows])
        return jnp.where(hit, 1.0, 0.0).astype(BF16)

    for group in range(lay.full):
        hot = [onehot([t[group] for t in ranks]) for ranks in row_targets]
        hot = jnp.concatenate(hot, axis=1) if len(hot) > 1 else hot[0]
        out_ref[:, group * lay.width : (group + 1) * lay.width] = dot(hot, stacked).astype(BF16)
    if lay.rest:
        hot, pieces = [], []
        for cut in range(lay.cuts):
            for ranks in row_targets:
                hot.append(onehot([shifted(t[lay.full], cut * lay.rest) for t in ranks]))
            pieces.append(stacked[:, cut * lay.piece : (cut + 1) * lay.piece])
        out_ref[:, lay.base :] = dot(
            jnp.concatenate(hot, axis=1), jnp.concatenate(pieces, axis=0)
        ).astype(BF16)


def row_onehot(rows, count):
    row_at = iota((rows[0].shape[0], count), 1)
    hit = functools.reduce(jnp.logical_or, [row_at == row for row in rows])
    return jnp.where(hit, 1.0, 0.0).astype(BF16)


def pick(lay, ranks, groups, tail):
    whole = []
    if groups is not None:
        whole = [row_onehot([t[at] for t in ranks], groups.shape[0]) for at in range(lay.full)]
    pieces = []
    for cut in range(lay.cuts):
        left = cut * lay.piece
        terms = [
            dot(hot, groups[:, at * lay.width + left : at * lay.width + left + lay.piece])
            for at, hot in enumerate(whole)
        ]
        if lay.rest and tail is not None:
            rows = [shifted(t[lay.full], cut * lay.rest) for t in ranks]
            terms.append(dot(row_onehot(rows, tail.shape[0]), tail))
        pieces.append(functools.reduce(jnp.add, terms))
    return jnp.concatenate(pieces, axis=1) if len(pieces) > 1 else pieces[0]


def rest_selection(lay, count):
    small = count // GROUP * lay.rest
    row = iota((small, count), 0)
    col = iota((small, count), 1)
    shift = lay.rest.bit_length() - 1
    home = lax.shift_right_logical(row, shift) * GROUP + (row & (lay.rest - 1))
    return [jnp.where(col == home + cut * lay.rest, 1.0, 0.0).astype(BF16) for cut in range(lay.cuts)]


def unpack(lay, message_ref, out_ref):
    count = message_ref.shape[0]
    for group in range(lay.full):
        out_ref[group * count : (group + 1) * count, :] = message_ref[
            :, group * lay.width : (group + 1) * lay.width
        ]
    if lay.rest:
        tail = message_ref[:, lay.base :]
        for cut, chosen in enumerate(rest_selection(lay, count)):
            out_ref[lay.full * count :, cut * lay.piece : (cut + 1) * lay.piece] = dot(
                chosen, tail
            ).astype(BF16)


def pack(lay, rows_ref, groups_ref, tail_ref, tail_at):
    count = tail_ref.shape[0]
    for group in range(lay.full):
        groups_ref[:, group * lay.width : (group + 1) * lay.width] = rows_ref[
            group * count : (group + 1) * count, :
        ].astype(BF16)
    if lay.rest:
        total = None
        for cut, chosen in enumerate(rest_selection(lay, count)):
            part = rows_ref[
                lay.full * count :, cut * lay.piece : (cut + 1) * lay.piece
            ].astype(BF16)
            term = lax.dot_general(
                chosen, part, (((0,), (0,)), ((), ())), preferred_element_type=F32
            )
            total = term if total is None else total + term
        tail_ref[:, tail_at : tail_at + lay.piece] = total.astype(BF16)


def send_tokens_kernel(lay, ids_ref, slots_ref, tokens_ref, out_ref):
    first = targets(lay, ids_ref[0:1, :], slots_ref[0:1, :])
    second = targets(lay, ids_ref[1:2, :], slots_ref[1:2, :])
    place(lay, [[first, second]], [tokens_ref[...]], out_ref)


def send_grads_kernel(
    lay, ids_ref, slots_ref, tokens_ref, router_ref, cot_ref, out_ref, gates_ref
):
    logits = dot_nt(router_ref[...], tokens_ref[...])
    expert_at = iota(logits.shape, 0)
    picked = [
        jnp.sum(jnp.where(expert_at == ids_ref[k : k + 1, :], logits, 0.0), axis=0, keepdims=True)
        for k in range(2)
    ]
    gates = [jax.nn.sigmoid(picked[0] - picked[1]), jax.nn.sigmoid(picked[1] - picked[0])]
    gates_ref[0:1, :] = gates[0]
    gates_ref[1:2, :] = gates[1]
    cot = cot_ref[...].astype(F32)
    scaled = [(as_column(gate) * cot).astype(BF16) for gate in gates]
    ranks = [[targets(lay, ids_ref[k : k + 1, :], slots_ref[k : k + 1, :])] for k in range(2)]
    place(lay, ranks, scaled, out_ref)


def forward_kernel(
    lay, message_ref, win_ref, wout_ref, hidden_ref, groups_ref, tail_ref, rows_ref, total_ref
):
    step = pl.program_id(0)

    @pl.when(step == 0)
    def _():
        unpack(lay, message_ref, rows_ref)

    hidden = jnp.maximum(dot(rows_ref[...], win_ref[0]), 0.0).astype(BF16)
    hidden_ref[...] = hidden
    term = dot(hidden, wout_ref[0])

    @pl.when(step == 0)
    def _():
        total_ref[...] = term

    @pl.when(step > 0)
    def _():
        total_ref[...] += term

    @pl.when(step == pl.num_programs(0) - 1)
    def _():
        pack(lay, total_ref, groups_ref, tail_ref, 0)


def backward_kernel(
    lay, message_ref, tail_ref, hidden_ref, win_ref, wout_ref, out_ref, rows_ref, total_ref
):
    step = pl.program_id(0)

    @pl.when(step == 0)
    def _():
        unpack(lay, message_ref, rows_ref)
        out_ref[:, lay.columns :] = tail_ref[...]

    back = dot_nt(rows_ref[...], wout_ref[0])
    back = jnp.where(hidden_ref[...].astype(F32) > 0.0, back, 0.0).astype(BF16)
    term = dot_nt(back, win_ref[0])

    @pl.when(step == 0)
    def _():
        total_ref[...] = term

    @pl.when(step > 0)
    def _():
        total_ref[...] += term

    @pl.when(step == pl.num_programs(0) - 1)
    def _():
        pack(lay, total_ref, out_ref, out_ref, lay.base)


def actions_kernel(lay, *refs):
    tail_ref, grads_ref, out_ref = refs[-3:]
    lane = iota(out_ref.shape, 1)
    parts = [
        (refs[0][:, at * lay.width : (at + 1) * lay.width], at * lay.width, lay.width)
        for at in range(lay.full)
    ]
    if lay.rest:
        parts.append((tail_ref[...], lay.base, lay.piece))
    out = jnp.zeros(out_ref.shape, F32)
    for at, (rows, start, width) in enumerate(parts):
        grads = grads_ref[:, start : start + width]
        action = jnp.sum(rows.astype(F32) * grads.astype(F32), axis=1, keepdims=True)
        high, low = split_in_two(action)
        out = jnp.where(lane == 2 * at, high.astype(F32), out)
        out = jnp.where(lane == 2 * at + 1, low.astype(F32), out)
    out_ref[...] = out.astype(BF16)


def column_targets(lay, ids_ref, slots_ref):
    ids = [as_column(ids_ref[k : k + 1, :].astype(F32)).astype(jnp.int32) for k in range(2)]
    slots = [as_column(slots_ref[k : k + 1, :].astype(F32)).astype(jnp.int32) for k in range(2)]
    return ids, [targets(lay, ids[k], slots[k]) for k in range(2)]


def split_in_two(x):
    high = x.astype(BF16)
    return high, (x - high.astype(F32)).astype(BF16)


def slope_kernel(
    lay, ids_ref, slots_ref, gates_ref, actions_ref, tokens_ref, router_ref, back_ref, partial_ref
):
    experts = router_ref.shape[0]
    toks = tokens_ref.shape[0]
    row_at = iota((actions_ref.shape[0], toks), 0)
    lanes = actions_ref[...].astype(F32)
    lane = iota(lanes.shape, 1)
    sums = [
        jnp.sum(jnp.where((lane == 2 * at) | (lane == 2 * at + 1), lanes, 0.0), axis=1, keepdims=True)
        for at in range(lay.full + (1 if lay.rest else 0))
    ]
    actions = []
    for k in range(2):
        found = targets(lay, ids_ref[k : k + 1, :], slots_ref[k : k + 1, :])
        picked = jnp.zeros(row_at.shape, F32)
        for at in range(lay.full):
            picked = picked + jnp.where(row_at == found[at], sums[at], 0.0)
        if lay.rest:
            for cut in range(lay.cuts):
                row = shifted(found[lay.full], cut * lay.rest)
                picked = picked + jnp.where(row_at == row, sums[lay.full], 0.0)
        actions.append(jnp.sum(picked, axis=0, keepdims=True))
    slope = gates_ref[1:2, :] * actions[0] - gates_ref[0:1, :] * actions[1]

    tokens, router = tokens_ref[...], router_ref[...]

    def signed(expert_at):
        signs = jnp.where(expert_at == ids_ref[0:1, :], 1.0, 0.0) - jnp.where(
            expert_at == ids_ref[1:2, :], 1.0, 0.0
        )
        return split_in_two(signs * slope)

    expert_at = iota((experts, toks), 0)
    high, low = signed(expert_of(expert_at, experts // PLANE))
    partial_ref[...] = (dot(high, tokens) + dot(low, tokens)) * (1.0 / toks)
    back = [
        lax.dot_general(part, router, (((0,), (0,)), ((), ())), preferred_element_type=F32)
        for part in signed(expert_at)
    ]
    back_ref[...] = back[0] + back[1]


def mix_kernel(lay, ids_ref, slots_ref, gates_ref, message_ref, mixed_ref):
    _, ranks = column_targets(lay, ids_ref, slots_ref)
    if lay.full:
        message = message_ref[...]
        gates = [as_column(gates_ref[k : k + 1, :]) for k in range(2)]
        choice = [pick(lay, [ranks[k]], message, None) for k in range(2)]
        mixed_ref[...] = gates[0] * choice[0] + gates[1] * choice[1]
    else:
        mixed_ref[...] = jnp.zeros(mixed_ref.shape, F32)


def last_kernel(
    lay,
    ids_ref,
    slots_ref,
    gates_ref,
    message_ref,
    mixed_ref,
    back_ref,
    own_ref,
    other_ref,
    out_mixed_ref,
    out_ref,
    router_ref,
):
    _, ranks = column_targets(lay, ids_ref, slots_ref)
    groups = message_ref[:, : lay.base] if lay.full else None
    tail = message_ref[:, lay.base : lay.columns]
    out_ref[...] = (pick(lay, ranks, groups, tail) + back_ref[...]).astype(BF16)
    mixed = mixed_ref[...]
    if lay.rest:
        tail = message_ref[:, lay.columns :]
        for k in range(2):
            gate = as_column(gates_ref[k : k + 1, :])
            mixed = mixed + gate * pick(lay, [ranks[k]], None, tail)
    out_mixed_ref[...] = mixed.astype(BF16)

    group = own_ref.shape[0] // 4
    device = number()
    swapped = (device & 1) == 1
    own, other = own_ref[...], other_ref[...]
    cores = (jnp.where(swapped, other, own), jnp.where(swapped, own, other))
    for core, rows in enumerate(cores):
        parts = [rows[part * group : (part + 1) * group] for part in range(4)]
        for bit in range(2):
            swapped = (lax.shift_right_logical(device, bit + 1) & 1) == 1
            parts = [jnp.where(swapped, parts[at ^ (1 << bit)], parts[at]) for at in range(4)]
        for chip in range(4):
            for row in range(group):
                at = row * PLANE + chip * 2 + core
                router_ref[at : at + 1, :] = parts[chip][row : row + 1]


def call(kernel, out_shape, flops, args, blocks=None):
    moved = sum(a.size * a.dtype.itemsize for a in args)
    moved += sum(o.size * o.dtype.itemsize for o in jax.tree.leaves(out_shape))
    grid = {}
    if blocks:
        specs = [pl.BlockSpec(a.shape, lambda j: (0, 0)) for a in args]
        for at, spec in blocks.items():
            specs[at] = spec
        outs = [pl.BlockSpec(o.shape, lambda j: (0, 0)) for o in out_shape]
        grid = dict(grid=(1,), in_specs=specs, out_specs=outs)
    return pl.pallas_call(
        kernel,
        out_shape=out_shape,
        compiler_params=pltpu.CompilerParams(vmem_limit_bytes=VMEM_BYTES),
        cost_estimate=pl.CostEstimate(flops=flops, bytes_accessed=moved, transcendentals=0),
        **grid,
    )(*args)


def expert_call(kernel, lay, message, in_weight, out_weight, backward=()):
    count = message.shape[0]
    ff = in_weight.shape[2]
    tile = min(512, ff)
    rows = count // GROUP * lay.rows

    def whole(columns):
        return pl.BlockSpec((count, columns), lambda j: (0, 0))

    win = pl.BlockSpec((1, lay.width, tile), lambda j: (0, 0, j))
    wout = pl.BlockSpec((1, tile, lay.width), lambda j: (0, j, 0))
    hid = pl.BlockSpec((rows, tile), lambda j: (0, j))
    tail = lay.columns - lay.base
    if backward:
        in_specs = [whole(lay.columns), whole(tail), hid, win, wout]
        out_specs = [whole(lay.columns + tail)]
        out_shape = [jax.ShapeDtypeStruct((count, lay.columns + tail), BF16)]
    else:
        in_specs = [whole(lay.columns), win, wout]
        out_specs = [hid, whole(lay.base + LANES), whole(tail)]
        out_shape = [
            jax.ShapeDtypeStruct((rows, ff), BF16),
            jax.ShapeDtypeStruct((count, lay.base + LANES), BF16),
            jax.ShapeDtypeStruct((count, tail), BF16),
        ]
    return pl.pallas_call(
        functools.partial(kernel, lay),
        grid=(ff // tile,),
        in_specs=in_specs,
        out_specs=out_specs,
        out_shape=out_shape,
        scratch_shapes=[pltpu.VMEM((rows, lay.width), BF16), pltpu.VMEM((rows, lay.width), F32)],
        compiler_params=pltpu.CompilerParams(vmem_limit_bytes=VMEM_BYTES),
        cost_estimate=pl.CostEstimate(
            flops=4 * rows * lay.width * ff,
            bytes_accessed=4 * lay.width * ff + 2 * rows * ff + 4 * rows * lay.width,
            transcendentals=0,
        ),
    )(message, *backward, in_weight, out_weight)


def with_actions(lay, produced, tail, grad_rows):
    count = produced.shape[0]
    specs = [
        pl.BlockSpec((count, lay.base), lambda j: (0, 0)),
        pl.BlockSpec(tail.shape, lambda j: (0, 0)),
        pl.BlockSpec(grad_rows.shape, lambda j: (0, 0)),
    ]
    operands = (produced, tail, grad_rows)
    start = 0 if lay.full else 1
    return pl.pallas_call(
        functools.partial(actions_kernel, lay),
        grid=(1,),
        in_specs=specs[start:],
        out_specs=pl.BlockSpec((count, LANES), lambda j: (0, lay.base // LANES)),
        out_shape=jax.ShapeDtypeStruct(produced.shape, BF16),
        input_output_aliases={0: 0} if lay.full else {},
        compiler_params=pltpu.CompilerParams(vmem_limit_bytes=VMEM_BYTES),
        cost_estimate=pl.CostEstimate(
            flops=2 * grad_rows.size, bytes_accessed=4 * grad_rows.size, transcendentals=0
        ),
    )(*operands[start:])


def exchange(x):
    return lax.all_to_all(x, AXES, split_axis=0, concat_axis=0, tiled=True)


def from_device(x, bits, devices):
    return lax.ppermute(x, AXES, [(d, d ^ bits) for d in range(devices)])


def expert_of(row, group):
    shift = group.bit_length() - 1
    part = lax.shift_right_logical(row, shift)
    low = ((part & 3) << 1) | lax.shift_right_logical(part, 2)
    return ((row & (group - 1)) * PLANE) | (low ^ (number() & (PLANE - 1)))


def sum_over_devices(x, devices):
    half, group = x.shape[0] // 2, x.shape[0] // PLANE
    own = x[:half] + from_device(x[half:], 1, devices)
    parts = [own[part * group : (part + 1) * group] for part in range(4)]
    parts[1:] = [from_device(parts[part], part * 2, devices) for part in range(1, 4)]
    mine = (parts[0] + parts[1]) + (parts[2] + parts[3])
    bit = PLANE
    while bit < devices:
        if 2 * bit < devices:
            near = mine + from_device(mine, bit, devices)
            far = from_device(mine, 2 * bit, devices) + from_device(mine, 3 * bit, devices)
            mine = near + far
        else:
            mine = mine + from_device(mine, bit, devices)
        bit *= 4
    own = jnp.concatenate([mine] + [from_device(mine, part * 2, devices) for part in range(1, 4)], axis=0)
    return own, from_device(own, 1, devices)


def on_device(tokens, router_weight, in_weight, out_weight, expert_ids, slot_ids, cotangent):
    tok_rows, model_width = tokens.shape
    experts = router_weight.shape[1]
    devices = lax.axis_size("outer") * lax.axis_size("inner")
    lay = Layout(3 * tok_rows // experts, model_width)
    message = jax.ShapeDtypeStruct((experts * GROUP, lay.columns), BF16)
    ids, slots, router = expert_ids.T, slot_ids.T, router_weight.T
    place_flops = 4 * experts * GROUP * tok_rows * model_width

    sent_tokens = call(
        functools.partial(send_tokens_kernel, lay), message, place_flops, (ids, slots, tokens)
    )
    sent_grads, gates = call(
        functools.partial(send_grads_kernel, lay),
        [message, jax.ShapeDtypeStruct((2, tok_rows), F32)],
        2 * place_flops,
        (ids, slots, tokens, router, cotangent),
    )
    arrived = exchange(sent_tokens)
    arrived, sent_grads = lax.optimization_barrier((arrived, sent_grads))
    grad_rows = exchange(sent_grads)
    hidden, produced, tail = expert_call(forward_kernel, lay, arrived, in_weight, out_weight)
    produced_back = exchange(with_actions(lay, produced, tail, grad_rows))
    (returned,) = expert_call(
        backward_kernel, lay, grad_rows, in_weight, out_weight, (tail, hidden)
    )
    returned, produced_back = lax.optimization_barrier((returned, produced_back))
    returned_back = exchange(returned)

    wide = jax.ShapeDtypeStruct((tok_rows, model_width), F32)
    narrow = jax.ShapeDtypeStruct((tok_rows, model_width), BF16)
    rows_of_router = jax.ShapeDtypeStruct((experts, model_width), F32)
    router_back, partial_grad = call(
        functools.partial(slope_kernel, lay),
        [wide, rows_of_router],
        place_flops // 4,
        (ids, slots, gates, produced_back, tokens, router),
        {3: pl.BlockSpec((experts * GROUP, LANES), lambda j: (0, lay.base // LANES))},
    )
    own_rows, other_rows = sum_over_devices(partial_grad, devices)
    first_mixed = call(
        functools.partial(mix_kernel, lay),
        wide,
        place_flops,
        (ids, slots, gates, produced_back),
    )
    mixed, grad_tokens, grad_router = call(
        functools.partial(last_kernel, lay),
        [narrow, narrow, rows_of_router],
        place_flops,
        (ids, slots, gates, returned_back, first_mixed, router_back, own_rows, other_rows),
    )
    return (mixed, grad_tokens, grad_router.T)


def solution(mesh):
    placed = (
        P(AXES, None),
        P(),
        P(AXES, None, None),
        P(AXES, None, None),
        P(AXES, None),
        P(AXES, None),
        P(AXES, None),
    )
    return jax.shard_map(
        on_device,
        mesh=mesh,
        in_specs=placed,
        out_specs=(P(AXES, None), P(AXES, None), P()),
        check_vma=False,
    )
```

```python
import functools

import jax
import jax.numpy as jnp
from jax import lax
from jax.experimental import pallas as pl
from jax.experimental.pallas import tpu as pltpu
from jax.sharding import PartitionSpec as P

AXES = ("outer", "inner")
F32 = jnp.float32
BF16 = jnp.bfloat16
GROUP = 8
VMEM_BYTES = 60 * 1024 * 1024


class Layout:
    def __init__(self, capacity, model_width):
        self.full, left = divmod(capacity, GROUP)
        self.rest = 0
        if left:
            self.rest = 1
            while self.rest < left:
                self.rest *= 2
        if self.rest == GROUP:
            self.full, self.rest = self.full + 1, 0
        self.capacity = capacity
        self.width = model_width
        self.cuts = GROUP // self.rest if self.rest else 1
        self.piece = model_width // self.cuts
        self.base = self.full * model_width
        self.columns = self.base + (self.piece if self.rest else 0)
        self.rows = self.full * GROUP + self.rest


def dot(a, b):
    return jnp.dot(a, b, preferred_element_type=F32)


def dot_nt(a, b):
    return lax.dot_general(a, b, (((1,), (1,)), ((), ())), preferred_element_type=F32)


def iota(shape, dim):
    return lax.broadcasted_iota(jnp.int32, shape, dim)


def as_column(row):
    count = row.shape[1]
    eye = iota((count, count), 0) == iota((count, count), 1)
    return jnp.sum(jnp.where(eye, row, 0.0), axis=1, keepdims=True)


def as_row(column):
    count = column.shape[0]
    eye = iota((count, count), 0) == iota((count, count), 1)
    return jnp.sum(jnp.where(eye, column, 0.0), axis=0, keepdims=True)


def targets(lay, ids, slots):
    found = []
    kept = slots < lay.capacity
    for group in range(lay.full):
        inside = kept & (slots >= group * GROUP) & (slots < (group + 1) * GROUP)
        found.append(jnp.where(inside, ids * GROUP + slots - group * GROUP, -1))
    if lay.rest:
        inside = kept & (slots >= lay.full * GROUP)
        found.append(jnp.where(inside, ids * GROUP + slots - lay.full * GROUP, -1))
    return found


def shifted(row, by):
    return jnp.where(row >= 0, row + by, -1)


def place(lay, row_targets, values, out_ref):
    count = out_ref.shape[0]
    toks = values[0].shape[0]
    row_at = iota((count, toks), 0)
    stacked = jnp.concatenate(values, axis=0) if len(values) > 1 else values[0]

    def onehot(rows):
        hit = functools.reduce(jnp.logical_or, [row_at == row for row in rows])
        return jnp.where(hit, 1.0, 0.0).astype(BF16)

    for group in range(lay.full):
        hot = [onehot([t[group] for t in ranks]) for ranks in row_targets]
        hot = jnp.concatenate(hot, axis=1) if len(hot) > 1 else hot[0]
        out_ref[:, group * lay.width : (group + 1) * lay.width] = dot(hot, stacked).astype(BF16)
    if lay.rest:
        hot, pieces = [], []
        for cut in range(lay.cuts):
            for ranks in row_targets:
                hot.append(onehot([shifted(t[lay.full], cut * lay.rest) for t in ranks]))
            pieces.append(stacked[:, cut * lay.piece : (cut + 1) * lay.piece])
        out_ref[:, lay.base :] = dot(
            jnp.concatenate(hot, axis=1), jnp.concatenate(pieces, axis=0)
        ).astype(BF16)


def pick(lay, ranks, message_ref):
    count = message_ref.shape[0]
    toks = ranks[0][0].shape[0]
    row_at = iota((toks, count), 1)

    def onehot(rows):
        hit = functools.reduce(jnp.logical_or, [row_at == row for row in rows])
        return jnp.where(hit, 1.0, 0.0).astype(BF16)

    whole = [onehot([t[group] for t in ranks]) for group in range(lay.full)]
    pieces = []
    for cut in range(lay.cuts):
        left = cut * lay.piece
        total = None
        for group in range(lay.full):
            start = group * lay.width + left
            term = dot(whole[group], message_ref[:, start : start + lay.piece])
            total = term if total is None else total + term
        if lay.rest:
            hot = onehot([shifted(t[lay.full], cut * lay.rest) for t in ranks])
            term = dot(hot, message_ref[:, lay.base : lay.base + lay.piece])
            total = term if total is None else total + term
        pieces.append(total)
    return jnp.concatenate(pieces, axis=1) if len(pieces) > 1 else pieces[0]


def rest_selection(lay, count):
    small = count // GROUP * lay.rest
    row = iota((small, count), 0)
    col = iota((small, count), 1)
    shift = lay.rest.bit_length() - 1
    home = lax.shift_right_logical(row, shift) * GROUP + (row & (lay.rest - 1))
    return [jnp.where(col == home + cut * lay.rest, 1.0, 0.0).astype(BF16) for cut in range(lay.cuts)]


def unpack(lay, message_ref, out_ref):
    count = message_ref.shape[0]
    for group in range(lay.full):
        out_ref[group * count : (group + 1) * count, :] = message_ref[
            :, group * lay.width : (group + 1) * lay.width
        ]
    if lay.rest:
        tail = message_ref[:, lay.base :]
        for cut, chosen in enumerate(rest_selection(lay, count)):
            out_ref[lay.full * count :, cut * lay.piece : (cut + 1) * lay.piece] = dot(
                chosen, tail
            ).astype(BF16)


def pack(lay, rows_ref, message_ref):
    count = message_ref.shape[0]
    for group in range(lay.full):
        message_ref[:, group * lay.width : (group + 1) * lay.width] = rows_ref[
            group * count : (group + 1) * count, :
        ].astype(BF16)
    if lay.rest:
        total = None
        for cut, chosen in enumerate(rest_selection(lay, count)):
            part = rows_ref[
                lay.full * count :, cut * lay.piece : (cut + 1) * lay.piece
            ].astype(BF16)
            term = lax.dot_general(
                chosen, part, (((0,), (0,)), ((), ())), preferred_element_type=F32
            )
            total = term if total is None else total + term
        message_ref[:, lay.base :] = total.astype(BF16)


def send_tokens_kernel(lay, ids_ref, slots_ref, tokens_ref, out_ref):
    first = targets(lay, ids_ref[0:1, :], slots_ref[0:1, :])
    second = targets(lay, ids_ref[1:2, :], slots_ref[1:2, :])
    place(lay, [[first, second]], [tokens_ref[...]], out_ref)


def send_grads_kernel(
    lay, ids_ref, slots_ref, tokens_ref, router_ref, cot_ref, out_ref, gates_ref
):
    logits = dot_nt(router_ref[...], tokens_ref[...])
    expert_at = iota(logits.shape, 0)
    picked = [
        jnp.sum(jnp.where(expert_at == ids_ref[k : k + 1, :], logits, 0.0), axis=0, keepdims=True)
        for k in range(2)
    ]
    gates = [jax.nn.sigmoid(picked[0] - picked[1]), jax.nn.sigmoid(picked[1] - picked[0])]
    gates_ref[0:1, :] = gates[0]
    gates_ref[1:2, :] = gates[1]
    cot = cot_ref[...].astype(F32)
    scaled = [(as_column(gate) * cot).astype(BF16) for gate in gates]
    ranks = [[targets(lay, ids_ref[k : k + 1, :], slots_ref[k : k + 1, :])] for k in range(2)]
    place(lay, ranks, scaled, out_ref)


def forward_kernel(lay, message_ref, win_ref, wout_ref, out_ref, hidden_ref, rows_ref, total_ref):
    step = pl.program_id(0)

    @pl.when(step == 0)
    def _():
        unpack(lay, message_ref, rows_ref)

    hidden = jnp.maximum(dot(rows_ref[...], win_ref[0]), 0.0).astype(BF16)
    hidden_ref[...] = hidden
    term = dot(hidden, wout_ref[0])

    @pl.when(step == 0)
    def _():
        total_ref[...] = term

    @pl.when(step > 0)
    def _():
        total_ref[...] += term

    @pl.when(step == pl.num_programs(0) - 1)
    def _():
        pack(lay, total_ref, out_ref)


def backward_kernel(lay, message_ref, hidden_ref, win_ref, wout_ref, out_ref, rows_ref, total_ref):
    step = pl.program_id(0)

    @pl.when(step == 0)
    def _():
        unpack(lay, message_ref, rows_ref)

    back = dot_nt(rows_ref[...], wout_ref[0])
    back = jnp.where(hidden_ref[...].astype(F32) > 0.0, back, 0.0).astype(BF16)
    term = dot_nt(back, win_ref[0])

    @pl.when(step == 0)
    def _():
        total_ref[...] = term

    @pl.when(step > 0)
    def _():
        total_ref[...] += term

    @pl.when(step == pl.num_programs(0) - 1)
    def _():
        pack(lay, total_ref, out_ref)


def column_targets(lay, ids_ref, slots_ref):
    ids = [as_column(ids_ref[k : k + 1, :].astype(F32)).astype(jnp.int32) for k in range(2)]
    slots = [as_column(slots_ref[k : k + 1, :].astype(F32)).astype(jnp.int32) for k in range(2)]
    return ids, [targets(lay, ids[k], slots[k]) for k in range(2)]


def split_in_two(x):
    high = x.astype(BF16)
    return high, (x - high.astype(F32)).astype(BF16)


def mix_kernel(
    lay,
    ids_ref,
    slots_ref,
    gates_ref,
    message_ref,
    cot_ref,
    tokens_ref,
    router_ref,
    mixed_ref,
    back_ref,
    partial_ref,
):
    experts = router_ref.shape[0]
    toks = tokens_ref.shape[0]
    ids, ranks = column_targets(lay, ids_ref, slots_ref)
    gates = [as_column(gates_ref[k : k + 1, :]) for k in range(2)]
    cot = cot_ref[...].astype(F32)
    choice = [pick(lay, [ranks[k]], message_ref) for k in range(2)]
    mixed_ref[...] = (gates[0] * choice[0] + gates[1] * choice[1]).astype(BF16)
    actions = [jnp.sum(choice[k] * cot, axis=1, keepdims=True) for k in range(2)]
    slope = gates[0] * gates[1] * (actions[0] - actions[1])

    expert_at = iota((toks, experts), 1)
    signs = jnp.where(expert_at == ids[0], 1.0, 0.0) - jnp.where(expert_at == ids[1], 1.0, 0.0)
    high, low = split_in_two(signs * slope)
    router = router_ref[...]
    back_ref[...] = dot(high, router) + dot(low, router)

    expert_at = iota((experts, toks), 0)
    signs = jnp.where(expert_at == ids_ref[0:1, :], 1.0, 0.0) - jnp.where(
        expert_at == ids_ref[1:2, :], 1.0, 0.0
    )
    high, low = split_in_two(signs * as_row(slope))
    tokens = tokens_ref[...]
    partial_ref[...] = (dot(high, tokens) + dot(low, tokens)) * (1.0 / toks)


def grad_kernel(lay, ids_ref, slots_ref, message_ref, back_ref, out_ref):
    _, ranks = column_targets(lay, ids_ref, slots_ref)
    out_ref[...] = (pick(lay, ranks, message_ref) + back_ref[...]).astype(BF16)


def call(kernel, out_shape, flops, args):
    moved = sum(a.size * a.dtype.itemsize for a in args)
    moved += sum(o.size * o.dtype.itemsize for o in jax.tree.leaves(out_shape))
    return pl.pallas_call(
        kernel,
        out_shape=out_shape,
        compiler_params=pltpu.CompilerParams(vmem_limit_bytes=VMEM_BYTES),
        cost_estimate=pl.CostEstimate(flops=flops, bytes_accessed=moved, transcendentals=0),
    )(*args)


def expert_call(kernel, lay, message, hidden, in_weight, out_weight):
    count = message.shape[0]
    ff = in_weight.shape[2]
    tile = min(512, ff)
    rows = count // GROUP * lay.rows
    whole = pl.BlockSpec(message.shape, lambda j: (0, 0))
    win = pl.BlockSpec((1, lay.width, tile), lambda j: (0, 0, j))
    wout = pl.BlockSpec((1, tile, lay.width), lambda j: (0, j, 0))
    hid = pl.BlockSpec((rows, tile), lambda j: (0, j))
    forward = hidden is None
    operands = (message, in_weight, out_weight) if forward else (message, hidden, in_weight, out_weight)
    message_out = jax.ShapeDtypeStruct(message.shape, BF16)
    return pl.pallas_call(
        functools.partial(kernel, lay),
        grid=(ff // tile,),
        in_specs=[whole, win, wout] if forward else [whole, hid, win, wout],
        out_specs=[whole, hid] if forward else whole,
        out_shape=[message_out, jax.ShapeDtypeStruct((rows, ff), BF16)] if forward else message_out,
        scratch_shapes=[pltpu.VMEM((rows, lay.width), BF16), pltpu.VMEM((rows, lay.width), F32)],
        compiler_params=pltpu.CompilerParams(vmem_limit_bytes=VMEM_BYTES),
        cost_estimate=pl.CostEstimate(
            flops=4 * rows * lay.width * ff,
            bytes_accessed=4 * lay.width * ff + 2 * rows * ff + 4 * message.size,
            transcendentals=0,
        ),
    )(*operands)


def exchange(x):
    return lax.all_to_all(x, AXES, split_axis=0, concat_axis=0, tiled=True)


def from_device(x, bits, devices):
    return lax.ppermute(x, AXES, [(d, d ^ bits) for d in range(devices)])


def sum_of_pairs(own, near, far, both):
    return (own + near) + (far + both)


def sum_over_devices(x, devices, beside):
    half = x.shape[0] // 2
    core = lax.axis_index("inner") % 2
    own = lax.dynamic_slice_in_dim(x, core * half, half, 0)
    other = lax.dynamic_slice_in_dim(x, (1 - core) * half, half, 0)
    own = own + from_device(other, 1, devices)
    bit = 2
    while bit < devices:
        sent = own if bit == 2 else own.astype(BF16)
        steps = [1, 2, 3] if 2 * bit < devices else [1]
        terms = [from_device(sent, step * bit, devices) for step in steps]
        if bit * 4 >= devices:
            beside, sent, *terms = lax.optimization_barrier((beside, sent, *terms))
        terms = [term.astype(F32) for term in [sent] + terms]
        own = sum_of_pairs(*terms) if len(terms) == 4 else terms[0] + terms[1]
        bit *= 4
    other = from_device(own, 1, devices)
    first = core == 0
    total = jnp.concatenate([jnp.where(first, own, other), jnp.where(first, other, own)], axis=0)
    return total, beside


def on_device(tokens, router_weight, in_weight, out_weight, expert_ids, slot_ids, cotangent):
    tok_rows, model_width = tokens.shape
    experts = router_weight.shape[1]
    devices = lax.axis_size("outer") * lax.axis_size("inner")
    lay = Layout(3 * tok_rows // experts, model_width)
    message = jax.ShapeDtypeStruct((experts * GROUP, lay.columns), BF16)
    ids, slots, router = expert_ids.T, slot_ids.T, router_weight.T
    place_flops = 4 * experts * GROUP * tok_rows * model_width

    sent_tokens = call(
        functools.partial(send_tokens_kernel, lay), message, place_flops, (ids, slots, tokens)
    )
    sent_grads, gates = call(
        functools.partial(send_grads_kernel, lay),
        [message, jax.ShapeDtypeStruct((2, tok_rows), F32)],
        2 * place_flops,
        (ids, slots, tokens, router, cotangent),
    )
    arrived = exchange(sent_tokens)
    arrived, sent_grads = lax.optimization_barrier((arrived, sent_grads))
    grad_rows = exchange(sent_grads)
    produced, hidden = expert_call(forward_kernel, lay, arrived, None, in_weight, out_weight)
    produced, grad_rows = lax.optimization_barrier((produced, grad_rows))
    produced_back = exchange(produced)
    returned = expert_call(backward_kernel, lay, grad_rows, hidden, in_weight, out_weight)
    returned, produced_back = lax.optimization_barrier((returned, produced_back))
    returned_back = exchange(returned)

    mixed, router_back, partial_grad = call(
        functools.partial(mix_kernel, lay),
        [
            jax.ShapeDtypeStruct((tok_rows, model_width), BF16),
            jax.ShapeDtypeStruct((tok_rows, model_width), F32),
            jax.ShapeDtypeStruct((experts, model_width), F32),
        ],
        2 * place_flops,
        (ids, slots, gates, produced_back, cotangent, tokens, router),
    )
    grad_tokens = call(
        functools.partial(grad_kernel, lay),
        jax.ShapeDtypeStruct((tok_rows, model_width), BF16),
        place_flops,
        (ids, slots, returned_back, router_back),
    )
    grad_router, grad_tokens = sum_over_devices(partial_grad, devices, grad_tokens)
    return (mixed, grad_tokens, grad_router.T)


def solution(mesh):
    placed = (
        P(AXES, None),
        P(),
        P(AXES, None, None),
        P(AXES, None, None),
        P(AXES, None),
        P(AXES, None),
        P(AXES, None),
    )
    return jax.shard_map(
        on_device,
        mesh=mesh,
        in_specs=placed,
        out_specs=(P(AXES, None), P(AXES, None), P()),
        check_vma=False,
    )
```

```python
import functools

import jax
import jax.numpy as jnp
from jax import lax
from jax.experimental import pallas as pl
from jax.experimental.pallas import tpu as pltpu
from jax.sharding import PartitionSpec as P

AXES = ("outer", "inner")
F32 = jnp.float32
BF16 = jnp.bfloat16
GROUP = 8
VMEM_BYTES = 60 * 1024 * 1024
SMALL_VMEM_BYTES = 24 * 1024 * 1024


class Layout:
    def __init__(self, capacity, model_width):
        self.full, left = divmod(capacity, GROUP)
        self.rest = 0
        if left:
            self.rest = 1
            while self.rest < left:
                self.rest *= 2
        if self.rest == GROUP:
            self.full, self.rest = self.full + 1, 0
        self.capacity = capacity
        self.width = model_width
        self.cuts = GROUP // self.rest if self.rest else 1
        self.piece = model_width // self.cuts
        self.base = self.full * model_width
        self.columns = self.base + (self.piece if self.rest else 0)
        self.rows = self.full * GROUP + self.rest


def dot(a, b):
    return jnp.dot(a, b, preferred_element_type=F32)


def dot_nt(a, b):
    return lax.dot_general(a, b, (((1,), (1,)), ((), ())), preferred_element_type=F32)


def iota(shape, dim):
    return lax.broadcasted_iota(jnp.int32, shape, dim)


def as_column(row):
    count = row.shape[1]
    eye = iota((count, count), 0) == iota((count, count), 1)
    return jnp.sum(jnp.where(eye, row, 0.0), axis=1, keepdims=True)


def as_row(column):
    count = column.shape[0]
    eye = iota((count, count), 0) == iota((count, count), 1)
    return jnp.sum(jnp.where(eye, column, 0.0), axis=0, keepdims=True)


def targets(lay, ids, slots):
    found = []
    kept = slots < lay.capacity
    for group in range(lay.full):
        inside = kept & (slots >= group * GROUP) & (slots < (group + 1) * GROUP)
        found.append(jnp.where(inside, ids * GROUP + slots - group * GROUP, -1))
    if lay.rest:
        inside = kept & (slots >= lay.full * GROUP)
        found.append(jnp.where(inside, ids * GROUP + slots - lay.full * GROUP, -1))
    return found


def shifted(row, by):
    return jnp.where(row >= 0, row + by, -1)


def place(lay, row_targets, values, out_ref):
    count = out_ref.shape[0]
    toks = values[0].shape[0]
    row_at = iota((count, toks), 0)
    stacked = jnp.concatenate(values, axis=0) if len(values) > 1 else values[0]

    def onehot(rows):
        hit = functools.reduce(jnp.logical_or, [row_at == row for row in rows])
        return jnp.where(hit, 1.0, 0.0).astype(BF16)

    for group in range(lay.full):
        hot = [onehot([t[group] for t in ranks]) for ranks in row_targets]
        hot = jnp.concatenate(hot, axis=1) if len(hot) > 1 else hot[0]
        out_ref[:, group * lay.width : (group + 1) * lay.width] = dot(hot, stacked).astype(BF16)
    if lay.rest:
        hot, pieces = [], []
        for cut in range(lay.cuts):
            for ranks in row_targets:
                hot.append(onehot([shifted(t[lay.full], cut * lay.rest) for t in ranks]))
            pieces.append(stacked[:, cut * lay.piece : (cut + 1) * lay.piece])
        out_ref[:, lay.base :] = dot(
            jnp.concatenate(hot, axis=1), jnp.concatenate(pieces, axis=0)
        ).astype(BF16)


def pick(lay, ranks, message_ref):
    count = message_ref.shape[0]
    toks = ranks[0][0].shape[0]
    row_at = iota((toks, count), 1)

    def onehot(rows):
        hit = functools.reduce(jnp.logical_or, [row_at == row for row in rows])
        return jnp.where(hit, 1.0, 0.0).astype(BF16)

    whole = [onehot([t[group] for t in ranks]) for group in range(lay.full)]
    pieces = []
    for cut in range(lay.cuts):
        left = cut * lay.piece
        total = None
        for group in range(lay.full):
            start = group * lay.width + left
            term = dot(whole[group], message_ref[:, start : start + lay.piece])
            total = term if total is None else total + term
        if lay.rest:
            hot = onehot([shifted(t[lay.full], cut * lay.rest) for t in ranks])
            term = dot(hot, message_ref[:, lay.base : lay.base + lay.piece])
            total = term if total is None else total + term
        pieces.append(total)
    return jnp.concatenate(pieces, axis=1) if len(pieces) > 1 else pieces[0]


def rest_selection(lay, count):
    small = count // GROUP * lay.rest
    row = iota((small, count), 0)
    col = iota((small, count), 1)
    shift = lay.rest.bit_length() - 1
    home = lax.shift_right_logical(row, shift) * GROUP + (row & (lay.rest - 1))
    return [jnp.where(col == home + cut * lay.rest, 1.0, 0.0).astype(BF16) for cut in range(lay.cuts)]


def unpack(lay, message_ref, out_ref):
    count = message_ref.shape[0]
    for group in range(lay.full):
        out_ref[group * count : (group + 1) * count, :] = message_ref[
            :, group * lay.width : (group + 1) * lay.width
        ]
    if lay.rest:
        tail = message_ref[:, lay.base :]
        for cut, chosen in enumerate(rest_selection(lay, count)):
            out_ref[lay.full * count :, cut * lay.piece : (cut + 1) * lay.piece] = dot(
                chosen, tail
            ).astype(BF16)


def pack(lay, rows_ref, message_ref):
    count = message_ref.shape[0]
    for group in range(lay.full):
        message_ref[:, group * lay.width : (group + 1) * lay.width] = rows_ref[
            group * count : (group + 1) * count, :
        ].astype(BF16)
    if lay.rest:
        total = None
        for cut, chosen in enumerate(rest_selection(lay, count)):
            part = rows_ref[
                lay.full * count :, cut * lay.piece : (cut + 1) * lay.piece
            ].astype(BF16)
            term = lax.dot_general(
                chosen, part, (((0,), (0,)), ((), ())), preferred_element_type=F32
            )
            total = term if total is None else total + term
        message_ref[:, lay.base :] = total.astype(BF16)


def send_tokens_kernel(lay, ids_ref, slots_ref, tokens_ref, out_ref):
    first = targets(lay, ids_ref[0:1, :], slots_ref[0:1, :])
    second = targets(lay, ids_ref[1:2, :], slots_ref[1:2, :])
    place(lay, [[first, second]], [tokens_ref[...]], out_ref)


def send_grads_kernel(
    lay, ids_ref, slots_ref, tokens_ref, router_ref, cot_ref, out_ref, gates_ref
):
    logits = dot_nt(router_ref[...], tokens_ref[...])
    expert_at = iota(logits.shape, 0)
    picked = [
        jnp.sum(jnp.where(expert_at == ids_ref[k : k + 1, :], logits, 0.0), axis=0, keepdims=True)
        for k in range(2)
    ]
    gates = [jax.nn.sigmoid(picked[0] - picked[1]), jax.nn.sigmoid(picked[1] - picked[0])]
    gates_ref[0:1, :] = gates[0]
    gates_ref[1:2, :] = gates[1]
    cot = cot_ref[...].astype(F32)
    scaled = [(as_column(gate) * cot).astype(BF16) for gate in gates]
    ranks = [[targets(lay, ids_ref[k : k + 1, :], slots_ref[k : k + 1, :])] for k in range(2)]
    place(lay, ranks, scaled, out_ref)


def forward_kernel(lay, message_ref, win_ref, wout_ref, out_ref, hidden_ref, rows_ref, total_ref):
    step = pl.program_id(0)

    @pl.when(step == 0)
    def _():
        unpack(lay, message_ref, rows_ref)

    hidden = jnp.maximum(dot(rows_ref[...], win_ref[0]), 0.0).astype(BF16)
    hidden_ref[...] = hidden
    term = dot(hidden, wout_ref[0])

    @pl.when(step == 0)
    def _():
        total_ref[...] = term

    @pl.when(step > 0)
    def _():
        total_ref[...] += term

    @pl.when(step == pl.num_programs(0) - 1)
    def _():
        pack(lay, total_ref, out_ref)


def backward_kernel(lay, message_ref, hidden_ref, win_ref, wout_ref, out_ref, rows_ref, total_ref):
    step = pl.program_id(0)

    @pl.when(step == 0)
    def _():
        unpack(lay, message_ref, rows_ref)

    back = dot_nt(rows_ref[...], wout_ref[0])
    back = jnp.where(hidden_ref[...].astype(F32) > 0.0, back, 0.0).astype(BF16)
    term = dot_nt(back, win_ref[0])

    @pl.when(step == 0)
    def _():
        total_ref[...] = term

    @pl.when(step > 0)
    def _():
        total_ref[...] += term

    @pl.when(step == pl.num_programs(0) - 1)
    def _():
        pack(lay, total_ref, out_ref)


def column_targets(lay, ids_ref, slots_ref):
    ids = [as_column(ids_ref[k : k + 1, :].astype(F32)).astype(jnp.int32) for k in range(2)]
    slots = [as_column(slots_ref[k : k + 1, :].astype(F32)).astype(jnp.int32) for k in range(2)]
    return ids, [targets(lay, ids[k], slots[k]) for k in range(2)]


def split_in_two(x):
    high = x.astype(BF16)
    return high, (x - high.astype(F32)).astype(BF16)


def mix_kernel(
    lay,
    ids_ref,
    slots_ref,
    gates_ref,
    message_ref,
    cot_ref,
    tokens_ref,
    router_ref,
    mixed_ref,
    back_ref,
    partial_ref,
):
    experts = router_ref.shape[0]
    toks = tokens_ref.shape[0]
    ids, ranks = column_targets(lay, ids_ref, slots_ref)
    gates = [as_column(gates_ref[k : k + 1, :]) for k in range(2)]
    cot = cot_ref[...].astype(F32)
    choice = [pick(lay, [ranks[k]], message_ref) for k in range(2)]
    mixed_ref[...] = (gates[0] * choice[0] + gates[1] * choice[1]).astype(BF16)
    actions = [jnp.sum(choice[k] * cot, axis=1, keepdims=True) for k in range(2)]
    slope = gates[0] * gates[1] * (actions[0] - actions[1])

    expert_at = iota((toks, experts), 1)
    signs = jnp.where(expert_at == ids[0], 1.0, 0.0) - jnp.where(expert_at == ids[1], 1.0, 0.0)
    high, low = split_in_two(signs * slope)
    router = router_ref[...]
    back_ref[...] = dot(high, router) + dot(low, router)

    expert_at = iota((experts, toks), 0)
    signs = jnp.where(expert_at == ids_ref[0:1, :], 1.0, 0.0) - jnp.where(
        expert_at == ids_ref[1:2, :], 1.0, 0.0
    )
    high, low = split_in_two(signs * as_row(slope))
    tokens = tokens_ref[...]
    partial_ref[...] = (dot(high, tokens) + dot(low, tokens)) * (1.0 / toks)


def grad_kernel(lay, ids_ref, slots_ref, message_ref, back_ref, out_ref):
    _, ranks = column_targets(lay, ids_ref, slots_ref)
    out_ref[...] = (pick(lay, ranks, message_ref) + back_ref[...]).astype(BF16)


def call(kernel, out_shape, flops, args, vmem_bytes=VMEM_BYTES):
    moved = sum(a.size * a.dtype.itemsize for a in args)
    moved += sum(o.size * o.dtype.itemsize for o in jax.tree.leaves(out_shape))
    return pl.pallas_call(
        kernel,
        out_shape=out_shape,
        compiler_params=pltpu.CompilerParams(vmem_limit_bytes=vmem_bytes),
        cost_estimate=pl.CostEstimate(flops=flops, bytes_accessed=moved, transcendentals=0),
    )(*args)


def expert_call(kernel, lay, message, hidden, in_weight, out_weight):
    count = message.shape[0]
    ff = in_weight.shape[2]
    tile = min(512, ff)
    rows = count // GROUP * lay.rows
    whole = pl.BlockSpec(message.shape, lambda j: (0, 0))
    win = pl.BlockSpec((1, lay.width, tile), lambda j: (0, 0, j))
    wout = pl.BlockSpec((1, tile, lay.width), lambda j: (0, j, 0))
    hid = pl.BlockSpec((rows, tile), lambda j: (0, j))
    forward = hidden is None
    operands = (message, in_weight, out_weight) if forward else (message, hidden, in_weight, out_weight)
    message_out = jax.ShapeDtypeStruct(message.shape, BF16)
    return pl.pallas_call(
        functools.partial(kernel, lay),
        grid=(ff // tile,),
        in_specs=[whole, win, wout] if forward else [whole, hid, win, wout],
        out_specs=[whole, hid] if forward else whole,
        out_shape=[message_out, jax.ShapeDtypeStruct((rows, ff), BF16)] if forward else message_out,
        scratch_shapes=[pltpu.VMEM((rows, lay.width), BF16), pltpu.VMEM((rows, lay.width), F32)],
        compiler_params=pltpu.CompilerParams(vmem_limit_bytes=VMEM_BYTES),
        cost_estimate=pl.CostEstimate(
            flops=4 * rows * lay.width * ff,
            bytes_accessed=4 * lay.width * ff + 2 * rows * ff + 4 * message.size,
            transcendentals=0,
        ),
    )(*operands)


def exchange(x):
    return lax.all_to_all(x, AXES, split_axis=0, concat_axis=0, tiled=True)


def from_device(x, bits, devices):
    return lax.ppermute(x, AXES, [(d, d ^ bits) for d in range(devices)])


def sum_of_pairs(own, near, far, both):
    return (own + near) + (far + both)


def sum_over_devices(x, devices, beside):
    half = x.shape[0] // 2
    core = lax.axis_index("inner") % 2
    own = lax.dynamic_slice_in_dim(x, core * half, half, 0)
    other = lax.dynamic_slice_in_dim(x, (1 - core) * half, half, 0)
    own = own + from_device(other, 1, devices)
    bit = 2
    while bit < devices:
        sent = own if bit == 2 else own.astype(BF16)
        steps = [1, 2, 3] if 2 * bit < devices else [1]
        terms = [from_device(sent, step * bit, devices) for step in steps]
        if bit * 4 >= devices:
            beside, sent, *terms = lax.optimization_barrier((beside, sent, *terms))
        terms = [term.astype(F32) for term in [sent] + terms]
        own = sum_of_pairs(*terms) if len(terms) == 4 else terms[0] + terms[1]
        bit *= 4
    other = from_device(own, 1, devices)
    first = core == 0
    total = jnp.concatenate([jnp.where(first, own, other), jnp.where(first, other, own)], axis=0)
    return total, beside


def on_device(tokens, router_weight, in_weight, out_weight, expert_ids, slot_ids, cotangent):
    tok_rows, model_width = tokens.shape
    experts = router_weight.shape[1]
    devices = lax.axis_size("outer") * lax.axis_size("inner")
    lay = Layout(3 * tok_rows // experts, model_width)
    message = jax.ShapeDtypeStruct((experts * GROUP, lay.columns), BF16)
    ids, slots, router = expert_ids.T, slot_ids.T, router_weight.T
    place_flops = 4 * experts * GROUP * tok_rows * model_width

    sent_tokens = call(
        functools.partial(send_tokens_kernel, lay), message, place_flops, (ids, slots, tokens)
    )
    sent_grads, gates = call(
        functools.partial(send_grads_kernel, lay),
        [message, jax.ShapeDtypeStruct((2, tok_rows), F32)],
        2 * place_flops,
        (ids, slots, tokens, router, cotangent),
    )
    arrived = exchange(sent_tokens)
    arrived, sent_grads = lax.optimization_barrier((arrived, sent_grads))
    grad_rows = exchange(sent_grads)
    produced, hidden = expert_call(forward_kernel, lay, arrived, None, in_weight, out_weight)
    produced, grad_rows = lax.optimization_barrier((produced, grad_rows))
    produced_back = exchange(produced)
    returned = expert_call(backward_kernel, lay, grad_rows, hidden, in_weight, out_weight)
    returned, produced_back = lax.optimization_barrier((returned, produced_back))
    returned_back = exchange(returned)

    mixed, router_back, partial_grad = call(
        functools.partial(mix_kernel, lay),
        [
            jax.ShapeDtypeStruct((tok_rows, model_width), BF16),
            jax.ShapeDtypeStruct((tok_rows, model_width), F32),
            jax.ShapeDtypeStruct((experts, model_width), F32),
        ],
        2 * place_flops,
        (ids, slots, gates, produced_back, cotangent, tokens, router),
        SMALL_VMEM_BYTES,
    )
    grad_tokens = call(
        functools.partial(grad_kernel, lay),
        jax.ShapeDtypeStruct((tok_rows, model_width), BF16),
        place_flops,
        (ids, slots, returned_back, router_back),
        SMALL_VMEM_BYTES,
    )
    grad_router, grad_tokens = sum_over_devices(partial_grad, devices, grad_tokens)
    return (mixed, grad_tokens, grad_router.T)


def solution(mesh):
    placed = (
        P(AXES, None),
        P(),
        P(AXES, None, None),
        P(AXES, None, None),
        P(AXES, None),
        P(AXES, None),
        P(AXES, None),
    )
    return jax.shard_map(
        on_device,
        mesh=mesh,
        in_specs=placed,
        out_specs=(P(AXES, None), P(AXES, None), P()),
        check_vma=False,
    )
```

```python
import functools

import jax
import jax.numpy as jnp
from jax import lax
from jax.experimental import pallas as pl
from jax.experimental.pallas import tpu as pltpu
from jax.sharding import PartitionSpec as P

AXES = ("outer", "inner")
F32 = jnp.float32
BF16 = jnp.bfloat16
GROUP = 8
VMEM_BYTES = 60 * 1024 * 1024
SMALL_VMEM_BYTES = 24 * 1024 * 1024


class Layout:
    def __init__(self, capacity, model_width):
        self.full, left = divmod(capacity, GROUP)
        self.rest = 0
        if left:
            self.rest = 1
            while self.rest < left:
                self.rest *= 2
        if self.rest == GROUP:
            self.full, self.rest = self.full + 1, 0
        self.capacity = capacity
        self.width = model_width
        self.cuts = GROUP // self.rest if self.rest else 1
        self.piece = model_width // self.cuts
        self.base = self.full * model_width
        self.columns = self.base + (self.piece if self.rest else 0)
        self.rows = self.full * GROUP + self.rest


def dot(a, b):
    return jnp.dot(a, b, preferred_element_type=F32)


def dot_nt(a, b):
    return lax.dot_general(a, b, (((1,), (1,)), ((), ())), preferred_element_type=F32)


def iota(shape, dim):
    return lax.broadcasted_iota(jnp.int32, shape, dim)


def as_column(row):
    count = row.shape[1]
    eye = iota((count, count), 0) == iota((count, count), 1)
    return jnp.sum(jnp.where(eye, row, 0.0), axis=1, keepdims=True)


def as_row(column):
    count = column.shape[0]
    eye = iota((count, count), 0) == iota((count, count), 1)
    return jnp.sum(jnp.where(eye, column, 0.0), axis=0, keepdims=True)


def targets(lay, ids, slots):
    found = []
    kept = slots < lay.capacity
    for group in range(lay.full):
        inside = kept & (slots >= group * GROUP) & (slots < (group + 1) * GROUP)
        found.append(jnp.where(inside, ids * GROUP + slots - group * GROUP, -1))
    if lay.rest:
        inside = kept & (slots >= lay.full * GROUP)
        found.append(jnp.where(inside, ids * GROUP + slots - lay.full * GROUP, -1))
    return found


def shifted(row, by):
    return jnp.where(row >= 0, row + by, -1)


class Order:
    def __init__(self, high, low, by_high):
        self.high, self.low, self.by_high = high, low, by_high
        self.arrays = high if by_high else 1
        self.blocks = high * low
        self.rows = self.blocks // self.arrays * GROUP

    def position(self, block):
        if self.by_high:
            return block
        shift = self.low.bit_length() - 1
        return (block & (self.low - 1)) * self.high + lax.shift_right_logical(block, shift)

    def block(self, position):
        if self.by_high:
            return position
        part, high = divmod(position, self.high)
        return high * self.low + part


def this_device():
    return lax.axis_index("outer") * lax.axis_size("inner") + lax.axis_index("inner")


def read_all(refs):
    return jnp.concatenate([ref[...] for ref in refs], axis=0)


def write_all(order, refs, start, values):
    for at, ref in enumerate(refs):
        ref[:, start : start + values.shape[1]] = values[at * order.rows : (at + 1) * order.rows, :]


def place(lay, order, row_targets, values, out_refs):
    count = order.arrays * order.rows
    toks = values[0].shape[0]
    row_at = iota((count, toks), 0)
    stacked = jnp.concatenate(values, axis=0) if len(values) > 1 else values[0]

    def onehot(rows):
        hit = functools.reduce(jnp.logical_or, [row_at == row for row in rows])
        return jnp.where(hit, 1.0, 0.0).astype(BF16)

    for group in range(lay.full):
        hot = [onehot([t[group] for t in ranks]) for ranks in row_targets]
        hot = jnp.concatenate(hot, axis=1) if len(hot) > 1 else hot[0]
        write_all(order, out_refs, group * lay.width, dot(hot, stacked).astype(BF16))
    if lay.rest:
        hot, pieces = [], []
        for cut in range(lay.cuts):
            for ranks in row_targets:
                hot.append(onehot([shifted(t[lay.full], cut * lay.rest) for t in ranks]))
            pieces.append(stacked[:, cut * lay.piece : (cut + 1) * lay.piece])
        placed = dot(jnp.concatenate(hot, axis=1), jnp.concatenate(pieces, axis=0))
        write_all(order, out_refs, lay.base, placed.astype(BF16))


def pick(lay, ranks, message):
    count = message.shape[0]
    toks = ranks[0][0].shape[0]
    row_at = iota((toks, count), 1)

    def onehot(rows):
        hit = functools.reduce(jnp.logical_or, [row_at == row for row in rows])
        return jnp.where(hit, 1.0, 0.0).astype(BF16)

    whole = [onehot([t[group] for t in ranks]) for group in range(lay.full)]
    pieces = []
    for cut in range(lay.cuts):
        left = cut * lay.piece
        total = None
        for group in range(lay.full):
            start = group * lay.width + left
            term = dot(whole[group], message[:, start : start + lay.piece])
            total = term if total is None else total + term
        if lay.rest:
            hot = onehot([shifted(t[lay.full], cut * lay.rest) for t in ranks])
            term = dot(hot, message[:, lay.base : lay.base + lay.piece])
            total = term if total is None else total + term
        pieces.append(total)
    return jnp.concatenate(pieces, axis=1) if len(pieces) > 1 else pieces[0]


def rest_selection(lay, order):
    count = order.arrays * order.rows
    small = count // GROUP * lay.rest
    row = iota((small, count), 0)
    col = iota((small, count), 1)
    shift = lay.rest.bit_length() - 1
    home = order.position(lax.shift_right_logical(row, shift)) * GROUP + (row & (lay.rest - 1))
    return [jnp.where(col == home + cut * lay.rest, 1.0, 0.0).astype(BF16) for cut in range(lay.cuts)]


def unpack(lay, order, message_refs, out_ref):
    count = order.arrays * order.rows
    message = read_all(message_refs)
    for group in range(lay.full):
        part = message[:, group * lay.width : (group + 1) * lay.width]
        if not order.by_high:
            part = part.astype(F32)
            blocks = [
                part[at * GROUP : (at + 1) * GROUP, :]
                for at in sorted(range(count // GROUP), key=order.block)
            ]
            part = jnp.concatenate(blocks, axis=0).astype(BF16)
        out_ref[group * count : (group + 1) * count, :] = part
    if lay.rest:
        tail = message[:, lay.base :]
        for cut, chosen in enumerate(rest_selection(lay, order)):
            out_ref[lay.full * count :, cut * lay.piece : (cut + 1) * lay.piece] = dot(
                chosen, tail
            ).astype(BF16)


def pack(lay, order, rows_ref, message_refs):
    count = order.arrays * order.rows
    for group in range(lay.full):
        part = rows_ref[group * count : (group + 1) * count, :]
        if not order.by_high:
            blocks = [order.block(at) * GROUP for at in range(count // GROUP)]
            part = jnp.concatenate([part[at : at + GROUP, :] for at in blocks], axis=0)
        write_all(order, message_refs, group * lay.width, part.astype(BF16))
    if lay.rest:
        total = None
        for cut, chosen in enumerate(rest_selection(lay, order)):
            part = rows_ref[
                lay.full * count :, cut * lay.piece : (cut + 1) * lay.piece
            ].astype(BF16)
            term = lax.dot_general(
                chosen, part, (((0,), (0,)), ((), ())), preferred_element_type=F32
            )
            total = term if total is None else total + term
        write_all(order, message_refs, lay.base, total.astype(BF16))


def repack_kernel(order, *refs):
    sources, outs = refs[: order.arrays], refs[order.arrays :]
    if order.by_high:
        blocks = [
            ref[part * GROUP : (part + 1) * GROUP, :] for part in range(order.low) for ref in sources
        ]
        outs[0][...] = jnp.concatenate(blocks, axis=0)
    else:
        for plane, out_ref in enumerate(outs):
            starts = [(part * order.high + plane) * GROUP for part in range(order.low)]
            blocks = [sources[0][start : start + GROUP, :] for start in starts]
            out_ref[...] = jnp.concatenate(blocks, axis=0)


def blocks_of(order, ids):
    return order.position(ids ^ (this_device() & -order.low))


def send_tokens_kernel(lay, order, ids_ref, slots_ref, tokens_ref, *out_refs):
    blocks = blocks_of(order, ids_ref[...])
    ranks = [targets(lay, blocks[k : k + 1, :], slots_ref[k : k + 1, :]) for k in range(2)]
    place(lay, order, [ranks], [tokens_ref[...]], out_refs)


def send_grads_kernel(
    lay, order, ids_ref, slots_ref, tokens_ref, router_ref, cot_ref, gates_ref, *out_refs
):
    logits = dot_nt(router_ref[...], tokens_ref[...])
    expert_at = iota(logits.shape, 0)
    picked = [
        jnp.sum(jnp.where(expert_at == ids_ref[k : k + 1, :], logits, 0.0), axis=0, keepdims=True)
        for k in range(2)
    ]
    gates = [jax.nn.sigmoid(picked[0] - picked[1]), jax.nn.sigmoid(picked[1] - picked[0])]
    gates_ref[0:1, :] = gates[0]
    gates_ref[1:2, :] = gates[1]
    cot = cot_ref[...].astype(F32)
    scaled = [(as_column(gate) * cot).astype(BF16) for gate in gates]
    blocks = blocks_of(order, ids_ref[...])
    ranks = [[targets(lay, blocks[k : k + 1, :], slots_ref[k : k + 1, :])] for k in range(2)]
    place(lay, order, ranks, scaled, out_refs)


def forward_kernel(lay, order, out_order, *refs):
    message_refs = refs[: order.arrays]
    win_ref, wout_ref, hidden_ref = refs[order.arrays : order.arrays + 3]
    out_refs, (rows_ref, total_ref) = refs[order.arrays + 3 : -2], refs[-2:]
    step = pl.program_id(0)

    @pl.when(step == 0)
    def _():
        unpack(lay, order, message_refs, rows_ref)

    hidden = jnp.maximum(dot(rows_ref[...], win_ref[0]), 0.0).astype(BF16)
    hidden_ref[...] = hidden
    term = dot(hidden, wout_ref[0])

    @pl.when(step == 0)
    def _():
        total_ref[...] = term

    @pl.when(step > 0)
    def _():
        total_ref[...] += term

    @pl.when(step == pl.num_programs(0) - 1)
    def _():
        pack(lay, out_order, total_ref, out_refs)


def backward_kernel(lay, order, out_order, *refs):
    message_refs = refs[: order.arrays]
    win_ref, wout_ref, hidden_ref = refs[order.arrays : order.arrays + 3]
    out_refs, (rows_ref, total_ref) = refs[order.arrays + 3 : -2], refs[-2:]
    step = pl.program_id(0)

    @pl.when(step == 0)
    def _():
        unpack(lay, order, message_refs, rows_ref)

    back = dot_nt(rows_ref[...], wout_ref[0])
    back = jnp.where(hidden_ref[...].astype(F32) > 0.0, back, 0.0).astype(BF16)
    term = dot_nt(back, win_ref[0])

    @pl.when(step == 0)
    def _():
        total_ref[...] = term

    @pl.when(step > 0)
    def _():
        total_ref[...] += term

    @pl.when(step == pl.num_programs(0) - 1)
    def _():
        pack(lay, out_order, total_ref, out_refs)


def column_targets(lay, order, ids_ref, slots_ref):
    ids = [as_column(ids_ref[k : k + 1, :].astype(F32)).astype(jnp.int32) for k in range(2)]
    slots = [as_column(slots_ref[k : k + 1, :].astype(F32)).astype(jnp.int32) for k in range(2)]
    return ids, [targets(lay, blocks_of(order, ids[k]), slots[k]) for k in range(2)]


def split_in_two(x):
    high = x.astype(BF16)
    return high, (x - high.astype(F32)).astype(BF16)


def mix_kernel(lay, order, ids_ref, slots_ref, gates_ref, cot_ref, tokens_ref, router_ref, *refs):
    message_refs, (mixed_ref, back_ref, partial_ref) = refs[: order.arrays], refs[order.arrays :]
    experts = router_ref.shape[0]
    toks = tokens_ref.shape[0]
    ids, ranks = column_targets(lay, order, ids_ref, slots_ref)
    gates = [as_column(gates_ref[k : k + 1, :]) for k in range(2)]
    cot = cot_ref[...].astype(F32)
    message = read_all(message_refs)
    choice = [pick(lay, [ranks[k]], message) for k in range(2)]
    mixed_ref[...] = (gates[0] * choice[0] + gates[1] * choice[1]).astype(BF16)
    actions = [jnp.sum(choice[k] * cot, axis=1, keepdims=True) for k in range(2)]
    slope = gates[0] * gates[1] * (actions[0] - actions[1])

    expert_at = iota((toks, experts), 1)
    signs = jnp.where(expert_at == ids[0], 1.0, 0.0) - jnp.where(expert_at == ids[1], 1.0, 0.0)
    high, low = split_in_two(signs * slope)
    router = router_ref[...]
    back_ref[...] = dot(high, router) + dot(low, router)

    expert_at = iota((experts, toks), 0)
    signs = jnp.where(expert_at == ids_ref[0:1, :], 1.0, 0.0) - jnp.where(
        expert_at == ids_ref[1:2, :], 1.0, 0.0
    )
    high, low = split_in_two(signs * as_row(slope))
    tokens = tokens_ref[...]
    partial_ref[...] = (dot(high, tokens) + dot(low, tokens)) * (1.0 / toks)


def grad_kernel(lay, order, ids_ref, slots_ref, back_ref, *refs):
    message_refs, out_ref = refs[: order.arrays], refs[order.arrays]
    _, ranks = column_targets(lay, order, ids_ref, slots_ref)
    message = read_all(message_refs)
    out_ref[...] = (pick(lay, ranks, message) + back_ref[...]).astype(BF16)


def call(kernel, out_shape, flops, args, vmem_bytes=VMEM_BYTES):
    moved = sum(a.size * a.dtype.itemsize for a in args)
    moved += sum(o.size * o.dtype.itemsize for o in jax.tree.leaves(out_shape))
    return pl.pallas_call(
        kernel,
        out_shape=out_shape,
        compiler_params=pltpu.CompilerParams(vmem_limit_bytes=vmem_bytes),
        cost_estimate=pl.CostEstimate(flops=flops, bytes_accessed=moved, transcendentals=0),
    )(*args)


def messages_of(lay, order):
    return [jax.ShapeDtypeStruct((order.rows, lay.columns), BF16)] * order.arrays


def expert_call(kernel, lay, order, out_order, message, hidden, in_weight, out_weight):
    ff = in_weight.shape[2]
    tile = min(512, ff)
    rows = order.blocks * lay.rows
    win = pl.BlockSpec((1, lay.width, tile), lambda j: (0, 0, j))
    wout = pl.BlockSpec((1, tile, lay.width), lambda j: (0, j, 0))
    hid = pl.BlockSpec((rows, tile), lambda j: (0, j))

    def whole(of):
        return [pl.BlockSpec((of.rows, lay.columns), lambda j: (0, 0))] * of.arrays

    forward = hidden is None
    hidden_shape = [jax.ShapeDtypeStruct((rows, ff), BF16)]
    return pl.pallas_call(
        functools.partial(kernel, lay, order, out_order),
        grid=(ff // tile,),
        in_specs=whole(order) + [win, wout] + ([] if forward else [hid]),
        out_specs=([hid] if forward else []) + whole(out_order),
        out_shape=(hidden_shape if forward else []) + messages_of(lay, out_order),
        scratch_shapes=[pltpu.VMEM((rows, lay.width), BF16), pltpu.VMEM((rows, lay.width), F32)],
        compiler_params=pltpu.CompilerParams(vmem_limit_bytes=VMEM_BYTES),
        cost_estimate=pl.CostEstimate(
            flops=4 * rows * lay.width * ff,
            bytes_accessed=4 * lay.width * ff + 2 * rows * ff + 4 * rows * lay.width,
            transcendentals=0,
        ),
    )(*message, in_weight, out_weight, *([] if forward else [hidden]))


def repack(lay, order, message):
    other = Order(order.high, order.low, not order.by_high)
    return call(
        functools.partial(repack_kernel, order),
        messages_of(lay, other),
        0,
        tuple(message),
        SMALL_VMEM_BYTES,
    )


def over_planes(order, message):
    devices = order.blocks
    return [message[0]] + [
        from_device(message[part], part * order.low, devices) for part in range(1, order.high)
    ]


def in_plane(order, message):
    groups = [list(range(at, at + order.low)) for at in range(0, order.blocks, order.low)]
    return [
        lax.all_to_all(
            message[0], AXES, split_axis=0, concat_axis=0, tiled=True, axis_index_groups=groups
        )
    ]


def tied(first, second):
    out = lax.optimization_barrier(tuple(first) + tuple(second))
    return list(out[: len(first)]), list(out[len(first) :])


def from_device(x, bits, devices):
    return lax.ppermute(x, AXES, [(d, d ^ bits) for d in range(devices)])


def sum_of_pairs(own, near, far, both):
    return (own + near) + (far + both)


def sum_over_devices(x, devices):
    half = x.shape[0] // 2
    core = lax.axis_index("inner") % 2
    own = lax.dynamic_slice_in_dim(x, core * half, half, 0)
    other = lax.dynamic_slice_in_dim(x, (1 - core) * half, half, 0)
    own = own + from_device(other, 1, devices)
    bit = 2
    while bit < devices:
        sent = own if bit == 2 else own.astype(BF16)
        steps = [1, 2, 3] if 2 * bit < devices else [1]
        terms = [from_device(sent, step * bit, devices) for step in steps]
        terms = [term.astype(F32) for term in [sent] + terms]
        own = sum_of_pairs(*terms) if len(terms) == 4 else terms[0] + terms[1]
        bit *= 4
    other = from_device(own, 1, devices)
    first = core == 0
    return jnp.concatenate([jnp.where(first, own, other), jnp.where(first, other, own)], axis=0)


def on_device(tokens, router_weight, in_weight, out_weight, expert_ids, slot_ids, cotangent):
    tok_rows, model_width = tokens.shape
    experts = router_weight.shape[1]
    devices = lax.axis_size("outer") * lax.axis_size("inner")
    lay = Layout(3 * tok_rows // experts, model_width)
    high = 4 if devices >= 16 else 1
    by_high, by_low = (Order(high, devices // high, flag) for flag in (True, False))
    ids, slots, router = expert_ids.T, slot_ids.T, router_weight.T
    place_flops = 4 * experts * GROUP * tok_rows * model_width

    sent_tokens = call(
        functools.partial(send_tokens_kernel, lay, by_high),
        messages_of(lay, by_high),
        place_flops,
        (ids, slots, tokens),
    )
    token_half = over_planes(by_high, sent_tokens)
    sent_tokens, (late_tokens,) = tied(sent_tokens, [tokens])

    gates, *sent_grads = call(
        functools.partial(send_grads_kernel, lay, by_low),
        [jax.ShapeDtypeStruct((2, tok_rows), F32)] + messages_of(lay, by_low),
        2 * place_flops,
        (ids, slots, late_tokens, router, cotangent),
    )
    grad_half = repack(lay, by_low, in_plane(by_low, sent_grads))
    token_half, grad_half = tied(token_half, grad_half)
    grad_rows = over_planes(by_high, grad_half)
    arrived = in_plane(by_low, repack(lay, by_high, token_half))

    hidden, *produced = expert_call(
        forward_kernel, lay, by_low, by_high, arrived, None, in_weight, out_weight
    )
    produced, grad_rows = tied(produced, grad_rows)
    produced_half = over_planes(by_high, produced)
    returned = expert_call(
        backward_kernel, lay, by_high, by_high, grad_rows, hidden, in_weight, out_weight
    )
    returned, produced_half = tied(returned, produced_half)
    returned_half = over_planes(by_high, returned)
    produced_back = in_plane(by_low, repack(lay, by_high, produced_half))

    mixed, router_back, partial_grad = call(
        functools.partial(mix_kernel, lay, by_low),
        [
            jax.ShapeDtypeStruct((tok_rows, model_width), BF16),
            jax.ShapeDtypeStruct((tok_rows, model_width), F32),
            jax.ShapeDtypeStruct((experts, model_width), F32),
        ],
        2 * place_flops,
        (ids, slots, gates, cotangent, tokens, router, *produced_back),
        SMALL_VMEM_BYTES,
    )
    returned_half, produced_back = tied(returned_half, produced_back)
    returned_back = in_plane(by_low, repack(lay, by_high, returned_half))
    grad_router = sum_over_devices(partial_grad, devices).T
    grad_tokens = call(
        functools.partial(grad_kernel, lay, by_low),
        jax.ShapeDtypeStruct((tok_rows, model_width), BF16),
        place_flops,
        (ids, slots, router_back, *returned_back),
        SMALL_VMEM_BYTES,
    )
    return (mixed, grad_tokens, grad_router)


def solution(mesh):
    placed = (
        P(AXES, None),
        P(),
        P(AXES, None, None),
        P(AXES, None, None),
        P(AXES, None),
        P(AXES, None),
        P(AXES, None),
    )
    return jax.shard_map(
        on_device,
        mesh=mesh,
        in_specs=placed,
        out_specs=(P(AXES, None), P(AXES, None), P()),
        check_vma=False,
    )
```

```python
import functools

import jax
import jax.numpy as jnp
from jax import lax
from jax.experimental import pallas as pl
from jax.experimental.pallas import tpu as pltpu
from jax.sharding import PartitionSpec as P

AXES = ("outer", "inner")
F32 = jnp.float32
BF16 = jnp.bfloat16
GROUP = 8
VMEM_BYTES = 60 * 1024 * 1024
SMALL_VMEM_BYTES = 24 * 1024 * 1024


class Layout:
    def __init__(self, capacity, model_width):
        self.full, left = divmod(capacity, GROUP)
        self.rest = 0
        if left:
            self.rest = 1
            while self.rest < left:
                self.rest *= 2
        if self.rest == GROUP:
            self.full, self.rest = self.full + 1, 0
        self.capacity = capacity
        self.width = model_width
        self.cuts = GROUP // self.rest if self.rest else 1
        self.piece = model_width // self.cuts
        self.base = self.full * model_width
        self.columns = self.base + (self.piece if self.rest else 0)
        self.rows = self.full * GROUP + self.rest


def dot(a, b):
    return jnp.dot(a, b, preferred_element_type=F32)


def dot_nt(a, b):
    return lax.dot_general(a, b, (((1,), (1,)), ((), ())), preferred_element_type=F32)


def iota(shape, dim):
    return lax.broadcasted_iota(jnp.int32, shape, dim)


def as_column(row):
    count = row.shape[1]
    eye = iota((count, count), 0) == iota((count, count), 1)
    return jnp.sum(jnp.where(eye, row, 0.0), axis=1, keepdims=True)


def as_row(column):
    count = column.shape[0]
    eye = iota((count, count), 0) == iota((count, count), 1)
    return jnp.sum(jnp.where(eye, column, 0.0), axis=0, keepdims=True)


def targets(lay, ids, slots):
    found = []
    kept = slots < lay.capacity
    for group in range(lay.full):
        inside = kept & (slots >= group * GROUP) & (slots < (group + 1) * GROUP)
        found.append(jnp.where(inside, ids * GROUP + slots - group * GROUP, -1))
    if lay.rest:
        inside = kept & (slots >= lay.full * GROUP)
        found.append(jnp.where(inside, ids * GROUP + slots - lay.full * GROUP, -1))
    return found


def shifted(row, by):
    return jnp.where(row >= 0, row + by, -1)


def place(lay, row_targets, values, out_ref):
    count = out_ref.shape[0]
    toks = values[0].shape[0]
    row_at = iota((count, toks), 0)
    stacked = jnp.concatenate(values, axis=0) if len(values) > 1 else values[0]

    def onehot(rows):
        hit = functools.reduce(jnp.logical_or, [row_at == row for row in rows])
        return jnp.where(hit, 1.0, 0.0).astype(BF16)

    for group in range(lay.full):
        hot = [onehot([t[group] for t in ranks]) for ranks in row_targets]
        hot = jnp.concatenate(hot, axis=1) if len(hot) > 1 else hot[0]
        out_ref[:, group * lay.width : (group + 1) * lay.width] = dot(hot, stacked).astype(BF16)
    if lay.rest:
        hot, pieces = [], []
        for cut in range(lay.cuts):
            for ranks in row_targets:
                hot.append(onehot([shifted(t[lay.full], cut * lay.rest) for t in ranks]))
            pieces.append(stacked[:, cut * lay.piece : (cut + 1) * lay.piece])
        out_ref[:, lay.base :] = dot(
            jnp.concatenate(hot, axis=1), jnp.concatenate(pieces, axis=0)
        ).astype(BF16)


def pick(lay, ranks, message_ref):
    count = message_ref.shape[0]
    toks = ranks[0][0].shape[0]
    row_at = iota((toks, count), 1)

    def onehot(rows):
        hit = functools.reduce(jnp.logical_or, [row_at == row for row in rows])
        return jnp.where(hit, 1.0, 0.0).astype(BF16)

    whole = [onehot([t[group] for t in ranks]) for group in range(lay.full)]
    pieces = []
    for cut in range(lay.cuts):
        left = cut * lay.piece
        total = None
        for group in range(lay.full):
            start = group * lay.width + left
            term = dot(whole[group], message_ref[:, start : start + lay.piece])
            total = term if total is None else total + term
        if lay.rest:
            hot = onehot([shifted(t[lay.full], cut * lay.rest) for t in ranks])
            term = dot(hot, message_ref[:, lay.base : lay.base + lay.piece])
            total = term if total is None else total + term
        pieces.append(total)
    return jnp.concatenate(pieces, axis=1) if len(pieces) > 1 else pieces[0]


def rest_selection(lay, count):
    small = count // GROUP * lay.rest
    row = iota((small, count), 0)
    col = iota((small, count), 1)
    shift = lay.rest.bit_length() - 1
    home = lax.shift_right_logical(row, shift) * GROUP + (row & (lay.rest - 1))
    return [jnp.where(col == home + cut * lay.rest, 1.0, 0.0).astype(BF16) for cut in range(lay.cuts)]


def unpack(lay, message_ref, out_ref):
    count = message_ref.shape[0]
    for group in range(lay.full):
        out_ref[group * count : (group + 1) * count, :] = message_ref[
            :, group * lay.width : (group + 1) * lay.width
        ]
    if lay.rest:
        tail = message_ref[:, lay.base :]
        for cut, chosen in enumerate(rest_selection(lay, count)):
            out_ref[lay.full * count :, cut * lay.piece : (cut + 1) * lay.piece] = dot(
                chosen, tail
            ).astype(BF16)


def pack(lay, rows_ref, message_ref):
    count = message_ref.shape[0]
    for group in range(lay.full):
        message_ref[:, group * lay.width : (group + 1) * lay.width] = rows_ref[
            group * count : (group + 1) * count, :
        ].astype(BF16)
    if lay.rest:
        total = None
        for cut, chosen in enumerate(rest_selection(lay, count)):
            part = rows_ref[
                lay.full * count :, cut * lay.piece : (cut + 1) * lay.piece
            ].astype(BF16)
            term = lax.dot_general(
                chosen, part, (((0,), (0,)), ((), ())), preferred_element_type=F32
            )
            total = term if total is None else total + term
        message_ref[:, lay.base :] = total.astype(BF16)


def send_tokens_kernel(
    lay, ids_hbm, slots_hbm, tokens_hbm, out_ref, ids_ref, slots_ref, tokens_ref, sems
):
    copies = [
        pltpu.make_async_copy(source, target, sems.at[at])
        for at, (source, target) in enumerate(
            ((ids_hbm, ids_ref), (slots_hbm, slots_ref), (tokens_hbm, tokens_ref))
        )
    ]
    for copy in copies:
        copy.start()
    for copy in copies:
        copy.wait()
    first = targets(lay, ids_ref[0:1, :], slots_ref[0:1, :])
    second = targets(lay, ids_ref[1:2, :], slots_ref[1:2, :])
    place(lay, [[first, second]], [tokens_ref[...]], out_ref)


def send_grads_kernel(
    lay, ids_ref, slots_ref, tokens_ref, router_ref, cot_ref, out_ref, gates_ref
):
    logits = dot_nt(router_ref[...], tokens_ref[...])
    expert_at = iota(logits.shape, 0)
    picked = [
        jnp.sum(jnp.where(expert_at == ids_ref[k : k + 1, :], logits, 0.0), axis=0, keepdims=True)
        for k in range(2)
    ]
    gates = [jax.nn.sigmoid(picked[0] - picked[1]), jax.nn.sigmoid(picked[1] - picked[0])]
    gates_ref[0:1, :] = gates[0]
    gates_ref[1:2, :] = gates[1]
    cot = cot_ref[...].astype(F32)
    scaled = [(as_column(gate) * cot).astype(BF16) for gate in gates]
    ranks = [[targets(lay, ids_ref[k : k + 1, :], slots_ref[k : k + 1, :])] for k in range(2)]
    place(lay, ranks, scaled, out_ref)


def forward_kernel(lay, message_ref, win_ref, wout_ref, out_ref, hidden_ref, rows_ref, total_ref):
    step = pl.program_id(0)

    @pl.when(step == 0)
    def _():
        unpack(lay, message_ref, rows_ref)

    hidden = jnp.maximum(dot(rows_ref[...], win_ref[0]), 0.0).astype(BF16)
    hidden_ref[...] = hidden
    term = dot(hidden, wout_ref[0])

    @pl.when(step == 0)
    def _():
        total_ref[...] = term

    @pl.when(step > 0)
    def _():
        total_ref[...] += term

    @pl.when(step == pl.num_programs(0) - 1)
    def _():
        pack(lay, total_ref, out_ref)


def backward_kernel(lay, message_ref, hidden_ref, win_ref, wout_ref, out_ref, rows_ref, total_ref):
    step = pl.program_id(0)

    @pl.when(step == 0)
    def _():
        unpack(lay, message_ref, rows_ref)

    back = dot_nt(rows_ref[...], wout_ref[0])
    back = jnp.where(hidden_ref[...].astype(F32) > 0.0, back, 0.0).astype(BF16)
    term = dot_nt(back, win_ref[0])

    @pl.when(step == 0)
    def _():
        total_ref[...] = term

    @pl.when(step > 0)
    def _():
        total_ref[...] += term

    @pl.when(step == pl.num_programs(0) - 1)
    def _():
        pack(lay, total_ref, out_ref)


def column_targets(lay, ids_ref, slots_ref):
    ids = [as_column(ids_ref[k : k + 1, :].astype(F32)).astype(jnp.int32) for k in range(2)]
    slots = [as_column(slots_ref[k : k + 1, :].astype(F32)).astype(jnp.int32) for k in range(2)]
    return ids, [targets(lay, ids[k], slots[k]) for k in range(2)]


def split_in_two(x):
    high = x.astype(BF16)
    return high, (x - high.astype(F32)).astype(BF16)


def mix_kernel(
    lay,
    ids_ref,
    slots_ref,
    gates_ref,
    message_ref,
    cot_ref,
    tokens_ref,
    router_ref,
    mixed_ref,
    back_ref,
    partial_ref,
):
    experts = router_ref.shape[0]
    toks = tokens_ref.shape[0]
    ids, ranks = column_targets(lay, ids_ref, slots_ref)
    gates = [as_column(gates_ref[k : k + 1, :]) for k in range(2)]
    cot = cot_ref[...].astype(F32)
    choice = [pick(lay, [ranks[k]], message_ref) for k in range(2)]
    mixed_ref[...] = (gates[0] * choice[0] + gates[1] * choice[1]).astype(BF16)
    actions = [jnp.sum(choice[k] * cot, axis=1, keepdims=True) for k in range(2)]
    slope = gates[0] * gates[1] * (actions[0] - actions[1])

    expert_at = iota((toks, experts), 1)
    signs = jnp.where(expert_at == ids[0], 1.0, 0.0) - jnp.where(expert_at == ids[1], 1.0, 0.0)
    high, low = split_in_two(signs * slope)
    router = router_ref[...]
    back_ref[...] = dot(high, router) + dot(low, router)

    expert_at = iota((experts, toks), 0)
    signs = jnp.where(expert_at == ids_ref[0:1, :], 1.0, 0.0) - jnp.where(
        expert_at == ids_ref[1:2, :], 1.0, 0.0
    )
    high, low = split_in_two(signs * as_row(slope))
    tokens = tokens_ref[...]
    partial_ref[...] = (dot(high, tokens) + dot(low, tokens)) * (1.0 / toks)


def grad_kernel(lay, ids_ref, slots_ref, message_ref, back_ref, out_ref):
    _, ranks = column_targets(lay, ids_ref, slots_ref)
    out_ref[...] = (pick(lay, ranks, message_ref) + back_ref[...]).astype(BF16)


def call(kernel, out_shape, flops, args, vmem_bytes=VMEM_BYTES):
    moved = sum(a.size * a.dtype.itemsize for a in args)
    moved += sum(o.size * o.dtype.itemsize for o in jax.tree.leaves(out_shape))
    return pl.pallas_call(
        kernel,
        out_shape=out_shape,
        compiler_params=pltpu.CompilerParams(vmem_limit_bytes=vmem_bytes),
        cost_estimate=pl.CostEstimate(flops=flops, bytes_accessed=moved, transcendentals=0),
    )(*args)


def expert_call(kernel, lay, message, hidden, in_weight, out_weight):
    count = message.shape[0]
    ff = in_weight.shape[2]
    tile = min(512, ff)
    rows = count // GROUP * lay.rows
    whole = pl.BlockSpec(message.shape, lambda j: (0, 0))
    win = pl.BlockSpec((1, lay.width, tile), lambda j: (0, 0, j))
    wout = pl.BlockSpec((1, tile, lay.width), lambda j: (0, j, 0))
    hid = pl.BlockSpec((rows, tile), lambda j: (0, j))
    forward = hidden is None
    operands = (message, in_weight, out_weight) if forward else (message, hidden, in_weight, out_weight)
    message_out = jax.ShapeDtypeStruct(message.shape, BF16)
    return pl.pallas_call(
        functools.partial(kernel, lay),
        grid=(ff // tile,),
        in_specs=[whole, win, wout] if forward else [whole, hid, win, wout],
        out_specs=[whole, hid] if forward else whole,
        out_shape=[message_out, jax.ShapeDtypeStruct((rows, ff), BF16)] if forward else message_out,
        scratch_shapes=[pltpu.VMEM((rows, lay.width), BF16), pltpu.VMEM((rows, lay.width), F32)],
        compiler_params=pltpu.CompilerParams(vmem_limit_bytes=VMEM_BYTES),
        cost_estimate=pl.CostEstimate(
            flops=4 * rows * lay.width * ff,
            bytes_accessed=4 * lay.width * ff + 2 * rows * ff + 4 * message.size,
            transcendentals=0,
        ),
    )(*operands)


def exchange(x):
    return lax.all_to_all(x, AXES, split_axis=0, concat_axis=0, tiled=True)


def from_device(x, bits, devices):
    return lax.ppermute(x, AXES, [(d, d ^ bits) for d in range(devices)])


def sum_of_pairs(own, near, far, both):
    return (own + near) + (far + both)


def sum_over_devices(x, devices, beside):
    half = x.shape[0] // 2
    core = lax.axis_index("inner") % 2
    own = lax.dynamic_slice_in_dim(x, core * half, half, 0)
    other = lax.dynamic_slice_in_dim(x, (1 - core) * half, half, 0)
    own = own + from_device(other, 1, devices)
    bit = 2
    while bit < devices:
        sent = own if bit == 2 else own.astype(BF16)
        steps = [1, 2, 3] if 2 * bit < devices else [1]
        terms = [from_device(sent, step * bit, devices) for step in steps]
        terms = [term.astype(F32) for term in [sent] + terms]
        own = sum_of_pairs(*terms) if len(terms) == 4 else terms[0] + terms[1]
        bit *= 4
    beside, own = lax.optimization_barrier((beside, own))
    other = from_device(own, 1, devices)
    first = core == 0
    total = jnp.concatenate([jnp.where(first, own, other), jnp.where(first, other, own)], axis=0)
    return total, beside


def on_device(tokens, router_weight, in_weight, out_weight, expert_ids, slot_ids, cotangent):
    tok_rows, model_width = tokens.shape
    experts = router_weight.shape[1]
    devices = lax.axis_size("outer") * lax.axis_size("inner")
    lay = Layout(3 * tok_rows // experts, model_width)
    message = jax.ShapeDtypeStruct((experts * GROUP, lay.columns), BF16)
    ids, slots, router = expert_ids.T, slot_ids.T, router_weight.T
    place_flops = 4 * experts * GROUP * tok_rows * model_width

    sent_tokens = pl.pallas_call(
        functools.partial(send_tokens_kernel, lay),
        out_shape=message,
        in_specs=[pl.BlockSpec(memory_space=pltpu.HBM)] * 3,
        scratch_shapes=[
            pltpu.VMEM(ids.shape, jnp.int32),
            pltpu.VMEM(slots.shape, jnp.int32),
            pltpu.VMEM(tokens.shape, BF16),
            pltpu.SemaphoreType.DMA((3,)),
        ],
        compiler_params=pltpu.CompilerParams(vmem_limit_bytes=SMALL_VMEM_BYTES),
        cost_estimate=pl.CostEstimate(
            flops=place_flops, bytes_accessed=2 * (tokens.size + message.size), transcendentals=0
        ),
    )(ids, slots, tokens)
    sent_grads, gates = call(
        functools.partial(send_grads_kernel, lay),
        [message, jax.ShapeDtypeStruct((2, tok_rows), F32)],
        2 * place_flops,
        (ids, slots, tokens, router, cotangent),
    )
    arrived = exchange(sent_tokens)
    arrived, sent_grads = lax.optimization_barrier((arrived, sent_grads))
    grad_rows = exchange(sent_grads)
    produced, hidden = expert_call(forward_kernel, lay, arrived, None, in_weight, out_weight)
    produced, grad_rows = lax.optimization_barrier((produced, grad_rows))
    produced_back = exchange(produced)
    returned = expert_call(backward_kernel, lay, grad_rows, hidden, in_weight, out_weight)
    returned, produced_back = lax.optimization_barrier((returned, produced_back))
    returned_back = exchange(returned)

    mixed, router_back, partial_grad = call(
        functools.partial(mix_kernel, lay),
        [
            jax.ShapeDtypeStruct((tok_rows, model_width), BF16),
            jax.ShapeDtypeStruct((tok_rows, model_width), F32),
            jax.ShapeDtypeStruct((experts, model_width), F32),
        ],
        2 * place_flops,
        (ids, slots, gates, produced_back, cotangent, tokens, router),
        SMALL_VMEM_BYTES,
    )
    grad_router, returned_back = sum_over_devices(partial_grad, devices, returned_back)
    grad_tokens = call(
        functools.partial(grad_kernel, lay),
        jax.ShapeDtypeStruct((tok_rows, model_width), BF16),
        place_flops,
        (ids, slots, returned_back, router_back),
        SMALL_VMEM_BYTES,
    )
    return (mixed, grad_tokens, grad_router.T)


def solution(mesh):
    placed = (
        P(AXES, None),
        P(),
        P(AXES, None, None),
        P(AXES, None, None),
        P(AXES, None),
        P(AXES, None),
        P(AXES, None),
    )
    return jax.shard_map(
        on_device,
        mesh=mesh,
        in_specs=placed,
        out_specs=(P(AXES, None), P(AXES, None), P()),
        check_vma=False,
    )
```

```python
import functools

import jax
import jax.numpy as jnp
from jax import lax
from jax.experimental import pallas as pl
from jax.experimental.pallas import tpu as pltpu
from jax.sharding import PartitionSpec as P

AXES = ("outer", "inner")
F32 = jnp.float32
BF16 = jnp.bfloat16
GROUP = 8
PLANE = 8
VMEM_BYTES = 60 * 1024 * 1024
SMALL_VMEM_BYTES = 24 * 1024 * 1024


class Layout:
    def __init__(self, capacity, model_width):
        self.full, left = divmod(capacity, GROUP)
        self.rest = 0
        if left:
            self.rest = 1
            while self.rest < left:
                self.rest *= 2
        if self.rest == GROUP:
            self.full, self.rest = self.full + 1, 0
        self.capacity = capacity
        self.width = model_width
        self.cuts = GROUP // self.rest if self.rest else 1
        self.piece = model_width // self.cuts
        self.base = self.full * model_width
        self.columns = self.base + (self.piece if self.rest else 0)
        self.rows = self.full * GROUP + self.rest


def dot(a, b):
    return jnp.dot(a, b, preferred_element_type=F32)


def dot_nt(a, b):
    return lax.dot_general(a, b, (((1,), (1,)), ((), ())), preferred_element_type=F32)


def iota(shape, dim):
    return lax.broadcasted_iota(jnp.int32, shape, dim)


def as_column(row):
    count = row.shape[1]
    eye = iota((count, count), 0) == iota((count, count), 1)
    return jnp.sum(jnp.where(eye, row, 0.0), axis=1, keepdims=True)


def as_row(column):
    count = column.shape[0]
    eye = iota((count, count), 0) == iota((count, count), 1)
    return jnp.sum(jnp.where(eye, column, 0.0), axis=0, keepdims=True)


def targets(lay, ids, slots):
    found = []
    kept = slots < lay.capacity
    for group in range(lay.full):
        inside = kept & (slots >= group * GROUP) & (slots < (group + 1) * GROUP)
        found.append(jnp.where(inside, ids * GROUP + slots - group * GROUP, -1))
    if lay.rest:
        inside = kept & (slots >= lay.full * GROUP)
        found.append(jnp.where(inside, ids * GROUP + slots - lay.full * GROUP, -1))
    return found


def shifted(row, by):
    return jnp.where(row >= 0, row + by, -1)


def place(lay, row_targets, values, out_ref):
    count = out_ref.shape[0]
    toks = values[0].shape[0]
    row_at = iota((count, toks), 0)
    stacked = jnp.concatenate(values, axis=0) if len(values) > 1 else values[0]

    def onehot(rows):
        hit = functools.reduce(jnp.logical_or, [row_at == row for row in rows])
        return jnp.where(hit, 1.0, 0.0).astype(BF16)

    for group in range(lay.full):
        hot = [onehot([t[group] for t in ranks]) for ranks in row_targets]
        hot = jnp.concatenate(hot, axis=1) if len(hot) > 1 else hot[0]
        out_ref[:, group * lay.width : (group + 1) * lay.width] = dot(hot, stacked).astype(BF16)
    if lay.rest:
        hot, pieces = [], []
        for cut in range(lay.cuts):
            for ranks in row_targets:
                hot.append(onehot([shifted(t[lay.full], cut * lay.rest) for t in ranks]))
            pieces.append(stacked[:, cut * lay.piece : (cut + 1) * lay.piece])
        out_ref[:, lay.base :] = dot(
            jnp.concatenate(hot, axis=1), jnp.concatenate(pieces, axis=0)
        ).astype(BF16)


def pick(lay, ranks, message_ref):
    count = message_ref.shape[0]
    toks = ranks[0][0].shape[0]
    row_at = iota((toks, count), 1)

    def onehot(rows):
        hit = functools.reduce(jnp.logical_or, [row_at == row for row in rows])
        return jnp.where(hit, 1.0, 0.0).astype(BF16)

    whole = [onehot([t[group] for t in ranks]) for group in range(lay.full)]
    pieces = []
    for cut in range(lay.cuts):
        left = cut * lay.piece
        total = None
        for group in range(lay.full):
            start = group * lay.width + left
            term = dot(whole[group], message_ref[:, start : start + lay.piece])
            total = term if total is None else total + term
        if lay.rest:
            hot = onehot([shifted(t[lay.full], cut * lay.rest) for t in ranks])
            term = dot(hot, message_ref[:, lay.base : lay.base + lay.piece])
            total = term if total is None else total + term
        pieces.append(total)
    return jnp.concatenate(pieces, axis=1) if len(pieces) > 1 else pieces[0]


def rest_selection(lay, count):
    small = count // GROUP * lay.rest
    row = iota((small, count), 0)
    col = iota((small, count), 1)
    shift = lay.rest.bit_length() - 1
    home = lax.shift_right_logical(row, shift) * GROUP + (row & (lay.rest - 1))
    return [jnp.where(col == home + cut * lay.rest, 1.0, 0.0).astype(BF16) for cut in range(lay.cuts)]


def unpack(lay, message_ref, out_ref):
    count = message_ref.shape[0]
    for group in range(lay.full):
        out_ref[group * count : (group + 1) * count, :] = message_ref[
            :, group * lay.width : (group + 1) * lay.width
        ]
    if lay.rest:
        tail = message_ref[:, lay.base :]
        for cut, chosen in enumerate(rest_selection(lay, count)):
            out_ref[lay.full * count :, cut * lay.piece : (cut + 1) * lay.piece] = dot(
                chosen, tail
            ).astype(BF16)


def pack(lay, rows_ref, message_ref):
    count = message_ref.shape[0]
    for group in range(lay.full):
        message_ref[:, group * lay.width : (group + 1) * lay.width] = rows_ref[
            group * count : (group + 1) * count, :
        ].astype(BF16)
    if lay.rest:
        total = None
        for cut, chosen in enumerate(rest_selection(lay, count)):
            part = rows_ref[
                lay.full * count :, cut * lay.piece : (cut + 1) * lay.piece
            ].astype(BF16)
            term = lax.dot_general(
                chosen, part, (((0,), (0,)), ((), ())), preferred_element_type=F32
            )
            total = term if total is None else total + term
        message_ref[:, lay.base :] = total.astype(BF16)


def send_tokens_kernel(lay, ids_ref, slots_ref, tokens_ref, out_ref):
    first = targets(lay, ids_ref[0:1, :], slots_ref[0:1, :])
    second = targets(lay, ids_ref[1:2, :], slots_ref[1:2, :])
    place(lay, [[first, second]], [tokens_ref[...]], out_ref)


def send_grads_kernel(
    lay, ids_ref, slots_ref, tokens_ref, router_ref, cot_ref, out_ref, gates_ref
):
    logits = dot_nt(router_ref[...], tokens_ref[...])
    expert_at = iota(logits.shape, 0)
    picked = [
        jnp.sum(jnp.where(expert_at == ids_ref[k : k + 1, :], logits, 0.0), axis=0, keepdims=True)
        for k in range(2)
    ]
    gates = [jax.nn.sigmoid(picked[0] - picked[1]), jax.nn.sigmoid(picked[1] - picked[0])]
    gates_ref[0:1, :] = gates[0]
    gates_ref[1:2, :] = gates[1]
    cot = cot_ref[...].astype(F32)
    scaled = [(as_column(gate) * cot).astype(BF16) for gate in gates]
    ranks = [[targets(lay, ids_ref[k : k + 1, :], slots_ref[k : k + 1, :])] for k in range(2)]
    place(lay, ranks, scaled, out_ref)


def forward_kernel(lay, message_ref, win_ref, wout_ref, out_ref, hidden_ref, rows_ref, total_ref):
    step = pl.program_id(0)

    @pl.when(step == 0)
    def _():
        unpack(lay, message_ref, rows_ref)

    hidden = jnp.maximum(dot(rows_ref[...], win_ref[0]), 0.0).astype(BF16)
    hidden_ref[...] = hidden
    term = dot(hidden, wout_ref[0])

    @pl.when(step == 0)
    def _():
        total_ref[...] = term

    @pl.when(step > 0)
    def _():
        total_ref[...] += term

    @pl.when(step == pl.num_programs(0) - 1)
    def _():
        pack(lay, total_ref, out_ref)


def backward_kernel(lay, message_ref, hidden_ref, win_ref, wout_ref, out_ref, rows_ref, total_ref):
    step = pl.program_id(0)

    @pl.when(step == 0)
    def _():
        unpack(lay, message_ref, rows_ref)

    back = dot_nt(rows_ref[...], wout_ref[0])
    back = jnp.where(hidden_ref[...].astype(F32) > 0.0, back, 0.0).astype(BF16)
    term = dot_nt(back, win_ref[0])

    @pl.when(step == 0)
    def _():
        total_ref[...] = term

    @pl.when(step > 0)
    def _():
        total_ref[...] += term

    @pl.when(step == pl.num_programs(0) - 1)
    def _():
        pack(lay, total_ref, out_ref)


def column_targets(lay, ids_ref, slots_ref):
    ids = [as_column(ids_ref[k : k + 1, :].astype(F32)).astype(jnp.int32) for k in range(2)]
    slots = [as_column(slots_ref[k : k + 1, :].astype(F32)).astype(jnp.int32) for k in range(2)]
    return ids, [targets(lay, ids[k], slots[k]) for k in range(2)]


def split_in_two(x):
    high = x.astype(BF16)
    return high, (x - high.astype(F32)).astype(BF16)


def mix_kernel(
    lay,
    ids_ref,
    slots_ref,
    gates_ref,
    message_ref,
    cot_ref,
    tokens_ref,
    router_ref,
    mixed_ref,
    back_ref,
    partial_ref,
):
    experts = router_ref.shape[0]
    toks = tokens_ref.shape[0]
    ids, ranks = column_targets(lay, ids_ref, slots_ref)
    gates = [as_column(gates_ref[k : k + 1, :]) for k in range(2)]
    cot = cot_ref[...].astype(F32)
    choice = [pick(lay, [ranks[k]], message_ref) for k in range(2)]
    mixed_ref[...] = (gates[0] * choice[0] + gates[1] * choice[1]).astype(BF16)
    actions = [jnp.sum(choice[k] * cot, axis=1, keepdims=True) for k in range(2)]
    slope = gates[0] * gates[1] * (actions[0] - actions[1])

    expert_at = iota((toks, experts), 1)
    signs = jnp.where(expert_at == ids[0], 1.0, 0.0) - jnp.where(expert_at == ids[1], 1.0, 0.0)
    high, low = split_in_two(signs * slope)
    router = router_ref[...]
    back_ref[...] = dot(high, router) + dot(low, router)

    expert_at = iota((experts, toks), 0)
    signs = jnp.where(expert_at == ids_ref[0:1, :], 1.0, 0.0) - jnp.where(
        expert_at == ids_ref[1:2, :], 1.0, 0.0
    )
    high, low = split_in_two(signs * as_row(slope))
    tokens = tokens_ref[...]
    partial_ref[...] = (dot(high, tokens) + dot(low, tokens)) * (1.0 / toks)


def grad_kernel(lay, ids_ref, slots_ref, message_ref, back_ref, out_ref):
    _, ranks = column_targets(lay, ids_ref, slots_ref)
    out_ref[...] = (pick(lay, ranks, message_ref) + back_ref[...]).astype(BF16)


def call(kernel, out_shape, flops, args, vmem_bytes=VMEM_BYTES):
    moved = sum(a.size * a.dtype.itemsize for a in args)
    moved += sum(o.size * o.dtype.itemsize for o in jax.tree.leaves(out_shape))
    return pl.pallas_call(
        kernel,
        out_shape=out_shape,
        compiler_params=pltpu.CompilerParams(vmem_limit_bytes=vmem_bytes),
        cost_estimate=pl.CostEstimate(flops=flops, bytes_accessed=moved, transcendentals=0),
    )(*args)


def expert_call(kernel, lay, message, hidden, in_weight, out_weight):
    count = message.shape[0]
    ff = in_weight.shape[2]
    tile = min(512, ff)
    rows = count // GROUP * lay.rows
    whole = pl.BlockSpec(message.shape, lambda j: (0, 0))
    win = pl.BlockSpec((1, lay.width, tile), lambda j: (0, 0, j))
    wout = pl.BlockSpec((1, tile, lay.width), lambda j: (0, j, 0))
    hid = pl.BlockSpec((rows, tile), lambda j: (0, j))
    forward = hidden is None
    operands = (message, in_weight, out_weight) if forward else (message, hidden, in_weight, out_weight)
    message_out = jax.ShapeDtypeStruct(message.shape, BF16)
    return pl.pallas_call(
        functools.partial(kernel, lay),
        grid=(ff // tile,),
        in_specs=[whole, win, wout] if forward else [whole, hid, win, wout],
        out_specs=[whole, hid] if forward else whole,
        out_shape=[message_out, jax.ShapeDtypeStruct((rows, ff), BF16)] if forward else message_out,
        scratch_shapes=[pltpu.VMEM((rows, lay.width), BF16), pltpu.VMEM((rows, lay.width), F32)],
        compiler_params=pltpu.CompilerParams(vmem_limit_bytes=VMEM_BYTES),
        cost_estimate=pl.CostEstimate(
            flops=4 * rows * lay.width * ff,
            bytes_accessed=4 * lay.width * ff + 2 * rows * ff + 4 * message.size,
            transcendentals=0,
        ),
    )(*operands)


def exchange(x):
    return lax.all_to_all(x, AXES, split_axis=0, concat_axis=0, tiled=True)


def from_device(x, bits, devices):
    return lax.ppermute(x, AXES, [(d, d ^ bits) for d in range(devices)])


def sum_of_pairs(own, near, far, both):
    return (own + near) + (far + both)


def sum_over_devices(x, devices, beside):
    half = x.shape[0] // 2
    core = lax.axis_index("inner") % 2
    own = lax.dynamic_slice_in_dim(x, core * half, half, 0)
    other = lax.dynamic_slice_in_dim(x, (1 - core) * half, half, 0)
    own = own + from_device(other, 1, devices)
    terms = [own] + [from_device(own, bits, devices) for bits in (2, 4, 6)]
    own = sum_of_pairs(*terms)
    bit = PLANE
    while bit < devices:
        sent = own.astype(BF16)
        own = sent.astype(F32) + from_device(sent, bit, devices).astype(F32)
        bit *= 2
    beside, own = lax.optimization_barrier((beside, own))
    other = from_device(own, 1, devices)
    first = core == 0
    total = jnp.concatenate([jnp.where(first, own, other), jnp.where(first, other, own)], axis=0)
    return total, beside


def on_device(tokens, router_weight, in_weight, out_weight, expert_ids, slot_ids, cotangent):
    tok_rows, model_width = tokens.shape
    experts = router_weight.shape[1]
    devices = lax.axis_size("outer") * lax.axis_size("inner")
    lay = Layout(3 * tok_rows // experts, model_width)
    message = jax.ShapeDtypeStruct((experts * GROUP, lay.columns), BF16)
    ids, slots, router = expert_ids.T, slot_ids.T, router_weight.T
    place_flops = 4 * experts * GROUP * tok_rows * model_width

    sent_tokens = call(
        functools.partial(send_tokens_kernel, lay), message, place_flops, (ids, slots, tokens)
    )
    sent_grads, gates = call(
        functools.partial(send_grads_kernel, lay),
        [message, jax.ShapeDtypeStruct((2, tok_rows), F32)],
        2 * place_flops,
        (ids, slots, tokens, router, cotangent),
    )
    arrived = exchange(sent_tokens)
    grad_rows = exchange(sent_grads)
    produced, hidden = expert_call(forward_kernel, lay, arrived, None, in_weight, out_weight)
    produced, grad_rows = lax.optimization_barrier((produced, grad_rows))
    produced_back = exchange(produced)
    returned = expert_call(backward_kernel, lay, grad_rows, hidden, in_weight, out_weight)
    returned, produced_back = lax.optimization_barrier((returned, produced_back))
    returned_back = exchange(returned)

    mixed, router_back, partial_grad = call(
        functools.partial(mix_kernel, lay),
        [
            jax.ShapeDtypeStruct((tok_rows, model_width), BF16),
            jax.ShapeDtypeStruct((tok_rows, model_width), F32),
            jax.ShapeDtypeStruct((experts, model_width), F32),
        ],
        2 * place_flops,
        (ids, slots, gates, produced_back, cotangent, tokens, router),
        SMALL_VMEM_BYTES,
    )
    grad_router, returned_back = sum_over_devices(partial_grad, devices, returned_back)
    grad_tokens = call(
        functools.partial(grad_kernel, lay),
        jax.ShapeDtypeStruct((tok_rows, model_width), BF16),
        place_flops,
        (ids, slots, returned_back, router_back),
        SMALL_VMEM_BYTES,
    )
    return (mixed, grad_tokens, grad_router.T)


def solution(mesh):
    placed = (
        P(AXES, None),
        P(),
        P(AXES, None, None),
        P(AXES, None, None),
        P(AXES, None),
        P(AXES, None),
        P(AXES, None),
    )
    return jax.shard_map(
        on_device,
        mesh=mesh,
        in_specs=placed,
        out_specs=(P(AXES, None), P(AXES, None), P()),
        check_vma=False,
    )
```

```python
import functools

import jax
import jax.numpy as jnp
from jax import lax
from jax.experimental import pallas as pl
from jax.experimental.pallas import tpu as pltpu
from jax.sharding import PartitionSpec as P

AXES = ("outer", "inner")
F32 = jnp.float32
BF16 = jnp.bfloat16
GROUP = 8
PLANE = 8
VMEM_BYTES = 60 * 1024 * 1024
SMALL_VMEM_BYTES = 24 * 1024 * 1024
EXPERT_VMEM_BYTES = 56 * 1024 * 1024 + 512 * 1024


class Layout:
    def __init__(self, capacity, model_width):
        self.full, left = divmod(capacity, GROUP)
        self.rest = 0
        if left:
            self.rest = 1
            while self.rest < left:
                self.rest *= 2
        if self.rest == GROUP:
            self.full, self.rest = self.full + 1, 0
        self.capacity = capacity
        self.width = model_width
        self.cuts = GROUP // self.rest if self.rest else 1
        self.piece = model_width // self.cuts
        self.base = self.full * model_width
        self.columns = self.base + (self.piece if self.rest else 0)
        self.rows = self.full * GROUP + self.rest


def dot(a, b):
    return jnp.dot(a, b, preferred_element_type=F32)


def dot_nt(a, b):
    return lax.dot_general(a, b, (((1,), (1,)), ((), ())), preferred_element_type=F32)


def iota(shape, dim):
    return lax.broadcasted_iota(jnp.int32, shape, dim)


def as_column(row):
    count = row.shape[1]
    eye = iota((count, count), 0) == iota((count, count), 1)
    return jnp.sum(jnp.where(eye, row, 0.0), axis=1, keepdims=True)


def as_row(column):
    count = column.shape[0]
    eye = iota((count, count), 0) == iota((count, count), 1)
    return jnp.sum(jnp.where(eye, column, 0.0), axis=0, keepdims=True)


def targets(lay, ids, slots):
    found = []
    kept = slots < lay.capacity
    for group in range(lay.full):
        inside = kept & (slots >= group * GROUP) & (slots < (group + 1) * GROUP)
        found.append(jnp.where(inside, ids * GROUP + slots - group * GROUP, -1))
    if lay.rest:
        inside = kept & (slots >= lay.full * GROUP)
        found.append(jnp.where(inside, ids * GROUP + slots - lay.full * GROUP, -1))
    return found


def shifted(row, by):
    return jnp.where(row >= 0, row + by, -1)


def place(lay, row_targets, values, out_ref):
    count = out_ref.shape[0]
    toks = values[0].shape[0]
    row_at = iota((count, toks), 0)
    stacked = jnp.concatenate(values, axis=0) if len(values) > 1 else values[0]

    def onehot(rows):
        hit = functools.reduce(jnp.logical_or, [row_at == row for row in rows])
        return jnp.where(hit, 1.0, 0.0).astype(BF16)

    for group in range(lay.full):
        hot = [onehot([t[group] for t in ranks]) for ranks in row_targets]
        hot = jnp.concatenate(hot, axis=1) if len(hot) > 1 else hot[0]
        out_ref[:, group * lay.width : (group + 1) * lay.width] = dot(hot, stacked).astype(BF16)
    if lay.rest:
        hot, pieces = [], []
        for cut in range(lay.cuts):
            for ranks in row_targets:
                hot.append(onehot([shifted(t[lay.full], cut * lay.rest) for t in ranks]))
            pieces.append(stacked[:, cut * lay.piece : (cut + 1) * lay.piece])
        out_ref[:, lay.base :] = dot(
            jnp.concatenate(hot, axis=1), jnp.concatenate(pieces, axis=0)
        ).astype(BF16)


def pick(lay, ranks, message_ref):
    count = message_ref.shape[0]
    toks = ranks[0][0].shape[0]
    row_at = iota((toks, count), 1)

    def onehot(rows):
        hit = functools.reduce(jnp.logical_or, [row_at == row for row in rows])
        return jnp.where(hit, 1.0, 0.0).astype(BF16)

    whole = [onehot([t[group] for t in ranks]) for group in range(lay.full)]
    pieces = []
    for cut in range(lay.cuts):
        left = cut * lay.piece
        total = None
        for group in range(lay.full):
            start = group * lay.width + left
            term = dot(whole[group], message_ref[:, start : start + lay.piece])
            total = term if total is None else total + term
        if lay.rest:
            hot = onehot([shifted(t[lay.full], cut * lay.rest) for t in ranks])
            term = dot(hot, message_ref[:, lay.base : lay.base + lay.piece])
            total = term if total is None else total + term
        pieces.append(total)
    return jnp.concatenate(pieces, axis=1) if len(pieces) > 1 else pieces[0]


def rest_selection(lay, count):
    small = count // GROUP * lay.rest
    row = iota((small, count), 0)
    col = iota((small, count), 1)
    shift = lay.rest.bit_length() - 1
    home = lax.shift_right_logical(row, shift) * GROUP + (row & (lay.rest - 1))
    return [jnp.where(col == home + cut * lay.rest, 1.0, 0.0).astype(BF16) for cut in range(lay.cuts)]


def unpack(lay, message_ref, out_ref):
    count = message_ref.shape[0]
    for group in range(lay.full):
        out_ref[group * count : (group + 1) * count, :] = message_ref[
            :, group * lay.width : (group + 1) * lay.width
        ]
    if lay.rest:
        tail = message_ref[:, lay.base :]
        for cut, chosen in enumerate(rest_selection(lay, count)):
            out_ref[lay.full * count :, cut * lay.piece : (cut + 1) * lay.piece] = dot(
                chosen, tail
            ).astype(BF16)


def pack(lay, rows_ref, message_ref):
    count = message_ref.shape[0]
    for group in range(lay.full):
        message_ref[:, group * lay.width : (group + 1) * lay.width] = rows_ref[
            group * count : (group + 1) * count, :
        ].astype(BF16)
    if lay.rest:
        total = None
        for cut, chosen in enumerate(rest_selection(lay, count)):
            part = rows_ref[
                lay.full * count :, cut * lay.piece : (cut + 1) * lay.piece
            ].astype(BF16)
            term = lax.dot_general(
                chosen, part, (((0,), (0,)), ((), ())), preferred_element_type=F32
            )
            total = term if total is None else total + term
        message_ref[:, lay.base :] = total.astype(BF16)


def send_tokens_kernel(lay, ids_ref, slots_ref, tokens_ref, out_ref):
    first = targets(lay, ids_ref[0:1, :], slots_ref[0:1, :])
    second = targets(lay, ids_ref[1:2, :], slots_ref[1:2, :])
    place(lay, [[first, second]], [tokens_ref[...]], out_ref)


def send_grads_kernel(
    lay, ids_ref, slots_ref, tokens_ref, router_ref, cot_ref, out_ref, gates_ref
):
    logits = dot_nt(router_ref[...], tokens_ref[...])
    expert_at = iota(logits.shape, 0)
    picked = [
        jnp.sum(jnp.where(expert_at == ids_ref[k : k + 1, :], logits, 0.0), axis=0, keepdims=True)
        for k in range(2)
    ]
    gates = [jax.nn.sigmoid(picked[0] - picked[1]), jax.nn.sigmoid(picked[1] - picked[0])]
    gates_ref[0:1, :] = gates[0]
    gates_ref[1:2, :] = gates[1]
    cot = cot_ref[...].astype(F32)
    scaled = [(as_column(gate) * cot).astype(BF16) for gate in gates]
    ranks = [[targets(lay, ids_ref[k : k + 1, :], slots_ref[k : k + 1, :])] for k in range(2)]
    place(lay, ranks, scaled, out_ref)


def forward_kernel(lay, message_ref, win_ref, wout_ref, out_ref, hidden_ref, rows_ref, total_ref):
    step = pl.program_id(0)

    @pl.when(step == 0)
    def _():
        unpack(lay, message_ref, rows_ref)

    hidden = jnp.maximum(dot(rows_ref[...], win_ref[0]), 0.0).astype(BF16)
    hidden_ref[...] = hidden
    term = dot(hidden, wout_ref[0])

    @pl.when(step == 0)
    def _():
        total_ref[...] = term

    @pl.when(step > 0)
    def _():
        total_ref[...] += term

    @pl.when(step == pl.num_programs(0) - 1)
    def _():
        pack(lay, total_ref, out_ref)


def backward_kernel(lay, message_ref, hidden_ref, win_ref, wout_ref, out_ref, rows_ref, total_ref):
    step = pl.program_id(0)

    @pl.when(step == 0)
    def _():
        unpack(lay, message_ref, rows_ref)

    back = dot_nt(rows_ref[...], wout_ref[0])
    back = jnp.where(hidden_ref[...].astype(F32) > 0.0, back, 0.0).astype(BF16)
    term = dot_nt(back, win_ref[0])

    @pl.when(step == 0)
    def _():
        total_ref[...] = term

    @pl.when(step > 0)
    def _():
        total_ref[...] += term

    @pl.when(step == pl.num_programs(0) - 1)
    def _():
        pack(lay, total_ref, out_ref)


def column_targets(lay, ids_ref, slots_ref):
    ids = [as_column(ids_ref[k : k + 1, :].astype(F32)).astype(jnp.int32) for k in range(2)]
    slots = [as_column(slots_ref[k : k + 1, :].astype(F32)).astype(jnp.int32) for k in range(2)]
    return ids, [targets(lay, ids[k], slots[k]) for k in range(2)]


def split_in_two(x):
    high = x.astype(BF16)
    return high, (x - high.astype(F32)).astype(BF16)


def mix_kernel(
    lay,
    ids_ref,
    slots_ref,
    gates_ref,
    message_ref,
    cot_ref,
    tokens_ref,
    router_ref,
    mixed_ref,
    back_ref,
    partial_ref,
):
    experts = router_ref.shape[0]
    toks = tokens_ref.shape[0]
    ids, ranks = column_targets(lay, ids_ref, slots_ref)
    gates = [as_column(gates_ref[k : k + 1, :]) for k in range(2)]
    cot = cot_ref[...].astype(F32)
    choice = [pick(lay, [ranks[k]], message_ref) for k in range(2)]
    mixed_ref[...] = (gates[0] * choice[0] + gates[1] * choice[1]).astype(BF16)
    actions = [jnp.sum(choice[k] * cot, axis=1, keepdims=True) for k in range(2)]
    slope = gates[0] * gates[1] * (actions[0] - actions[1])

    expert_at = iota((toks, experts), 1)
    signs = jnp.where(expert_at == ids[0], 1.0, 0.0) - jnp.where(expert_at == ids[1], 1.0, 0.0)
    high, low = split_in_two(signs * slope)
    router = router_ref[...]
    back_ref[...] = dot(high, router) + dot(low, router)

    expert_at = iota((experts, toks), 0)
    signs = jnp.where(expert_at == ids_ref[0:1, :], 1.0, 0.0) - jnp.where(
        expert_at == ids_ref[1:2, :], 1.0, 0.0
    )
    high, low = split_in_two(signs * as_row(slope))
    tokens = tokens_ref[...]
    partial_ref[...] = (dot(high, tokens) + dot(low, tokens)) * (1.0 / toks)


def grad_kernel(lay, ids_ref, slots_ref, message_ref, back_ref, out_ref):
    _, ranks = column_targets(lay, ids_ref, slots_ref)
    out_ref[...] = (pick(lay, ranks, message_ref) + back_ref[...]).astype(BF16)


def call(kernel, out_shape, flops, args, vmem_bytes=VMEM_BYTES):
    moved = sum(a.size * a.dtype.itemsize for a in args)
    moved += sum(o.size * o.dtype.itemsize for o in jax.tree.leaves(out_shape))
    return pl.pallas_call(
        kernel,
        out_shape=out_shape,
        compiler_params=pltpu.CompilerParams(vmem_limit_bytes=vmem_bytes),
        cost_estimate=pl.CostEstimate(flops=flops, bytes_accessed=moved, transcendentals=0),
    )(*args)


def expert_call(kernel, lay, message, hidden, in_weight, out_weight):
    count = message.shape[0]
    ff = in_weight.shape[2]
    tile = min(512, ff)
    rows = count // GROUP * lay.rows
    whole = pl.BlockSpec(message.shape, lambda j: (0, 0))
    win = pl.BlockSpec((1, lay.width, tile), lambda j: (0, 0, j))
    wout = pl.BlockSpec((1, tile, lay.width), lambda j: (0, j, 0))
    hid = pl.BlockSpec((rows, tile), lambda j: (0, j))
    forward = hidden is None
    operands = (message, in_weight, out_weight) if forward else (message, hidden, in_weight, out_weight)
    message_out = jax.ShapeDtypeStruct(message.shape, BF16)
    return pl.pallas_call(
        functools.partial(kernel, lay),
        grid=(ff // tile,),
        in_specs=[whole, win, wout] if forward else [whole, hid, win, wout],
        out_specs=[whole, hid] if forward else whole,
        out_shape=[message_out, jax.ShapeDtypeStruct((rows, ff), BF16)] if forward else message_out,
        scratch_shapes=[pltpu.VMEM((rows, lay.width), BF16), pltpu.VMEM((rows, lay.width), F32)],
        compiler_params=pltpu.CompilerParams(vmem_limit_bytes=EXPERT_VMEM_BYTES),
        cost_estimate=pl.CostEstimate(
            flops=4 * rows * lay.width * ff,
            bytes_accessed=4 * lay.width * ff + 2 * rows * ff + 4 * message.size,
            transcendentals=0,
        ),
    )(*operands)


def exchange(x):
    return lax.all_to_all(x, AXES, split_axis=0, concat_axis=0, tiled=True)


def from_device(x, bits, devices):
    return lax.ppermute(x, AXES, [(d, d ^ bits) for d in range(devices)])


def sum_of_pairs(own, near, far, both):
    return (own + near) + (far + both)


def sum_over_devices(x, devices, beside):
    half = x.shape[0] // 2
    core = lax.axis_index("inner") % 2
    own = lax.dynamic_slice_in_dim(x, core * half, half, 0)
    other = lax.dynamic_slice_in_dim(x, (1 - core) * half, half, 0)
    own = own + from_device(other, 1, devices)
    terms = [own] + [from_device(own, bits, devices) for bits in (2, 4, 6)]
    own = sum_of_pairs(*terms)
    bit = PLANE
    while bit < devices:
        sent = own.astype(BF16)
        own = sent.astype(F32) + from_device(sent, bit, devices).astype(F32)
        bit *= 2
    beside, own = lax.optimization_barrier((beside, own))
    other = from_device(own, 1, devices)
    first = core == 0
    total = jnp.concatenate([jnp.where(first, own, other), jnp.where(first, other, own)], axis=0)
    return total, beside


def on_device(tokens, router_weight, in_weight, out_weight, expert_ids, slot_ids, cotangent):
    tok_rows, model_width = tokens.shape
    experts = router_weight.shape[1]
    devices = lax.axis_size("outer") * lax.axis_size("inner")
    lay = Layout(3 * tok_rows // experts, model_width)
    message = jax.ShapeDtypeStruct((experts * GROUP, lay.columns), BF16)
    ids, slots, router = expert_ids.T, slot_ids.T, router_weight.T
    place_flops = 4 * experts * GROUP * tok_rows * model_width

    sent_tokens = call(
        functools.partial(send_tokens_kernel, lay), message, place_flops, (ids, slots, tokens)
    )
    sent_grads, gates = call(
        functools.partial(send_grads_kernel, lay),
        [message, jax.ShapeDtypeStruct((2, tok_rows), F32)],
        2 * place_flops,
        (ids, slots, tokens, router, cotangent),
        EXPERT_VMEM_BYTES,
    )
    arrived = exchange(sent_tokens)
    grad_rows = exchange(sent_grads)
    produced, hidden = expert_call(forward_kernel, lay, arrived, None, in_weight, out_weight)
    produced, grad_rows = lax.optimization_barrier((produced, grad_rows))
    produced_back = exchange(produced)
    returned = expert_call(backward_kernel, lay, grad_rows, hidden, in_weight, out_weight)
    returned, produced_back = lax.optimization_barrier((returned, produced_back))
    returned_back = exchange(returned)

    mixed, router_back, partial_grad = call(
        functools.partial(mix_kernel, lay),
        [
            jax.ShapeDtypeStruct((tok_rows, model_width), BF16),
            jax.ShapeDtypeStruct((tok_rows, model_width), F32),
            jax.ShapeDtypeStruct((experts, model_width), F32),
        ],
        2 * place_flops,
        (ids, slots, gates, produced_back, cotangent, tokens, router),
        SMALL_VMEM_BYTES,
    )
    grad_router, returned_back = sum_over_devices(partial_grad, devices, returned_back)
    grad_tokens = call(
        functools.partial(grad_kernel, lay),
        jax.ShapeDtypeStruct((tok_rows, model_width), BF16),
        place_flops,
        (ids, slots, returned_back, router_back),
        SMALL_VMEM_BYTES,
    )
    return (mixed, grad_tokens, grad_router.T)


def solution(mesh):
    placed = (
        P(AXES, None),
        P(),
        P(AXES, None, None),
        P(AXES, None, None),
        P(AXES, None),
        P(AXES, None),
        P(AXES, None),
    )
    return jax.shard_map(
        on_device,
        mesh=mesh,
        in_specs=placed,
        out_specs=(P(AXES, None), P(AXES, None), P()),
        check_vma=False,
    )
```

```python
import functools

import jax
import jax.numpy as jnp
from jax import lax
from jax.experimental import pallas as pl
from jax.experimental.pallas import tpu as pltpu
from jax.sharding import PartitionSpec as P

AXES = ("outer", "inner")
F32 = jnp.float32
BF16 = jnp.bfloat16
GROUP = 8
PLANE = 8
VMEM_BYTES = 60 * 1024 * 1024
SMALL_VMEM_BYTES = 24 * 1024 * 1024


class Layout:
    def __init__(self, capacity, model_width):
        self.full, left = divmod(capacity, GROUP)
        self.rest = 0
        if left:
            self.rest = 1
            while self.rest < left:
                self.rest *= 2
        if self.rest == GROUP:
            self.full, self.rest = self.full + 1, 0
        self.capacity = capacity
        self.width = model_width
        self.cuts = GROUP // self.rest if self.rest else 1
        self.piece = model_width // self.cuts
        self.base = self.full * model_width
        self.columns = self.base + (self.piece if self.rest else 0)
        self.rows = self.full * GROUP + self.rest


def dot(a, b):
    return jnp.dot(a, b, preferred_element_type=F32)


def dot_nt(a, b):
    return lax.dot_general(a, b, (((1,), (1,)), ((), ())), preferred_element_type=F32)


def iota(shape, dim):
    return lax.broadcasted_iota(jnp.int32, shape, dim)


def as_column(row):
    count = row.shape[1]
    eye = iota((count, count), 0) == iota((count, count), 1)
    return jnp.sum(jnp.where(eye, row, 0.0), axis=1, keepdims=True)


def as_row(column):
    count = column.shape[0]
    eye = iota((count, count), 0) == iota((count, count), 1)
    return jnp.sum(jnp.where(eye, column, 0.0), axis=0, keepdims=True)


def targets(lay, experts, ids, slots):
    ids = rank_of(ids, experts)
    found = []
    kept = slots < lay.capacity
    for group in range(lay.full):
        inside = kept & (slots >= group * GROUP) & (slots < (group + 1) * GROUP)
        found.append(jnp.where(inside, ids * GROUP + slots - group * GROUP, -1))
    if lay.rest:
        inside = kept & (slots >= lay.full * GROUP)
        found.append(jnp.where(inside, ids * GROUP + slots - lay.full * GROUP, -1))
    return found


def shifted(row, by):
    return jnp.where(row >= 0, row + by, -1)


def place(lay, row_targets, values, out_ref):
    count = out_ref.shape[0]
    toks = values[0].shape[0]
    row_at = iota((count, toks), 0)
    stacked = jnp.concatenate(values, axis=0) if len(values) > 1 else values[0]

    def onehot(rows):
        hit = functools.reduce(jnp.logical_or, [row_at == row for row in rows])
        return jnp.where(hit, 1.0, 0.0).astype(BF16)

    for group in range(lay.full):
        hot = [onehot([t[group] for t in ranks]) for ranks in row_targets]
        hot = jnp.concatenate(hot, axis=1) if len(hot) > 1 else hot[0]
        out_ref[:, group * lay.width : (group + 1) * lay.width] = dot(hot, stacked).astype(BF16)
    if lay.rest:
        hot, pieces = [], []
        for cut in range(lay.cuts):
            for ranks in row_targets:
                hot.append(onehot([shifted(t[lay.full], cut * lay.rest) for t in ranks]))
            pieces.append(stacked[:, cut * lay.piece : (cut + 1) * lay.piece])
        out_ref[:, lay.base :] = dot(
            jnp.concatenate(hot, axis=1), jnp.concatenate(pieces, axis=0)
        ).astype(BF16)


def pick(lay, ranks, message_ref):
    count = message_ref.shape[0]
    toks = ranks[0][0].shape[0]
    row_at = iota((toks, count), 1)

    def onehot(rows):
        hit = functools.reduce(jnp.logical_or, [row_at == row for row in rows])
        return jnp.where(hit, 1.0, 0.0).astype(BF16)

    whole = [onehot([t[group] for t in ranks]) for group in range(lay.full)]
    pieces = []
    for cut in range(lay.cuts):
        left = cut * lay.piece
        total = None
        for group in range(lay.full):
            start = group * lay.width + left
            term = dot(whole[group], message_ref[:, start : start + lay.piece])
            total = term if total is None else total + term
        if lay.rest:
            hot = onehot([shifted(t[lay.full], cut * lay.rest) for t in ranks])
            term = dot(hot, message_ref[:, lay.base : lay.base + lay.piece])
            total = term if total is None else total + term
        pieces.append(total)
    return jnp.concatenate(pieces, axis=1) if len(pieces) > 1 else pieces[0]


def rest_selection(lay, count):
    small = count // GROUP * lay.rest
    row = iota((small, count), 0)
    col = iota((small, count), 1)
    shift = lay.rest.bit_length() - 1
    home = lax.shift_right_logical(row, shift) * GROUP + (row & (lay.rest - 1))
    return [jnp.where(col == home + cut * lay.rest, 1.0, 0.0).astype(BF16) for cut in range(lay.cuts)]


def unpack(lay, message_ref, out_ref):
    count = message_ref.shape[0]
    for group in range(lay.full):
        out_ref[group * count : (group + 1) * count, :] = message_ref[
            :, group * lay.width : (group + 1) * lay.width
        ]
    if lay.rest:
        tail = message_ref[:, lay.base :]
        for cut, chosen in enumerate(rest_selection(lay, count)):
            out_ref[lay.full * count :, cut * lay.piece : (cut + 1) * lay.piece] = dot(
                chosen, tail
            ).astype(BF16)


def pack(lay, rows_ref, message_ref):
    count = message_ref.shape[0]
    for group in range(lay.full):
        message_ref[:, group * lay.width : (group + 1) * lay.width] = rows_ref[
            group * count : (group + 1) * count, :
        ].astype(BF16)
    if lay.rest:
        total = None
        for cut, chosen in enumerate(rest_selection(lay, count)):
            part = rows_ref[
                lay.full * count :, cut * lay.piece : (cut + 1) * lay.piece
            ].astype(BF16)
            term = lax.dot_general(
                chosen, part, (((0,), (0,)), ((), ())), preferred_element_type=F32
            )
            total = term if total is None else total + term
        message_ref[:, lay.base :] = total.astype(BF16)


def send_tokens_kernel(lay, ids_ref, slots_ref, tokens_ref, out_ref):
    first = targets(lay, out_ref.shape[0] // GROUP, ids_ref[0:1, :], slots_ref[0:1, :])
    second = targets(lay, out_ref.shape[0] // GROUP, ids_ref[1:2, :], slots_ref[1:2, :])
    place(lay, [[first, second]], [tokens_ref[...]], out_ref)


def send_grads_kernel(
    lay, ids_ref, slots_ref, tokens_ref, router_ref, cot_ref, out_ref, gates_ref
):
    logits = dot_nt(router_ref[...], tokens_ref[...])
    expert_at = iota(logits.shape, 0)
    picked = [
        jnp.sum(jnp.where(expert_at == ids_ref[k : k + 1, :], logits, 0.0), axis=0, keepdims=True)
        for k in range(2)
    ]
    gates = [jax.nn.sigmoid(picked[0] - picked[1]), jax.nn.sigmoid(picked[1] - picked[0])]
    gates_ref[0:1, :] = gates[0]
    gates_ref[1:2, :] = gates[1]
    cot = cot_ref[...].astype(F32)
    scaled = [(as_column(gate) * cot).astype(BF16) for gate in gates]
    experts = out_ref.shape[0] // GROUP
    ranks = [
        [targets(lay, experts, ids_ref[k : k + 1, :], slots_ref[k : k + 1, :])] for k in range(2)
    ]
    place(lay, ranks, scaled, out_ref)


def forward_kernel(lay, message_ref, win_ref, wout_ref, out_ref, hidden_ref, rows_ref, total_ref):
    step = pl.program_id(0)

    @pl.when(step == 0)
    def _():
        unpack(lay, message_ref, rows_ref)

    hidden = jnp.maximum(dot(rows_ref[...], win_ref[0]), 0.0).astype(BF16)
    hidden_ref[...] = hidden
    term = dot(hidden, wout_ref[0])

    @pl.when(step == 0)
    def _():
        total_ref[...] = term

    @pl.when(step > 0)
    def _():
        total_ref[...] += term

    @pl.when(step == pl.num_programs(0) - 1)
    def _():
        pack(lay, total_ref, out_ref)


def backward_kernel(lay, message_ref, hidden_ref, win_ref, wout_ref, out_ref, rows_ref, total_ref):
    step = pl.program_id(0)

    @pl.when(step == 0)
    def _():
        unpack(lay, message_ref, rows_ref)

    back = dot_nt(rows_ref[...], wout_ref[0])
    back = jnp.where(hidden_ref[...].astype(F32) > 0.0, back, 0.0).astype(BF16)
    term = dot_nt(back, win_ref[0])

    @pl.when(step == 0)
    def _():
        total_ref[...] = term

    @pl.when(step > 0)
    def _():
        total_ref[...] += term

    @pl.when(step == pl.num_programs(0) - 1)
    def _():
        pack(lay, total_ref, out_ref)


def column_targets(lay, experts, ids_ref, slots_ref):
    ids = [as_column(ids_ref[k : k + 1, :].astype(F32)).astype(jnp.int32) for k in range(2)]
    slots = [as_column(slots_ref[k : k + 1, :].astype(F32)).astype(jnp.int32) for k in range(2)]
    return ids, [targets(lay, experts, ids[k], slots[k]) for k in range(2)]


def split_in_two(x):
    high = x.astype(BF16)
    return high, (x - high.astype(F32)).astype(BF16)


def mix_kernel(
    lay,
    ids_ref,
    slots_ref,
    gates_ref,
    message_ref,
    cot_ref,
    tokens_ref,
    router_ref,
    mixed_ref,
    back_ref,
    partial_ref,
):
    experts = router_ref.shape[0]
    toks = tokens_ref.shape[0]
    ids, ranks = column_targets(lay, experts, ids_ref, slots_ref)
    gates = [as_column(gates_ref[k : k + 1, :]) for k in range(2)]
    cot = cot_ref[...].astype(F32)
    choice = [pick(lay, [ranks[k]], message_ref) for k in range(2)]
    mixed_ref[...] = (gates[0] * choice[0] + gates[1] * choice[1]).astype(BF16)
    actions = [jnp.sum(choice[k] * cot, axis=1, keepdims=True) for k in range(2)]
    slope = gates[0] * gates[1] * (actions[0] - actions[1])

    expert_at = iota((toks, experts), 1)
    signs = jnp.where(expert_at == ids[0], 1.0, 0.0) - jnp.where(expert_at == ids[1], 1.0, 0.0)
    high, low = split_in_two(signs * slope)
    router = router_ref[...]
    back_ref[...] = dot(high, router) + dot(low, router)

    expert_at = iota((experts, toks), 0)
    signs = jnp.where(expert_at == ids_ref[0:1, :], 1.0, 0.0) - jnp.where(
        expert_at == ids_ref[1:2, :], 1.0, 0.0
    )
    high, low = split_in_two(signs * as_row(slope))
    tokens = tokens_ref[...]
    partial_ref[...] = (dot(high, tokens) + dot(low, tokens)) * (1.0 / toks)


def grad_kernel(lay, ids_ref, slots_ref, message_ref, back_ref, out_ref):
    _, ranks = column_targets(lay, message_ref.shape[0] // GROUP, ids_ref, slots_ref)
    out_ref[...] = (pick(lay, ranks, message_ref) + back_ref[...]).astype(BF16)


def call(kernel, out_shape, flops, args, vmem_bytes=VMEM_BYTES):
    moved = sum(a.size * a.dtype.itemsize for a in args)
    moved += sum(o.size * o.dtype.itemsize for o in jax.tree.leaves(out_shape))
    return pl.pallas_call(
        kernel,
        out_shape=out_shape,
        compiler_params=pltpu.CompilerParams(vmem_limit_bytes=vmem_bytes),
        cost_estimate=pl.CostEstimate(flops=flops, bytes_accessed=moved, transcendentals=0),
    )(*args)


def expert_call(kernel, lay, message, hidden, in_weight, out_weight):
    count = message.shape[0]
    ff = in_weight.shape[2]
    tile = min(512, ff)
    rows = count // GROUP * lay.rows
    whole = pl.BlockSpec(message.shape, lambda j: (0, 0))
    win = pl.BlockSpec((1, lay.width, tile), lambda j: (0, 0, j))
    wout = pl.BlockSpec((1, tile, lay.width), lambda j: (0, j, 0))
    hid = pl.BlockSpec((rows, tile), lambda j: (0, j))
    forward = hidden is None
    operands = (message, in_weight, out_weight) if forward else (message, hidden, in_weight, out_weight)
    message_out = jax.ShapeDtypeStruct(message.shape, BF16)
    return pl.pallas_call(
        functools.partial(kernel, lay),
        grid=(ff // tile,),
        in_specs=[whole, win, wout] if forward else [whole, hid, win, wout],
        out_specs=[whole, hid] if forward else whole,
        out_shape=[message_out, jax.ShapeDtypeStruct((rows, ff), BF16)] if forward else message_out,
        scratch_shapes=[pltpu.VMEM((rows, lay.width), BF16), pltpu.VMEM((rows, lay.width), F32)],
        compiler_params=pltpu.CompilerParams(vmem_limit_bytes=VMEM_BYTES),
        cost_estimate=pl.CostEstimate(
            flops=4 * rows * lay.width * ff,
            bytes_accessed=4 * lay.width * ff + 2 * rows * ff + 4 * message.size,
            transcendentals=0,
        ),
    )(*operands)


def rank_of(device, devices):
    half = devices // 2
    return (device & (half - 1)) * 2 + jnp.where(device >= half, 1, 0)


def exchange(x, devices):
    order = [rank // 2 + rank % 2 * (devices // 2) for rank in range(devices)]
    return lax.all_to_all(
        x, AXES, split_axis=0, concat_axis=0, tiled=True, axis_index_groups=[order]
    )


def from_device(x, bits, devices):
    return lax.ppermute(x, AXES, [(d, d ^ bits) for d in range(devices)])


def sum_of_pairs(own, near, far, both):
    return (own + near) + (far + both)


def sum_over_devices(x, devices, beside):
    half = x.shape[0] // 2
    core = lax.axis_index("inner") % 2
    own = lax.dynamic_slice_in_dim(x, core * half, half, 0)
    other = lax.dynamic_slice_in_dim(x, (1 - core) * half, half, 0)
    own = own + from_device(other, 1, devices)
    terms = [own] + [from_device(own, bits, devices) for bits in (2, 4, 6)]
    own = sum_of_pairs(*terms)
    bit = PLANE
    while bit < devices:
        sent = own.astype(BF16)
        own = sent.astype(F32) + from_device(sent, bit, devices).astype(F32)
        bit *= 2
    beside, own = lax.optimization_barrier((beside, own))
    other = from_device(own, 1, devices)
    first = core == 0
    total = jnp.concatenate([jnp.where(first, own, other), jnp.where(first, other, own)], axis=0)
    return total, beside


def on_device(tokens, router_weight, in_weight, out_weight, expert_ids, slot_ids, cotangent):
    tok_rows, model_width = tokens.shape
    experts = router_weight.shape[1]
    devices = lax.axis_size("outer") * lax.axis_size("inner")
    lay = Layout(3 * tok_rows // experts, model_width)
    message = jax.ShapeDtypeStruct((experts * GROUP, lay.columns), BF16)
    ids, slots, router = expert_ids.T, slot_ids.T, router_weight.T
    place_flops = 4 * experts * GROUP * tok_rows * model_width

    sent_tokens = call(
        functools.partial(send_tokens_kernel, lay), message, place_flops, (ids, slots, tokens)
    )
    sent_grads, gates = call(
        functools.partial(send_grads_kernel, lay),
        [message, jax.ShapeDtypeStruct((2, tok_rows), F32)],
        2 * place_flops,
        (ids, slots, tokens, router, cotangent),
    )
    arrived = exchange(sent_tokens, devices)
    grad_rows = exchange(sent_grads, devices)
    produced, hidden = expert_call(forward_kernel, lay, arrived, None, in_weight, out_weight)
    produced, grad_rows = lax.optimization_barrier((produced, grad_rows))
    produced_back = exchange(produced, devices)
    returned = expert_call(backward_kernel, lay, grad_rows, hidden, in_weight, out_weight)
    returned, produced_back = lax.optimization_barrier((returned, produced_back))
    returned_back = exchange(returned, devices)

    mixed, router_back, partial_grad = call(
        functools.partial(mix_kernel, lay),
        [
            jax.ShapeDtypeStruct((tok_rows, model_width), BF16),
            jax.ShapeDtypeStruct((tok_rows, model_width), F32),
            jax.ShapeDtypeStruct((experts, model_width), F32),
        ],
        2 * place_flops,
        (ids, slots, gates, produced_back, cotangent, tokens, router),
        SMALL_VMEM_BYTES,
    )
    grad_router, returned_back = sum_over_devices(partial_grad, devices, returned_back)
    grad_tokens = call(
        functools.partial(grad_kernel, lay),
        jax.ShapeDtypeStruct((tok_rows, model_width), BF16),
        place_flops,
        (ids, slots, returned_back, router_back),
        SMALL_VMEM_BYTES,
    )
    return (mixed, grad_tokens, grad_router.T)


def solution(mesh):
    placed = (
        P(AXES, None),
        P(),
        P(AXES, None, None),
        P(AXES, None, None),
        P(AXES, None),
        P(AXES, None),
        P(AXES, None),
    )
    return jax.shard_map(
        on_device,
        mesh=mesh,
        in_specs=placed,
        out_specs=(P(AXES, None), P(AXES, None), P()),
        check_vma=False,
    )
```

```python
import functools

import jax
import jax.numpy as jnp
from jax import lax
from jax.experimental import pallas as pl
from jax.experimental.pallas import tpu as pltpu
from jax.sharding import PartitionSpec as P

AXES = ("outer", "inner")
F32 = jnp.float32
BF16 = jnp.bfloat16
GROUP = 8
PLANE = 8
VMEM_BYTES = 60 * 1024 * 1024
SMALL_VMEM_BYTES = 24 * 1024 * 1024


class Layout:
    def __init__(self, capacity, model_width):
        self.full, left = divmod(capacity, GROUP)
        self.rest = 0
        if left:
            self.rest = 1
            while self.rest < left:
                self.rest *= 2
        if self.rest == GROUP:
            self.full, self.rest = self.full + 1, 0
        self.capacity = capacity
        self.width = model_width
        self.cuts = GROUP // self.rest if self.rest else 1
        self.piece = model_width // self.cuts
        self.base = self.full * model_width
        self.columns = self.base + (self.piece if self.rest else 0)
        self.rows = self.full * GROUP + self.rest


def dot(a, b):
    return jnp.dot(a, b, preferred_element_type=F32)


def dot_nt(a, b):
    return lax.dot_general(a, b, (((1,), (1,)), ((), ())), preferred_element_type=F32)


def iota(shape, dim):
    return lax.broadcasted_iota(jnp.int32, shape, dim)


def as_column(row):
    count = row.shape[1]
    eye = iota((count, count), 0) == iota((count, count), 1)
    return jnp.sum(jnp.where(eye, row, 0.0), axis=1, keepdims=True)


def as_row(column):
    count = column.shape[0]
    eye = iota((count, count), 0) == iota((count, count), 1)
    return jnp.sum(jnp.where(eye, column, 0.0), axis=0, keepdims=True)


def targets(lay, ids, slots):
    found = []
    kept = slots < lay.capacity
    for group in range(lay.full):
        inside = kept & (slots >= group * GROUP) & (slots < (group + 1) * GROUP)
        found.append(jnp.where(inside, ids * GROUP + slots - group * GROUP, -1))
    if lay.rest:
        inside = kept & (slots >= lay.full * GROUP)
        found.append(jnp.where(inside, ids * GROUP + slots - lay.full * GROUP, -1))
    return found


def shifted(row, by):
    return jnp.where(row >= 0, row + by, -1)


def place(lay, row_targets, values, out_ref):
    count = out_ref.shape[0]
    toks = values[0].shape[0]
    row_at = iota((count, toks), 0)
    stacked = jnp.concatenate(values, axis=0) if len(values) > 1 else values[0]

    def onehot(rows):
        hit = functools.reduce(jnp.logical_or, [row_at == row for row in rows])
        return jnp.where(hit, 1.0, 0.0).astype(BF16)

    for group in range(lay.full):
        hot = [onehot([t[group] for t in ranks]) for ranks in row_targets]
        hot = jnp.concatenate(hot, axis=1) if len(hot) > 1 else hot[0]
        out_ref[:, group * lay.width : (group + 1) * lay.width] = dot(hot, stacked).astype(BF16)
    if lay.rest:
        hot, pieces = [], []
        for cut in range(lay.cuts):
            for ranks in row_targets:
                hot.append(onehot([shifted(t[lay.full], cut * lay.rest) for t in ranks]))
            pieces.append(stacked[:, cut * lay.piece : (cut + 1) * lay.piece])
        out_ref[:, lay.base :] = dot(
            jnp.concatenate(hot, axis=1), jnp.concatenate(pieces, axis=0)
        ).astype(BF16)


def pick(lay, ranks, message_ref):
    count = message_ref.shape[0]
    toks = ranks[0][0].shape[0]
    row_at = iota((toks, count), 1)

    def onehot(rows):
        hit = functools.reduce(jnp.logical_or, [row_at == row for row in rows])
        return jnp.where(hit, 1.0, 0.0).astype(BF16)

    whole = [onehot([t[group] for t in ranks]) for group in range(lay.full)]
    pieces = []
    for cut in range(lay.cuts):
        left = cut * lay.piece
        total = None
        for group in range(lay.full):
            start = group * lay.width + left
            term = dot(whole[group], message_ref[:, start : start + lay.piece])
            total = term if total is None else total + term
        if lay.rest:
            hot = onehot([shifted(t[lay.full], cut * lay.rest) for t in ranks])
            term = dot(hot, message_ref[:, lay.base : lay.base + lay.piece])
            total = term if total is None else total + term
        pieces.append(total)
    return jnp.concatenate(pieces, axis=1) if len(pieces) > 1 else pieces[0]


def rest_selection(lay, count):
    small = count // GROUP * lay.rest
    row = iota((small, count), 0)
    col = iota((small, count), 1)
    shift = lay.rest.bit_length() - 1
    home = lax.shift_right_logical(row, shift) * GROUP + (row & (lay.rest - 1))
    return [jnp.where(col == home + cut * lay.rest, 1.0, 0.0).astype(BF16) for cut in range(lay.cuts)]


def unpack(lay, message_ref, out_ref):
    count = message_ref.shape[0]
    for group in range(lay.full):
        out_ref[group * count : (group + 1) * count, :] = message_ref[
            :, group * lay.width : (group + 1) * lay.width
        ]
    if lay.rest:
        tail = message_ref[:, lay.base :]
        for cut, chosen in enumerate(rest_selection(lay, count)):
            out_ref[lay.full * count :, cut * lay.piece : (cut + 1) * lay.piece] = dot(
                chosen, tail
            ).astype(BF16)


def pack(lay, rows_ref, message_ref):
    count = message_ref.shape[0]
    for group in range(lay.full):
        message_ref[:, group * lay.width : (group + 1) * lay.width] = rows_ref[
            group * count : (group + 1) * count, :
        ].astype(BF16)
    if lay.rest:
        total = None
        for cut, chosen in enumerate(rest_selection(lay, count)):
            part = rows_ref[
                lay.full * count :, cut * lay.piece : (cut + 1) * lay.piece
            ].astype(BF16)
            term = lax.dot_general(
                chosen, part, (((0,), (0,)), ((), ())), preferred_element_type=F32
            )
            total = term if total is None else total + term
        message_ref[:, lay.base :] = total.astype(BF16)


def send_tokens_kernel(
    lay, ids_hbm, slots_hbm, tokens_hbm, out_hbm, ids_ref, slots_ref, tokens_ref, rows_ref, sems, out_sems
):
    pairs = ((ids_hbm, ids_ref), (slots_hbm, slots_ref), (tokens_hbm, tokens_ref))
    copies = [
        pltpu.make_async_copy(source, target, sems.at[at]) for at, (source, target) in enumerate(pairs)
    ]
    for copy in copies:
        copy.start()
    for copy in copies[:2]:
        copy.wait()
    count, toks = rows_ref.shape[0], tokens_ref.shape[0]
    row_at = iota((count, toks), 0)
    first, second = [
        targets(lay, ids_ref[k : k + 1, :], slots_ref[k : k + 1, :]) for k in range(2)
    ]

    def onehot(at, by):
        hit = (row_at == shifted(first[at], by)) | (row_at == shifted(second[at], by))
        return jnp.where(hit, 1.0, 0.0).astype(BF16)

    whole = [onehot(group, 0) for group in range(lay.full)]
    cut = [onehot(lay.full, at * lay.rest) for at in range(lay.cuts)] if lay.rest else []
    copies[2].wait()

    sent = []

    def send(start, width, values):
        rows_ref[:, start : start + width] = values.astype(BF16)
        copy = pltpu.make_async_copy(
            rows_ref.at[:, start : start + width],
            out_hbm.at[:, start : start + width],
            out_sems.at[len(sent)],
        )
        copy.start()
        sent.append(copy)

    half = lay.width // 2
    for group, hot in enumerate(whole):
        for at in (0, half):
            send(group * lay.width + at, half, dot(hot, tokens_ref[:, at : at + half]))
    if lay.rest:
        pieces = [tokens_ref[:, at * lay.piece : (at + 1) * lay.piece] for at in range(lay.cuts)]
        send(
            lay.base,
            lay.piece,
            dot(jnp.concatenate(cut, axis=1), jnp.concatenate(pieces, axis=0)),
        )
    for copy in sent:
        copy.wait()


def send_grads_kernel(
    lay, ids_ref, slots_ref, tokens_ref, router_ref, cot_ref, out_ref, gates_ref
):
    logits = dot_nt(router_ref[...], tokens_ref[...])
    expert_at = iota(logits.shape, 0)
    picked = [
        jnp.sum(jnp.where(expert_at == ids_ref[k : k + 1, :], logits, 0.0), axis=0, keepdims=True)
        for k in range(2)
    ]
    gates = [jax.nn.sigmoid(picked[0] - picked[1]), jax.nn.sigmoid(picked[1] - picked[0])]
    gates_ref[0:1, :] = gates[0]
    gates_ref[1:2, :] = gates[1]
    cot = cot_ref[...].astype(F32)
    scaled = [(as_column(gate) * cot).astype(BF16) for gate in gates]
    ranks = [[targets(lay, ids_ref[k : k + 1, :], slots_ref[k : k + 1, :])] for k in range(2)]
    place(lay, ranks, scaled, out_ref)


def forward_kernel(lay, message_ref, win_ref, wout_ref, out_ref, hidden_ref, rows_ref, total_ref):
    step = pl.program_id(0)

    @pl.when(step == 0)
    def _():
        unpack(lay, message_ref, rows_ref)

    hidden = jnp.maximum(dot(rows_ref[...], win_ref[0]), 0.0).astype(BF16)
    hidden_ref[...] = hidden
    term = dot(hidden, wout_ref[0])

    @pl.when(step == 0)
    def _():
        total_ref[...] = term

    @pl.when(step > 0)
    def _():
        total_ref[...] += term

    @pl.when(step == pl.num_programs(0) - 1)
    def _():
        pack(lay, total_ref, out_ref)


def backward_kernel(lay, message_ref, hidden_ref, win_ref, wout_ref, out_ref, rows_ref, total_ref):
    step = pl.program_id(0)

    @pl.when(step == 0)
    def _():
        unpack(lay, message_ref, rows_ref)

    back = dot_nt(rows_ref[...], wout_ref[0])
    back = jnp.where(hidden_ref[...].astype(F32) > 0.0, back, 0.0).astype(BF16)
    term = dot_nt(back, win_ref[0])

    @pl.when(step == 0)
    def _():
        total_ref[...] = term

    @pl.when(step > 0)
    def _():
        total_ref[...] += term

    @pl.when(step == pl.num_programs(0) - 1)
    def _():
        pack(lay, total_ref, out_ref)


def column_targets(lay, ids_ref, slots_ref):
    ids = [as_column(ids_ref[k : k + 1, :].astype(F32)).astype(jnp.int32) for k in range(2)]
    slots = [as_column(slots_ref[k : k + 1, :].astype(F32)).astype(jnp.int32) for k in range(2)]
    return ids, [targets(lay, ids[k], slots[k]) for k in range(2)]


def split_in_two(x):
    high = x.astype(BF16)
    return high, (x - high.astype(F32)).astype(BF16)


def mix_kernel(
    lay,
    ids_ref,
    slots_ref,
    gates_ref,
    message_ref,
    cot_ref,
    tokens_ref,
    router_ref,
    mixed_ref,
    back_ref,
    partial_ref,
):
    experts = router_ref.shape[0]
    toks = tokens_ref.shape[0]
    ids, ranks = column_targets(lay, ids_ref, slots_ref)
    gates = [as_column(gates_ref[k : k + 1, :]) for k in range(2)]
    cot = cot_ref[...].astype(F32)
    choice = [pick(lay, [ranks[k]], message_ref) for k in range(2)]
    mixed_ref[...] = (gates[0] * choice[0] + gates[1] * choice[1]).astype(BF16)
    actions = [jnp.sum(choice[k] * cot, axis=1, keepdims=True) for k in range(2)]
    slope = gates[0] * gates[1] * (actions[0] - actions[1])

    expert_at = iota((toks, experts), 1)
    signs = jnp.where(expert_at == ids[0], 1.0, 0.0) - jnp.where(expert_at == ids[1], 1.0, 0.0)
    high, low = split_in_two(signs * slope)
    router = router_ref[...]
    back_ref[...] = dot(high, router) + dot(low, router)

    expert_at = iota((experts, toks), 0)
    signs = jnp.where(expert_at == ids_ref[0:1, :], 1.0, 0.0) - jnp.where(
        expert_at == ids_ref[1:2, :], 1.0, 0.0
    )
    high, low = split_in_two(signs * as_row(slope))
    tokens = tokens_ref[...]
    partial_ref[...] = (dot(high, tokens) + dot(low, tokens)) * (1.0 / toks)


def grad_kernel(lay, ids_ref, slots_ref, message_ref, back_ref, out_ref):
    _, ranks = column_targets(lay, ids_ref, slots_ref)
    out_ref[...] = (pick(lay, ranks, message_ref) + back_ref[...]).astype(BF16)


def call(kernel, out_shape, flops, args, vmem_bytes=VMEM_BYTES):
    moved = sum(a.size * a.dtype.itemsize for a in args)
    moved += sum(o.size * o.dtype.itemsize for o in jax.tree.leaves(out_shape))
    return pl.pallas_call(
        kernel,
        out_shape=out_shape,
        compiler_params=pltpu.CompilerParams(vmem_limit_bytes=vmem_bytes),
        cost_estimate=pl.CostEstimate(flops=flops, bytes_accessed=moved, transcendentals=0),
    )(*args)


def expert_call(kernel, lay, message, hidden, in_weight, out_weight):
    count = message.shape[0]
    ff = in_weight.shape[2]
    tile = min(512, ff)
    rows = count // GROUP * lay.rows
    whole = pl.BlockSpec(message.shape, lambda j: (0, 0))
    win = pl.BlockSpec((1, lay.width, tile), lambda j: (0, 0, j))
    wout = pl.BlockSpec((1, tile, lay.width), lambda j: (0, j, 0))
    hid = pl.BlockSpec((rows, tile), lambda j: (0, j))
    forward = hidden is None
    operands = (message, in_weight, out_weight) if forward else (message, hidden, in_weight, out_weight)
    message_out = jax.ShapeDtypeStruct(message.shape, BF16)
    return pl.pallas_call(
        functools.partial(kernel, lay),
        grid=(ff // tile,),
        in_specs=[whole, win, wout] if forward else [whole, hid, win, wout],
        out_specs=[whole, hid] if forward else whole,
        out_shape=[message_out, jax.ShapeDtypeStruct((rows, ff), BF16)] if forward else message_out,
        scratch_shapes=[pltpu.VMEM((rows, lay.width), BF16), pltpu.VMEM((rows, lay.width), F32)],
        compiler_params=pltpu.CompilerParams(vmem_limit_bytes=VMEM_BYTES),
        cost_estimate=pl.CostEstimate(
            flops=4 * rows * lay.width * ff,
            bytes_accessed=4 * lay.width * ff + 2 * rows * ff + 4 * message.size,
            transcendentals=0,
        ),
    )(*operands)


def exchange(x):
    return lax.all_to_all(x, AXES, split_axis=0, concat_axis=0, tiled=True)


def from_device(x, bits, devices):
    return lax.ppermute(x, AXES, [(d, d ^ bits) for d in range(devices)])


def sum_of_pairs(own, near, far, both):
    return (own + near) + (far + both)


def sum_over_devices(x, devices, beside):
    half = x.shape[0] // 2
    core = lax.axis_index("inner") % 2
    own = lax.dynamic_slice_in_dim(x, core * half, half, 0)
    other = lax.dynamic_slice_in_dim(x, (1 - core) * half, half, 0)
    own = own + from_device(other, 1, devices)
    sent = own.astype(BF16)
    terms = [sent] + [from_device(sent, bits, devices) for bits in (2, 4, 6)]
    own = sum_of_pairs(*[term.astype(F32) for term in terms])
    bit = PLANE
    while bit < devices:
        sent = own.astype(BF16)
        own = sent.astype(F32) + from_device(sent, bit, devices).astype(F32)
        bit *= 2
    beside, own = lax.optimization_barrier((beside, own))
    other = from_device(own, 1, devices)
    first = core == 0
    total = jnp.concatenate([jnp.where(first, own, other), jnp.where(first, other, own)], axis=0)
    return total, beside


def on_device(tokens, router_weight, in_weight, out_weight, expert_ids, slot_ids, cotangent):
    tok_rows, model_width = tokens.shape
    experts = router_weight.shape[1]
    devices = lax.axis_size("outer") * lax.axis_size("inner")
    lay = Layout(3 * tok_rows // experts, model_width)
    message = jax.ShapeDtypeStruct((experts * GROUP, lay.columns), BF16)
    ids, slots, router = expert_ids.T, slot_ids.T, router_weight.T
    place_flops = 4 * experts * GROUP * tok_rows * model_width

    sent_tokens = pl.pallas_call(
        functools.partial(send_tokens_kernel, lay),
        out_shape=message,
        in_specs=[pl.BlockSpec(memory_space=pl.ANY)] * 3,
        out_specs=pl.BlockSpec(memory_space=pl.ANY),
        scratch_shapes=[
            pltpu.VMEM(ids.shape, jnp.int32),
            pltpu.VMEM(slots.shape, jnp.int32),
            pltpu.VMEM(tokens.shape, BF16),
            pltpu.VMEM(message.shape, BF16),
            pltpu.SemaphoreType.DMA((3,)),
            pltpu.SemaphoreType.DMA((2 * lay.full + 1,)),
        ],
        compiler_params=pltpu.CompilerParams(vmem_limit_bytes=VMEM_BYTES),
        cost_estimate=pl.CostEstimate(
            flops=place_flops, bytes_accessed=2 * (tokens.size + message.size), transcendentals=0
        ),
    )(ids, slots, tokens)
    sent_grads, gates = call(
        functools.partial(send_grads_kernel, lay),
        [message, jax.ShapeDtypeStruct((2, tok_rows), F32)],
        2 * place_flops,
        (ids, slots, tokens, router, cotangent),
    )
    arrived = exchange(sent_tokens)
    grad_rows = exchange(sent_grads)
    produced, hidden = expert_call(forward_kernel, lay, arrived, None, in_weight, out_weight)
    produced, grad_rows = lax.optimization_barrier((produced, grad_rows))
    produced_back = exchange(produced)
    returned = expert_call(backward_kernel, lay, grad_rows, hidden, in_weight, out_weight)
    returned, produced_back = lax.optimization_barrier((returned, produced_back))
    returned_back = exchange(returned)

    mixed, router_back, partial_grad = call(
        functools.partial(mix_kernel, lay),
        [
            jax.ShapeDtypeStruct((tok_rows, model_width), BF16),
            jax.ShapeDtypeStruct((tok_rows, model_width), F32),
            jax.ShapeDtypeStruct((experts, model_width), F32),
        ],
        2 * place_flops,
        (ids, slots, gates, produced_back, cotangent, tokens, router),
        SMALL_VMEM_BYTES,
    )
    grad_router, returned_back = sum_over_devices(partial_grad, devices, returned_back)
    grad_tokens = call(
        functools.partial(grad_kernel, lay),
        jax.ShapeDtypeStruct((tok_rows, model_width), BF16),
        place_flops,
        (ids, slots, returned_back, router_back),
        SMALL_VMEM_BYTES,
    )
    return (mixed, grad_tokens, grad_router.T)


def solution(mesh):
    placed = (
        P(AXES, None),
        P(),
        P(AXES, None, None),
        P(AXES, None, None),
        P(AXES, None),
        P(AXES, None),
        P(AXES, None),
    )
    return jax.shard_map(
        on_device,
        mesh=mesh,
        in_specs=placed,
        out_specs=(P(AXES, None), P(AXES, None), P()),
        check_vma=False,
    )
```

```python
import functools

import jax
import jax.numpy as jnp
from jax import lax
from jax.experimental import pallas as pl
from jax.experimental.pallas import tpu as pltpu
from jax.sharding import PartitionSpec as P

AXES = ("outer", "inner")
F32 = jnp.float32
BF16 = jnp.bfloat16
GROUP = 8
PLANE = 8
VMEM_BYTES = 60 * 1024 * 1024
SMALL_VMEM_BYTES = 24 * 1024 * 1024


class Layout:
    def __init__(self, capacity, model_width):
        self.full, left = divmod(capacity, GROUP)
        self.rest = 0
        if left:
            self.rest = 1
            while self.rest < left:
                self.rest *= 2
        if self.rest == GROUP:
            self.full, self.rest = self.full + 1, 0
        self.capacity = capacity
        self.width = model_width
        self.cuts = GROUP // self.rest if self.rest else 1
        self.piece = model_width // self.cuts
        self.base = self.full * model_width
        self.columns = self.base + (self.piece if self.rest else 0)
        self.rows = self.full * GROUP + self.rest


def dot(a, b):
    return jnp.dot(a, b, preferred_element_type=F32)


def dot_nt(a, b):
    return lax.dot_general(a, b, (((1,), (1,)), ((), ())), preferred_element_type=F32)


def iota(shape, dim):
    return lax.broadcasted_iota(jnp.int32, shape, dim)


def as_column(row):
    count = row.shape[1]
    eye = iota((count, count), 0) == iota((count, count), 1)
    return jnp.sum(jnp.where(eye, row, 0.0), axis=1, keepdims=True)


def as_row(column):
    count = column.shape[0]
    eye = iota((count, count), 0) == iota((count, count), 1)
    return jnp.sum(jnp.where(eye, column, 0.0), axis=0, keepdims=True)


def targets(lay, ids, slots):
    found = []
    kept = slots < lay.capacity
    for group in range(lay.full):
        inside = kept & (slots >= group * GROUP) & (slots < (group + 1) * GROUP)
        found.append(jnp.where(inside, ids * GROUP + slots - group * GROUP, -1))
    if lay.rest:
        inside = kept & (slots >= lay.full * GROUP)
        found.append(jnp.where(inside, ids * GROUP + slots - lay.full * GROUP, -1))
    return found


def shifted(row, by):
    return jnp.where(row >= 0, row + by, -1)


def place(lay, row_targets, values, out_ref):
    count = out_ref.shape[0]
    toks = values[0].shape[0]
    row_at = iota((count, toks), 0)
    stacked = jnp.concatenate(values, axis=0) if len(values) > 1 else values[0]

    def onehot(rows):
        hit = functools.reduce(jnp.logical_or, [row_at == row for row in rows])
        return jnp.where(hit, 1.0, 0.0).astype(BF16)

    for group in range(lay.full):
        hot = [onehot([t[group] for t in ranks]) for ranks in row_targets]
        hot = jnp.concatenate(hot, axis=1) if len(hot) > 1 else hot[0]
        out_ref[:, group * lay.width : (group + 1) * lay.width] = dot(hot, stacked).astype(BF16)
    if lay.rest:
        hot, pieces = [], []
        for cut in range(lay.cuts):
            for ranks in row_targets:
                hot.append(onehot([shifted(t[lay.full], cut * lay.rest) for t in ranks]))
            pieces.append(stacked[:, cut * lay.piece : (cut + 1) * lay.piece])
        out_ref[:, lay.base :] = dot(
            jnp.concatenate(hot, axis=1), jnp.concatenate(pieces, axis=0)
        ).astype(BF16)


def pick(lay, ranks, message_ref):
    count = message_ref.shape[0]
    toks = ranks[0][0].shape[0]
    row_at = iota((toks, count), 1)

    def onehot(rows):
        hit = functools.reduce(jnp.logical_or, [row_at == row for row in rows])
        return jnp.where(hit, 1.0, 0.0).astype(BF16)

    whole = [onehot([t[group] for t in ranks]) for group in range(lay.full)]
    pieces = []
    for cut in range(lay.cuts):
        left = cut * lay.piece
        total = None
        for group in range(lay.full):
            start = group * lay.width + left
            term = dot(whole[group], message_ref[:, start : start + lay.piece])
            total = term if total is None else total + term
        if lay.rest:
            hot = onehot([shifted(t[lay.full], cut * lay.rest) for t in ranks])
            term = dot(hot, message_ref[:, lay.base : lay.base + lay.piece])
            total = term if total is None else total + term
        pieces.append(total)
    return jnp.concatenate(pieces, axis=1) if len(pieces) > 1 else pieces[0]


def rest_selection(lay, count):
    small = count // GROUP * lay.rest
    row = iota((small, count), 0)
    col = iota((small, count), 1)
    shift = lay.rest.bit_length() - 1
    home = lax.shift_right_logical(row, shift) * GROUP + (row & (lay.rest - 1))
    return [jnp.where(col == home + cut * lay.rest, 1.0, 0.0).astype(BF16) for cut in range(lay.cuts)]


def unpack(lay, message_ref, out_ref):
    count = message_ref.shape[0]
    for group in range(lay.full):
        out_ref[group * count : (group + 1) * count, :] = message_ref[
            :, group * lay.width : (group + 1) * lay.width
        ]
    if lay.rest:
        tail = message_ref[:, lay.base :]
        for cut, chosen in enumerate(rest_selection(lay, count)):
            out_ref[lay.full * count :, cut * lay.piece : (cut + 1) * lay.piece] = dot(
                chosen, tail
            ).astype(BF16)


def pack(lay, rows_ref, message_ref):
    count = message_ref.shape[0]
    for group in range(lay.full):
        message_ref[:, group * lay.width : (group + 1) * lay.width] = rows_ref[
            group * count : (group + 1) * count, :
        ].astype(BF16)
    if lay.rest:
        total = None
        for cut, chosen in enumerate(rest_selection(lay, count)):
            part = rows_ref[
                lay.full * count :, cut * lay.piece : (cut + 1) * lay.piece
            ].astype(BF16)
            term = lax.dot_general(
                chosen, part, (((0,), (0,)), ((), ())), preferred_element_type=F32
            )
            total = term if total is None else total + term
        message_ref[:, lay.base :] = total.astype(BF16)


def send_tokens_kernel(
    lay, ids_hbm, slots_hbm, tokens_hbm, out_hbm, ids_ref, slots_ref, tokens_ref, rows_ref, sems, out_sems
):
    pairs = ((ids_hbm, ids_ref), (slots_hbm, slots_ref), (tokens_hbm, tokens_ref))
    copies = [
        pltpu.make_async_copy(source, target, sems.at[at]) for at, (source, target) in enumerate(pairs)
    ]
    for copy in copies:
        copy.start()
    for copy in copies[:2]:
        copy.wait()
    count, toks = rows_ref.shape[0], tokens_ref.shape[0]
    row_at = iota((count, toks), 0)
    first, second = [
        targets(lay, ids_ref[k : k + 1, :], slots_ref[k : k + 1, :]) for k in range(2)
    ]

    def onehot(at, by):
        hit = (row_at == shifted(first[at], by)) | (row_at == shifted(second[at], by))
        return jnp.where(hit, 1.0, 0.0).astype(BF16)

    whole = [onehot(group, 0) for group in range(lay.full)]
    cut = [onehot(lay.full, at * lay.rest) for at in range(lay.cuts)] if lay.rest else []
    copies[2].wait()

    sent = []

    def send(start, width, values):
        rows_ref[:, start : start + width] = values.astype(BF16)
        copy = pltpu.make_async_copy(
            rows_ref.at[:, start : start + width],
            out_hbm.at[:, start : start + width],
            out_sems.at[len(sent)],
        )
        copy.start()
        sent.append(copy)

    half = lay.width // 2
    for group, hot in enumerate(whole):
        for at in (0, half):
            send(group * lay.width + at, half, dot(hot, tokens_ref[:, at : at + half]))
    if lay.rest:
        pieces = [tokens_ref[:, at * lay.piece : (at + 1) * lay.piece] for at in range(lay.cuts)]
        send(
            lay.base,
            lay.piece,
            dot(jnp.concatenate(cut, axis=1), jnp.concatenate(pieces, axis=0)),
        )
    for copy in sent:
        copy.wait()


def send_grads_kernel(
    lay, ids_ref, slots_ref, tokens_ref, router_ref, cot_ref, out_ref, gates_ref
):
    logits = dot_nt(router_ref[...], tokens_ref[...])
    expert_at = iota(logits.shape, 0)
    picked = [
        jnp.sum(jnp.where(expert_at == ids_ref[k : k + 1, :], logits, 0.0), axis=0, keepdims=True)
        for k in range(2)
    ]
    gates = [jax.nn.sigmoid(picked[0] - picked[1]), jax.nn.sigmoid(picked[1] - picked[0])]
    gates_ref[0:1, :] = gates[0]
    gates_ref[1:2, :] = gates[1]
    cot = cot_ref[...].astype(F32)
    scaled = [(as_column(gate) * cot).astype(BF16) for gate in gates]
    ranks = [[targets(lay, ids_ref[k : k + 1, :], slots_ref[k : k + 1, :])] for k in range(2)]
    place(lay, ranks, scaled, out_ref)


def forward_kernel(lay, message_ref, win_ref, wout_ref, out_ref, hidden_ref, rows_ref, total_ref):
    step = pl.program_id(0)

    @pl.when(step == 0)
    def _():
        unpack(lay, message_ref, rows_ref)

    hidden = jnp.maximum(dot(rows_ref[...], win_ref[0]), 0.0).astype(BF16)
    hidden_ref[...] = hidden
    term = dot(hidden, wout_ref[0])

    @pl.when(step == 0)
    def _():
        total_ref[...] = term

    @pl.when(step > 0)
    def _():
        total_ref[...] += term

    @pl.when(step == pl.num_programs(0) - 1)
    def _():
        pack(lay, total_ref, out_ref)


def backward_kernel(lay, message_ref, hidden_ref, win_ref, wout_ref, out_ref, rows_ref, total_ref):
    step = pl.program_id(0)

    @pl.when(step == 0)
    def _():
        unpack(lay, message_ref, rows_ref)

    back = dot_nt(rows_ref[...], wout_ref[0])
    back = jnp.where(hidden_ref[...].astype(F32) > 0.0, back, 0.0).astype(BF16)
    term = dot_nt(back, win_ref[0])

    @pl.when(step == 0)
    def _():
        total_ref[...] = term

    @pl.when(step > 0)
    def _():
        total_ref[...] += term

    @pl.when(step == pl.num_programs(0) - 1)
    def _():
        pack(lay, total_ref, out_ref)


def column_targets(lay, ids_ref, slots_ref):
    ids = [as_column(ids_ref[k : k + 1, :].astype(F32)).astype(jnp.int32) for k in range(2)]
    slots = [as_column(slots_ref[k : k + 1, :].astype(F32)).astype(jnp.int32) for k in range(2)]
    return ids, [targets(lay, ids[k], slots[k]) for k in range(2)]


def split_in_two(x):
    high = x.astype(BF16)
    return high, (x - high.astype(F32)).astype(BF16)


def mix_kernel(
    lay,
    ids_ref,
    slots_ref,
    gates_ref,
    message_ref,
    cot_ref,
    tokens_ref,
    router_ref,
    mixed_ref,
    back_ref,
    partial_ref,
):
    experts = router_ref.shape[0]
    toks = tokens_ref.shape[0]
    ids, ranks = column_targets(lay, ids_ref, slots_ref)
    gates = [as_column(gates_ref[k : k + 1, :]) for k in range(2)]
    cot = cot_ref[...].astype(F32)
    choice = [pick(lay, [ranks[k]], message_ref) for k in range(2)]
    mixed_ref[...] = (gates[0] * choice[0] + gates[1] * choice[1]).astype(BF16)
    actions = [jnp.sum(choice[k] * cot, axis=1, keepdims=True) for k in range(2)]
    slope = gates[0] * gates[1] * (actions[0] - actions[1])

    expert_at = iota((toks, experts), 1)
    signs = jnp.where(expert_at == ids[0], 1.0, 0.0) - jnp.where(expert_at == ids[1], 1.0, 0.0)
    high, low = split_in_two(signs * slope)
    router = router_ref[...]
    back_ref[...] = dot(high, router) + dot(low, router)

    expert_at = iota((experts, toks), 0)
    signs = jnp.where(expert_at == ids_ref[0:1, :], 1.0, 0.0) - jnp.where(
        expert_at == ids_ref[1:2, :], 1.0, 0.0
    )
    high, low = split_in_two(signs * as_row(slope))
    tokens = tokens_ref[...]
    partial_ref[...] = (dot(high, tokens) + dot(low, tokens)) * (1.0 / toks)


def last_kernel(
    lay, ids_ref, slots_ref, message_ref, back_ref, near_ref, far_ref, out_ref, router_ref
):
    _, ranks = column_targets(lay, ids_ref, slots_ref)
    out_ref[...] = (pick(lay, ranks, message_ref) + back_ref[...]).astype(BF16)
    router_ref[...] = near_ref[...].astype(F32) + far_ref[...].astype(F32)


def call(kernel, out_shape, flops, args, vmem_bytes=VMEM_BYTES):
    moved = sum(a.size * a.dtype.itemsize for a in args)
    moved += sum(o.size * o.dtype.itemsize for o in jax.tree.leaves(out_shape))
    return pl.pallas_call(
        kernel,
        out_shape=out_shape,
        compiler_params=pltpu.CompilerParams(vmem_limit_bytes=vmem_bytes),
        cost_estimate=pl.CostEstimate(flops=flops, bytes_accessed=moved, transcendentals=0),
    )(*args)


def expert_call(kernel, lay, message, hidden, in_weight, out_weight):
    count = message.shape[0]
    ff = in_weight.shape[2]
    tile = min(512, ff)
    rows = count // GROUP * lay.rows
    whole = pl.BlockSpec(message.shape, lambda j: (0, 0))
    win = pl.BlockSpec((1, lay.width, tile), lambda j: (0, 0, j))
    wout = pl.BlockSpec((1, tile, lay.width), lambda j: (0, j, 0))
    hid = pl.BlockSpec((rows, tile), lambda j: (0, j))
    forward = hidden is None
    operands = (message, in_weight, out_weight) if forward else (message, hidden, in_weight, out_weight)
    message_out = jax.ShapeDtypeStruct(message.shape, BF16)
    return pl.pallas_call(
        functools.partial(kernel, lay),
        grid=(ff // tile,),
        in_specs=[whole, win, wout] if forward else [whole, hid, win, wout],
        out_specs=[whole, hid] if forward else whole,
        out_shape=[message_out, jax.ShapeDtypeStruct((rows, ff), BF16)] if forward else message_out,
        scratch_shapes=[pltpu.VMEM((rows, lay.width), BF16), pltpu.VMEM((rows, lay.width), F32)],
        compiler_params=pltpu.CompilerParams(vmem_limit_bytes=VMEM_BYTES),
        cost_estimate=pl.CostEstimate(
            flops=4 * rows * lay.width * ff,
            bytes_accessed=4 * lay.width * ff + 2 * rows * ff + 4 * message.size,
            transcendentals=0,
        ),
    )(*operands)


def exchange(x):
    return lax.all_to_all(x, AXES, split_axis=0, concat_axis=0, tiled=True)


def from_device(x, bits, devices):
    return lax.ppermute(x, AXES, [(d, d ^ bits) for d in range(devices)])


def sum_of_pairs(own, near, far, both):
    return (own + near) + (far + both)


def sum_over_devices(x, devices):
    half = x.shape[0] // 2
    core = lax.axis_index("inner") % 2
    own = lax.dynamic_slice_in_dim(x, core * half, half, 0)
    other = lax.dynamic_slice_in_dim(x, (1 - core) * half, half, 0)
    own = own + from_device(other, 1, devices)
    sent = own.astype(BF16)
    terms = [sent] + [from_device(sent, bits, devices) for bits in (2, 4, 6)]
    own = sum_of_pairs(*[term.astype(F32) for term in terms])
    bit = PLANE
    while 2 * bit < devices:
        sent = own.astype(BF16)
        own = sent.astype(F32) + from_device(sent, bit, devices).astype(F32)
        bit *= 2
    sent = own.astype(BF16)
    other = from_device(sent, 1, devices)
    first = core == 0
    sent = jnp.concatenate([jnp.where(first, sent, other), jnp.where(first, other, sent)], axis=0)
    return sent, from_device(sent, bit, devices)


def on_device(tokens, router_weight, in_weight, out_weight, expert_ids, slot_ids, cotangent):
    tok_rows, model_width = tokens.shape
    experts = router_weight.shape[1]
    devices = lax.axis_size("outer") * lax.axis_size("inner")
    lay = Layout(3 * tok_rows // experts, model_width)
    message = jax.ShapeDtypeStruct((experts * GROUP, lay.columns), BF16)
    ids, slots, router = expert_ids.T, slot_ids.T, router_weight.T
    place_flops = 4 * experts * GROUP * tok_rows * model_width

    sent_tokens = pl.pallas_call(
        functools.partial(send_tokens_kernel, lay),
        out_shape=message,
        in_specs=[pl.BlockSpec(memory_space=pl.ANY)] * 3,
        out_specs=pl.BlockSpec(memory_space=pl.ANY),
        scratch_shapes=[
            pltpu.VMEM(ids.shape, jnp.int32),
            pltpu.VMEM(slots.shape, jnp.int32),
            pltpu.VMEM(tokens.shape, BF16),
            pltpu.VMEM(message.shape, BF16),
            pltpu.SemaphoreType.DMA((3,)),
            pltpu.SemaphoreType.DMA((2 * lay.full + 1,)),
        ],
        compiler_params=pltpu.CompilerParams(vmem_limit_bytes=VMEM_BYTES),
        cost_estimate=pl.CostEstimate(
            flops=place_flops, bytes_accessed=2 * (tokens.size + message.size), transcendentals=0
        ),
    )(ids, slots, tokens)
    sent_grads, gates = call(
        functools.partial(send_grads_kernel, lay),
        [message, jax.ShapeDtypeStruct((2, tok_rows), F32)],
        2 * place_flops,
        (ids, slots, tokens, router, cotangent),
    )
    arrived = exchange(sent_tokens)
    grad_rows = exchange(sent_grads)
    produced, hidden = expert_call(forward_kernel, lay, arrived, None, in_weight, out_weight)
    produced, grad_rows = lax.optimization_barrier((produced, grad_rows))
    produced_back = exchange(produced)
    returned = expert_call(backward_kernel, lay, grad_rows, hidden, in_weight, out_weight)
    returned, produced_back = lax.optimization_barrier((returned, produced_back))
    returned_back = exchange(returned)

    mixed, router_back, partial_grad = call(
        functools.partial(mix_kernel, lay),
        [
            jax.ShapeDtypeStruct((tok_rows, model_width), BF16),
            jax.ShapeDtypeStruct((tok_rows, model_width), F32),
            jax.ShapeDtypeStruct((experts, model_width), F32),
        ],
        2 * place_flops,
        (ids, slots, gates, produced_back, cotangent, tokens, router),
        SMALL_VMEM_BYTES,
    )
    near, far = sum_over_devices(partial_grad, devices)
    grad_tokens, grad_router = call(
        functools.partial(last_kernel, lay),
        [
            jax.ShapeDtypeStruct((tok_rows, model_width), BF16),
            jax.ShapeDtypeStruct((experts, model_width), F32),
        ],
        place_flops,
        (ids, slots, returned_back, router_back, near, far),
        SMALL_VMEM_BYTES,
    )
    return (mixed, grad_tokens, grad_router.T)


def solution(mesh):
    placed = (
        P(AXES, None),
        P(),
        P(AXES, None, None),
        P(AXES, None, None),
        P(AXES, None),
        P(AXES, None),
        P(AXES, None),
    )
    return jax.shard_map(
        on_device,
        mesh=mesh,
        in_specs=placed,
        out_specs=(P(AXES, None), P(AXES, None), P()),
        check_vma=False,
    )
```

```python
import functools

import jax
import jax.numpy as jnp
from jax import lax
from jax.experimental import pallas as pl
from jax.experimental.pallas import tpu as pltpu
from jax.sharding import PartitionSpec as P

AXES = ("outer", "inner")
F32 = jnp.float32
BF16 = jnp.bfloat16
GROUP = 8
PLANE = 8
VMEM_BYTES = 60 * 1024 * 1024
SMALL_VMEM_BYTES = 24 * 1024 * 1024


class Layout:
    def __init__(self, capacity, model_width):
        self.full, left = divmod(capacity, GROUP)
        self.rest = 0
        if left:
            self.rest = 1
            while self.rest < left:
                self.rest *= 2
        if self.rest == GROUP:
            self.full, self.rest = self.full + 1, 0
        self.capacity = capacity
        self.width = model_width
        self.cuts = GROUP // self.rest if self.rest else 1
        self.piece = model_width // self.cuts
        self.base = self.full * model_width
        self.columns = self.base + (self.piece if self.rest else 0)
        self.rows = self.full * GROUP + self.rest


def dot(a, b):
    return jnp.dot(a, b, preferred_element_type=F32)


def dot_nt(a, b):
    return lax.dot_general(a, b, (((1,), (1,)), ((), ())), preferred_element_type=F32)


def iota(shape, dim):
    return lax.broadcasted_iota(jnp.int32, shape, dim)


def as_column(row):
    count = row.shape[1]
    eye = iota((count, count), 0) == iota((count, count), 1)
    return jnp.sum(jnp.where(eye, row, 0.0), axis=1, keepdims=True)


def as_row(column):
    count = column.shape[0]
    eye = iota((count, count), 0) == iota((count, count), 1)
    return jnp.sum(jnp.where(eye, column, 0.0), axis=0, keepdims=True)


def targets(lay, experts, ids, slots):
    ids = rank_of(ids, experts)
    found = []
    kept = slots < lay.capacity
    for group in range(lay.full):
        inside = kept & (slots >= group * GROUP) & (slots < (group + 1) * GROUP)
        found.append(jnp.where(inside, ids * GROUP + slots - group * GROUP, -1))
    if lay.rest:
        inside = kept & (slots >= lay.full * GROUP)
        found.append(jnp.where(inside, ids * GROUP + slots - lay.full * GROUP, -1))
    return found


def shifted(row, by):
    return jnp.where(row >= 0, row + by, -1)


def place(lay, row_targets, values, out_ref):
    count = out_ref.shape[0]
    toks = values[0].shape[0]
    row_at = iota((count, toks), 0)
    stacked = jnp.concatenate(values, axis=0) if len(values) > 1 else values[0]

    def onehot(rows):
        hit = functools.reduce(jnp.logical_or, [row_at == row for row in rows])
        return jnp.where(hit, 1.0, 0.0).astype(BF16)

    for group in range(lay.full):
        hot = [onehot([t[group] for t in ranks]) for ranks in row_targets]
        hot = jnp.concatenate(hot, axis=1) if len(hot) > 1 else hot[0]
        out_ref[:, group * lay.width : (group + 1) * lay.width] = dot(hot, stacked).astype(BF16)
    if lay.rest:
        hot, pieces = [], []
        for cut in range(lay.cuts):
            for ranks in row_targets:
                hot.append(onehot([shifted(t[lay.full], cut * lay.rest) for t in ranks]))
            pieces.append(stacked[:, cut * lay.piece : (cut + 1) * lay.piece])
        out_ref[:, lay.base :] = dot(
            jnp.concatenate(hot, axis=1), jnp.concatenate(pieces, axis=0)
        ).astype(BF16)


def pick(lay, ranks, message_ref):
    count = message_ref.shape[0]
    toks = ranks[0][0].shape[0]
    row_at = iota((toks, count), 1)

    def onehot(rows):
        hit = functools.reduce(jnp.logical_or, [row_at == row for row in rows])
        return jnp.where(hit, 1.0, 0.0).astype(BF16)

    whole = [onehot([t[group] for t in ranks]) for group in range(lay.full)]
    pieces = []
    for cut in range(lay.cuts):
        left = cut * lay.piece
        total = None
        for group in range(lay.full):
            start = group * lay.width + left
            term = dot(whole[group], message_ref[:, start : start + lay.piece])
            total = term if total is None else total + term
        if lay.rest:
            hot = onehot([shifted(t[lay.full], cut * lay.rest) for t in ranks])
            term = dot(hot, message_ref[:, lay.base : lay.base + lay.piece])
            total = term if total is None else total + term
        pieces.append(total)
    return jnp.concatenate(pieces, axis=1) if len(pieces) > 1 else pieces[0]


def rest_selection(lay, count):
    small = count // GROUP * lay.rest
    row = iota((small, count), 0)
    col = iota((small, count), 1)
    shift = lay.rest.bit_length() - 1
    home = lax.shift_right_logical(row, shift) * GROUP + (row & (lay.rest - 1))
    return [jnp.where(col == home + cut * lay.rest, 1.0, 0.0).astype(BF16) for cut in range(lay.cuts)]


def unpack(lay, message_ref, out_ref):
    count = message_ref.shape[0]
    for group in range(lay.full):
        out_ref[group * count : (group + 1) * count, :] = message_ref[
            :, group * lay.width : (group + 1) * lay.width
        ]
    if lay.rest:
        tail = message_ref[:, lay.base :]
        for cut, chosen in enumerate(rest_selection(lay, count)):
            out_ref[lay.full * count :, cut * lay.piece : (cut + 1) * lay.piece] = dot(
                chosen, tail
            ).astype(BF16)


def pack(lay, rows_ref, message_ref):
    count = message_ref.shape[0]
    for group in range(lay.full):
        message_ref[:, group * lay.width : (group + 1) * lay.width] = rows_ref[
            group * count : (group + 1) * count, :
        ].astype(BF16)
    if lay.rest:
        total = None
        for cut, chosen in enumerate(rest_selection(lay, count)):
            part = rows_ref[
                lay.full * count :, cut * lay.piece : (cut + 1) * lay.piece
            ].astype(BF16)
            term = lax.dot_general(
                chosen, part, (((0,), (0,)), ((), ())), preferred_element_type=F32
            )
            total = term if total is None else total + term
        message_ref[:, lay.base :] = total.astype(BF16)


def send_tokens_kernel(
    lay, ids_hbm, slots_hbm, tokens_hbm, out_hbm, ids_ref, slots_ref, tokens_ref, rows_ref, sems, out_sems
):
    pairs = ((ids_hbm, ids_ref), (slots_hbm, slots_ref), (tokens_hbm, tokens_ref))
    copies = [
        pltpu.make_async_copy(source, target, sems.at[at]) for at, (source, target) in enumerate(pairs)
    ]
    for copy in copies:
        copy.start()
    for copy in copies[:2]:
        copy.wait()
    count, toks = rows_ref.shape[0], tokens_ref.shape[0]
    row_at = iota((count, toks), 0)
    first, second = [
        targets(lay, count // GROUP, ids_ref[k : k + 1, :], slots_ref[k : k + 1, :])
        for k in range(2)
    ]

    def onehot(at, by):
        hit = (row_at == shifted(first[at], by)) | (row_at == shifted(second[at], by))
        return jnp.where(hit, 1.0, 0.0).astype(BF16)

    whole = [onehot(group, 0) for group in range(lay.full)]
    cut = [onehot(lay.full, at * lay.rest) for at in range(lay.cuts)] if lay.rest else []
    copies[2].wait()

    sent = []

    def send(start, width, values):
        rows_ref[:, start : start + width] = values.astype(BF16)
        copy = pltpu.make_async_copy(
            rows_ref.at[:, start : start + width],
            out_hbm.at[:, start : start + width],
            out_sems.at[len(sent)],
        )
        copy.start()
        sent.append(copy)

    half = lay.width // 2
    for group, hot in enumerate(whole):
        for at in (0, half):
            send(group * lay.width + at, half, dot(hot, tokens_ref[:, at : at + half]))
    if lay.rest:
        pieces = [tokens_ref[:, at * lay.piece : (at + 1) * lay.piece] for at in range(lay.cuts)]
        send(
            lay.base,
            lay.piece,
            dot(jnp.concatenate(cut, axis=1), jnp.concatenate(pieces, axis=0)),
        )
    for copy in sent:
        copy.wait()


def send_grads_kernel(
    lay, ids_ref, slots_ref, tokens_ref, router_ref, cot_ref, out_ref, gates_ref
):
    logits = dot_nt(router_ref[...], tokens_ref[...])
    expert_at = iota(logits.shape, 0)
    picked = [
        jnp.sum(jnp.where(expert_at == ids_ref[k : k + 1, :], logits, 0.0), axis=0, keepdims=True)
        for k in range(2)
    ]
    gates = [jax.nn.sigmoid(picked[0] - picked[1]), jax.nn.sigmoid(picked[1] - picked[0])]
    gates_ref[0:1, :] = gates[0]
    gates_ref[1:2, :] = gates[1]
    cot = cot_ref[...].astype(F32)
    scaled = [(as_column(gate) * cot).astype(BF16) for gate in gates]
    experts = out_ref.shape[0] // GROUP
    ranks = [
        [targets(lay, experts, ids_ref[k : k + 1, :], slots_ref[k : k + 1, :])] for k in range(2)
    ]
    place(lay, ranks, scaled, out_ref)


def forward_kernel(lay, message_ref, win_ref, wout_ref, out_ref, hidden_ref, rows_ref, total_ref):
    step = pl.program_id(0)

    @pl.when(step == 0)
    def _():
        unpack(lay, message_ref, rows_ref)

    hidden = jnp.maximum(dot(rows_ref[...], win_ref[0]), 0.0).astype(BF16)
    hidden_ref[...] = hidden
    term = dot(hidden, wout_ref[0])

    @pl.when(step == 0)
    def _():
        total_ref[...] = term

    @pl.when(step > 0)
    def _():
        total_ref[...] += term

    @pl.when(step == pl.num_programs(0) - 1)
    def _():
        pack(lay, total_ref, out_ref)


def backward_kernel(lay, message_ref, hidden_ref, win_ref, wout_ref, out_ref, rows_ref, total_ref):
    step = pl.program_id(0)

    @pl.when(step == 0)
    def _():
        unpack(lay, message_ref, rows_ref)

    back = dot_nt(rows_ref[...], wout_ref[0])
    back = jnp.where(hidden_ref[...].astype(F32) > 0.0, back, 0.0).astype(BF16)
    term = dot_nt(back, win_ref[0])

    @pl.when(step == 0)
    def _():
        total_ref[...] = term

    @pl.when(step > 0)
    def _():
        total_ref[...] += term

    @pl.when(step == pl.num_programs(0) - 1)
    def _():
        pack(lay, total_ref, out_ref)


def column_targets(lay, experts, ids_ref, slots_ref):
    ids = [as_column(ids_ref[k : k + 1, :].astype(F32)).astype(jnp.int32) for k in range(2)]
    slots = [as_column(slots_ref[k : k + 1, :].astype(F32)).astype(jnp.int32) for k in range(2)]
    return ids, [targets(lay, experts, ids[k], slots[k]) for k in range(2)]


def split_in_two(x):
    high = x.astype(BF16)
    return high, (x - high.astype(F32)).astype(BF16)


def mix_kernel(
    lay,
    ids_ref,
    slots_ref,
    gates_ref,
    message_ref,
    cot_ref,
    tokens_ref,
    router_ref,
    mixed_ref,
    back_ref,
    partial_ref,
):
    experts = router_ref.shape[0]
    toks = tokens_ref.shape[0]
    ids, ranks = column_targets(lay, experts, ids_ref, slots_ref)
    gates = [as_column(gates_ref[k : k + 1, :]) for k in range(2)]
    cot = cot_ref[...].astype(F32)
    choice = [pick(lay, [ranks[k]], message_ref) for k in range(2)]
    mixed_ref[...] = (gates[0] * choice[0] + gates[1] * choice[1]).astype(BF16)
    actions = [jnp.sum(choice[k] * cot, axis=1, keepdims=True) for k in range(2)]
    slope = gates[0] * gates[1] * (actions[0] - actions[1])

    expert_at = iota((toks, experts), 1)
    signs = jnp.where(expert_at == ids[0], 1.0, 0.0) - jnp.where(expert_at == ids[1], 1.0, 0.0)
    high, low = split_in_two(signs * slope)
    router = router_ref[...]
    back_ref[...] = dot(high, router) + dot(low, router)

    expert_at = iota((experts, toks), 0)
    signs = jnp.where(expert_at == ids_ref[0:1, :], 1.0, 0.0) - jnp.where(
        expert_at == ids_ref[1:2, :], 1.0, 0.0
    )
    high, low = split_in_two(signs * as_row(slope))
    tokens = tokens_ref[...]
    partial_ref[...] = (dot(high, tokens) + dot(low, tokens)) * (1.0 / toks)


def grad_kernel(lay, ids_ref, slots_ref, message_ref, back_ref, out_ref):
    _, ranks = column_targets(lay, message_ref.shape[0] // GROUP, ids_ref, slots_ref)
    out_ref[...] = (pick(lay, ranks, message_ref) + back_ref[...]).astype(BF16)


def call(kernel, out_shape, flops, args, vmem_bytes=VMEM_BYTES):
    moved = sum(a.size * a.dtype.itemsize for a in args)
    moved += sum(o.size * o.dtype.itemsize for o in jax.tree.leaves(out_shape))
    return pl.pallas_call(
        kernel,
        out_shape=out_shape,
        compiler_params=pltpu.CompilerParams(vmem_limit_bytes=vmem_bytes),
        cost_estimate=pl.CostEstimate(flops=flops, bytes_accessed=moved, transcendentals=0),
    )(*args)


def expert_call(kernel, lay, message, hidden, in_weight, out_weight):
    count = message.shape[0]
    ff = in_weight.shape[2]
    tile = min(512, ff)
    rows = count // GROUP * lay.rows
    whole = pl.BlockSpec(message.shape, lambda j: (0, 0))
    win = pl.BlockSpec((1, lay.width, tile), lambda j: (0, 0, j))
    wout = pl.BlockSpec((1, tile, lay.width), lambda j: (0, j, 0))
    hid = pl.BlockSpec((rows, tile), lambda j: (0, j))
    forward = hidden is None
    operands = (message, in_weight, out_weight) if forward else (message, hidden, in_weight, out_weight)
    message_out = jax.ShapeDtypeStruct(message.shape, BF16)
    return pl.pallas_call(
        functools.partial(kernel, lay),
        grid=(ff // tile,),
        in_specs=[whole, win, wout] if forward else [whole, hid, win, wout],
        out_specs=[whole, hid] if forward else whole,
        out_shape=[message_out, jax.ShapeDtypeStruct((rows, ff), BF16)] if forward else message_out,
        scratch_shapes=[pltpu.VMEM((rows, lay.width), BF16), pltpu.VMEM((rows, lay.width), F32)],
        compiler_params=pltpu.CompilerParams(vmem_limit_bytes=VMEM_BYTES),
        cost_estimate=pl.CostEstimate(
            flops=4 * rows * lay.width * ff,
            bytes_accessed=4 * lay.width * ff + 2 * rows * ff + 4 * message.size,
            transcendentals=0,
        ),
    )(*operands)


def rank_of(device, devices):
    return (device - devices // 4) & (devices - 1)


def exchange(x, devices):
    order = [(rank + devices // 4) % devices for rank in range(devices)]
    return lax.all_to_all(
        x, AXES, split_axis=0, concat_axis=0, tiled=True, axis_index_groups=[order]
    )


def from_device(x, bits, devices):
    return lax.ppermute(x, AXES, [(d, d ^ bits) for d in range(devices)])


def sum_of_pairs(own, near, far, both):
    return (own + near) + (far + both)


def sum_over_devices(x, devices, beside):
    half = x.shape[0] // 2
    core = lax.axis_index("inner") % 2
    own = lax.dynamic_slice_in_dim(x, core * half, half, 0)
    other = lax.dynamic_slice_in_dim(x, (1 - core) * half, half, 0)
    own = own + from_device(other, 1, devices)
    sent = own.astype(BF16)
    terms = [sent] + [from_device(sent, bits, devices) for bits in (2, 4, 6)]
    own = sum_of_pairs(*[term.astype(F32) for term in terms])
    bit = PLANE
    while bit < devices:
        sent = own.astype(BF16)
        own = sent.astype(F32) + from_device(sent, bit, devices).astype(F32)
        bit *= 2
    beside, own = lax.optimization_barrier((beside, own))
    other = from_device(own, 1, devices)
    first = core == 0
    total = jnp.concatenate([jnp.where(first, own, other), jnp.where(first, other, own)], axis=0)
    return total, beside


def on_device(tokens, router_weight, in_weight, out_weight, expert_ids, slot_ids, cotangent):
    tok_rows, model_width = tokens.shape
    experts = router_weight.shape[1]
    devices = lax.axis_size("outer") * lax.axis_size("inner")
    lay = Layout(3 * tok_rows // experts, model_width)
    message = jax.ShapeDtypeStruct((experts * GROUP, lay.columns), BF16)
    ids, slots, router = expert_ids.T, slot_ids.T, router_weight.T
    place_flops = 4 * experts * GROUP * tok_rows * model_width

    sent_tokens = pl.pallas_call(
        functools.partial(send_tokens_kernel, lay),
        out_shape=message,
        in_specs=[pl.BlockSpec(memory_space=pl.ANY)] * 3,
        out_specs=pl.BlockSpec(memory_space=pl.ANY),
        scratch_shapes=[
            pltpu.VMEM(ids.shape, jnp.int32),
            pltpu.VMEM(slots.shape, jnp.int32),
            pltpu.VMEM(tokens.shape, BF16),
            pltpu.VMEM(message.shape, BF16),
            pltpu.SemaphoreType.DMA((3,)),
            pltpu.SemaphoreType.DMA((2 * lay.full + 1,)),
        ],
        compiler_params=pltpu.CompilerParams(vmem_limit_bytes=VMEM_BYTES),
        cost_estimate=pl.CostEstimate(
            flops=place_flops, bytes_accessed=2 * (tokens.size + message.size), transcendentals=0
        ),
    )(ids, slots, tokens)
    sent_grads, gates = call(
        functools.partial(send_grads_kernel, lay),
        [message, jax.ShapeDtypeStruct((2, tok_rows), F32)],
        2 * place_flops,
        (ids, slots, tokens, router, cotangent),
    )
    arrived = exchange(sent_tokens, devices)
    grad_rows = exchange(sent_grads, devices)
    produced, hidden = expert_call(forward_kernel, lay, arrived, None, in_weight, out_weight)
    produced, grad_rows = lax.optimization_barrier((produced, grad_rows))
    produced_back = exchange(produced, devices)
    returned = expert_call(backward_kernel, lay, grad_rows, hidden, in_weight, out_weight)
    returned, produced_back = lax.optimization_barrier((returned, produced_back))
    returned_back = exchange(returned, devices)

    mixed, router_back, partial_grad = call(
        functools.partial(mix_kernel, lay),
        [
            jax.ShapeDtypeStruct((tok_rows, model_width), BF16),
            jax.ShapeDtypeStruct((tok_rows, model_width), F32),
            jax.ShapeDtypeStruct((experts, model_width), F32),
        ],
        2 * place_flops,
        (ids, slots, gates, produced_back, cotangent, tokens, router),
        SMALL_VMEM_BYTES,
    )
    grad_router, returned_back = sum_over_devices(partial_grad, devices, returned_back)
    grad_tokens = call(
        functools.partial(grad_kernel, lay),
        jax.ShapeDtypeStruct((tok_rows, model_width), BF16),
        place_flops,
        (ids, slots, returned_back, router_back),
        SMALL_VMEM_BYTES,
    )
    return (mixed, grad_tokens, grad_router.T)


def solution(mesh):
    placed = (
        P(AXES, None),
        P(),
        P(AXES, None, None),
        P(AXES, None, None),
        P(AXES, None),
        P(AXES, None),
        P(AXES, None),
    )
    return jax.shard_map(
        on_device,
        mesh=mesh,
        in_specs=placed,
        out_specs=(P(AXES, None), P(AXES, None), P()),
        check_vma=False,
    )
```

```python
import functools

import jax
import jax.numpy as jnp
from jax import lax
from jax.experimental import pallas as pl
from jax.experimental.pallas import tpu as pltpu
from jax.sharding import PartitionSpec as P

AXES = ("outer", "inner")
F32 = jnp.float32
BF16 = jnp.bfloat16
GROUP = 8
PLANE = 8
VMEM_BYTES = 60 * 1024 * 1024
SMALL_VMEM_BYTES = 24 * 1024 * 1024


class Layout:
    def __init__(self, capacity, model_width):
        self.full, left = divmod(capacity, GROUP)
        self.rest = 0
        if left:
            self.rest = 1
            while self.rest < left:
                self.rest *= 2
        if self.rest == GROUP:
            self.full, self.rest = self.full + 1, 0
        self.capacity = capacity
        self.width = model_width
        self.cuts = GROUP // self.rest if self.rest else 1
        self.piece = model_width // self.cuts
        self.base = self.full * model_width
        self.columns = self.base + (self.piece if self.rest else 0)
        self.rows = self.full * GROUP + self.rest


def dot(a, b):
    return jnp.dot(a, b, preferred_element_type=F32)


def dot_nt(a, b):
    return lax.dot_general(a, b, (((1,), (1,)), ((), ())), preferred_element_type=F32)


def iota(shape, dim):
    return lax.broadcasted_iota(jnp.int32, shape, dim)


def as_column(row):
    count = row.shape[1]
    eye = iota((count, count), 0) == iota((count, count), 1)
    return jnp.sum(jnp.where(eye, row, 0.0), axis=1, keepdims=True)


def as_row(column):
    count = column.shape[0]
    eye = iota((count, count), 0) == iota((count, count), 1)
    return jnp.sum(jnp.where(eye, column, 0.0), axis=0, keepdims=True)


def targets(lay, ids, slots):
    found = []
    kept = slots < lay.capacity
    for group in range(lay.full):
        inside = kept & (slots >= group * GROUP) & (slots < (group + 1) * GROUP)
        found.append(jnp.where(inside, ids * GROUP + slots - group * GROUP, -1))
    if lay.rest:
        inside = kept & (slots >= lay.full * GROUP)
        found.append(jnp.where(inside, ids * GROUP + slots - lay.full * GROUP, -1))
    return found


def shifted(row, by):
    return jnp.where(row >= 0, row + by, -1)


def place(lay, row_targets, values, out_ref):
    count = out_ref.shape[0]
    toks = values[0].shape[0]
    row_at = iota((count, toks), 0)
    stacked = jnp.concatenate(values, axis=0) if len(values) > 1 else values[0]

    def onehot(rows):
        hit = functools.reduce(jnp.logical_or, [row_at == row for row in rows])
        return jnp.where(hit, 1.0, 0.0).astype(BF16)

    for group in range(lay.full):
        hot = [onehot([t[group] for t in ranks]) for ranks in row_targets]
        hot = jnp.concatenate(hot, axis=1) if len(hot) > 1 else hot[0]
        out_ref[:, group * lay.width : (group + 1) * lay.width] = dot(hot, stacked).astype(BF16)
    if lay.rest:
        hot, pieces = [], []
        for cut in range(lay.cuts):
            for ranks in row_targets:
                hot.append(onehot([shifted(t[lay.full], cut * lay.rest) for t in ranks]))
            pieces.append(stacked[:, cut * lay.piece : (cut + 1) * lay.piece])
        out_ref[:, lay.base :] = dot(
            jnp.concatenate(hot, axis=1), jnp.concatenate(pieces, axis=0)
        ).astype(BF16)


def pick(lay, ranks, message_ref):
    count = message_ref.shape[0]
    toks = ranks[0][0].shape[0]
    row_at = iota((toks, count), 1)

    def onehot(rows):
        hit = functools.reduce(jnp.logical_or, [row_at == row for row in rows])
        return jnp.where(hit, 1.0, 0.0).astype(BF16)

    whole = [onehot([t[group] for t in ranks]) for group in range(lay.full)]
    pieces = []
    for cut in range(lay.cuts):
        left = cut * lay.piece
        total = None
        for group in range(lay.full):
            start = group * lay.width + left
            term = dot(whole[group], message_ref[:, start : start + lay.piece])
            total = term if total is None else total + term
        if lay.rest:
            hot = onehot([shifted(t[lay.full], cut * lay.rest) for t in ranks])
            term = dot(hot, message_ref[:, lay.base : lay.base + lay.piece])
            total = term if total is None else total + term
        pieces.append(total)
    return jnp.concatenate(pieces, axis=1) if len(pieces) > 1 else pieces[0]


def rest_selection(lay, count):
    small = count // GROUP * lay.rest
    row = iota((small, count), 0)
    col = iota((small, count), 1)
    shift = lay.rest.bit_length() - 1
    home = lax.shift_right_logical(row, shift) * GROUP + (row & (lay.rest - 1))
    return [jnp.where(col == home + cut * lay.rest, 1.0, 0.0).astype(BF16) for cut in range(lay.cuts)]


def unpack(lay, message_ref, out_ref):
    count = message_ref.shape[0]
    for group in range(lay.full):
        out_ref[group * count : (group + 1) * count, :] = message_ref[
            :, group * lay.width : (group + 1) * lay.width
        ]
    if lay.rest:
        tail = message_ref[:, lay.base :]
        for cut, chosen in enumerate(rest_selection(lay, count)):
            out_ref[lay.full * count :, cut * lay.piece : (cut + 1) * lay.piece] = dot(
                chosen, tail
            ).astype(BF16)


def pack(lay, rows_ref, message_ref):
    count = message_ref.shape[0]
    for group in range(lay.full):
        message_ref[:, group * lay.width : (group + 1) * lay.width] = rows_ref[
            group * count : (group + 1) * count, :
        ].astype(BF16)
    if lay.rest:
        total = None
        for cut, chosen in enumerate(rest_selection(lay, count)):
            part = rows_ref[
                lay.full * count :, cut * lay.piece : (cut + 1) * lay.piece
            ].astype(BF16)
            term = lax.dot_general(
                chosen, part, (((0,), (0,)), ((), ())), preferred_element_type=F32
            )
            total = term if total is None else total + term
        message_ref[:, lay.base :] = total.astype(BF16)


def send_tokens_kernel(
    lay, ids_hbm, slots_hbm, tokens_hbm, out_hbm, ids_ref, slots_ref, tokens_ref, rows_ref, sems, out_sems
):
    pairs = ((ids_hbm, ids_ref), (slots_hbm, slots_ref), (tokens_hbm, tokens_ref))
    copies = [
        pltpu.make_async_copy(source, target, sems.at[at]) for at, (source, target) in enumerate(pairs)
    ]
    for copy in copies:
        copy.start()
    for copy in copies[:2]:
        copy.wait()
    count, toks = rows_ref.shape[0], tokens_ref.shape[0]
    row_at = iota((count, toks), 0)
    first, second = [
        targets(lay, ids_ref[k : k + 1, :], slots_ref[k : k + 1, :]) for k in range(2)
    ]

    def onehot(at, by):
        hit = (row_at == shifted(first[at], by)) | (row_at == shifted(second[at], by))
        return jnp.where(hit, 1.0, 0.0).astype(BF16)

    whole = [onehot(group, 0) for group in range(lay.full)]
    cut = [onehot(lay.full, at * lay.rest) for at in range(lay.cuts)] if lay.rest else []
    copies[2].wait()

    sent = []

    def send(start, width, values):
        rows_ref[:, start : start + width] = values.astype(BF16)
        copy = pltpu.make_async_copy(
            rows_ref.at[:, start : start + width],
            out_hbm.at[:, start : start + width],
            out_sems.at[len(sent)],
        )
        copy.start()
        sent.append(copy)

    half = lay.width // 2
    for group, hot in enumerate(whole):
        for at in (0, half):
            send(group * lay.width + at, half, dot(hot, tokens_ref[:, at : at + half]))
    if lay.rest:
        pieces = [tokens_ref[:, at * lay.piece : (at + 1) * lay.piece] for at in range(lay.cuts)]
        send(
            lay.base,
            lay.piece,
            dot(jnp.concatenate(cut, axis=1), jnp.concatenate(pieces, axis=0)),
        )
    for copy in sent:
        copy.wait()


def send_grads_kernel(
    lay, ids_ref, slots_ref, tokens_ref, router_ref, cot_ref, out_ref, gates_ref
):
    logits = dot_nt(router_ref[...], tokens_ref[...])
    expert_at = iota(logits.shape, 0)
    picked = [
        jnp.sum(jnp.where(expert_at == ids_ref[k : k + 1, :], logits, 0.0), axis=0, keepdims=True)
        for k in range(2)
    ]
    gates = [jax.nn.sigmoid(picked[0] - picked[1]), jax.nn.sigmoid(picked[1] - picked[0])]
    gates_ref[0:1, :] = gates[0]
    gates_ref[1:2, :] = gates[1]
    cot = cot_ref[...].astype(F32)
    scaled = [(as_column(gate) * cot).astype(BF16) for gate in gates]
    ranks = [[targets(lay, ids_ref[k : k + 1, :], slots_ref[k : k + 1, :])] for k in range(2)]
    place(lay, ranks, scaled, out_ref)


def forward_kernel(lay, message_ref, win_ref, wout_ref, out_ref, hidden_ref, rows_ref, total_ref):
    step = pl.program_id(0)

    @pl.when(step == 0)
    def _():
        unpack(lay, message_ref, rows_ref)

    hidden = jnp.maximum(dot(rows_ref[...], win_ref[0]), 0.0).astype(BF16)
    hidden_ref[...] = hidden
    term = dot(hidden, wout_ref[0])

    @pl.when(step == 0)
    def _():
        total_ref[...] = term

    @pl.when(step > 0)
    def _():
        total_ref[...] += term

    @pl.when(step == pl.num_programs(0) - 1)
    def _():
        pack(lay, total_ref, out_ref)


def backward_kernel(lay, message_ref, hidden_ref, win_ref, wout_ref, out_ref, rows_ref, total_ref):
    step = pl.program_id(0)

    @pl.when(step == 0)
    def _():
        unpack(lay, message_ref, rows_ref)

    back = dot_nt(rows_ref[...], wout_ref[0])
    back = jnp.where(hidden_ref[...].astype(F32) > 0.0, back, 0.0).astype(BF16)
    term = dot_nt(back, win_ref[0])

    @pl.when(step == 0)
    def _():
        total_ref[...] = term

    @pl.when(step > 0)
    def _():
        total_ref[...] += term

    @pl.when(step == pl.num_programs(0) - 1)
    def _():
        pack(lay, total_ref, out_ref)


def column_targets(lay, ids_ref, slots_ref):
    ids = [as_column(ids_ref[k : k + 1, :].astype(F32)).astype(jnp.int32) for k in range(2)]
    slots = [as_column(slots_ref[k : k + 1, :].astype(F32)).astype(jnp.int32) for k in range(2)]
    return ids, [targets(lay, ids[k], slots[k]) for k in range(2)]


def split_in_two(x):
    high = x.astype(BF16)
    return high, (x - high.astype(F32)).astype(BF16)


def mix_kernel(
    lay,
    ids_ref,
    slots_ref,
    gates_ref,
    message_ref,
    cot_ref,
    tokens_ref,
    router_ref,
    mixed_ref,
    back_ref,
    partial_ref,
):
    experts = router_ref.shape[0]
    toks = tokens_ref.shape[0]
    ids, ranks = column_targets(lay, ids_ref, slots_ref)
    gates = [as_column(gates_ref[k : k + 1, :]) for k in range(2)]
    cot = cot_ref[...].astype(F32)
    choice = [pick(lay, [ranks[k]], message_ref) for k in range(2)]
    mixed_ref[...] = (gates[0] * choice[0] + gates[1] * choice[1]).astype(BF16)
    actions = [jnp.sum(choice[k] * cot, axis=1, keepdims=True) for k in range(2)]
    slope = gates[0] * gates[1] * (actions[0] - actions[1])

    expert_at = iota((toks, experts), 1)
    signs = jnp.where(expert_at == ids[0], 1.0, 0.0) - jnp.where(expert_at == ids[1], 1.0, 0.0)
    high, low = split_in_two(signs * slope)
    router = router_ref[...]
    back_ref[...] = dot(high, router) + dot(low, router)

    expert_at = iota((experts, toks), 0)
    signs = jnp.where(expert_at == ids_ref[0:1, :], 1.0, 0.0) - jnp.where(
        expert_at == ids_ref[1:2, :], 1.0, 0.0
    )
    high, low = split_in_two(signs * as_row(slope))
    tokens = tokens_ref[...]
    partial_ref[...] = (dot(high, tokens) + dot(low, tokens)) * (1.0 / toks)


def grad_kernel(lay, ids_ref, slots_ref, message_ref, back_ref, out_ref):
    _, ranks = column_targets(lay, ids_ref, slots_ref)
    out_ref[...] = (pick(lay, ranks, message_ref) + back_ref[...]).astype(BF16)


def call(kernel, out_shape, flops, args, vmem_bytes=VMEM_BYTES):
    moved = sum(a.size * a.dtype.itemsize for a in args)
    moved += sum(o.size * o.dtype.itemsize for o in jax.tree.leaves(out_shape))
    return pl.pallas_call(
        kernel,
        out_shape=out_shape,
        compiler_params=pltpu.CompilerParams(vmem_limit_bytes=vmem_bytes),
        cost_estimate=pl.CostEstimate(flops=flops, bytes_accessed=moved, transcendentals=0),
    )(*args)


def expert_call(kernel, lay, message, hidden, in_weight, out_weight):
    count = message.shape[0]
    ff = in_weight.shape[2]
    tile = min(512, ff)
    rows = count // GROUP * lay.rows
    whole = pl.BlockSpec(message.shape, lambda j: (0, 0))
    win = pl.BlockSpec((1, lay.width, tile), lambda j: (0, 0, j))
    wout = pl.BlockSpec((1, tile, lay.width), lambda j: (0, j, 0))
    hid = pl.BlockSpec((rows, tile), lambda j: (0, j))
    forward = hidden is None
    operands = (message, in_weight, out_weight) if forward else (message, hidden, in_weight, out_weight)
    message_out = jax.ShapeDtypeStruct(message.shape, BF16)
    return pl.pallas_call(
        functools.partial(kernel, lay),
        grid=(ff // tile,),
        in_specs=[whole, win, wout] if forward else [whole, hid, win, wout],
        out_specs=[whole, hid] if forward else whole,
        out_shape=[message_out, jax.ShapeDtypeStruct((rows, ff), BF16)] if forward else message_out,
        scratch_shapes=[pltpu.VMEM((rows, lay.width), BF16), pltpu.VMEM((rows, lay.width), F32)],
        compiler_params=pltpu.CompilerParams(vmem_limit_bytes=VMEM_BYTES),
        cost_estimate=pl.CostEstimate(
            flops=4 * rows * lay.width * ff,
            bytes_accessed=4 * lay.width * ff + 2 * rows * ff + 4 * message.size,
            transcendentals=0,
        ),
    )(*operands)


def exchange(x):
    return lax.all_to_all(x, AXES, split_axis=0, concat_axis=0, tiled=True)


def from_device(x, bits, devices):
    return lax.ppermute(x, AXES, [(d, d ^ bits) for d in range(devices)])


def sum_of_pairs(own, near, far, both):
    return (own + near) + (far + both)


def sum_over_devices(x, devices, beside):
    half = x.shape[0] // 2
    core = lax.axis_index("inner") % 2
    own = lax.dynamic_slice_in_dim(x, core * half, half, 0)
    other = lax.dynamic_slice_in_dim(x, (1 - core) * half, half, 0)
    own = own + from_device(other, 1, devices)
    sent = own.astype(BF16)
    terms = [sent] + [from_device(sent, bits, devices) for bits in (2, 4, 6)]
    own = sum_of_pairs(*[term.astype(F32) for term in terms])
    bit = PLANE
    while bit < devices:
        sent = own.astype(BF16)
        steps = (1, 2, 3) if 2 * bit < devices else (1,)
        terms = [sent] + [from_device(sent, step * bit, devices) for step in steps]
        terms = [term.astype(F32) for term in terms]
        own = sum_of_pairs(*terms) if len(terms) == 4 else terms[0] + terms[1]
        bit *= 4
    beside, own = lax.optimization_barrier((beside, own))
    other = from_device(own, 1, devices)
    first = core == 0
    total = jnp.concatenate([jnp.where(first, own, other), jnp.where(first, other, own)], axis=0)
    return total, beside


def on_device(tokens, router_weight, in_weight, out_weight, expert_ids, slot_ids, cotangent):
    tok_rows, model_width = tokens.shape
    experts = router_weight.shape[1]
    devices = lax.axis_size("outer") * lax.axis_size("inner")
    lay = Layout(3 * tok_rows // experts, model_width)
    message = jax.ShapeDtypeStruct((experts * GROUP, lay.columns), BF16)
    ids, slots, router = expert_ids.T, slot_ids.T, router_weight.T
    place_flops = 4 * experts * GROUP * tok_rows * model_width

    sent_tokens = pl.pallas_call(
        functools.partial(send_tokens_kernel, lay),
        out_shape=message,
        in_specs=[pl.BlockSpec(memory_space=pl.ANY)] * 3,
        out_specs=pl.BlockSpec(memory_space=pl.ANY),
        scratch_shapes=[
            pltpu.VMEM(ids.shape, jnp.int32),
            pltpu.VMEM(slots.shape, jnp.int32),
            pltpu.VMEM(tokens.shape, BF16),
            pltpu.VMEM(message.shape, BF16),
            pltpu.SemaphoreType.DMA((3,)),
            pltpu.SemaphoreType.DMA((2 * lay.full + 1,)),
        ],
        compiler_params=pltpu.CompilerParams(vmem_limit_bytes=VMEM_BYTES),
        cost_estimate=pl.CostEstimate(
            flops=place_flops, bytes_accessed=2 * (tokens.size + message.size), transcendentals=0
        ),
    )(ids, slots, tokens)
    sent_grads, gates = call(
        functools.partial(send_grads_kernel, lay),
        [message, jax.ShapeDtypeStruct((2, tok_rows), F32)],
        2 * place_flops,
        (ids, slots, tokens, router, cotangent),
    )
    arrived = exchange(sent_tokens)
    grad_rows = exchange(sent_grads)
    produced, hidden = expert_call(forward_kernel, lay, arrived, None, in_weight, out_weight)
    produced, grad_rows = lax.optimization_barrier((produced, grad_rows))
    produced_back = exchange(produced)
    returned = expert_call(backward_kernel, lay, grad_rows, hidden, in_weight, out_weight)
    returned, produced_back = lax.optimization_barrier((returned, produced_back))
    returned_back = exchange(returned)

    mixed, router_back, partial_grad = call(
        functools.partial(mix_kernel, lay),
        [
            jax.ShapeDtypeStruct((tok_rows, model_width), BF16),
            jax.ShapeDtypeStruct((tok_rows, model_width), F32),
            jax.ShapeDtypeStruct((experts, model_width), F32),
        ],
        2 * place_flops,
        (ids, slots, gates, produced_back, cotangent, tokens, router),
        SMALL_VMEM_BYTES,
    )
    grad_router, returned_back = sum_over_devices(partial_grad, devices, returned_back)
    grad_tokens = call(
        functools.partial(grad_kernel, lay),
        jax.ShapeDtypeStruct((tok_rows, model_width), BF16),
        place_flops,
        (ids, slots, returned_back, router_back),
        SMALL_VMEM_BYTES,
    )
    return (mixed, grad_tokens, grad_router.T)


def solution(mesh):
    placed = (
        P(AXES, None),
        P(),
        P(AXES, None, None),
        P(AXES, None, None),
        P(AXES, None),
        P(AXES, None),
        P(AXES, None),
    )
    return jax.shard_map(
        on_device,
        mesh=mesh,
        in_specs=placed,
        out_specs=(P(AXES, None), P(AXES, None), P()),
        check_vma=False,
    )
```

```python
import functools

import jax
import jax.numpy as jnp
from jax import lax
from jax.experimental import pallas as pl
from jax.experimental.pallas import tpu as pltpu
from jax.sharding import PartitionSpec as P

AXES = ("outer", "inner")
F32 = jnp.float32
BF16 = jnp.bfloat16
GROUP = 8
PLANE = 8
VMEM_BYTES = 60 * 1024 * 1024
SMALL_VMEM_BYTES = 24 * 1024 * 1024


class Layout:
    def __init__(self, capacity, model_width):
        self.full, left = divmod(capacity, GROUP)
        self.rest = 0
        if left:
            self.rest = 1
            while self.rest < left:
                self.rest *= 2
        if self.rest == GROUP:
            self.full, self.rest = self.full + 1, 0
        self.capacity = capacity
        self.width = model_width
        self.cuts = GROUP // self.rest if self.rest else 1
        self.piece = model_width // self.cuts
        self.base = self.full * model_width
        self.columns = self.base + (self.piece if self.rest else 0)
        self.rows = self.full * GROUP + self.rest


def dot(a, b):
    return jnp.dot(a, b, preferred_element_type=F32)


def dot_nt(a, b):
    return lax.dot_general(a, b, (((1,), (1,)), ((), ())), preferred_element_type=F32)


def iota(shape, dim):
    return lax.broadcasted_iota(jnp.int32, shape, dim)


def as_column(row):
    count = row.shape[1]
    eye = iota((count, count), 0) == iota((count, count), 1)
    return jnp.sum(jnp.where(eye, row, 0.0), axis=1, keepdims=True)


def as_row(column):
    count = column.shape[0]
    eye = iota((count, count), 0) == iota((count, count), 1)
    return jnp.sum(jnp.where(eye, column, 0.0), axis=0, keepdims=True)


def targets(lay, ids, slots):
    found = []
    kept = slots < lay.capacity
    for group in range(lay.full):
        inside = kept & (slots >= group * GROUP) & (slots < (group + 1) * GROUP)
        found.append(jnp.where(inside, ids * GROUP + slots - group * GROUP, -1))
    if lay.rest:
        inside = kept & (slots >= lay.full * GROUP)
        found.append(jnp.where(inside, ids * GROUP + slots - lay.full * GROUP, -1))
    return found


def shifted(row, by):
    return jnp.where(row >= 0, row + by, -1)


def place(lay, row_targets, values, out_ref):
    count = out_ref.shape[0]
    toks = values[0].shape[0]
    row_at = iota((count, toks), 0)
    stacked = jnp.concatenate(values, axis=0) if len(values) > 1 else values[0]

    def onehot(rows):
        hit = functools.reduce(jnp.logical_or, [row_at == row for row in rows])
        return jnp.where(hit, 1.0, 0.0).astype(BF16)

    for group in range(lay.full):
        hot = [onehot([t[group] for t in ranks]) for ranks in row_targets]
        hot = jnp.concatenate(hot, axis=1) if len(hot) > 1 else hot[0]
        out_ref[:, group * lay.width : (group + 1) * lay.width] = dot(hot, stacked).astype(BF16)
    if lay.rest:
        hot, pieces = [], []
        for cut in range(lay.cuts):
            for ranks in row_targets:
                hot.append(onehot([shifted(t[lay.full], cut * lay.rest) for t in ranks]))
            pieces.append(stacked[:, cut * lay.piece : (cut + 1) * lay.piece])
        out_ref[:, lay.base :] = dot(
            jnp.concatenate(hot, axis=1), jnp.concatenate(pieces, axis=0)
        ).astype(BF16)


def row_onehots(lay, ranks, count):
    toks = ranks[0].shape[0]
    row_at = iota((toks, count), 1)
    rows = list(ranks[: lay.full])
    if lay.rest:
        rows += [shifted(ranks[lay.full], cut * lay.rest) for cut in range(lay.cuts)]
    return [jnp.where(row_at == row, 1.0, 0.0).astype(BF16) for row in rows]


def pick(lay, hots, message_ref):
    pieces = []
    for cut in range(lay.cuts):
        left = cut * lay.piece
        total = None
        for group in range(lay.full):
            start = group * lay.width + left
            term = dot(hots[group], message_ref[:, start : start + lay.piece])
            total = term if total is None else total + term
        if lay.rest:
            term = dot(hots[lay.full + cut], message_ref[:, lay.base : lay.base + lay.piece])
            total = term if total is None else total + term
        pieces.append(total)
    return jnp.concatenate(pieces, axis=1) if len(pieces) > 1 else pieces[0]


def rest_selection(lay, count):
    small = count // GROUP * lay.rest
    row = iota((small, count), 0)
    col = iota((small, count), 1)
    shift = lay.rest.bit_length() - 1
    home = lax.shift_right_logical(row, shift) * GROUP + (row & (lay.rest - 1))
    return [jnp.where(col == home + cut * lay.rest, 1.0, 0.0).astype(BF16) for cut in range(lay.cuts)]


def unpack(lay, message_ref, out_ref):
    count = message_ref.shape[0]
    for group in range(lay.full):
        out_ref[group * count : (group + 1) * count, :] = message_ref[
            :, group * lay.width : (group + 1) * lay.width
        ]
    if lay.rest:
        tail = message_ref[:, lay.base :]
        for cut, chosen in enumerate(rest_selection(lay, count)):
            out_ref[lay.full * count :, cut * lay.piece : (cut + 1) * lay.piece] = dot(
                chosen, tail
            ).astype(BF16)


def pack(lay, rows_ref, message_ref):
    count = message_ref.shape[0]
    for group in range(lay.full):
        message_ref[:, group * lay.width : (group + 1) * lay.width] = rows_ref[
            group * count : (group + 1) * count, :
        ].astype(BF16)
    if lay.rest:
        total = None
        for cut, chosen in enumerate(rest_selection(lay, count)):
            part = rows_ref[
                lay.full * count :, cut * lay.piece : (cut + 1) * lay.piece
            ].astype(BF16)
            term = lax.dot_general(
                chosen, part, (((0,), (0,)), ((), ())), preferred_element_type=F32
            )
            total = term if total is None else total + term
        message_ref[:, lay.base :] = total.astype(BF16)


def send_tokens_kernel(
    lay, ids_hbm, slots_hbm, tokens_hbm, out_hbm, ids_ref, slots_ref, tokens_ref, rows_ref, sems, out_sems
):
    pairs = ((ids_hbm, ids_ref), (slots_hbm, slots_ref), (tokens_hbm, tokens_ref))
    copies = [
        pltpu.make_async_copy(source, target, sems.at[at]) for at, (source, target) in enumerate(pairs)
    ]
    for copy in copies:
        copy.start()
    for copy in copies[:2]:
        copy.wait()
    count, toks = rows_ref.shape[0], tokens_ref.shape[0]
    row_at = iota((count, toks), 0)
    first, second = [
        targets(lay, ids_ref[k : k + 1, :], slots_ref[k : k + 1, :]) for k in range(2)
    ]

    def onehot(at, by):
        hit = (row_at == shifted(first[at], by)) | (row_at == shifted(second[at], by))
        return jnp.where(hit, 1.0, 0.0).astype(BF16)

    whole = [onehot(group, 0) for group in range(lay.full)]
    cut = [onehot(lay.full, at * lay.rest) for at in range(lay.cuts)] if lay.rest else []
    copies[2].wait()

    sent = []

    def send(start, width, values):
        rows_ref[:, start : start + width] = values.astype(BF16)
        copy = pltpu.make_async_copy(
            rows_ref.at[:, start : start + width],
            out_hbm.at[:, start : start + width],
            out_sems.at[len(sent)],
        )
        copy.start()
        sent.append(copy)

    half = lay.width // 2
    for group, hot in enumerate(whole):
        for at in (0, half):
            send(group * lay.width + at, half, dot(hot, tokens_ref[:, at : at + half]))
    if lay.rest:
        pieces = [tokens_ref[:, at * lay.piece : (at + 1) * lay.piece] for at in range(lay.cuts)]
        send(
            lay.base,
            lay.piece,
            dot(jnp.concatenate(cut, axis=1), jnp.concatenate(pieces, axis=0)),
        )
    for copy in sent:
        copy.wait()


def send_grads_kernel(
    lay, ids_ref, slots_ref, tokens_ref, router_ref, cot_ref, out_ref, gates_ref
):
    logits = dot_nt(router_ref[...], tokens_ref[...])
    expert_at = iota(logits.shape, 0)
    picked = [
        jnp.sum(jnp.where(expert_at == ids_ref[k : k + 1, :], logits, 0.0), axis=0, keepdims=True)
        for k in range(2)
    ]
    gates = [jax.nn.sigmoid(picked[0] - picked[1]), jax.nn.sigmoid(picked[1] - picked[0])]
    gates_ref[0:1, :] = gates[0]
    gates_ref[1:2, :] = gates[1]
    cot = cot_ref[...].astype(F32)
    scaled = [(as_column(gate) * cot).astype(BF16) for gate in gates]
    ranks = [[targets(lay, ids_ref[k : k + 1, :], slots_ref[k : k + 1, :])] for k in range(2)]
    place(lay, ranks, scaled, out_ref)


def forward_kernel(lay, message_ref, win_ref, wout_ref, out_ref, hidden_ref, rows_ref, total_ref):
    step = pl.program_id(0)

    @pl.when(step == 0)
    def _():
        unpack(lay, message_ref, rows_ref)

    hidden = jnp.maximum(dot(rows_ref[...], win_ref[0]), 0.0).astype(BF16)
    hidden_ref[...] = hidden
    term = dot(hidden, wout_ref[0])

    @pl.when(step == 0)
    def _():
        total_ref[...] = term

    @pl.when(step > 0)
    def _():
        total_ref[...] += term

    @pl.when(step == pl.num_programs(0) - 1)
    def _():
        pack(lay, total_ref, out_ref)


def backward_kernel(lay, message_ref, hidden_ref, win_ref, wout_ref, out_ref, rows_ref, total_ref):
    step = pl.program_id(0)

    @pl.when(step == 0)
    def _():
        unpack(lay, message_ref, rows_ref)

    back = dot_nt(rows_ref[...], wout_ref[0])
    back = jnp.where(hidden_ref[...].astype(F32) > 0.0, back, 0.0).astype(BF16)
    term = dot_nt(back, win_ref[0])

    @pl.when(step == 0)
    def _():
        total_ref[...] = term

    @pl.when(step > 0)
    def _():
        total_ref[...] += term

    @pl.when(step == pl.num_programs(0) - 1)
    def _():
        pack(lay, total_ref, out_ref)


def column_targets(lay, ids_ref, slots_ref):
    ids = [as_column(ids_ref[k : k + 1, :].astype(F32)).astype(jnp.int32) for k in range(2)]
    slots = [as_column(slots_ref[k : k + 1, :].astype(F32)).astype(jnp.int32) for k in range(2)]
    return ids, [targets(lay, ids[k], slots[k]) for k in range(2)]


def split_in_two(x):
    high = x.astype(BF16)
    return high, (x - high.astype(F32)).astype(BF16)


def mix_kernel(
    lay,
    ids_ref,
    slots_ref,
    gates_ref,
    message_ref,
    cot_ref,
    tokens_ref,
    router_ref,
    mixed_ref,
    back_ref,
    partial_ref,
    hots_ref,
):
    experts = router_ref.shape[0]
    toks = tokens_ref.shape[0]
    ids, ranks = column_targets(lay, ids_ref, slots_ref)
    gates = [as_column(gates_ref[k : k + 1, :]) for k in range(2)]
    cot = cot_ref[...].astype(F32)
    count = message_ref.shape[0]
    hots = [row_onehots(lay, ranks[k], count) for k in range(2)]
    choice = [pick(lay, hots[k], message_ref) for k in range(2)]
    for at, (one, two) in enumerate(zip(*hots)):
        hots_ref[:, at * count : (at + 1) * count] = one + two
    mixed_ref[...] = (gates[0] * choice[0] + gates[1] * choice[1]).astype(BF16)
    actions = [jnp.sum(choice[k] * cot, axis=1, keepdims=True) for k in range(2)]
    slope = gates[0] * gates[1] * (actions[0] - actions[1])

    expert_at = iota((toks, experts), 1)
    signs = jnp.where(expert_at == ids[0], 1.0, 0.0) - jnp.where(expert_at == ids[1], 1.0, 0.0)
    high, low = split_in_two(signs * slope)
    router = router_ref[...]
    back_ref[...] = dot(high, router) + dot(low, router)

    expert_at = iota((experts, toks), 0)
    signs = jnp.where(expert_at == ids_ref[0:1, :], 1.0, 0.0) - jnp.where(
        expert_at == ids_ref[1:2, :], 1.0, 0.0
    )
    high, low = split_in_two(signs * as_row(slope))
    tokens = tokens_ref[...]
    partial_ref[...] = (dot(high, tokens) + dot(low, tokens)) * (1.0 / toks)


def grad_kernel(lay, hots_ref, message_ref, back_ref, out_ref):
    count = message_ref.shape[0]
    hots = [hots_ref[:, at : at + count] for at in range(0, hots_ref.shape[1], count)]
    out_ref[...] = (pick(lay, hots, message_ref) + back_ref[...]).astype(BF16)


def call(kernel, out_shape, flops, args, vmem_bytes=VMEM_BYTES):
    moved = sum(a.size * a.dtype.itemsize for a in args)
    moved += sum(o.size * o.dtype.itemsize for o in jax.tree.leaves(out_shape))
    return pl.pallas_call(
        kernel,
        out_shape=out_shape,
        compiler_params=pltpu.CompilerParams(vmem_limit_bytes=vmem_bytes),
        cost_estimate=pl.CostEstimate(flops=flops, bytes_accessed=moved, transcendentals=0),
    )(*args)


def expert_call(kernel, lay, message, hidden, in_weight, out_weight):
    count = message.shape[0]
    ff = in_weight.shape[2]
    tile = min(512, ff)
    rows = count // GROUP * lay.rows
    whole = pl.BlockSpec(message.shape, lambda j: (0, 0))
    win = pl.BlockSpec((1, lay.width, tile), lambda j: (0, 0, j))
    wout = pl.BlockSpec((1, tile, lay.width), lambda j: (0, j, 0))
    hid = pl.BlockSpec((rows, tile), lambda j: (0, j))
    forward = hidden is None
    operands = (message, in_weight, out_weight) if forward else (message, hidden, in_weight, out_weight)
    message_out = jax.ShapeDtypeStruct(message.shape, BF16)
    return pl.pallas_call(
        functools.partial(kernel, lay),
        grid=(ff // tile,),
        in_specs=[whole, win, wout] if forward else [whole, hid, win, wout],
        out_specs=[whole, hid] if forward else whole,
        out_shape=[message_out, jax.ShapeDtypeStruct((rows, ff), BF16)] if forward else message_out,
        scratch_shapes=[pltpu.VMEM((rows, lay.width), BF16), pltpu.VMEM((rows, lay.width), F32)],
        compiler_params=pltpu.CompilerParams(vmem_limit_bytes=VMEM_BYTES),
        cost_estimate=pl.CostEstimate(
            flops=4 * rows * lay.width * ff,
            bytes_accessed=4 * lay.width * ff + 2 * rows * ff + 4 * message.size,
            transcendentals=0,
        ),
    )(*operands)


def exchange(x):
    return lax.all_to_all(x, AXES, split_axis=0, concat_axis=0, tiled=True)


def from_device(x, bits, devices):
    return lax.ppermute(x, AXES, [(d, d ^ bits) for d in range(devices)])


def sum_of_pairs(own, near, far, both):
    return (own + near) + (far + both)


def sum_over_devices(x, devices, beside):
    half = x.shape[0] // 2
    core = lax.axis_index("inner") % 2
    own = lax.dynamic_slice_in_dim(x, core * half, half, 0)
    other = lax.dynamic_slice_in_dim(x, (1 - core) * half, half, 0)
    own = own + from_device(other, 1, devices)
    sent = own.astype(BF16)
    terms = [sent] + [from_device(sent, bits, devices) for bits in (2, 4, 6)]
    own = sum_of_pairs(*[term.astype(F32) for term in terms])
    bit = PLANE
    while bit < devices:
        sent = own.astype(BF16)
        own = sent.astype(F32) + from_device(sent, bit, devices).astype(F32)
        bit *= 2
    beside, own = lax.optimization_barrier((beside, own))
    other = from_device(own, 1, devices)
    first = core == 0
    total = jnp.concatenate([jnp.where(first, own, other), jnp.where(first, other, own)], axis=0)
    return total, beside


def on_device(tokens, router_weight, in_weight, out_weight, expert_ids, slot_ids, cotangent):
    tok_rows, model_width = tokens.shape
    experts = router_weight.shape[1]
    devices = lax.axis_size("outer") * lax.axis_size("inner")
    lay = Layout(3 * tok_rows // experts, model_width)
    message = jax.ShapeDtypeStruct((experts * GROUP, lay.columns), BF16)
    ids, slots, router = expert_ids.T, slot_ids.T, router_weight.T
    place_flops = 4 * experts * GROUP * tok_rows * model_width

    sent_tokens = pl.pallas_call(
        functools.partial(send_tokens_kernel, lay),
        out_shape=message,
        in_specs=[pl.BlockSpec(memory_space=pl.ANY)] * 3,
        out_specs=pl.BlockSpec(memory_space=pl.ANY),
        scratch_shapes=[
            pltpu.VMEM(ids.shape, jnp.int32),
            pltpu.VMEM(slots.shape, jnp.int32),
            pltpu.VMEM(tokens.shape, BF16),
            pltpu.VMEM(message.shape, BF16),
            pltpu.SemaphoreType.DMA((3,)),
            pltpu.SemaphoreType.DMA((2 * lay.full + 1,)),
        ],
        compiler_params=pltpu.CompilerParams(vmem_limit_bytes=VMEM_BYTES),
        cost_estimate=pl.CostEstimate(
            flops=place_flops, bytes_accessed=2 * (tokens.size + message.size), transcendentals=0
        ),
    )(ids, slots, tokens)
    sent_grads, gates = call(
        functools.partial(send_grads_kernel, lay),
        [message, jax.ShapeDtypeStruct((2, tok_rows), F32)],
        2 * place_flops,
        (ids, slots, tokens, router, cotangent),
    )
    arrived = exchange(sent_tokens)
    grad_rows = exchange(sent_grads)
    produced, hidden = expert_call(forward_kernel, lay, arrived, None, in_weight, out_weight)
    produced, grad_rows = lax.optimization_barrier((produced, grad_rows))
    produced_back = exchange(produced)
    returned = expert_call(backward_kernel, lay, grad_rows, hidden, in_weight, out_weight)
    returned, produced_back = lax.optimization_barrier((returned, produced_back))
    returned_back = exchange(returned)

    hot_columns = experts * GROUP * (lay.full + (lay.cuts if lay.rest else 0))
    mixed, router_back, partial_grad, hots = call(
        functools.partial(mix_kernel, lay),
        [
            jax.ShapeDtypeStruct((tok_rows, model_width), BF16),
            jax.ShapeDtypeStruct((tok_rows, model_width), F32),
            jax.ShapeDtypeStruct((experts, model_width), F32),
            jax.ShapeDtypeStruct((tok_rows, hot_columns), BF16),
        ],
        2 * place_flops,
        (ids, slots, gates, produced_back, cotangent, tokens, router),
        SMALL_VMEM_BYTES,
    )
    grad_router, returned_back = sum_over_devices(partial_grad, devices, returned_back)
    grad_tokens = call(
        functools.partial(grad_kernel, lay),
        jax.ShapeDtypeStruct((tok_rows, model_width), BF16),
        place_flops,
        (hots, returned_back, router_back),
        SMALL_VMEM_BYTES,
    )
    return (mixed, grad_tokens, grad_router.T)


def solution(mesh):
    placed = (
        P(AXES, None),
        P(),
        P(AXES, None, None),
        P(AXES, None, None),
        P(AXES, None),
        P(AXES, None),
        P(AXES, None),
    )
    return jax.shard_map(
        on_device,
        mesh=mesh,
        in_specs=placed,
        out_specs=(P(AXES, None), P(AXES, None), P()),
        check_vma=False,
    )
```

```python
import functools

import jax
import jax.numpy as jnp
from jax import lax
from jax.experimental import pallas as pl
from jax.experimental.pallas import tpu as pltpu
from jax.sharding import PartitionSpec as P

AXES = ("outer", "inner")
F32 = jnp.float32
BF16 = jnp.bfloat16
GROUP = 8
PLANE = 8
VMEM_BYTES = 60 * 1024 * 1024
SMALL_VMEM_BYTES = 24 * 1024 * 1024


class Layout:
    def __init__(self, capacity, model_width):
        self.full, left = divmod(capacity, GROUP)
        self.rest = 0
        if left:
            self.rest = 1
            while self.rest < left:
                self.rest *= 2
        if self.rest == GROUP:
            self.full, self.rest = self.full + 1, 0
        self.capacity = capacity
        self.width = model_width
        self.cuts = GROUP // self.rest if self.rest else 1
        self.piece = model_width // self.cuts
        self.base = self.full * model_width
        self.columns = self.base + (self.piece if self.rest else 0)
        self.rows = self.full * GROUP + self.rest


def dot(a, b):
    return jnp.dot(a, b, preferred_element_type=F32)


def dot_nt(a, b):
    return lax.dot_general(a, b, (((1,), (1,)), ((), ())), preferred_element_type=F32)


def iota(shape, dim):
    return lax.broadcasted_iota(jnp.int32, shape, dim)


def as_column(row):
    count = row.shape[1]
    eye = iota((count, count), 0) == iota((count, count), 1)
    return jnp.sum(jnp.where(eye, row, 0.0), axis=1, keepdims=True)


def as_row(column):
    count = column.shape[0]
    eye = iota((count, count), 0) == iota((count, count), 1)
    return jnp.sum(jnp.where(eye, column, 0.0), axis=0, keepdims=True)


def targets(lay, experts, ids, slots):
    ids = rank_of(ids, experts)
    found = []
    kept = slots < lay.capacity
    for group in range(lay.full):
        inside = kept & (slots >= group * GROUP) & (slots < (group + 1) * GROUP)
        found.append(jnp.where(inside, ids * GROUP + slots - group * GROUP, -1))
    if lay.rest:
        inside = kept & (slots >= lay.full * GROUP)
        found.append(jnp.where(inside, ids * GROUP + slots - lay.full * GROUP, -1))
    return found


def shifted(row, by):
    return jnp.where(row >= 0, row + by, -1)


def place(lay, row_targets, values, out_ref):
    count = out_ref.shape[0]
    toks = values[0].shape[0]
    row_at = iota((count, toks), 0)
    stacked = jnp.concatenate(values, axis=0) if len(values) > 1 else values[0]

    def onehot(rows):
        hit = functools.reduce(jnp.logical_or, [row_at == row for row in rows])
        return jnp.where(hit, 1.0, 0.0).astype(BF16)

    for group in range(lay.full):
        hot = [onehot([t[group] for t in ranks]) for ranks in row_targets]
        hot = jnp.concatenate(hot, axis=1) if len(hot) > 1 else hot[0]
        out_ref[:, group * lay.width : (group + 1) * lay.width] = dot(hot, stacked).astype(BF16)
    if lay.rest:
        hot, pieces = [], []
        for cut in range(lay.cuts):
            for ranks in row_targets:
                hot.append(onehot([shifted(t[lay.full], cut * lay.rest) for t in ranks]))
            pieces.append(stacked[:, cut * lay.piece : (cut + 1) * lay.piece])
        out_ref[:, lay.base :] = dot(
            jnp.concatenate(hot, axis=1), jnp.concatenate(pieces, axis=0)
        ).astype(BF16)


def pick(lay, ranks, message_ref):
    count = message_ref.shape[0]
    toks = ranks[0][0].shape[0]
    row_at = iota((toks, count), 1)

    def onehot(rows):
        hit = functools.reduce(jnp.logical_or, [row_at == row for row in rows])
        return jnp.where(hit, 1.0, 0.0).astype(BF16)

    whole = [onehot([t[group] for t in ranks]) for group in range(lay.full)]
    pieces = []
    for cut in range(lay.cuts):
        left = cut * lay.piece
        total = None
        for group in range(lay.full):
            start = group * lay.width + left
            term = dot(whole[group], message_ref[:, start : start + lay.piece])
            total = term if total is None else total + term
        if lay.rest:
            hot = onehot([shifted(t[lay.full], cut * lay.rest) for t in ranks])
            term = dot(hot, message_ref[:, lay.base : lay.base + lay.piece])
            total = term if total is None else total + term
        pieces.append(total)
    return jnp.concatenate(pieces, axis=1) if len(pieces) > 1 else pieces[0]


def rest_selection(lay, count):
    small = count // GROUP * lay.rest
    row = iota((small, count), 0)
    col = iota((small, count), 1)
    shift = lay.rest.bit_length() - 1
    home = lax.shift_right_logical(row, shift) * GROUP + (row & (lay.rest - 1))
    return [jnp.where(col == home + cut * lay.rest, 1.0, 0.0).astype(BF16) for cut in range(lay.cuts)]


def unpack(lay, message_ref, out_ref):
    count = message_ref.shape[0]
    for group in range(lay.full):
        out_ref[group * count : (group + 1) * count, :] = message_ref[
            :, group * lay.width : (group + 1) * lay.width
        ]
    if lay.rest:
        tail = message_ref[:, lay.base :]
        for cut, chosen in enumerate(rest_selection(lay, count)):
            out_ref[lay.full * count :, cut * lay.piece : (cut + 1) * lay.piece] = dot(
                chosen, tail
            ).astype(BF16)


def pack(lay, rows_ref, message_ref):
    count = message_ref.shape[0]
    for group in range(lay.full):
        message_ref[:, group * lay.width : (group + 1) * lay.width] = rows_ref[
            group * count : (group + 1) * count, :
        ].astype(BF16)
    if lay.rest:
        total = None
        for cut, chosen in enumerate(rest_selection(lay, count)):
            part = rows_ref[
                lay.full * count :, cut * lay.piece : (cut + 1) * lay.piece
            ].astype(BF16)
            term = lax.dot_general(
                chosen, part, (((0,), (0,)), ((), ())), preferred_element_type=F32
            )
            total = term if total is None else total + term
        message_ref[:, lay.base :] = total.astype(BF16)


def send_tokens_kernel(
    lay, ids_hbm, slots_hbm, tokens_hbm, out_hbm, ids_ref, slots_ref, tokens_ref, rows_ref, sems, out_sems
):
    pairs = ((ids_hbm, ids_ref), (slots_hbm, slots_ref), (tokens_hbm, tokens_ref))
    copies = [
        pltpu.make_async_copy(source, target, sems.at[at]) for at, (source, target) in enumerate(pairs)
    ]
    for copy in copies:
        copy.start()
    for copy in copies[:2]:
        copy.wait()
    count, toks = rows_ref.shape[0], tokens_ref.shape[0]
    row_at = iota((count, toks), 0)
    first, second = [
        targets(lay, count // GROUP, ids_ref[k : k + 1, :], slots_ref[k : k + 1, :])
        for k in range(2)
    ]

    def onehot(at, by):
        hit = (row_at == shifted(first[at], by)) | (row_at == shifted(second[at], by))
        return jnp.where(hit, 1.0, 0.0).astype(BF16)

    whole = [onehot(group, 0) for group in range(lay.full)]
    cut = [onehot(lay.full, at * lay.rest) for at in range(lay.cuts)] if lay.rest else []
    copies[2].wait()

    sent = []

    def send(start, width, values):
        rows_ref[:, start : start + width] = values.astype(BF16)
        copy = pltpu.make_async_copy(
            rows_ref.at[:, start : start + width],
            out_hbm.at[:, start : start + width],
            out_sems.at[len(sent)],
        )
        copy.start()
        sent.append(copy)

    half = lay.width // 2
    for group, hot in enumerate(whole):
        for at in (0, half):
            send(group * lay.width + at, half, dot(hot, tokens_ref[:, at : at + half]))
    if lay.rest:
        pieces = [tokens_ref[:, at * lay.piece : (at + 1) * lay.piece] for at in range(lay.cuts)]
        send(
            lay.base,
            lay.piece,
            dot(jnp.concatenate(cut, axis=1), jnp.concatenate(pieces, axis=0)),
        )
    for copy in sent:
        copy.wait()


def send_grads_kernel(
    lay, ids_ref, slots_ref, tokens_ref, router_ref, cot_ref, out_ref, gates_ref
):
    logits = dot_nt(router_ref[...], tokens_ref[...])
    expert_at = iota(logits.shape, 0)
    picked = [
        jnp.sum(jnp.where(expert_at == ids_ref[k : k + 1, :], logits, 0.0), axis=0, keepdims=True)
        for k in range(2)
    ]
    gates = [jax.nn.sigmoid(picked[0] - picked[1]), jax.nn.sigmoid(picked[1] - picked[0])]
    gates_ref[0:1, :] = gates[0]
    gates_ref[1:2, :] = gates[1]
    cot = cot_ref[...].astype(F32)
    scaled = [(as_column(gate) * cot).astype(BF16) for gate in gates]
    experts = out_ref.shape[0] // GROUP
    ranks = [
        [targets(lay, experts, ids_ref[k : k + 1, :], slots_ref[k : k + 1, :])] for k in range(2)
    ]
    place(lay, ranks, scaled, out_ref)


def forward_kernel(lay, message_ref, win_ref, wout_ref, out_ref, hidden_ref, rows_ref, total_ref):
    step = pl.program_id(0)

    @pl.when(step == 0)
    def _():
        unpack(lay, message_ref, rows_ref)

    hidden = jnp.maximum(dot(rows_ref[...], win_ref[0]), 0.0).astype(BF16)
    hidden_ref[...] = hidden
    term = dot(hidden, wout_ref[0])

    @pl.when(step == 0)
    def _():
        total_ref[...] = term

    @pl.when(step > 0)
    def _():
        total_ref[...] += term

    @pl.when(step == pl.num_programs(0) - 1)
    def _():
        pack(lay, total_ref, out_ref)


def backward_kernel(lay, message_ref, hidden_ref, win_ref, wout_ref, out_ref, rows_ref, total_ref):
    step = pl.program_id(0)

    @pl.when(step == 0)
    def _():
        unpack(lay, message_ref, rows_ref)

    back = dot_nt(rows_ref[...], wout_ref[0])
    back = jnp.where(hidden_ref[...].astype(F32) > 0.0, back, 0.0).astype(BF16)
    term = dot_nt(back, win_ref[0])

    @pl.when(step == 0)
    def _():
        total_ref[...] = term

    @pl.when(step > 0)
    def _():
        total_ref[...] += term

    @pl.when(step == pl.num_programs(0) - 1)
    def _():
        pack(lay, total_ref, out_ref)


def column_targets(lay, experts, ids_ref, slots_ref):
    ids = [as_column(ids_ref[k : k + 1, :].astype(F32)).astype(jnp.int32) for k in range(2)]
    slots = [as_column(slots_ref[k : k + 1, :].astype(F32)).astype(jnp.int32) for k in range(2)]
    return ids, [targets(lay, experts, ids[k], slots[k]) for k in range(2)]


def split_in_two(x):
    high = x.astype(BF16)
    return high, (x - high.astype(F32)).astype(BF16)


def mix_kernel(
    lay,
    ids_ref,
    slots_ref,
    gates_ref,
    message_ref,
    cot_ref,
    tokens_ref,
    router_ref,
    mixed_ref,
    back_ref,
    partial_ref,
):
    experts = router_ref.shape[0]
    toks = tokens_ref.shape[0]
    ids, ranks = column_targets(lay, experts, ids_ref, slots_ref)
    gates = [as_column(gates_ref[k : k + 1, :]) for k in range(2)]
    cot = cot_ref[...].astype(F32)
    choice = [pick(lay, [ranks[k]], message_ref) for k in range(2)]
    mixed_ref[...] = (gates[0] * choice[0] + gates[1] * choice[1]).astype(BF16)
    actions = [jnp.sum(choice[k] * cot, axis=1, keepdims=True) for k in range(2)]
    slope = gates[0] * gates[1] * (actions[0] - actions[1])

    expert_at = iota((toks, experts), 1)
    signs = jnp.where(expert_at == ids[0], 1.0, 0.0) - jnp.where(expert_at == ids[1], 1.0, 0.0)
    high, low = split_in_two(signs * slope)
    router = router_ref[...]
    back_ref[...] = dot(high, router) + dot(low, router)

    expert_at = iota((experts, toks), 0)
    signs = jnp.where(expert_at == ids_ref[0:1, :], 1.0, 0.0) - jnp.where(
        expert_at == ids_ref[1:2, :], 1.0, 0.0
    )
    high, low = split_in_two(signs * as_row(slope))
    tokens = tokens_ref[...]
    partial_ref[...] = (dot(high, tokens) + dot(low, tokens)) * (1.0 / toks)


def grad_kernel(lay, ids_ref, slots_ref, message_ref, back_ref, out_ref):
    _, ranks = column_targets(lay, message_ref.shape[0] // GROUP, ids_ref, slots_ref)
    out_ref[...] = (pick(lay, ranks, message_ref) + back_ref[...]).astype(BF16)


def call(kernel, out_shape, flops, args, vmem_bytes=VMEM_BYTES):
    moved = sum(a.size * a.dtype.itemsize for a in args)
    moved += sum(o.size * o.dtype.itemsize for o in jax.tree.leaves(out_shape))
    return pl.pallas_call(
        kernel,
        out_shape=out_shape,
        compiler_params=pltpu.CompilerParams(vmem_limit_bytes=vmem_bytes),
        cost_estimate=pl.CostEstimate(flops=flops, bytes_accessed=moved, transcendentals=0),
    )(*args)


def expert_call(kernel, lay, message, hidden, in_weight, out_weight):
    count = message.shape[0]
    ff = in_weight.shape[2]
    tile = min(512, ff)
    rows = count // GROUP * lay.rows
    whole = pl.BlockSpec(message.shape, lambda j: (0, 0))
    win = pl.BlockSpec((1, lay.width, tile), lambda j: (0, 0, j))
    wout = pl.BlockSpec((1, tile, lay.width), lambda j: (0, j, 0))
    hid = pl.BlockSpec((rows, tile), lambda j: (0, j))
    forward = hidden is None
    operands = (message, in_weight, out_weight) if forward else (message, hidden, in_weight, out_weight)
    message_out = jax.ShapeDtypeStruct(message.shape, BF16)
    return pl.pallas_call(
        functools.partial(kernel, lay),
        grid=(ff // tile,),
        in_specs=[whole, win, wout] if forward else [whole, hid, win, wout],
        out_specs=[whole, hid] if forward else whole,
        out_shape=[message_out, jax.ShapeDtypeStruct((rows, ff), BF16)] if forward else message_out,
        scratch_shapes=[pltpu.VMEM((rows, lay.width), BF16), pltpu.VMEM((rows, lay.width), F32)],
        compiler_params=pltpu.CompilerParams(vmem_limit_bytes=VMEM_BYTES),
        cost_estimate=pl.CostEstimate(
            flops=4 * rows * lay.width * ff,
            bytes_accessed=4 * lay.width * ff + 2 * rows * ff + 4 * message.size,
            transcendentals=0,
        ),
    )(*operands)


def rank_of(device, devices):
    half = devices // 2
    return (device & (half - 1)) * 2 + jnp.where(device >= half, 1, 0)


def exchange(x, devices):
    order = [rank // 2 + rank % 2 * (devices // 2) for rank in range(devices)]
    return lax.all_to_all(
        x, AXES, split_axis=0, concat_axis=0, tiled=True, axis_index_groups=[order]
    )


def from_device(x, bits, devices):
    return lax.ppermute(x, AXES, [(d, d ^ bits) for d in range(devices)])


def sum_of_pairs(own, near, far, both):
    return (own + near) + (far + both)


def sum_over_devices(x, devices, beside):
    half = x.shape[0] // 2
    core = lax.axis_index("inner") % 2
    own = lax.dynamic_slice_in_dim(x, core * half, half, 0)
    other = lax.dynamic_slice_in_dim(x, (1 - core) * half, half, 0)
    own = own + from_device(other, 1, devices)
    sent = own.astype(BF16)
    terms = [sent] + [from_device(sent, bits, devices) for bits in (2, 4, 6)]
    own = sum_of_pairs(*[term.astype(F32) for term in terms])
    bit = PLANE
    while bit < devices:
        sent = own.astype(BF16)
        own = sent.astype(F32) + from_device(sent, bit, devices).astype(F32)
        bit *= 2
    beside, own = lax.optimization_barrier((beside, own))
    other = from_device(own, 1, devices)
    first = core == 0
    total = jnp.concatenate([jnp.where(first, own, other), jnp.where(first, other, own)], axis=0)
    return total, beside


def on_device(tokens, router_weight, in_weight, out_weight, expert_ids, slot_ids, cotangent):
    tok_rows, model_width = tokens.shape
    experts = router_weight.shape[1]
    devices = lax.axis_size("outer") * lax.axis_size("inner")
    lay = Layout(3 * tok_rows // experts, model_width)
    message = jax.ShapeDtypeStruct((experts * GROUP, lay.columns), BF16)
    ids, slots, router = expert_ids.T, slot_ids.T, router_weight.T
    place_flops = 4 * experts * GROUP * tok_rows * model_width

    sent_tokens = pl.pallas_call(
        functools.partial(send_tokens_kernel, lay),
        out_shape=message,
        in_specs=[pl.BlockSpec(memory_space=pl.ANY)] * 3,
        out_specs=pl.BlockSpec(memory_space=pl.ANY),
        scratch_shapes=[
            pltpu.VMEM(ids.shape, jnp.int32),
            pltpu.VMEM(slots.shape, jnp.int32),
            pltpu.VMEM(tokens.shape, BF16),
            pltpu.VMEM(message.shape, BF16),
            pltpu.SemaphoreType.DMA((3,)),
            pltpu.SemaphoreType.DMA((2 * lay.full + 1,)),
        ],
        compiler_params=pltpu.CompilerParams(vmem_limit_bytes=VMEM_BYTES),
        cost_estimate=pl.CostEstimate(
            flops=place_flops, bytes_accessed=2 * (tokens.size + message.size), transcendentals=0
        ),
    )(ids, slots, tokens)
    sent_grads, gates = call(
        functools.partial(send_grads_kernel, lay),
        [message, jax.ShapeDtypeStruct((2, tok_rows), F32)],
        2 * place_flops,
        (ids, slots, tokens, router, cotangent),
    )
    arrived = exchange(sent_tokens, devices)
    grad_rows = exchange(sent_grads, devices)
    produced, hidden = expert_call(forward_kernel, lay, arrived, None, in_weight, out_weight)
    produced, grad_rows = lax.optimization_barrier((produced, grad_rows))
    produced_back = exchange(produced, devices)
    returned = expert_call(backward_kernel, lay, grad_rows, hidden, in_weight, out_weight)
    returned, produced_back = lax.optimization_barrier((returned, produced_back))
    returned_back = exchange(returned, devices)

    mixed, router_back, partial_grad = call(
        functools.partial(mix_kernel, lay),
        [
            jax.ShapeDtypeStruct((tok_rows, model_width), BF16),
            jax.ShapeDtypeStruct((tok_rows, model_width), F32),
            jax.ShapeDtypeStruct((experts, model_width), F32),
        ],
        2 * place_flops,
        (ids, slots, gates, produced_back, cotangent, tokens, router),
        SMALL_VMEM_BYTES,
    )
    grad_router, returned_back = sum_over_devices(partial_grad, devices, returned_back)
    grad_tokens = call(
        functools.partial(grad_kernel, lay),
        jax.ShapeDtypeStruct((tok_rows, model_width), BF16),
        place_flops,
        (ids, slots, returned_back, router_back),
        SMALL_VMEM_BYTES,
    )
    return (mixed, grad_tokens, grad_router.T)


def solution(mesh):
    placed = (
        P(AXES, None),
        P(),
        P(AXES, None, None),
        P(AXES, None, None),
        P(AXES, None),
        P(AXES, None),
        P(AXES, None),
    )
    return jax.shard_map(
        on_device,
        mesh=mesh,
        in_specs=placed,
        out_specs=(P(AXES, None), P(AXES, None), P()),
        check_vma=False,
    )
```

```python
import functools

import jax
import jax.numpy as jnp
from jax import lax
from jax.experimental import pallas as pl
from jax.experimental.pallas import tpu as pltpu
from jax.sharding import PartitionSpec as P

AXES = ("outer", "inner")
F32 = jnp.float32
BF16 = jnp.bfloat16
GROUP = 8
PLANE = 8
VMEM_BYTES = 60 * 1024 * 1024
SMALL_VMEM_BYTES = 24 * 1024 * 1024


class Layout:
    def __init__(self, capacity, model_width):
        self.full, left = divmod(capacity, GROUP)
        self.rest = 0
        if left:
            self.rest = 1
            while self.rest < left:
                self.rest *= 2
        if self.rest == GROUP:
            self.full, self.rest = self.full + 1, 0
        self.capacity = capacity
        self.width = model_width
        self.cuts = GROUP // self.rest if self.rest else 1
        self.piece = model_width // self.cuts
        self.base = self.full * model_width
        self.columns = self.base + (self.piece if self.rest else 0)
        self.rows = self.full * GROUP + self.rest


def dot(a, b):
    return jnp.dot(a, b, preferred_element_type=F32)


def dot_nt(a, b):
    return lax.dot_general(a, b, (((1,), (1,)), ((), ())), preferred_element_type=F32)


def iota(shape, dim):
    return lax.broadcasted_iota(jnp.int32, shape, dim)


def as_column(row):
    count = row.shape[1]
    eye = iota((count, count), 0) == iota((count, count), 1)
    return jnp.sum(jnp.where(eye, row, 0.0), axis=1, keepdims=True)


def as_row(column):
    count = column.shape[0]
    eye = iota((count, count), 0) == iota((count, count), 1)
    return jnp.sum(jnp.where(eye, column, 0.0), axis=0, keepdims=True)


def targets(lay, ids, slots):
    found = []
    kept = slots < lay.capacity
    for group in range(lay.full):
        inside = kept & (slots >= group * GROUP) & (slots < (group + 1) * GROUP)
        found.append(jnp.where(inside, ids * GROUP + slots - group * GROUP, -1))
    if lay.rest:
        inside = kept & (slots >= lay.full * GROUP)
        found.append(jnp.where(inside, ids * GROUP + slots - lay.full * GROUP, -1))
    return found


def shifted(row, by):
    return jnp.where(row >= 0, row + by, -1)


def place(lay, row_targets, values, out_ref):
    count = out_ref.shape[0]
    toks = values[0].shape[0]
    row_at = iota((count, toks), 0)
    stacked = jnp.concatenate(values, axis=0) if len(values) > 1 else values[0]

    def onehot(rows):
        hit = functools.reduce(jnp.logical_or, [row_at == row for row in rows])
        return jnp.where(hit, 1.0, 0.0).astype(BF16)

    for group in range(lay.full):
        hot = [onehot([t[group] for t in ranks]) for ranks in row_targets]
        hot = jnp.concatenate(hot, axis=1) if len(hot) > 1 else hot[0]
        out_ref[:, group * lay.width : (group + 1) * lay.width] = dot(hot, stacked).astype(BF16)
    if lay.rest:
        hot, pieces = [], []
        for cut in range(lay.cuts):
            for ranks in row_targets:
                hot.append(onehot([shifted(t[lay.full], cut * lay.rest) for t in ranks]))
            pieces.append(stacked[:, cut * lay.piece : (cut + 1) * lay.piece])
        out_ref[:, lay.base :] = dot(
            jnp.concatenate(hot, axis=1), jnp.concatenate(pieces, axis=0)
        ).astype(BF16)


def pick(lay, ranks, message_ref):
    count = message_ref.shape[0]
    toks = ranks[0][0].shape[0]
    row_at = iota((toks, count), 1)

    def onehot(rows):
        hit = functools.reduce(jnp.logical_or, [row_at == row for row in rows])
        return jnp.where(hit, 1.0, 0.0).astype(BF16)

    whole = [onehot([t[group] for t in ranks]) for group in range(lay.full)]
    pieces = []
    for cut in range(lay.cuts):
        left = cut * lay.piece
        total = None
        for group in range(lay.full):
            start = group * lay.width + left
            term = dot(whole[group], message_ref[:, start : start + lay.piece])
            total = term if total is None else total + term
        if lay.rest:
            hot = onehot([shifted(t[lay.full], cut * lay.rest) for t in ranks])
            term = dot(hot, message_ref[:, lay.base : lay.base + lay.piece])
            total = term if total is None else total + term
        pieces.append(total)
    return jnp.concatenate(pieces, axis=1) if len(pieces) > 1 else pieces[0]


def rest_selection(lay, count):
    small = count // GROUP * lay.rest
    row = iota((small, count), 0)
    col = iota((small, count), 1)
    shift = lay.rest.bit_length() - 1
    home = lax.shift_right_logical(row, shift) * GROUP + (row & (lay.rest - 1))
    return [jnp.where(col == home + cut * lay.rest, 1.0, 0.0).astype(BF16) for cut in range(lay.cuts)]


def unpack(lay, message_ref, out_ref):
    count = message_ref.shape[0]
    for group in range(lay.full):
        out_ref[group * count : (group + 1) * count, :] = message_ref[
            :, group * lay.width : (group + 1) * lay.width
        ]
    if lay.rest:
        tail = message_ref[:, lay.base :]
        for cut, chosen in enumerate(rest_selection(lay, count)):
            out_ref[lay.full * count :, cut * lay.piece : (cut + 1) * lay.piece] = dot(
                chosen, tail
            ).astype(BF16)


def pack(lay, rows_ref, message_ref):
    count = message_ref.shape[0]
    for group in range(lay.full):
        message_ref[:, group * lay.width : (group + 1) * lay.width] = rows_ref[
            group * count : (group + 1) * count, :
        ].astype(BF16)
    if lay.rest:
        total = None
        for cut, chosen in enumerate(rest_selection(lay, count)):
            part = rows_ref[
                lay.full * count :, cut * lay.piece : (cut + 1) * lay.piece
            ].astype(BF16)
            term = lax.dot_general(
                chosen, part, (((0,), (0,)), ((), ())), preferred_element_type=F32
            )
            total = term if total is None else total + term
        message_ref[:, lay.base :] = total.astype(BF16)


def send_tokens_kernel(
    lay, ids_hbm, slots_hbm, tokens_hbm, out_hbm, ids_ref, slots_ref, tokens_ref, rows_ref, sems, out_sems
):
    pairs = ((ids_hbm, ids_ref), (slots_hbm, slots_ref), (tokens_hbm, tokens_ref))
    copies = [
        pltpu.make_async_copy(source, target, sems.at[at]) for at, (source, target) in enumerate(pairs)
    ]
    for copy in copies:
        copy.start()
    for copy in copies[:2]:
        copy.wait()
    count, toks = rows_ref.shape[0], tokens_ref.shape[0]
    row_at = iota((count, toks), 0)
    first, second = [
        targets(lay, ids_ref[k : k + 1, :], slots_ref[k : k + 1, :]) for k in range(2)
    ]

    def onehot(at, by):
        hit = (row_at == shifted(first[at], by)) | (row_at == shifted(second[at], by))
        return jnp.where(hit, 1.0, 0.0).astype(BF16)

    whole = [onehot(group, 0) for group in range(lay.full)]
    cut = [onehot(lay.full, at * lay.rest) for at in range(lay.cuts)] if lay.rest else []
    copies[2].wait()

    sent = []

    def send(start, width, values):
        rows_ref[:, start : start + width] = values.astype(BF16)
        copy = pltpu.make_async_copy(
            rows_ref.at[:, start : start + width],
            out_hbm.at[:, start : start + width],
            out_sems.at[len(sent)],
        )
        copy.start()
        sent.append(copy)

    half = lay.width // 2
    for group, hot in enumerate(whole):
        for at in (0, half):
            send(group * lay.width + at, half, dot(hot, tokens_ref[:, at : at + half]))
    if lay.rest:
        pieces = [tokens_ref[:, at * lay.piece : (at + 1) * lay.piece] for at in range(lay.cuts)]
        send(
            lay.base,
            lay.piece,
            dot(jnp.concatenate(cut, axis=1), jnp.concatenate(pieces, axis=0)),
        )
    for copy in sent:
        copy.wait()


def send_grads_kernel(
    lay, ids_ref, slots_ref, tokens_ref, router_ref, cot_ref, out_ref, gates_ref
):
    logits = dot_nt(router_ref[...], tokens_ref[...])
    expert_at = iota(logits.shape, 0)
    picked = [
        jnp.sum(jnp.where(expert_at == ids_ref[k : k + 1, :], logits, 0.0), axis=0, keepdims=True)
        for k in range(2)
    ]
    gates = [jax.nn.sigmoid(picked[0] - picked[1]), jax.nn.sigmoid(picked[1] - picked[0])]
    gates_ref[0:1, :] = gates[0]
    gates_ref[1:2, :] = gates[1]
    cot = cot_ref[...].astype(F32)
    scaled = [(as_column(gate) * cot).astype(BF16) for gate in gates]
    ranks = [[targets(lay, ids_ref[k : k + 1, :], slots_ref[k : k + 1, :])] for k in range(2)]
    place(lay, ranks, scaled, out_ref)


def forward_kernel(lay, message_ref, win_ref, wout_ref, out_ref, hidden_ref, rows_ref, total_ref):
    step = pl.program_id(0)

    @pl.when(step == 0)
    def _():
        unpack(lay, message_ref, rows_ref)

    hidden = jnp.maximum(dot(rows_ref[...], win_ref[0]), 0.0).astype(BF16)
    hidden_ref[...] = hidden
    term = dot(hidden, wout_ref[0])

    @pl.when(step == 0)
    def _():
        total_ref[...] = term

    @pl.when(step > 0)
    def _():
        total_ref[...] += term

    @pl.when(step == pl.num_programs(0) - 1)
    def _():
        pack(lay, total_ref, out_ref)


def backward_kernel(lay, message_ref, hidden_ref, win_ref, wout_ref, out_ref, rows_ref, total_ref):
    step = pl.program_id(0)

    @pl.when(step == 0)
    def _():
        unpack(lay, message_ref, rows_ref)

    back = dot_nt(rows_ref[...], wout_ref[0])
    back = jnp.where(hidden_ref[...].astype(F32) > 0.0, back, 0.0).astype(BF16)
    term = dot_nt(back, win_ref[0])

    @pl.when(step == 0)
    def _():
        total_ref[...] = term

    @pl.when(step > 0)
    def _():
        total_ref[...] += term

    @pl.when(step == pl.num_programs(0) - 1)
    def _():
        pack(lay, total_ref, out_ref)


def column_targets(lay, ids_ref, slots_ref):
    ids = [as_column(ids_ref[k : k + 1, :].astype(F32)).astype(jnp.int32) for k in range(2)]
    slots = [as_column(slots_ref[k : k + 1, :].astype(F32)).astype(jnp.int32) for k in range(2)]
    return ids, [targets(lay, ids[k], slots[k]) for k in range(2)]


def split_in_two(x):
    high = x.astype(BF16)
    return high, (x - high.astype(F32)).astype(BF16)


def mix_kernel(
    lay,
    ids_ref,
    slots_ref,
    gates_ref,
    message_ref,
    cot_ref,
    tokens_ref,
    router_ref,
    mixed_ref,
    back_ref,
    partial_ref,
):
    experts = router_ref.shape[0]
    toks = tokens_ref.shape[0]
    ids, ranks = column_targets(lay, ids_ref, slots_ref)
    gates = [as_column(gates_ref[k : k + 1, :]) for k in range(2)]
    cot = cot_ref[...].astype(F32)
    choice = [pick(lay, [ranks[k]], message_ref) for k in range(2)]
    mixed_ref[...] = (gates[0] * choice[0] + gates[1] * choice[1]).astype(BF16)
    actions = [jnp.sum(choice[k] * cot, axis=1, keepdims=True) for k in range(2)]
    slope = gates[0] * gates[1] * (actions[0] - actions[1])

    expert_at = iota((toks, experts), 1)
    signs = jnp.where(expert_at == ids[0], 1.0, 0.0) - jnp.where(expert_at == ids[1], 1.0, 0.0)
    high, low = split_in_two(signs * slope)
    router = router_ref[...]
    back_ref[...] = dot(high, router) + dot(low, router)

    expert_at = iota((experts, toks), 0)
    signs = jnp.where(expert_at == ids_ref[0:1, :], 1.0, 0.0) - jnp.where(
        expert_at == ids_ref[1:2, :], 1.0, 0.0
    )
    high, low = split_in_two(signs * as_row(slope))
    tokens = tokens_ref[...]
    partial_ref[...] = (dot(high, tokens) + dot(low, tokens)) * (1.0 / toks)


def grad_kernel(lay, ids_ref, slots_ref, message_ref, back_ref, out_ref):
    _, ranks = column_targets(lay, ids_ref, slots_ref)
    out_ref[...] = (pick(lay, ranks, message_ref) + back_ref[...]).astype(BF16)


def call(kernel, out_shape, flops, args, vmem_bytes=VMEM_BYTES):
    moved = sum(a.size * a.dtype.itemsize for a in args)
    moved += sum(o.size * o.dtype.itemsize for o in jax.tree.leaves(out_shape))
    return pl.pallas_call(
        kernel,
        out_shape=out_shape,
        compiler_params=pltpu.CompilerParams(vmem_limit_bytes=vmem_bytes),
        cost_estimate=pl.CostEstimate(flops=flops, bytes_accessed=moved, transcendentals=0),
    )(*args)


def expert_call(kernel, lay, message, hidden, in_weight, out_weight):
    count = message.shape[0]
    ff = in_weight.shape[2]
    tile = min(512, ff)
    rows = count // GROUP * lay.rows
    whole = pl.BlockSpec(message.shape, lambda j: (0, 0))
    win = pl.BlockSpec((1, lay.width, tile), lambda j: (0, 0, j))
    wout = pl.BlockSpec((1, tile, lay.width), lambda j: (0, j, 0))
    hid = pl.BlockSpec((rows, tile), lambda j: (0, j))
    forward = hidden is None
    operands = (message, in_weight, out_weight) if forward else (message, hidden, in_weight, out_weight)
    message_out = jax.ShapeDtypeStruct(message.shape, BF16)
    return pl.pallas_call(
        functools.partial(kernel, lay),
        grid=(ff // tile,),
        in_specs=[whole, win, wout] if forward else [whole, hid, win, wout],
        out_specs=[whole, hid] if forward else whole,
        out_shape=[message_out, jax.ShapeDtypeStruct((rows, ff), BF16)] if forward else message_out,
        scratch_shapes=[pltpu.VMEM((rows, lay.width), BF16), pltpu.VMEM((rows, lay.width), F32)],
        compiler_params=pltpu.CompilerParams(vmem_limit_bytes=VMEM_BYTES),
        cost_estimate=pl.CostEstimate(
            flops=4 * rows * lay.width * ff,
            bytes_accessed=4 * lay.width * ff + 2 * rows * ff + 4 * message.size,
            transcendentals=0,
        ),
    )(*operands)


def exchange(x):
    return lax.all_to_all(x, AXES, split_axis=0, concat_axis=0, tiled=True)


def from_device(x, bits, devices):
    return lax.ppermute(x, AXES, [(d, d ^ bits) for d in range(devices)])


def sum_of_pairs(own, near, far, both):
    return (own + near) + (far + both)


def sum_over_devices(x, devices, beside):
    half = x.shape[0] // 2
    core = lax.axis_index("inner") % 2
    own = lax.dynamic_slice_in_dim(x, core * half, half, 0)
    other = lax.dynamic_slice_in_dim(x, (1 - core) * half, half, 0)
    own = own + from_device(other, 1, devices)
    sent = own.astype(BF16)
    terms = [sent] + [from_device(sent, bits, devices) for bits in (2, 4, 6)]
    own = sum_of_pairs(*[term.astype(F32) for term in terms])
    bit = PLANE
    while bit < devices:
        sent = own.astype(BF16)
        own = sent.astype(F32) + from_device(sent, bit, devices).astype(F32)
        bit *= 2
    beside, own = lax.optimization_barrier((beside, own))
    other = from_device(own, 1, devices)
    mine = lax.broadcasted_iota(jnp.int32, (2, 1, 1), 0) == core
    total = jnp.where(mine, own[None], other[None]).reshape(x.shape)
    return total, beside


def on_device(tokens, router_weight, in_weight, out_weight, expert_ids, slot_ids, cotangent):
    tok_rows, model_width = tokens.shape
    experts = router_weight.shape[1]
    devices = lax.axis_size("outer") * lax.axis_size("inner")
    lay = Layout(3 * tok_rows // experts, model_width)
    message = jax.ShapeDtypeStruct((experts * GROUP, lay.columns), BF16)
    ids, slots, router = expert_ids.T, slot_ids.T, router_weight.T
    place_flops = 4 * experts * GROUP * tok_rows * model_width

    sent_tokens = pl.pallas_call(
        functools.partial(send_tokens_kernel, lay),
        out_shape=message,
        in_specs=[pl.BlockSpec(memory_space=pl.ANY)] * 3,
        out_specs=pl.BlockSpec(memory_space=pl.ANY),
        scratch_shapes=[
            pltpu.VMEM(ids.shape, jnp.int32),
            pltpu.VMEM(slots.shape, jnp.int32),
            pltpu.VMEM(tokens.shape, BF16),
            pltpu.VMEM(message.shape, BF16),
            pltpu.SemaphoreType.DMA((3,)),
            pltpu.SemaphoreType.DMA((2 * lay.full + 1,)),
        ],
        compiler_params=pltpu.CompilerParams(vmem_limit_bytes=VMEM_BYTES),
        cost_estimate=pl.CostEstimate(
            flops=place_flops, bytes_accessed=2 * (tokens.size + message.size), transcendentals=0
        ),
    )(ids, slots, tokens)
    sent_grads, gates = call(
        functools.partial(send_grads_kernel, lay),
        [message, jax.ShapeDtypeStruct((2, tok_rows), F32)],
        2 * place_flops,
        (ids, slots, tokens, router, cotangent),
    )
    arrived = exchange(sent_tokens)
    grad_rows = exchange(sent_grads)
    produced, hidden = expert_call(forward_kernel, lay, arrived, None, in_weight, out_weight)
    produced, grad_rows = lax.optimization_barrier((produced, grad_rows))
    produced_back = exchange(produced)
    returned = expert_call(backward_kernel, lay, grad_rows, hidden, in_weight, out_weight)
    returned, produced_back = lax.optimization_barrier((returned, produced_back))
    returned_back = exchange(returned)

    mixed, router_back, partial_grad = call(
        functools.partial(mix_kernel, lay),
        [
            jax.ShapeDtypeStruct((tok_rows, model_width), BF16),
            jax.ShapeDtypeStruct((tok_rows, model_width), F32),
            jax.ShapeDtypeStruct((experts, model_width), F32),
        ],
        2 * place_flops,
        (ids, slots, gates, produced_back, cotangent, tokens, router),
        SMALL_VMEM_BYTES,
    )
    grad_router, returned_back = sum_over_devices(partial_grad, devices, returned_back)
    grad_tokens = call(
        functools.partial(grad_kernel, lay),
        jax.ShapeDtypeStruct((tok_rows, model_width), BF16),
        place_flops,
        (ids, slots, returned_back, router_back),
        SMALL_VMEM_BYTES,
    )
    return (mixed, grad_tokens, grad_router.T)


def solution(mesh):
    placed = (
        P(AXES, None),
        P(),
        P(AXES, None, None),
        P(AXES, None, None),
        P(AXES, None),
        P(AXES, None),
        P(AXES, None),
    )
    return jax.shard_map(
        on_device,
        mesh=mesh,
        in_specs=placed,
        out_specs=(P(AXES, None), P(AXES, None), P()),
        check_vma=False,
    )
```

```python
import functools

import jax
import jax.numpy as jnp
from jax import lax
from jax.experimental import pallas as pl
from jax.experimental.pallas import tpu as pltpu
from jax.sharding import PartitionSpec as P

AXES = ("outer", "inner")
F32 = jnp.float32
BF16 = jnp.bfloat16
GROUP = 8
PLANE = 8
VMEM_BYTES = 60 * 1024 * 1024
SMALL_VMEM_BYTES = 24 * 1024 * 1024


class Layout:
    def __init__(self, capacity, model_width):
        self.full, left = divmod(capacity, GROUP)
        self.rest = 0
        if left:
            self.rest = 1
            while self.rest < left:
                self.rest *= 2
        if self.rest == GROUP:
            self.full, self.rest = self.full + 1, 0
        self.capacity = capacity
        self.width = model_width
        self.cuts = GROUP // self.rest if self.rest else 1
        self.piece = model_width // self.cuts
        self.base = self.full * model_width
        self.columns = self.base + (self.piece if self.rest else 0)
        self.rows = self.full * GROUP + self.rest


def dot(a, b):
    return jnp.dot(a, b, preferred_element_type=F32)


def dot_nt(a, b):
    return lax.dot_general(a, b, (((1,), (1,)), ((), ())), preferred_element_type=F32)


def iota(shape, dim):
    return lax.broadcasted_iota(jnp.int32, shape, dim)


def as_column(row):
    count = row.shape[1]
    eye = iota((count, count), 0) == iota((count, count), 1)
    return jnp.sum(jnp.where(eye, row, 0.0), axis=1, keepdims=True)


def as_row(column):
    count = column.shape[0]
    eye = iota((count, count), 0) == iota((count, count), 1)
    return jnp.sum(jnp.where(eye, column, 0.0), axis=0, keepdims=True)


def targets(lay, ids, slots):
    found = []
    kept = slots < lay.capacity
    for group in range(lay.full):
        inside = kept & (slots >= group * GROUP) & (slots < (group + 1) * GROUP)
        found.append(jnp.where(inside, ids * GROUP + slots - group * GROUP, -1))
    if lay.rest:
        inside = kept & (slots >= lay.full * GROUP)
        found.append(jnp.where(inside, ids * GROUP + slots - lay.full * GROUP, -1))
    return found


def shifted(row, by):
    return jnp.where(row >= 0, row + by, -1)


def place(lay, row_targets, values, out_ref):
    count = out_ref.shape[0]
    toks = values[0].shape[0]
    row_at = iota((count, toks), 0)
    stacked = jnp.concatenate(values, axis=0) if len(values) > 1 else values[0]

    def onehot(rows):
        hit = functools.reduce(jnp.logical_or, [row_at == row for row in rows])
        return jnp.where(hit, 1.0, 0.0).astype(BF16)

    for group in range(lay.full):
        hot = [onehot([t[group] for t in ranks]) for ranks in row_targets]
        hot = jnp.concatenate(hot, axis=1) if len(hot) > 1 else hot[0]
        out_ref[:, group * lay.width : (group + 1) * lay.width] = dot(hot, stacked).astype(BF16)
    if lay.rest:
        hot, pieces = [], []
        for cut in range(lay.cuts):
            for ranks in row_targets:
                hot.append(onehot([shifted(t[lay.full], cut * lay.rest) for t in ranks]))
            pieces.append(stacked[:, cut * lay.piece : (cut + 1) * lay.piece])
        out_ref[:, lay.base :] = dot(
            jnp.concatenate(hot, axis=1), jnp.concatenate(pieces, axis=0)
        ).astype(BF16)


def pick(lay, ranks, message_ref):
    count = message_ref.shape[0]
    toks = ranks[0][0].shape[0]
    row_at = iota((toks, count), 1)

    def onehot(rows):
        hit = functools.reduce(jnp.logical_or, [row_at == row for row in rows])
        return jnp.where(hit, 1.0, 0.0).astype(BF16)

    whole = [onehot([t[group] for t in ranks]) for group in range(lay.full)]
    pieces = []
    for cut in range(lay.cuts):
        left = cut * lay.piece
        total = None
        for group in range(lay.full):
            start = group * lay.width + left
            term = dot(whole[group], message_ref[:, start : start + lay.piece])
            total = term if total is None else total + term
        if lay.rest:
            hot = onehot([shifted(t[lay.full], cut * lay.rest) for t in ranks])
            term = dot(hot, message_ref[:, lay.base : lay.base + lay.piece])
            total = term if total is None else total + term
        pieces.append(total)
    return jnp.concatenate(pieces, axis=1) if len(pieces) > 1 else pieces[0]


def rest_selection(lay, count):
    small = count // GROUP * lay.rest
    row = iota((small, count), 0)
    col = iota((small, count), 1)
    shift = lay.rest.bit_length() - 1
    home = lax.shift_right_logical(row, shift) * GROUP + (row & (lay.rest - 1))
    return [jnp.where(col == home + cut * lay.rest, 1.0, 0.0).astype(BF16) for cut in range(lay.cuts)]


def unpack(lay, message_ref, out_ref):
    count = message_ref.shape[0]
    for group in range(lay.full):
        out_ref[group * count : (group + 1) * count, :] = message_ref[
            :, group * lay.width : (group + 1) * lay.width
        ]
    if lay.rest:
        tail = message_ref[:, lay.base :]
        for cut, chosen in enumerate(rest_selection(lay, count)):
            out_ref[lay.full * count :, cut * lay.piece : (cut + 1) * lay.piece] = dot(
                chosen, tail
            ).astype(BF16)


def pack(lay, rows_ref, message_ref):
    count = message_ref.shape[0]
    for group in range(lay.full):
        message_ref[:, group * lay.width : (group + 1) * lay.width] = rows_ref[
            group * count : (group + 1) * count, :
        ].astype(BF16)
    if lay.rest:
        total = None
        for cut, chosen in enumerate(rest_selection(lay, count)):
            part = rows_ref[
                lay.full * count :, cut * lay.piece : (cut + 1) * lay.piece
            ].astype(BF16)
            term = lax.dot_general(
                chosen, part, (((0,), (0,)), ((), ())), preferred_element_type=F32
            )
            total = term if total is None else total + term
        message_ref[:, lay.base :] = total.astype(BF16)


def send_tokens_kernel(
    lay, ids_hbm, slots_hbm, tokens_hbm, out_hbm, ids_ref, slots_ref, tokens_ref, rows_ref, sems, out_sems
):
    pairs = ((ids_hbm, ids_ref), (slots_hbm, slots_ref), (tokens_hbm, tokens_ref))
    copies = [
        pltpu.make_async_copy(source, target, sems.at[at]) for at, (source, target) in enumerate(pairs)
    ]
    for copy in copies:
        copy.start()
    for copy in copies[:2]:
        copy.wait()
    count, toks = rows_ref.shape[0], tokens_ref.shape[0]
    row_at = iota((count, toks), 0)
    first, second = [
        targets(lay, ids_ref[k : k + 1, :], slots_ref[k : k + 1, :]) for k in range(2)
    ]

    def onehot(at, by):
        hit = (row_at == shifted(first[at], by)) | (row_at == shifted(second[at], by))
        return jnp.where(hit, 1.0, 0.0).astype(BF16)

    whole = [onehot(group, 0) for group in range(lay.full)]
    cut = [onehot(lay.full, at * lay.rest) for at in range(lay.cuts)] if lay.rest else []
    copies[2].wait()

    sent = []

    def send(start, width, values):
        rows_ref[:, start : start + width] = values.astype(BF16)
        copy = pltpu.make_async_copy(
            rows_ref.at[:, start : start + width],
            out_hbm.at[:, start : start + width],
            out_sems.at[len(sent)],
        )
        copy.start()
        sent.append(copy)

    half = lay.width // 2
    for group, hot in enumerate(whole):
        for at in (0, half):
            send(group * lay.width + at, half, dot(hot, tokens_ref[:, at : at + half]))
    if lay.rest:
        pieces = [tokens_ref[:, at * lay.piece : (at + 1) * lay.piece] for at in range(lay.cuts)]
        send(
            lay.base,
            lay.piece,
            dot(jnp.concatenate(cut, axis=1), jnp.concatenate(pieces, axis=0)),
        )
    for copy in sent:
        copy.wait()


def send_grads_kernel(
    lay, ids_ref, slots_ref, tokens_ref, router_ref, cot_ref, out_ref, gates_ref
):
    logits = dot_nt(router_ref[...], tokens_ref[...])
    expert_at = iota(logits.shape, 0)
    picked = [
        jnp.sum(jnp.where(expert_at == ids_ref[k : k + 1, :], logits, 0.0), axis=0, keepdims=True)
        for k in range(2)
    ]
    gates = [jax.nn.sigmoid(picked[0] - picked[1]), jax.nn.sigmoid(picked[1] - picked[0])]
    gates_ref[0:1, :] = gates[0]
    gates_ref[1:2, :] = gates[1]
    cot = cot_ref[...].astype(F32)
    scaled = [(as_column(gate) * cot).astype(BF16) for gate in gates]
    ranks = [[targets(lay, ids_ref[k : k + 1, :], slots_ref[k : k + 1, :])] for k in range(2)]
    place(lay, ranks, scaled, out_ref)


def forward_kernel(lay, message_ref, win_ref, wout_ref, out_ref, hidden_ref, rows_ref, total_ref):
    step = pl.program_id(0)

    @pl.when(step == 0)
    def _():
        unpack(lay, message_ref, rows_ref)

    hidden = jnp.maximum(dot(rows_ref[...], win_ref[0]), 0.0).astype(BF16)
    hidden_ref[...] = hidden
    term = dot(hidden, wout_ref[0])

    @pl.when(step == 0)
    def _():
        total_ref[...] = term

    @pl.when(step > 0)
    def _():
        total_ref[...] += term

    @pl.when(step == pl.num_programs(0) - 1)
    def _():
        pack(lay, total_ref, out_ref)


def backward_kernel(lay, message_ref, hidden_ref, win_ref, wout_ref, out_ref, rows_ref, total_ref):
    step = pl.program_id(0)

    @pl.when(step == 0)
    def _():
        unpack(lay, message_ref, rows_ref)

    back = dot_nt(rows_ref[...], wout_ref[0])
    back = jnp.where(hidden_ref[...].astype(F32) > 0.0, back, 0.0).astype(BF16)
    term = dot_nt(back, win_ref[0])

    @pl.when(step == 0)
    def _():
        total_ref[...] = term

    @pl.when(step > 0)
    def _():
        total_ref[...] += term

    @pl.when(step == pl.num_programs(0) - 1)
    def _():
        pack(lay, total_ref, out_ref)


def column_targets(lay, ids_ref, slots_ref):
    ids = [as_column(ids_ref[k : k + 1, :].astype(F32)).astype(jnp.int32) for k in range(2)]
    slots = [as_column(slots_ref[k : k + 1, :].astype(F32)).astype(jnp.int32) for k in range(2)]
    return ids, [targets(lay, ids[k], slots[k]) for k in range(2)]


def split_in_two(x):
    high = x.astype(BF16)
    return high, (x - high.astype(F32)).astype(BF16)


def mix_kernel(
    lay,
    ids_ref,
    slots_ref,
    gates_ref,
    message_ref,
    cot_ref,
    tokens_ref,
    router_ref,
    mixed_ref,
    back_ref,
    partial_ref,
):
    experts = router_ref.shape[0]
    toks = tokens_ref.shape[0]
    ids, ranks = column_targets(lay, ids_ref, slots_ref)
    gates = [as_column(gates_ref[k : k + 1, :]) for k in range(2)]
    cot = cot_ref[...].astype(F32)
    choice = [pick(lay, [ranks[k]], message_ref) for k in range(2)]
    mixed_ref[...] = (gates[0] * choice[0] + gates[1] * choice[1]).astype(BF16)
    actions = [jnp.sum(choice[k] * cot, axis=1, keepdims=True) for k in range(2)]
    slope = gates[0] * gates[1] * (actions[0] - actions[1])

    expert_at = iota((toks, experts), 1)
    signs = jnp.where(expert_at == ids[0], 1.0, 0.0) - jnp.where(expert_at == ids[1], 1.0, 0.0)
    high, low = split_in_two(signs * slope)
    router = router_ref[...]
    back_ref[...] = dot(high, router) + dot(low, router)

    expert_at = iota((experts, toks), 0)
    signs = jnp.where(expert_at == ids_ref[0:1, :], 1.0, 0.0) - jnp.where(
        expert_at == ids_ref[1:2, :], 1.0, 0.0
    )
    high, low = split_in_two(signs * as_row(slope))
    tokens = tokens_ref[...]
    partial_ref[...] = (dot(high, tokens) + dot(low, tokens)) * (1.0 / toks)


def grad_kernel(lay, ids_ref, slots_ref, message_ref, back_ref, out_ref):
    _, ranks = column_targets(lay, ids_ref, slots_ref)
    out_ref[...] = (pick(lay, ranks, message_ref) + back_ref[...]).astype(BF16)


def call(kernel, out_shape, flops, args, vmem_bytes=VMEM_BYTES):
    moved = sum(a.size * a.dtype.itemsize for a in args)
    moved += sum(o.size * o.dtype.itemsize for o in jax.tree.leaves(out_shape))
    return pl.pallas_call(
        kernel,
        out_shape=out_shape,
        compiler_params=pltpu.CompilerParams(vmem_limit_bytes=vmem_bytes),
        cost_estimate=pl.CostEstimate(flops=flops, bytes_accessed=moved, transcendentals=0),
    )(*args)


def expert_call(kernel, lay, message, hidden, in_weight, out_weight):
    count = message.shape[0]
    ff = in_weight.shape[2]
    tile = min(512, ff)
    rows = count // GROUP * lay.rows
    whole = pl.BlockSpec(message.shape, lambda j: (0, 0))
    win = pl.BlockSpec((1, lay.width, tile), lambda j: (0, 0, j))
    wout = pl.BlockSpec((1, tile, lay.width), lambda j: (0, j, 0))
    hid = pl.BlockSpec((rows, tile), lambda j: (0, j))
    forward = hidden is None
    operands = (message, in_weight, out_weight) if forward else (message, hidden, in_weight, out_weight)
    message_out = jax.ShapeDtypeStruct(message.shape, BF16)
    return pl.pallas_call(
        functools.partial(kernel, lay),
        grid=(ff // tile,),
        in_specs=[whole, win, wout] if forward else [whole, hid, win, wout],
        out_specs=[whole, hid] if forward else whole,
        out_shape=[message_out, jax.ShapeDtypeStruct((rows, ff), BF16)] if forward else message_out,
        scratch_shapes=[pltpu.VMEM((rows, lay.width), BF16), pltpu.VMEM((rows, lay.width), F32)],
        compiler_params=pltpu.CompilerParams(vmem_limit_bytes=VMEM_BYTES),
        cost_estimate=pl.CostEstimate(
            flops=4 * rows * lay.width * ff,
            bytes_accessed=4 * lay.width * ff + 2 * rows * ff + 4 * message.size,
            transcendentals=0,
        ),
    )(*operands)


def exchange(x):
    return lax.all_to_all(x, AXES, split_axis=0, concat_axis=0, tiled=True)


def from_device(x, bits, devices):
    return lax.ppermute(x, AXES, [(d, d ^ bits) for d in range(devices)])


def sum_of_pairs(own, near, far, both):
    return (own + near) + (far + both)


def sum_over_devices(x, devices, beside):
    half = x.shape[0] // 2
    core = lax.axis_index("inner") % 2
    own = lax.dynamic_slice_in_dim(x, core * half, half, 0)
    other = lax.dynamic_slice_in_dim(x, (1 - core) * half, half, 0)
    own = own + from_device(other.astype(BF16), 1, devices).astype(F32)
    sent = own.astype(BF16)
    terms = [sent] + [from_device(sent, bits, devices) for bits in (2, 4, 6)]
    own = sum_of_pairs(*[term.astype(F32) for term in terms])
    bit = PLANE
    while bit < devices:
        sent = own.astype(BF16)
        own = sent.astype(F32) + from_device(sent, bit, devices).astype(F32)
        bit *= 2
    beside, own = lax.optimization_barrier((beside, own))
    other = from_device(own, 1, devices)
    first = core == 0
    total = jnp.concatenate([jnp.where(first, own, other), jnp.where(first, other, own)], axis=0)
    return total, beside


def on_device(tokens, router_weight, in_weight, out_weight, expert_ids, slot_ids, cotangent):
    tok_rows, model_width = tokens.shape
    experts = router_weight.shape[1]
    devices = lax.axis_size("outer") * lax.axis_size("inner")
    lay = Layout(3 * tok_rows // experts, model_width)
    message = jax.ShapeDtypeStruct((experts * GROUP, lay.columns), BF16)
    ids, slots, router = expert_ids.T, slot_ids.T, router_weight.T
    place_flops = 4 * experts * GROUP * tok_rows * model_width

    sent_tokens = pl.pallas_call(
        functools.partial(send_tokens_kernel, lay),
        out_shape=message,
        in_specs=[pl.BlockSpec(memory_space=pl.ANY)] * 3,
        out_specs=pl.BlockSpec(memory_space=pl.ANY),
        scratch_shapes=[
            pltpu.VMEM(ids.shape, jnp.int32),
            pltpu.VMEM(slots.shape, jnp.int32),
            pltpu.VMEM(tokens.shape, BF16),
            pltpu.VMEM(message.shape, BF16),
            pltpu.SemaphoreType.DMA((3,)),
            pltpu.SemaphoreType.DMA((2 * lay.full + 1,)),
        ],
        compiler_params=pltpu.CompilerParams(vmem_limit_bytes=VMEM_BYTES),
        cost_estimate=pl.CostEstimate(
            flops=place_flops, bytes_accessed=2 * (tokens.size + message.size), transcendentals=0
        ),
    )(ids, slots, tokens)
    sent_grads, gates = call(
        functools.partial(send_grads_kernel, lay),
        [message, jax.ShapeDtypeStruct((2, tok_rows), F32)],
        2 * place_flops,
        (ids, slots, tokens, router, cotangent),
    )
    arrived = exchange(sent_tokens)
    grad_rows = exchange(sent_grads)
    produced, hidden = expert_call(forward_kernel, lay, arrived, None, in_weight, out_weight)
    produced, grad_rows = lax.optimization_barrier((produced, grad_rows))
    produced_back = exchange(produced)
    returned = expert_call(backward_kernel, lay, grad_rows, hidden, in_weight, out_weight)
    returned, produced_back = lax.optimization_barrier((returned, produced_back))
    returned_back = exchange(returned)

    mixed, router_back, partial_grad = call(
        functools.partial(mix_kernel, lay),
        [
            jax.ShapeDtypeStruct((tok_rows, model_width), BF16),
            jax.ShapeDtypeStruct((tok_rows, model_width), F32),
            jax.ShapeDtypeStruct((experts, model_width), F32),
        ],
        2 * place_flops,
        (ids, slots, gates, produced_back, cotangent, tokens, router),
        SMALL_VMEM_BYTES,
    )
    grad_router, returned_back = sum_over_devices(partial_grad, devices, returned_back)
    grad_tokens = call(
        functools.partial(grad_kernel, lay),
        jax.ShapeDtypeStruct((tok_rows, model_width), BF16),
        place_flops,
        (ids, slots, returned_back, router_back),
        SMALL_VMEM_BYTES,
    )
    return (mixed, grad_tokens, grad_router.T)


def solution(mesh):
    placed = (
        P(AXES, None),
        P(),
        P(AXES, None, None),
        P(AXES, None, None),
        P(AXES, None),
        P(AXES, None),
        P(AXES, None),
    )
    return jax.shard_map(
        on_device,
        mesh=mesh,
        in_specs=placed,
        out_specs=(P(AXES, None), P(AXES, None), P()),
        check_vma=False,
    )
```
